32 devices in a mesh: members: 2 (over y), lon: 16 (over z, x, core).
Axes of the slice: x: 2, y: 2, z: 4, core: 2. Of those that a mesh axis runs over, the one named last changes fastest.
Arguments:
- source: float32 [1024, 2240], P(('members', 'lon')), parts along dimension 0, may hold values from -6 to 6
- diagonal: float32 [1024, 2240], P(('members', 'lon')), parts along dimension 0, may hold values from 0.02 to 0.5
- u_vel: float32 [6, 1024, 2240], P(None, ('members', 'lon')), parts along dimension 1, may hold values from -6 to 6
- v_vel: float32 [6, 1024, 2240], P(None, ('members', 'lon')), parts along dimension 1, may hold values from -6 to 6
- bottom: int32 [1024, 2240], P(('members', 'lon')), parts along dimension 0, may hold values from 0 to 6
Outputs:
- surface: float32 [1024, 2240], P(('members', 'lon')), parts along dimension 0
- u_new: float32 [6, 1024, 2240], P(None, ('members', 'lon')), parts along dimension 1
- v_new: float32 [6, 1024, 2240], P(None, ('members', 'lon')), parts along dimension 1
- w_vel: float32 [6, 1024, 2240], P(None, ('members', 'lon')), parts along dimension 1
The draws below stay inside these ranges and needn't reach their ends.
There are 2 independent parts, one for each index of `members`. The reference program is written for one: setup_inputs(seed, part) draws one part's arguments, and reference() takes and returns one part's arrays. A program takes and returns all parts, laid end to end along the dimension named above; each array names one. Nothing has to cross between parts.
All inputs are finite; a program needn't handle non-finite values.
Results may differ from the reference program's by a relative error of at most 0.0001.
Values sent between devices are 32-bit elements; how exact they have to be, the bound alone decides.
No kernel may reach another device: no remote copies, remote signals or barrier semaphores. Data moves between devices by JAX's collectives and lax.ppermute only.
A program may use at most 64 MiB of HBM per device.

```python
import math
import jax
import jax.numpy as jnp
from jax import lax

CX = 32
LT = 112
OV = 8
NT = 20
KL = 6
ITERS = 2
NX = 512
NY = 2240
N_LON = 16


def with_ends(array, own_key, smallest, largest):
    index_at = [jax.random.randint(jax.random.fold_in(own_key, axis), (), 0, length) for axis, length in enumerate(array.shape)]
    main_axis = array.shape.index(max(array.shape))
    beside = index_at[:main_axis] + [(index_at[main_axis] + 1) % array.shape[main_axis]] + index_at[main_axis + 1:]
    return array.at[tuple(index_at)].set(smallest).at[tuple(beside)].set(largest)


def level_of(stream_key, extent, shards, least, largest):
    loudness = 1.0
    for position, parts in shards:
        draws = jax.random.uniform(jax.random.fold_in(jax.random.fold_in(stream_key, 6), position), (parts,), jnp.float32, least / len(shards), largest / len(shards))
        loudness = loudness * jnp.repeat(jnp.exp(draws), extent[position] // parts).reshape((-1,) + (1,) * (len(extent) - 1 - position))
    return loudness


def gaussian(own_key, shape, spread, bound, shards=(), held_as=jnp.bfloat16):
    result = spread * jax.random.normal(own_key, shape, jnp.float32)
    if shards:
        result = result * level_of(own_key, shape, shards, -0.22, 0.18)
    return jnp.clip(result, -bound, bound).astype(held_as)


def setup_inputs(seed: int = 0, part: int = 0) -> dict:
    keys = jax.random.split(jax.random.key(seed), 6)
    own_keys = jax.random.split(jax.random.fold_in(keys[5], part), 6)
    return {
        "source": gaussian(own_keys[0], (NX, NY), 1.0, 6.0, ((0, 16),), jnp.float32),
        "diagonal": jnp.clip(jnp.exp(math.log(0.5) - 3.218876 * jax.random.uniform(own_keys[1], (NX, NY), jnp.float32) ** level_of(own_keys[1], (NX, NY), ((0, 16),), -0.2, 0.2)), 0.02, 0.5),
        "u_vel": gaussian(own_keys[2], (KL, NX, NY), 1.0, 6.0, ((1, 16),), jnp.float32),
        "v_vel": gaussian(own_keys[3], (KL, NX, NY), 1.0, 6.0, ((1, 16),), jnp.float32),
        "bottom": with_ends(jax.random.randint(own_keys[4], (NX, NY), 0, KL + 1), jax.random.fold_in(own_keys[4], 1), 0, KL).astype(jnp.int32),
    }


tile_shift = 0.1
gravity_step = 0.5

def sine_basis(length):
    ordinal = jnp.arange(length, dtype=jnp.float32) + 1.0
    angles = math.pi * ordinal[:, None] * ordinal[None, :] / (length + 1)
    basis_matrix = jnp.sqrt(2.0 / (length + 1)) * jnp.sin(angles)
    eigen_value = 2.0 - 2.0 * jnp.cos(math.pi * ordinal / (length + 1))
    return (basis_matrix, eigen_value)

def split_windows(padded, block_len, blocks, margin):
    leading = padded.shape[:-1]
    extra_cols = block_len * (blocks + 1) - padded.shape[-1]
    padded = jnp.pad(padded, [(0, 0)] * len(leading) + [(0, extra_cols)])
    main_part = padded[..., :block_len * blocks].reshape(leading + (blocks, block_len))
    tail_part = padded[..., block_len:block_len * (blocks + 1)].reshape(leading + (blocks, block_len))[..., :2 * margin]
    return jnp.concatenate([main_part, tail_part], axis=-1)

def join_windows(windows, block_len, blocks, margin):
    leading = windows.shape[:-2]
    main_part = windows[..., :block_len].reshape(leading + (blocks * block_len,))
    tail_part = jnp.pad(windows[..., block_len:], [(0, 0)] * (len(leading) + 1) + [(0, block_len - 2 * margin)])
    tail_part = tail_part.reshape(leading + (blocks * block_len,))
    widths = [(0, 0)] * len(leading)
    summed = jnp.pad(main_part, widths + [(0, block_len)]) + jnp.pad(tail_part, widths + [(block_len, 0)])
    return summed[..., :block_len * blocks + 2 * margin]

def precondition(residue, wet_mask, lon_basis, lon_value, lat_basis, lat_value):
    highest = lax.Precision.HIGHEST
    masked = wet_mask * residue
    padded = jnp.pad(masked, ((0, 0), (OV, OV)))
    lat_windows = split_windows(padded, LT, NT, OV)
    rolled = jnp.roll(lat_windows, OV, axis=0)
    cycle_rows = jnp.concatenate([rolled, rolled[:2 * OV]], axis=0)
    cycle_rows = jnp.transpose(cycle_rows, (1, 2, 0))
    windows = split_windows(cycle_rows, CX, N_LON, OV)
    spectral = jnp.einsum('tbia,ac->tbic', windows, lon_basis, precision=highest)
    spectral = jnp.einsum('tbic,bd->tdic', spectral, lat_basis, precision=highest)
    spectral = spectral / (lat_value[None, :, None, None] + lon_value[None, None, None, :] + tile_shift)
    restored = jnp.einsum('tdic,bd->tbic', spectral, lat_basis, precision=highest)
    restored = jnp.einsum('tbic,ac->tbia', restored, lon_basis, precision=highest)
    joined = join_windows(restored, CX, N_LON, OV)
    centre = joined[..., OV:OV + NX]
    centre = centre.at[..., NX - OV:].add(joined[..., :OV])
    centre = centre.at[..., :OV].add(joined[..., NX + OV:])
    lat_rows = jnp.transpose(centre, (2, 0, 1))
    full_rows = join_windows(lat_rows, LT, NT, OV)[:, OV:OV + NY]
    return wet_mask * full_rows + (1.0 - wet_mask) * residue

def operate(field, wet_mask, diagonal):
    masked = wet_mask * field
    beside = jnp.roll(masked, 1, axis=0) + jnp.roll(masked, -1, axis=0)
    padded = jnp.pad(masked, ((0, 0), (1, 1)))
    beside = beside + padded[:, 2:] + padded[:, :-2]
    return wet_mask * ((4.0 + diagonal) * field - beside) + (1.0 - wet_mask) * field

def reference(source, diagonal, u_vel, v_vel, bottom):
    wet_mask = (bottom > 0).astype(jnp.float32)
    lon_basis, lon_value = sine_basis(CX + 2 * OV)
    lat_basis, lat_value = sine_basis(LT + 2 * OV)
    solution = jnp.zeros_like(source)
    residue = source
    precond = precondition(residue, wet_mask, lon_basis, lon_value, lat_basis, lat_value)
    norm_now = jnp.sum(residue * precond)
    direction = precond
    for iteration in range(ITERS):
        image = operate(direction, wet_mask, diagonal)
        step_length = norm_now / jnp.sum(direction * image)
        solution = solution + step_length * direction
        residue = residue - step_length * image
        if iteration + 1 < ITERS:
            precond = precondition(residue, wet_mask, lon_basis, lon_value, lat_basis, lat_value)
            norm_next = jnp.sum(residue * precond)
            direction = precond + norm_next / norm_now * direction
            norm_now = norm_next
    levels = jnp.arange(KL, dtype=jnp.int32).reshape(KL, 1, 1)
    east_depth = jnp.roll(bottom, -1, axis=0)
    u_face = (levels < jnp.minimum(bottom, east_depth)[None]).astype(jnp.float32)
    u_new = u_face * (u_vel - gravity_step * (jnp.roll(solution, -1, axis=0) - solution)[None])
    north_depth = jnp.concatenate([bottom[:, 1:], jnp.zeros_like(bottom[:, :1])], axis=1)
    north_surface = jnp.concatenate([solution[:, 1:], jnp.zeros_like(solution[:, :1])], axis=1)
    v_face = (levels < jnp.minimum(bottom, north_depth)[None]).astype(jnp.float32)
    v_new = v_face * (v_vel - gravity_step * (north_surface - solution)[None])
    wet_levels = (levels < bottom[None]).astype(jnp.float32)
    south_v = jnp.pad(v_new[:, :, :-1], ((0, 0), (0, 0), (1, 0)))
    divergence = wet_levels * (u_new - jnp.roll(u_new, 1, axis=1) + (v_new - south_v))
    w_vel = jnp.cumsum(divergence[::-1], axis=0)[::-1]
    return (solution, u_new, v_new, w_vel)
```

```python
import math

import jax
import jax.numpy as jnp
from jax import lax
from jax.sharding import PartitionSpec as P

LT = 112
OV = 8
KL = 6
ITERS = 2


tile_shift = 0.1
gravity_step = 0.5


def sine_basis(length):
    ordinal = jnp.arange(length, dtype=jnp.float32) + 1.0
    angles = math.pi * ordinal[:, None] * ordinal[None, :] / (length + 1)
    basis_matrix = jnp.sqrt(2.0 / (length + 1)) * jnp.sin(angles)
    eigen_value = 2.0 - 2.0 * jnp.cos(math.pi * ordinal / (length + 1))
    return (basis_matrix, eigen_value)


def split_windows(padded, block_len, blocks, margin):
    leading = padded.shape[:-1]
    extra_cols = block_len * (blocks + 1) - padded.shape[-1]
    padded = jnp.pad(padded, [(0, 0)] * len(leading) + [(0, extra_cols)])
    main_part = padded[..., : block_len * blocks].reshape(leading + (blocks, block_len))
    tail_part = padded[..., block_len : block_len * (blocks + 1)].reshape(
        leading + (blocks, block_len)
    )[..., : 2 * margin]
    return jnp.concatenate([main_part, tail_part], axis=-1)


def join_windows(windows, block_len, blocks, margin):
    leading = windows.shape[:-2]
    main_part = windows[..., :block_len].reshape(leading + (blocks * block_len,))
    tail_part = jnp.pad(
        windows[..., block_len:], [(0, 0)] * (len(leading) + 1) + [(0, block_len - 2 * margin)]
    )
    tail_part = tail_part.reshape(leading + (blocks * block_len,))
    widths = [(0, 0)] * len(leading)
    summed = jnp.pad(main_part, widths + [(0, block_len)]) + jnp.pad(
        tail_part, widths + [(block_len, 0)]
    )
    return summed[..., : block_len * blocks + 2 * margin]


def swap_pairs(block, outward):
    devices = lax.axis_size("lon")
    if outward:
        route = [(i, (i - 1 if i % 2 == 0 else i + 1) % devices) for i in range(devices)]
    else:
        route = [(i, i ^ 1) for i in range(devices)]
    return lax.ppermute(block, "lon", route)


def exchange(to_west, to_east):
    even = lax.axis_index("lon") % 2 == 0
    inner = swap_pairs(jnp.where(even, to_east, to_west), False)
    outer = swap_pairs(jnp.where(even, to_west, to_east), True)
    return jnp.where(even, outer, inner), jnp.where(even, inner, outer)


def total(parts):
    devices = lax.axis_size("lon")
    sent = jnp.broadcast_to(parts[None], (devices,) + parts.shape)
    return jnp.sum(lax.all_to_all(sent, "lon", 0, 0), axis=0)


def body(source, diagonal, u_vel, v_vel, bottom):
    highest = lax.Precision.HIGHEST
    cells, lat_cells = source.shape
    tiles = lat_cells // LT
    depths = bottom.astype(jnp.float32)
    wet = (bottom > 0).astype(jnp.float32)
    coef = wet * (4.0 + diagonal)
    masked = wet * source
    lon_basis, lon_value = sine_basis(cells + 2 * OV)
    lat_basis, lat_value = sine_basis(LT + 2 * OV)

    def tile_solve(rows):
        padded = jnp.pad(rows, ((0, 0), (OV, OV)))
        windows = split_windows(padded, LT, tiles, OV)
        spectral = jnp.einsum("atb,ac->ctb", windows, lon_basis, precision=highest)
        spectral = jnp.einsum("ctb,bd->ctd", spectral, lat_basis, precision=highest)
        spectral = spectral / (lon_value[:, None, None] + lat_value[None, None, :] + tile_shift)
        restored = jnp.einsum("ctd,bd->ctb", spectral, lat_basis, precision=highest)
        restored = jnp.einsum("ctb,ac->atb", restored, lon_basis, precision=highest)
        return join_windows(restored, LT, tiles, OV)[:, OV : OV + lat_cells]

    def lat_beside(x):
        p = jnp.pad(x, ((0, 0), (1, 1)))
        return p[:, 2:] + p[:, :-2]

    west, east = exchange(masked[:OV], masked[cells - OV :])
    first = tile_solve(jnp.concatenate([west, masked, east], axis=0))
    edge = OV + 1
    west, east = exchange(
        jnp.concatenate([first[: 2 * OV + 1], coef[:edge]], axis=0),
        jnp.concatenate([first[cells - 1 :], coef[cells - edge :]], axis=0),
    )
    wide = 2 * OV + 1
    z = jnp.pad(first, ((1, 1), (0, 0)))
    z = z + jnp.concatenate(
        [west[:wide], jnp.zeros((cells + 2 * edge - 2 * wide, lat_cells)), east[:wide]], axis=0
    )
    coef_wide = jnp.concatenate([west[wide:], coef, east[wide:]], axis=0)
    z = jnp.where(coef_wide > 0, z, 0.0)
    inner = coef_wide[1:-1]
    y = jnp.where(inner > 0, inner * z[1:-1] - (z[:-2] + z[2:] + lat_beside(z[1:-1])), 0.0)

    second = tile_solve(y)
    west, east = exchange(
        jnp.concatenate([second[: OV + 1], depths[:1], jnp.zeros((KL, lat_cells))], axis=0),
        jnp.concatenate([second[cells + OV - 1 :], depths[-1:], u_vel[:, cells - 1]], axis=0),
    )
    w = second[OV - 1 : cells + OV + 1]
    w = w + jnp.concatenate(
        [west[: OV + 1], jnp.zeros((cells + 2 - 2 * edge, lat_cells)), east[: OV + 1]], axis=0
    )
    near = coef_wide[OV : cells + OV + 2]
    w = jnp.where(near > 0, w, 0.0)
    z_near = z[OV : cells + OV + 2]
    wet_own = wet > 0
    x = jnp.where(wet_own, coef * w[1:-1] - (w[:-2] + w[2:] + lat_beside(w[1:-1])), 0.0)
    z_own, w_own, y_own = z_near[1:-1], w[1:-1], y[OV : cells + OV]
    land = source - masked

    def partial(a, b):
        return jnp.sum(a * b, axis=0)

    sums = total(
        jnp.stack(
            [
                partial(masked, z_own),
                partial(z_own, y_own),
                partial(masked, w_own),
                partial(y_own, w_own),
                partial(z_own, x),
                partial(w_own, x),
                partial(land, land),
            ]
        ).reshape(7, -1, LT).sum(axis=1)
    )
    rz, zy, rw, yw, zx, wx, ll = [jnp.sum(sums[i]) for i in range(7)]
    step0 = (rz + ll) / (zy + ll)
    rest = (zy - rz) / (zy + ll)
    new = rz - step0 * (zy + rw) + step0 * step0 * yw + rest * rest * ll
    beta = new / (rz + ll)
    grown = 1.0 + beta
    bent = grown * grown * zy - grown * step0 * (zx + yw) + step0 * step0 * wx
    step1 = new / (bent + (rest + beta) * (rest + beta) * ll)
    of_z = step0 + step1 * grown
    of_w = -step1 * step0
    of_land = step0 + step1 * (rest + beta)

    surface = of_z * z_near + of_w * w
    solution = surface[1:-1] + of_land * land
    levels = jnp.arange(KL, dtype=jnp.float32).reshape(KL, 1, 1)
    depth = jnp.concatenate([west[edge : edge + 1], depths, east[edge : edge + 1]], axis=0)
    u_wide = jnp.concatenate([west[edge + 1 :][:, None], u_vel], axis=1)
    u_face = levels < jnp.minimum(depth[:-1], depth[1:])[None]
    slope = gravity_step * (surface[1:] - surface[:-1])
    u_wide = jnp.where(u_face, u_wide - slope[None], 0.0)
    north_depth = jnp.pad(depths[:, 1:], ((0, 0), (0, 1)))
    north_surface = jnp.pad(solution[:, 1:], ((0, 0), (0, 1)))
    v_face = levels < jnp.minimum(depths, north_depth)[None]
    v_new = jnp.where(v_face, v_vel - gravity_step * (north_surface - solution)[None], 0.0)
    south_v = jnp.pad(v_new[:, :, :-1], ((0, 0), (0, 0), (1, 0)))
    u_new = u_wide[:, 1:]
    divergence = u_new - u_wide[:, :-1] + (v_new - south_v)
    divergence = jnp.where(levels < depths[None], divergence, 0.0)
    w_vel = [divergence[KL - 1]]
    for level in range(KL - 2, -1, -1):
        w_vel.append(w_vel[-1] + divergence[level])
    return solution, u_new, v_new, jnp.stack(w_vel[::-1])


def solution(mesh):
    return jax.shard_map(
        body,
        mesh=mesh,
        in_specs=(
            P(("members", "lon"), None),
            P(("members", "lon"), None),
            P(None, ("members", "lon"), None),
            P(None, ("members", "lon"), None),
            P(("members", "lon"), None),
        ),
        out_specs=(
            P(("members", "lon"), None),
            P(None, ("members", "lon"), None),
            P(None, ("members", "lon"), None),
            P(None, ("members", "lon"), None),
        ),
        check_vma=False,
    )
```

```python
import math

import jax
import jax.numpy as jnp
import ml_dtypes
import numpy as np
from jax import lax
from jax.experimental import pallas as pl
from jax.experimental.pallas import tpu as pltpu
from jax.sharding import PartitionSpec as P

LT = 112
OV = 8
KL = 6
LANE = 128

tile_shift = 0.1
gravity_step = 0.5

F32 = jnp.float32
BF16 = jnp.bfloat16
VM = pl.BlockSpec(memory_space=pltpu.VMEM)
SM = pl.BlockSpec(memory_space=pltpu.SMEM)
HB = pl.BlockSpec(memory_space=pl.ANY)
PARAMS = pltpu.CompilerParams(vmem_limit_bytes=40 * 1024 * 1024)


def sine_basis(length):
    ordinal = np.arange(length, dtype=np.float64) + 1.0
    angles = math.pi * ordinal[:, None] * ordinal[None, :] / (length + 1)
    basis_matrix = np.sqrt(2.0 / (length + 1)) * np.sin(angles)
    eigen_value = 2.0 - 2.0 * np.cos(math.pi * ordinal / (length + 1))
    return basis_matrix, eigen_value


def halves(matrix):
    high = matrix.astype(ml_dtypes.bfloat16)
    low = (matrix - high.astype(np.float64)).astype(ml_dtypes.bfloat16)
    return high, low


def window_at(tile):
    return divmod(tile * LT - OV + LANE, LANE)


def tables(span):
    lon_basis, lon_value = sine_basis(span)
    lat_basis, lat_value = sine_basis(LT + 2 * OV)
    high, low = halves(lat_basis)
    forward = np.zeros((8, 2 * LANE, 2 * LANE), ml_dtypes.bfloat16)
    inverse = np.zeros((8, 2 * LANE, 2 * LANE), ml_dtypes.bfloat16)
    for kind in range(8):
        lane = window_at(kind)[1]
        forward[kind, lane : lane + LANE, :LANE] = high
        forward[kind, lane : lane + LANE, LANE:] = low
        inverse[kind, :LANE, lane : lane + LANE] = high.T
        inverse[kind, LANE:, lane : lane + LANE] = low.T
    high, low = halves(lon_basis)
    lon = np.concatenate([high, low, high], axis=1)
    scale = 1.0 / (lon_value[:, None] + lat_value[None, :] + tile_shift)
    return forward, inverse, lon, scale.astype(np.float32)


def split(x):
    high = x.astype(BF16)
    return high, (x - high.astype(F32)).astype(BF16)


def tile_solve(x, forward, inverse, lon, scale, wide, spectral, restored, out):
    span, lat = x.shape
    tiles = lat // LT
    high, low = split(x)
    wide[:, :LANE] = jnp.zeros((2 * span, LANE), BF16)
    wide[:, LANE + lat :] = jnp.zeros((2 * span, wide.shape[1] - LANE - lat), BF16)
    wide[:span, LANE : LANE + lat] = high
    wide[span:, LANE : LANE + lat] = low
    for kind in range(8):
        group = range(kind, tiles, 8)
        starts = [window_at(t)[0] * LANE for t in group]
        rows = jnp.concatenate([wide[:, s : s + 2 * LANE] for s in starts], axis=0)
        product = jnp.dot(rows, forward[kind], preferred_element_type=F32)
        for i, t in enumerate(group):
            part = product[2 * span * i : 2 * span * (i + 1)]
            part = part[:, :LANE] + part[:, LANE:]
            high, low = split(part[:span] + part[span:])
            at = pl.ds(t * LANE, LANE)
            spectral[:span, at] = high
            spectral[span : 2 * span, at] = high
            spectral[2 * span :, at] = low
    chunk = 4
    for first in range(0, tiles, chunk):
        n = min(chunk, tiles - first)
        c = jnp.dot(lon[...], spectral[:, pl.ds(first * LANE, n * LANE)], preferred_element_type=F32)
        c = c * jnp.concatenate([scale[...]] * n, axis=1)
        high, low = split(c)
        c = jnp.concatenate([high, high, low], axis=0)
        c = jnp.dot(lon[...], c, preferred_element_type=F32)
        high, low = split(c)
        for i in range(n):
            for side in range(2):
                at = pl.ds((2 * (first + i) + side) * LANE, LANE)
                restored[:span, at] = high[:, i * LANE : (i + 1) * LANE]
                restored[span:, at] = low[:, i * LANE : (i + 1) * LANE]
    out[...] = jnp.zeros(out.shape, F32)
    for kind in range(8):
        group = range(kind, tiles, 8)
        rows = jnp.concatenate(
            [restored[:, pl.ds(2 * t * LANE, 2 * LANE)] for t in group], axis=0
        )
        product = jnp.dot(rows, inverse[kind], preferred_element_type=F32)
        for i, t in enumerate(group):
            part = product[2 * span * i : 2 * span * (i + 1)]
            at = pl.ds(window_at(t)[0] * LANE, 2 * LANE)
            out[:, at] += part[:span] + part[span:]


def solve_scratch(span, lat):
    tiles = lat // LT
    lanes = (window_at(tiles - 1)[0] + 2) * LANE
    return [
        pltpu.VMEM((2 * span, lanes), BF16),
        pltpu.VMEM((3 * span, tiles * LANE), BF16),
        pltpu.VMEM((2 * span, 2 * tiles * LANE), BF16),
        pltpu.VMEM((span, lanes), F32),
    ]


def is_even(parity, shape):
    return jnp.full(shape, parity[0], jnp.int32) == 0


def lat_beside(m):
    zero = jnp.zeros((m.shape[0], 1), m.dtype)
    return jnp.concatenate([m[:, 1:], zero], axis=1) + jnp.concatenate([zero, m[:, :-1]], axis=1)


def first_edges(parity, source_w, bottom_w, source_e, bottom_e, inner, outer):
    even = is_even(parity, inner.shape)
    west = jnp.where(bottom_w[...] > 0, source_w[...], 0.0)
    east = jnp.where(bottom_e[...] > 0, source_e[...], 0.0)
    inner[...] = jnp.where(even, east, west)
    outer[...] = jnp.where(even, west, east)


def first_solve(parity, inner_in, outer_in, source, diagonal, bottom, forward, inverse, lon, scale,
                first, inner, outer, wide, spectral, restored, out):
    cells, lat = source.shape
    even = is_even(parity, inner_in.shape)
    west = jnp.where(even, outer_in[...], inner_in[...])
    east = jnp.where(even, inner_in[...], outer_in[...])
    wet = bottom[...] > 0
    masked = jnp.where(wet, source[...], 0.0)
    x = jnp.concatenate([west, masked, east], axis=0)
    tile_solve(x, forward, inverse, lon, scale, wide, spectral, restored, out)
    first[...] = out[:, LANE : LANE + lat]
    coef = jnp.where(wet, 4.0 + diagonal[...], 0.0)
    blank = jnp.zeros((6, lat), F32)
    span = cells + 2 * OV
    to_west = jnp.concatenate(
        [first[2 * OV : 2 * OV + 1], coef[OV : OV + 1], blank, first[: 2 * OV], coef[:OV]], axis=0
    )
    to_east = jnp.concatenate(
        [blank, coef[cells - OV - 1 : cells - OV], first[cells - 1 : cells], first[cells:span],
         coef[cells - OV :]], axis=0
    )
    even = is_even(parity, inner.shape)
    inner[...] = jnp.where(even, to_east, to_west)
    outer[...] = jnp.where(even, to_west, to_east)


def second_solve(parity, inner_in, outer_in, first, diagonal, bottom, u_hbm, v_hbm, forward, inverse, lon, scale,
                 z, y, coef, second, inner, outer, u_vmem, v_vmem, wide, spectral, restored, out, m_rows, sems):
    cells, lat = diagonal.shape
    span = cells + 2 * OV
    fetch_u = pltpu.make_async_copy(u_hbm, u_vmem, sems.at[0])
    fetch_v = pltpu.make_async_copy(v_hbm, v_vmem, sems.at[1])
    fetch_u.start()
    fetch_v.start()
    even = is_even(parity, inner_in.shape)
    west = jnp.where(even, outer_in[...], inner_in[...])
    east = jnp.where(even, inner_in[...], outer_in[...])
    wet = bottom[...] > 0
    coef[:OV] = west[3 * OV :]
    coef[OV : OV + cells] = jnp.where(wet, 4.0 + diagonal[...], 0.0)
    coef[OV + cells :] = east[3 * OV :]
    m_rows[: 2 * OV] = jnp.where(coef[: 2 * OV] > 0, first[: 2 * OV] + west[OV : 3 * OV], 0.0)
    m_rows[cells:span] = jnp.where(coef[cells:] > 0, first[cells:] + east[OV : 3 * OV], 0.0)
    m_rows[2 * OV : cells] = jnp.where(coef[2 * OV : cells] > 0, first[2 * OV : cells], 0.0)
    m = m_rows[:span]
    z[...] = m
    row_w = jnp.where(west[OV - 2 : OV - 1] > 0, west[OV - 1 : OV], 0.0)
    row_e = jnp.where(east[1:2] > 0, east[0:1], 0.0)
    beside = jnp.concatenate([row_w, m[:-1]], axis=0) + jnp.concatenate([m[1:], row_e], axis=0)
    c = coef[...]
    image = jnp.where(c > 0, c * m - (beside + lat_beside(m)), 0.0)
    y[...] = image
    tile_solve(image, forward, inverse, lon, scale, wide, spectral, restored, out)
    second[...] = out[:, LANE : LANE + lat]
    depth = bottom[...].astype(F32)
    blank = jnp.zeros((6, lat), F32)
    fetch_u.wait()
    fetch_v.wait()
    to_west = jnp.concatenate([second[OV : OV + 1], depth[:1], blank, second[:OV]], axis=0)
    u_rows = [u_vmem[level, cells - 1 : cells] for level in range(KL)]
    to_east = jnp.concatenate(
        [depth[cells - 1 :]] + u_rows + [second[span - OV - 1 : span - OV], second[span - OV :]], axis=0
    )
    even = is_even(parity, inner.shape)
    inner[...] = jnp.where(even, to_east, to_west)
    outer[...] = jnp.where(even, to_west, to_east)


def sums(parity, inner_in, outer_in, second, z, y, coef, source, w, edges, sent):
    cells, lat = source.shape
    even = is_even(parity, inner_in.shape)
    west = jnp.where(even, outer_in[...], inner_in[...])
    east = jnp.where(even, inner_in[...], outer_in[...])
    own = slice(OV, OV + cells)
    full = second[own] + jnp.concatenate(
        [west[OV:], jnp.zeros((cells - 2 * OV, lat), F32), east[OV:]], axis=0
    )
    wet = coef[own] > 0
    m = jnp.where(wet, full, 0.0)
    row_w = second[OV - 1 : OV] + west[OV - 1 : OV]
    row_w = jnp.where(coef[OV - 1 : OV] > 0, row_w, 0.0)
    row_e = second[OV + cells : OV + cells + 1] + east[0:1]
    row_e = jnp.where(coef[OV + cells : OV + cells + 1] > 0, row_e, 0.0)
    w[:OV] = jnp.broadcast_to(row_w, (OV, lat))
    w[own] = m
    w[OV + cells :] = jnp.broadcast_to(row_e, (OV, lat))
    edges[: OV] = west[:OV]
    edges[OV :] = east[:OV]
    beside = jnp.concatenate([row_w, m[:-1]], axis=0) + jnp.concatenate([m[1:], row_e], axis=0)
    x = jnp.where(wet, coef[own] * m - (beside + lat_beside(m)), 0.0)
    masked = jnp.where(wet, source[...], 0.0)
    land = jnp.where(wet, 0.0, source[...])
    z_own, y_own = z[own], y[own]

    def partial(a, b):
        rows = jnp.sum(a * b, axis=0, keepdims=True)
        whole = lat // LANE * LANE
        total = rows[:, :LANE]
        for at in range(LANE, whole, LANE):
            total = total + rows[:, at : at + LANE]
        if whole < lat:
            rest = jnp.concatenate([rows[:, whole:], jnp.zeros((1, LANE - lat + whole), F32)], axis=1)
            total = total + rest
        return total

    parts = [
        partial(masked, z_own),
        partial(z_own, y_own),
        partial(masked, m),
        partial(y_own, m),
        partial(z_own, x),
        partial(m, x),
        partial(land, land),
        jnp.zeros((1, LANE), F32),
    ]
    sent[...] = jnp.broadcast_to(jnp.concatenate(parts, axis=0)[None], sent.shape)


def finish(came, z, w, edges, source, bottom, u_vel, v_vel, solution, u_new, v_new, w_vel,
           s_rows, d_rows, u_rows, v_out, w_out, s_out, sems):
    cells, lat = source.shape
    total = jnp.sum(jnp.sum(came[...], axis=0), axis=1, keepdims=True)
    rz, zy, rw, yw, zx, wx, ll = [total[i : i + 1] for i in range(7)]
    step0 = (rz + ll) / (zy + ll)
    rest = (zy - rz) / (zy + ll)
    new = rz - step0 * (zy + rw) + step0 * step0 * yw + rest * rest * ll
    beta = new / (rz + ll)
    grown = 1.0 + beta
    bent = grown * grown * zy - grown * step0 * (zx + yw) + step0 * step0 * wx
    step1 = new / (bent + (rest + beta) * (rest + beta) * ll)
    of_z = jnp.broadcast_to(step0 + step1 * grown, (OV, lat))
    of_w = jnp.broadcast_to(-step1 * step0, (OV, lat))
    of_land = jnp.broadcast_to(step0 + step1 * (rest + beta), (OV, lat))

    copies = []
    d_rows[:OV] = jnp.broadcast_to(edges[:1], (OV, lat))
    d_rows[OV : OV + cells] = bottom[...].astype(F32)
    d_rows[OV + cells :] = jnp.broadcast_to(edges[OV + 1 : OV + 2], (OV, lat))
    for at in range(0, cells + 2 * OV, OV):
        s = of_z * z[at : at + OV] + of_w * w[at : at + OV]
        if OV <= at < OV + cells:
            d = d_rows[at : at + OV]
            s = jnp.where(d > 0, s, of_land * source[at - OV : at])
            s_out[at - OV : at] = s
        s_rows[at : at + OV] = s
    copies.append(pltpu.make_async_copy(s_out, solution, sems.at[0]))
    copies[-1].start()

    s_west = s_rows[OV - 1 : OV]
    s_first = s_rows[OV : OV + 1]
    d_west = jnp.minimum(d_rows[OV - 1 : OV], d_rows[OV : OV + 1])
    for level in range(KL):
        left = edges[level + 1 : level + 2] - gravity_step * (s_first - s_west)
        u_rows[level, :OV] = jnp.broadcast_to(jnp.where(d_west > level, left, 0.0), (OV, lat))
    zero = jnp.zeros((OV, 1), F32)
    for block in range(cells // OV):
        at = OV + block * OV
        own = slice(at - OV, at)
        s = s_rows[at : at + OV]
        d = d_rows[at : at + OV]
        slope_e = gravity_step * (s_rows[at + 1 : at + OV + 1] - s)
        depth_e = jnp.minimum(d, d_rows[at + 1 : at + OV + 1])
        slope_n = gravity_step * (jnp.concatenate([s[:, 1:], zero], axis=1) - s)
        depth_n = jnp.minimum(d, jnp.concatenate([d[:, 1:], zero], axis=1))
        w_sum = jnp.zeros((OV, lat), F32)
        for level in range(KL - 1, -1, -1):
            u = jnp.where(depth_e > level, u_vel[level, own] - slope_e, 0.0)
            u_rows[level, at : at + OV] = u
            v = jnp.where(depth_n > level, v_vel[level, own] - slope_n, 0.0)
            v_out[level, own] = v
            south = jnp.concatenate([zero, v[:, :-1]], axis=1)
            flow = (u - u_rows[level, at - 1 : at + OV - 1]) + (v - south)
            w_sum = w_sum + jnp.where(d > level, flow, 0.0)
            w_out[level, own] = w_sum
        for i, (held, result) in enumerate(
            [(u_rows.at[:, at : at + OV], u_new), (v_out.at[:, own], v_new), (w_out.at[:, own], w_vel)]
        ):
            copies.append(pltpu.make_async_copy(held, result.at[:, own], sems.at[1 + 3 * block + i]))
            copies[-1].start()
    for copy in copies:
        copy.wait()


def swap_pairs(block, outward):
    devices = lax.axis_size("lon")
    if outward:
        route = [(i, (i - 1 if i % 2 == 0 else i + 1) % devices) for i in range(devices)]
    else:
        route = [(i, i ^ 1) for i in range(devices)]
    return lax.ppermute(block, "lon", route)


def shape(*dims):
    return jax.ShapeDtypeStruct(dims, F32)


def body(source, diagonal, u_vel, v_vel, bottom):
    cells, lat = source.shape
    span = cells + 2 * OV
    devices = lax.axis_size("lon")
    parity = (lax.axis_index("lon") % 2).astype(jnp.int32).reshape(1)
    consts = [jnp.asarray(table) for table in tables(span)]
    last = cells // OV - 1

    row_w = pl.BlockSpec((OV, lat), lambda i: (0, 0))
    row_e = pl.BlockSpec((OV, lat), lambda i: (last, 0))
    inner, outer = pl.pallas_call(
        first_edges,
        grid=(1,),
        in_specs=[SM, row_w, row_w, row_e, row_e],
        out_specs=[row_w, row_w],
        out_shape=[shape(OV, lat)] * 2,
        name="first_edges",
    )(parity, source, bottom, source, bottom)
    inner, outer = swap_pairs(inner, False), swap_pairs(outer, True)

    first, inner, outer = pl.pallas_call(
        first_solve,
        in_specs=[SM] + [VM] * 9,
        out_specs=[VM] * 3,
        out_shape=[shape(span, lat), shape(4 * OV, lat), shape(4 * OV, lat)],
        scratch_shapes=solve_scratch(span, lat),
        compiler_params=PARAMS,
        name="first_solve",
    )(parity, inner, outer, source, diagonal, bottom, *consts)
    inner, outer = swap_pairs(inner, False), swap_pairs(outer, True)

    z, y, coef, second, inner, outer, u_near, v_near = pl.pallas_call(
        second_solve,
        in_specs=[SM] + [VM] * 5 + [HB] * 2 + [VM] * 4,
        out_specs=[VM] * 8,
        out_shape=[shape(span, lat)] * 4 + [shape(2 * OV, lat)] * 2 + [shape(KL, cells, lat)] * 2,
        scratch_shapes=solve_scratch(span, lat)
        + [pltpu.VMEM((span, lat), F32), pltpu.SemaphoreType.DMA((2,))],
        compiler_params=PARAMS,
        name="second_solve",
    )(parity, inner, outer, first, diagonal, bottom, u_vel, v_vel, *consts)
    inner, outer = swap_pairs(inner, False), swap_pairs(outer, True)

    w, edges, sent = pl.pallas_call(
        sums,
        in_specs=[SM] + [VM] * 7,
        out_specs=[VM] * 3,
        out_shape=[shape(span, lat), shape(2 * OV, lat), shape(devices, 8, LANE)],
        compiler_params=PARAMS,
        name="sums",
    )(parity, inner, outer, second, z, y, coef, source)
    came = lax.all_to_all(sent, "lon", 0, 0)

    return pl.pallas_call(
        finish,
        in_specs=[VM] * 8,
        out_specs=[HB] * 4,
        out_shape=[shape(cells, lat)] + [shape(KL, cells, lat)] * 3,
        scratch_shapes=[
            pltpu.VMEM((span, lat), F32),
            pltpu.VMEM((span, lat), F32),
            pltpu.VMEM((KL, OV + cells, lat), F32),
            pltpu.VMEM((KL, cells, lat), F32),
            pltpu.VMEM((KL, cells, lat), F32),
            pltpu.VMEM((cells, lat), F32),
            pltpu.SemaphoreType.DMA((1 + 3 * (cells // OV),)),
        ],
        compiler_params=PARAMS,
        name="finish",
    )(came, z, w, edges, source, bottom, u_near, v_near)


def solution(mesh):
    return jax.shard_map(
        body,
        mesh=mesh,
        in_specs=(
            P(("members", "lon"), None),
            P(("members", "lon"), None),
            P(None, ("members", "lon"), None),
            P(None, ("members", "lon"), None),
            P(("members", "lon"), None),
        ),
        out_specs=(
            P(("members", "lon"), None),
            P(None, ("members", "lon"), None),
            P(None, ("members", "lon"), None),
            P(None, ("members", "lon"), None),
        ),
        check_vma=False,
    )
```

```python
import math

import jax
import jax.numpy as jnp
import ml_dtypes
import numpy as np
from jax import lax
from jax.experimental import pallas as pl
from jax.experimental.pallas import tpu as pltpu
from jax.sharding import PartitionSpec as P

LT = 112
OV = 8
KL = 6
LANE = 128

tile_shift = 0.1
gravity_step = 0.5

F32 = jnp.float32
BF16 = jnp.bfloat16
VM = pl.BlockSpec(memory_space=pltpu.VMEM)
SM = pl.BlockSpec(memory_space=pltpu.SMEM)
HB = pl.BlockSpec(memory_space=pl.ANY)
PARAMS = pltpu.CompilerParams(vmem_limit_bytes=32 * 1024 * 1024)


def sine_basis(length):
    ordinal = np.arange(length, dtype=np.float64) + 1.0
    angles = math.pi * ordinal[:, None] * ordinal[None, :] / (length + 1)
    basis_matrix = np.sqrt(2.0 / (length + 1)) * np.sin(angles)
    eigen_value = 2.0 - 2.0 * np.cos(math.pi * ordinal / (length + 1))
    return basis_matrix, eigen_value


def halves(matrix):
    high = matrix.astype(ml_dtypes.bfloat16)
    low = (matrix - high.astype(np.float64)).astype(ml_dtypes.bfloat16)
    return high, low


def window_at(tile):
    return divmod(tile * LT - OV + LANE, LANE)


def tables(span):
    lon_basis, lon_value = sine_basis(span)
    lat_basis, lat_value = sine_basis(LT + 2 * OV)
    high, low = halves(lat_basis)
    forward = np.zeros((8, 2 * LANE, 2 * LANE), ml_dtypes.bfloat16)
    inverse = np.zeros((8, 2 * LANE, 2 * LANE), ml_dtypes.bfloat16)
    for kind in range(8):
        lane = window_at(kind)[1]
        forward[kind, lane : lane + LANE, :LANE] = high
        forward[kind, lane : lane + LANE, LANE:] = low
        inverse[kind, :LANE, lane : lane + LANE] = high.T
        inverse[kind, LANE:, lane : lane + LANE] = low.T
    high, low = halves(lon_basis)
    lon = np.concatenate([high, low, high], axis=1)
    scale = 1.0 / (lon_value[:, None] + lat_value[None, :] + tile_shift)
    return forward, inverse, lon, scale.astype(np.float32)


def split(x):
    high = x.astype(BF16)
    return high, (x - high.astype(F32)).astype(BF16)


def tile_solve(x, forward, inverse, lon, scale, wide, spectral, restored, out):
    span, lat = x.shape
    tiles = lat // LT
    high, low = split(x)
    wide[:, :LANE] = jnp.zeros((2 * span, LANE), BF16)
    wide[:, LANE + lat :] = jnp.zeros((2 * span, wide.shape[1] - LANE - lat), BF16)
    wide[:span, LANE : LANE + lat] = high
    wide[span:, LANE : LANE + lat] = low
    for kind in range(8):
        group = range(kind, tiles, 8)
        starts = [window_at(t)[0] * LANE for t in group]
        rows = jnp.concatenate([wide[:, s : s + 2 * LANE] for s in starts], axis=0)
        product = jnp.dot(rows, forward[kind], preferred_element_type=F32)
        for i, t in enumerate(group):
            part = product[2 * span * i : 2 * span * (i + 1)]
            part = part[:, :LANE] + part[:, LANE:]
            high, low = split(part[:span] + part[span:])
            at = pl.ds(t * LANE, LANE)
            spectral[:span, at] = high
            spectral[span : 2 * span, at] = high
            spectral[2 * span :, at] = low
    chunk = 4
    for first in range(0, tiles, chunk):
        n = min(chunk, tiles - first)
        c = jnp.dot(lon[...], spectral[:, pl.ds(first * LANE, n * LANE)], preferred_element_type=F32)
        c = c * jnp.concatenate([scale[...]] * n, axis=1)
        high, low = split(c)
        c = jnp.concatenate([high, high, low], axis=0)
        c = jnp.dot(lon[...], c, preferred_element_type=F32)
        high, low = split(c)
        for i in range(n):
            for side in range(2):
                at = pl.ds((2 * (first + i) + side) * LANE, LANE)
                restored[:span, at] = high[:, i * LANE : (i + 1) * LANE]
                restored[span:, at] = low[:, i * LANE : (i + 1) * LANE]
    out[...] = jnp.zeros(out.shape, F32)
    for kind in range(8):
        group = range(kind, tiles, 8)
        rows = jnp.concatenate(
            [restored[:, pl.ds(2 * t * LANE, 2 * LANE)] for t in group], axis=0
        )
        product = jnp.dot(rows, inverse[kind], preferred_element_type=F32)
        for i, t in enumerate(group):
            part = product[2 * span * i : 2 * span * (i + 1)]
            at = pl.ds(window_at(t)[0] * LANE, 2 * LANE)
            out[:, at] += part[:span] + part[span:]


def solve_scratch(span, lat):
    tiles = lat // LT
    lanes = (window_at(tiles - 1)[0] + 2) * LANE
    return [
        pltpu.VMEM((2 * span, lanes), BF16),
        pltpu.VMEM((3 * span, tiles * LANE), BF16),
        pltpu.VMEM((2 * span, 2 * tiles * LANE), BF16),
        pltpu.VMEM((span, lanes), F32),
    ]


def pick(parity, inner, outer):
    even = jnp.full(inner.shape, parity[0], jnp.int32) == 0
    return jnp.where(even, outer, inner), jnp.where(even, inner, outer)


def lat_beside(m):
    zero = jnp.zeros((m.shape[0], 1), m.dtype)
    return jnp.concatenate([m[:, 1:], zero], axis=1) + jnp.concatenate([zero, m[:, :-1]], axis=1)


def pack(message, rows):
    n, lat = rows.shape
    for block, at in enumerate(range(0, lat, LANE)):
        width = min(LANE, lat - at)
        message[block * n : (block + 1) * n, :width] = rows[:, at : at + width]


def unpack(message, n, lat):
    blocks = [message[i * n : (i + 1) * n] for i in range(-(-lat // LANE))]
    return jnp.concatenate(blocks, axis=1)[:, :lat]


def first_edges(parity, source_w, bottom_w, source_e, bottom_e, inner, outer):
    west = jnp.where(bottom_w[...] > 0, source_w[...], 0.0)
    east = jnp.where(bottom_e[...] > 0, source_e[...], 0.0)
    outer[...], inner[...] = pick(parity, east, west)


def prepare(parity, inner_w, outer_w, source_h, diagonal_h, bottom_h, u_h, v_h, *refs):
    tables_h, refs = refs[:4], refs[4:]
    inner, outer, masked, coef, depth, source, u, v = refs[:8]
    held, (diagonal, bottom, sems) = refs[8:12], refs[12:]
    pairs = [(source_h, source), (bottom_h, bottom), (diagonal_h, diagonal), (u_h, u)]
    pairs += list(zip(tables_h, held)) + [(v_h, v)]
    copies = [pltpu.make_async_copy(a, b, sems.at[i]) for i, (a, b) in enumerate(pairs)]
    for copy in copies:
        copy.start()
    for copy in copies[:3]:
        copy.wait()
    cells, lat = source.shape
    wet = bottom[...] > 0
    masked[...] = jnp.where(wet, source[...], 0.0)
    coef[...] = jnp.where(wet, 4.0 + diagonal[...], 0.0)
    depth[...] = bottom[...].astype(F32)
    copies[3].wait()
    edge = OV + 1
    to_west = jnp.concatenate(
        [coef[:edge], jnp.zeros((2 * OV - edge - 1, lat), F32), depth[:1]], axis=0
    )
    u_rows = [u[level, cells - 1 : cells] for level in range(KL)]
    to_east = jnp.concatenate(u_rows + [depth[cells - 1 :], coef[cells - edge :]], axis=0)
    outer[...], inner[...] = pick(parity, to_east, to_west)
    for copy in copies[4:]:
        copy.wait()


def first_solve(parity, inner_in, outer_in, masked, forward, inverse, lon, scale,
                first, inner, outer, wide, spectral, restored, out):
    cells, lat = masked.shape
    west, east = pick(parity, inner_in[...], outer_in[...])
    x = jnp.concatenate([west, masked[...], east], axis=0)
    tile_solve(x, forward, inverse, lon, scale, wide, spectral, restored, out)
    first[...] = out[:, LANE : LANE + lat]
    reach = 2 * OV + 1
    to_outer, to_inner = pick(parity, first[cells - 1 :], first[:reach])
    pack(inner, to_inner)
    pack(outer, to_outer)


def second_solve(parity, inner_in, outer_in, inner_far, outer_far, first, coef_own, forward, inverse, lon, scale,
                 z, y, coef, second, edges, inner, outer, wide, spectral, restored, out, m_rows, c_rows):
    cells, lat = coef_own.shape
    span = cells + 2 * OV
    reach = 2 * OV + 1
    far_w, far_e = pick(parity, inner_far[...], outer_far[...])
    edges[:OV] = far_w[:OV]
    edges[OV:] = far_e[OV:]
    c_rows[: 2 * OV] = far_w
    c_rows[: OV - 1] = jnp.zeros((OV - 1, lat), F32)
    c_rows[2 * OV : 2 * OV + cells] = coef_own[...]
    c_rows[2 * OV + cells :] = far_e
    west, east = pick(parity, unpack(inner_in, reach, lat), unpack(outer_in, reach, lat))
    m_rows[:OV] = jnp.zeros((OV, lat), F32)
    m_rows[OV : OV + span] = first[...]
    m_rows[OV + span :] = jnp.zeros((OV, lat), F32)
    m_rows[OV - 1 : OV - 1 + reach] += west
    m_rows[OV + cells : OV + cells + reach] += east
    m_rows[...] = jnp.where(c_rows[...] > 0, m_rows[...], 0.0)
    inside = slice(OV, OV + span)
    c, m = c_rows[inside], m_rows[inside]
    coef[...] = c
    z[...] = m
    beside = m_rows[OV - 1 : OV - 1 + span] + m_rows[OV + 1 : OV + 1 + span]
    image = jnp.where(c > 0, c * m - (beside + lat_beside(m)), 0.0)
    y[...] = image
    tile_solve(image, forward, inverse, lon, scale, wide, spectral, restored, out)
    second[...] = out[:, LANE : LANE + lat]
    to_outer, to_inner = pick(parity, second[span - OV - 1 :], second[: OV + 1])
    pack(inner, to_inner)
    pack(outer, to_outer)


def sums(parity, inner_in, outer_in, second, z, y, coef, source, w, sent):
    cells, lat = source.shape
    west, east = pick(parity, unpack(inner_in, OV + 1, lat), unpack(outer_in, OV + 1, lat))
    w[...] = second[...]
    w[OV - 1 : 2 * OV] += west
    w[cells : cells + OV + 1] += east
    w[...] = jnp.where(coef[...] > 0, w[...], 0.0)
    own = slice(OV, OV + cells)
    c, m = coef[own], w[own]
    wet = c > 0
    beside = w[OV - 1 : OV - 1 + cells] + w[OV + 1 : OV + 1 + cells]
    x = jnp.where(wet, c * m - (beside + lat_beside(m)), 0.0)
    masked = jnp.where(wet, source[...], 0.0)
    land = jnp.where(wet, 0.0, source[...])
    z_own, y_own = z[own], y[own]

    def partial(a, b):
        rows = jnp.sum(a * b, axis=0, keepdims=True)
        whole = lat // LANE * LANE
        total = rows[:, :LANE]
        for at in range(LANE, whole, LANE):
            total = total + rows[:, at : at + LANE]
        if whole < lat:
            rest = jnp.concatenate([rows[:, whole:], jnp.zeros((1, LANE - lat + whole), F32)], axis=1)
            total = total + rest
        return total

    parts = [
        partial(masked, z_own),
        partial(z_own, y_own),
        partial(masked, m),
        partial(y_own, m),
        partial(z_own, x),
        partial(m, x),
        partial(land, land),
        jnp.zeros((1, LANE), F32),
    ]
    sent[...] = jnp.broadcast_to(jnp.concatenate(parts, axis=0)[None], sent.shape)


def finish(came, z, w, edges, source, depth, u_vel, v_vel, solution, u_new, v_new, w_vel,
           s_rows, d_rows, u_rows, v_out, w_out, s_out, sems):
    cells, lat = source.shape
    total = jnp.sum(jnp.sum(came[...], axis=0), axis=1, keepdims=True)
    rz, zy, rw, yw, zx, wx, ll = [total[i : i + 1] for i in range(7)]
    step0 = (rz + ll) / (zy + ll)
    rest = (zy - rz) / (zy + ll)
    new = rz - step0 * (zy + rw) + step0 * step0 * yw + rest * rest * ll
    beta = new / (rz + ll)
    grown = 1.0 + beta
    bent = grown * grown * zy - grown * step0 * (zx + yw) + step0 * step0 * wx
    step1 = new / (bent + (rest + beta) * (rest + beta) * ll)
    of_z = jnp.broadcast_to(step0 + step1 * grown, (OV, lat))
    of_w = jnp.broadcast_to(-step1 * step0, (OV, lat))
    of_land = jnp.broadcast_to(step0 + step1 * (rest + beta), (OV, lat))

    copies = []
    d_rows[:OV] = jnp.broadcast_to(edges[KL : KL + 1], (OV, lat))
    d_rows[OV : OV + cells] = depth[...]
    d_rows[OV + cells :] = jnp.broadcast_to(edges[2 * OV - 1 :], (OV, lat))
    for at in range(0, cells + 2 * OV, OV):
        s = of_z * z[at : at + OV] + of_w * w[at : at + OV]
        if OV <= at < OV + cells:
            d = d_rows[at : at + OV]
            s = jnp.where(d > 0, s, of_land * source[at - OV : at])
            s_out[at - OV : at] = s
        s_rows[at : at + OV] = s
    copies.append(pltpu.make_async_copy(s_out, solution, sems.at[0]))
    copies[-1].start()

    s_west = s_rows[OV - 1 : OV]
    s_first = s_rows[OV : OV + 1]
    d_west = jnp.minimum(d_rows[OV - 1 : OV], d_rows[OV : OV + 1])
    for level in range(KL):
        left = edges[level : level + 1] - gravity_step * (s_first - s_west)
        u_rows[level, :OV] = jnp.broadcast_to(jnp.where(d_west > level, left, 0.0), (OV, lat))
    zero = jnp.zeros((OV, 1), F32)
    for block in range(cells // OV):
        at = OV + block * OV
        own = slice(at - OV, at)
        s = s_rows[at : at + OV]
        d = d_rows[at : at + OV]
        slope_e = gravity_step * (s_rows[at + 1 : at + OV + 1] - s)
        depth_e = jnp.minimum(d, d_rows[at + 1 : at + OV + 1])
        slope_n = gravity_step * (jnp.concatenate([s[:, 1:], zero], axis=1) - s)
        depth_n = jnp.minimum(d, jnp.concatenate([d[:, 1:], zero], axis=1))
        w_sum = jnp.zeros((OV, lat), F32)
        for level in range(KL - 1, -1, -1):
            u = jnp.where(depth_e > level, u_vel[level, own] - slope_e, 0.0)
            u_rows[level, at : at + OV] = u
            v = jnp.where(depth_n > level, v_vel[level, own] - slope_n, 0.0)
            v_out[level, own] = v
            south = jnp.concatenate([zero, v[:, :-1]], axis=1)
            flow = (u - u_rows[level, at - 1 : at + OV - 1]) + (v - south)
            w_sum = w_sum + jnp.where(d > level, flow, 0.0)
            w_out[level, own] = w_sum
        for i, (held, result) in enumerate(
            [(u_rows.at[:, at : at + OV], u_new), (v_out.at[:, own], v_new), (w_out.at[:, own], w_vel)]
        ):
            copies.append(pltpu.make_async_copy(held, result.at[:, own], sems.at[1 + 3 * block + i]))
            copies[-1].start()
    for copy in copies:
        copy.wait()


def swap_pairs(block, outward):
    devices = lax.axis_size("lon")
    if outward:
        route = [(i, (i - 1 if i % 2 == 0 else i + 1) % devices) for i in range(devices)]
    else:
        route = [(i, i ^ 1) for i in range(devices)]
    return lax.ppermute(block, "lon", route)


def in_hbm(x):
    return pltpu.with_memory_space_constraint(x, pltpu.HBM)


def shape(*dims):
    return jax.ShapeDtypeStruct(dims, F32)


def body(source, diagonal, u_vel, v_vel, bottom):
    cells, lat = source.shape
    span = cells + 2 * OV
    devices = lax.axis_size("lon")
    parity = (lax.axis_index("lon") % 2).astype(jnp.int32).reshape(1)
    consts = [jnp.asarray(table) for table in tables(span)]
    last = cells // OV - 1

    row_w = pl.BlockSpec((OV, lat), lambda i: (0, 0))
    row_e = pl.BlockSpec((OV, lat), lambda i: (last, 0))
    inner, outer = pl.pallas_call(
        first_edges,
        grid=(1,),
        in_specs=[SM, row_w, row_w, row_e, row_e],
        out_specs=[row_w, row_w],
        out_shape=[shape(OV, lat)] * 2,
        name="first_edges",
    )(parity, source, bottom, source, bottom)
    near = swap_pairs(inner, False), swap_pairs(outer, True)

    inner, outer, masked, coef_own, depth, source_v, u_v, v_v, *held = pl.pallas_call(
        prepare,
        in_specs=[SM] + [HB] * 11,
        out_specs=[VM] * 12,
        out_shape=[pltpu.VMEM((2 * OV, lat), F32)] * 2
        + [pltpu.VMEM((cells, lat), F32)] * 4
        + [pltpu.VMEM((KL, cells, lat), F32)] * 2
        + [pltpu.VMEM(table.shape, table.dtype) for table in consts],
        scratch_shapes=[
            pltpu.VMEM((cells, lat), F32),
            pltpu.VMEM((cells, lat), jnp.int32),
            pltpu.SemaphoreType.DMA((9,)),
        ],
        compiler_params=pltpu.CompilerParams(vmem_limit_bytes=16 * 1024 * 1024),
        cost_estimate=pl.CostEstimate(flops=10**6, bytes_accessed=7 * 10**6, transcendentals=0),
        name="prepare",
    )(parity, inner, outer, *[in_hbm(x) for x in (source, diagonal, bottom, u_vel, v_vel, *consts)])
    far = swap_pairs(inner, False), swap_pairs(outer, True)

    blocks = -(-lat // LANE)
    first, inner, outer = pl.pallas_call(
        first_solve,
        in_specs=[SM] + [VM] * 7,
        out_specs=[VM] * 3,
        out_shape=[shape(span, lat)] + [shape((2 * OV + 1) * blocks, LANE)] * 2,
        scratch_shapes=solve_scratch(span, lat),
        compiler_params=PARAMS,
        cost_estimate=pl.CostEstimate(flops=10**6, bytes_accessed=10**6, transcendentals=0),
        name="first_solve",
    )(parity, *near, masked, *held)
    near = swap_pairs(inner, False), swap_pairs(outer, True)

    z, y, coef, second, edges, inner, outer = pl.pallas_call(
        second_solve,
        in_specs=[SM] + [VM] * 10,
        out_specs=[VM] * 7,
        out_shape=[shape(span, lat)] * 4 + [shape(2 * OV, lat)] + [shape((OV + 1) * blocks, LANE)] * 2,
        scratch_shapes=solve_scratch(span, lat) + [pltpu.VMEM((span + 2 * OV, lat), F32)] * 2,
        compiler_params=PARAMS,
        name="second_solve",
    )(parity, *near, *far, first, coef_own, *held)
    near = swap_pairs(inner, False), swap_pairs(outer, True)

    w, sent = pl.pallas_call(
        sums,
        in_specs=[SM] + [VM] * 7,
        out_specs=[VM] * 2,
        out_shape=[shape(span, lat), shape(devices, 8, LANE)],
        compiler_params=PARAMS,
        name="sums",
    )(parity, *near, second, z, y, coef, source_v)
    came = lax.all_to_all(sent, "lon", 0, 0)

    return pl.pallas_call(
        finish,
        in_specs=[VM] * 8,
        out_specs=[HB] * 4,
        out_shape=[shape(cells, lat)] + [shape(KL, cells, lat)] * 3,
        scratch_shapes=[
            pltpu.VMEM((span, lat), F32),
            pltpu.VMEM((span, lat), F32),
            pltpu.VMEM((KL, OV + cells, lat), F32),
            pltpu.VMEM((KL, cells, lat), F32),
            pltpu.VMEM((KL, cells, lat), F32),
            pltpu.VMEM((cells, lat), F32),
            pltpu.SemaphoreType.DMA((1 + 3 * (cells // OV),)),
        ],
        compiler_params=PARAMS,
        name="finish",
    )(came, z, w, edges, source_v, depth, u_v, v_v)


def solution(mesh):
    return jax.shard_map(
        body,
        mesh=mesh,
        in_specs=(
            P(("members", "lon"), None),
            P(("members", "lon"), None),
            P(None, ("members", "lon"), None),
            P(None, ("members", "lon"), None),
            P(("members", "lon"), None),
        ),
        out_specs=(
            P(("members", "lon"), None),
            P(None, ("members", "lon"), None),
            P(None, ("members", "lon"), None),
            P(None, ("members", "lon"), None),
        ),
        check_vma=False,
    )
```

```python
import math

import jax
import jax.numpy as jnp
import ml_dtypes
import numpy as np
from jax import lax
from jax.experimental import pallas as pl
from jax.experimental.pallas import tpu as pltpu
from jax.sharding import PartitionSpec as P

LT = 112
OV = 8
KL = 6
LANE = 128

tile_shift = 0.1
gravity_step = 0.5

F32 = jnp.float32
BF16 = jnp.bfloat16
VM = pl.BlockSpec(memory_space=pltpu.VMEM)
SM = pl.BlockSpec(memory_space=pltpu.SMEM)
HB = pl.BlockSpec(memory_space=pl.ANY)
PARAMS = pltpu.CompilerParams(vmem_limit_bytes=32 * 1024 * 1024)


def sine_basis(length):
    ordinal = np.arange(length, dtype=np.float64) + 1.0
    angles = math.pi * ordinal[:, None] * ordinal[None, :] / (length + 1)
    basis_matrix = np.sqrt(2.0 / (length + 1)) * np.sin(angles)
    eigen_value = 2.0 - 2.0 * np.cos(math.pi * ordinal / (length + 1))
    return basis_matrix, eigen_value


def halves(matrix):
    high = matrix.astype(ml_dtypes.bfloat16)
    low = (matrix - high.astype(np.float64)).astype(ml_dtypes.bfloat16)
    return high, low


def window_at(tile):
    return divmod(tile * LT - OV + LANE, LANE)


def tables(span):
    lon_basis, lon_value = sine_basis(span)
    lat_basis, lat_value = sine_basis(LT + 2 * OV)
    high, low = halves(lat_basis)
    forward = np.zeros((8, 2 * LANE, 2 * LANE), ml_dtypes.bfloat16)
    inverse = np.zeros((8, 2 * LANE, 2 * LANE), ml_dtypes.bfloat16)
    for kind in range(8):
        lane = window_at(kind)[1]
        forward[kind, lane : lane + LANE, :LANE] = high
        forward[kind, lane : lane + LANE, LANE:] = low
        inverse[kind, :LANE, lane : lane + LANE] = high.T
        inverse[kind, LANE:, lane : lane + LANE] = low.T
    high, low = halves(lon_basis)
    lon = np.concatenate([high, low, high], axis=1)
    scale = 1.0 / (lon_value[:, None] + lat_value[None, :] + tile_shift)
    return forward, inverse, lon, scale.astype(np.float32)


def split(x):
    high = x.astype(BF16)
    return high, (x - high.astype(F32)).astype(BF16)


def tile_solve(x, forward, inverse, lon, scale, wide, spectral, restored, out):
    span, lat = x.shape
    tiles = lat // LT
    high, low = split(x)
    wide[:, :LANE] = jnp.zeros((2 * span, LANE), BF16)
    wide[:, LANE + lat :] = jnp.zeros((2 * span, wide.shape[1] - LANE - lat), BF16)
    wide[:span, LANE : LANE + lat] = high
    wide[span:, LANE : LANE + lat] = low
    for kind in range(8):
        group = range(kind, tiles, 8)
        starts = [window_at(t)[0] * LANE for t in group]
        rows = jnp.concatenate([wide[:, s : s + 2 * LANE] for s in starts], axis=0)
        product = jnp.dot(rows, forward[kind], preferred_element_type=F32)
        for i, t in enumerate(group):
            part = product[2 * span * i : 2 * span * (i + 1)]
            part = part[:, :LANE] + part[:, LANE:]
            high, low = split(part[:span] + part[span:])
            at = pl.ds(t * LANE, LANE)
            spectral[:span, at] = high
            spectral[span : 2 * span, at] = high
            spectral[2 * span :, at] = low
    chunk = 4
    for first in range(0, tiles, chunk):
        n = min(chunk, tiles - first)
        c = jnp.dot(lon[...], spectral[:, pl.ds(first * LANE, n * LANE)], preferred_element_type=F32)
        c = c * jnp.concatenate([scale[...]] * n, axis=1)
        high, low = split(c)
        c = jnp.concatenate([high, high, low], axis=0)
        c = jnp.dot(lon[...], c, preferred_element_type=F32)
        high, low = split(c)
        for i in range(n):
            for side in range(2):
                at = pl.ds((2 * (first + i) + side) * LANE, LANE)
                restored[:span, at] = high[:, i * LANE : (i + 1) * LANE]
                restored[span:, at] = low[:, i * LANE : (i + 1) * LANE]
    out[...] = jnp.zeros(out.shape, F32)
    for kind in range(8):
        group = range(kind, tiles, 8)
        rows = jnp.concatenate(
            [restored[:, pl.ds(2 * t * LANE, 2 * LANE)] for t in group], axis=0
        )
        product = jnp.dot(rows, inverse[kind], preferred_element_type=F32)
        for i, t in enumerate(group):
            part = product[2 * span * i : 2 * span * (i + 1)]
            at = pl.ds(window_at(t)[0] * LANE, 2 * LANE)
            out[:, at] += part[:span] + part[span:]


def solve_scratch(span, lat):
    tiles = lat // LT
    lanes = (window_at(tiles - 1)[0] + 2) * LANE
    return [
        pltpu.VMEM((2 * span, lanes), BF16),
        pltpu.VMEM((3 * span, tiles * LANE), BF16),
        pltpu.VMEM((2 * span, 2 * tiles * LANE), BF16),
        pltpu.VMEM((span, lanes), F32),
    ]


def pick(parity, inner, outer):
    even = jnp.full(inner.shape, parity[0], jnp.int32) == 0
    return jnp.where(even, outer, inner), jnp.where(even, inner, outer)


def lat_beside(m):
    zero = jnp.zeros((m.shape[0], 1), m.dtype)
    return jnp.concatenate([m[:, 1:], zero], axis=1) + jnp.concatenate([zero, m[:, :-1]], axis=1)


def pack(message, rows):
    n, lat = rows.shape
    for block, at in enumerate(range(0, lat, LANE)):
        width = min(LANE, lat - at)
        message[block * n : (block + 1) * n, :width] = rows[:, at : at + width]


def unpack(message, n, lat):
    blocks = [message[i * n : (i + 1) * n] for i in range(-(-lat // LANE))]
    return jnp.concatenate(blocks, axis=1)[:, :lat]


def first_edges(parity, source, bottom, inner, outer, source_w, source_e, bottom_w, bottom_e, sems):
    last = source.shape[0] - OV
    pairs = [(source, 0, source_w), (bottom, 0, bottom_w), (source, last, source_e), (bottom, last, bottom_e)]
    copies = [
        pltpu.make_async_copy(held.at[pl.ds(at, OV)], block, sems.at[i])
        for i, (held, at, block) in enumerate(pairs)
    ]
    for copy in copies:
        copy.start()
    for copy in copies:
        copy.wait()
    west = jnp.where(bottom_w[...] > 0, source_w[...], 0.0)
    east = jnp.where(bottom_e[...] > 0, source_e[...], 0.0)
    outer[...], inner[...] = pick(parity, east, west)


def prepare(inner, outer, source_h, diagonal_h, bottom_h, *refs):
    tables_h, (masked, coef, depth, source), held = refs[:4], refs[4:8], refs[8:12]
    diagonal, bottom, sems = refs[12:]
    pairs = [(source_h, source), (bottom_h, bottom), (diagonal_h, diagonal)]
    pairs += list(zip(tables_h, held))
    copies = [pltpu.make_async_copy(a, b, sems.at[i]) for i, (a, b) in enumerate(pairs)]
    for copy in copies:
        copy.start()
    for copy in copies[:3]:
        copy.wait()
    wet = bottom[...] > 0
    masked[...] = jnp.where(wet, source[...], 0.0)
    coef[...] = jnp.where(wet, 4.0 + diagonal[...], 0.0)
    depth[...] = bottom[...].astype(F32)
    for copy in copies[3:]:
        copy.wait()


def first_solve(parity, inner_in, outer_in, masked, coef, u_h, v_h, forward, inverse, lon, scale,
                first, inner, outer, u, v, wide, spectral, restored, out, sems):
    cells, lat = masked.shape
    copies = [pltpu.make_async_copy(a, b, sems.at[i]) for i, (a, b) in enumerate([(u_h, u), (v_h, v)])]
    for copy in copies:
        copy.start()
    west, east = pick(parity, inner_in[...], outer_in[...])
    x = jnp.concatenate([west, masked[...], east], axis=0)
    tile_solve(x, forward, inverse, lon, scale, wide, spectral, restored, out)
    first[...] = out[:, LANE : LANE + lat]
    reach, edge = 2 * OV + 1, OV + 1
    to_west = jnp.concatenate([first[:reach], coef[:edge]], axis=0)
    to_east = jnp.concatenate([first[cells - 1 :], coef[cells - edge :]], axis=0)
    to_outer, to_inner = pick(parity, to_east, to_west)
    pack(inner, to_inner)
    pack(outer, to_outer)
    for copy in copies:
        copy.wait()


def second_solve(parity, inner_in, outer_in, first, coef_own, depth, u, forward, inverse, lon, scale,
                 z, y, coef, second, inner, outer, wide, spectral, restored, out, m_rows, c_rows):
    cells, lat = coef_own.shape
    span = cells + 2 * OV
    reach, edge = 2 * OV + 1, OV + 1
    west, east = pick(
        parity, unpack(inner_in, reach + edge, lat), unpack(outer_in, reach + edge, lat)
    )
    c_rows[:OV] = jnp.zeros((OV, lat), F32)
    c_rows[OV - 1 : 2 * OV] = west[reach:]
    c_rows[2 * OV : 2 * OV + cells] = coef_own[...]
    c_rows[2 * OV + cells + OV :] = jnp.zeros((OV, lat), F32)
    c_rows[2 * OV + cells : 2 * OV + cells + edge] = east[reach:]
    m_rows[:OV] = jnp.zeros((OV, lat), F32)
    m_rows[OV : OV + span] = first[...]
    m_rows[OV + span :] = jnp.zeros((OV, lat), F32)
    m_rows[OV - 1 : OV - 1 + reach] += west[:reach]
    m_rows[OV + cells : OV + cells + reach] += east[:reach]
    m_rows[...] = jnp.where(c_rows[...] > 0, m_rows[...], 0.0)
    inside = slice(OV, OV + span)
    c, m = c_rows[inside], m_rows[inside]
    coef[...] = c
    z[...] = m
    beside = m_rows[OV - 1 : OV - 1 + span] + m_rows[OV + 1 : OV + 1 + span]
    image = jnp.where(c > 0, c * m - (beside + lat_beside(m)), 0.0)
    y[...] = image
    tile_solve(image, forward, inverse, lon, scale, wide, spectral, restored, out)
    second[...] = out[:, LANE : LANE + lat]
    to_west = jnp.concatenate([second[:edge], depth[:1], jnp.zeros((KL, lat), F32)], axis=0)
    u_rows = [u[level, cells - 1 : cells] for level in range(KL)]
    to_east = jnp.concatenate([second[span - edge :], depth[cells - 1 :]] + u_rows, axis=0)
    outer[...], inner[...] = pick(parity, to_east, to_west)


def sums(parity, inner_in, outer_in, second, z, y, coef, source, w, edges, sent):
    cells, lat = source.shape
    west, east = pick(parity, inner_in[...], outer_in[...])
    edges[:OV] = west[OV:]
    edges[OV:] = east[OV:]
    w[...] = second[...]
    w[OV - 1 : 2 * OV] += west[: OV + 1]
    w[cells : cells + OV + 1] += east[: OV + 1]
    w[...] = jnp.where(coef[...] > 0, w[...], 0.0)
    own = slice(OV, OV + cells)
    c, m = coef[own], w[own]
    wet = c > 0
    beside = w[OV - 1 : OV - 1 + cells] + w[OV + 1 : OV + 1 + cells]
    x = jnp.where(wet, c * m - (beside + lat_beside(m)), 0.0)
    masked = jnp.where(wet, source[...], 0.0)
    land = jnp.where(wet, 0.0, source[...])
    z_own, y_own = z[own], y[own]

    def partial(a, b):
        product = a * b
        rows = product[:OV]
        for at in range(OV, cells, OV):
            rows = rows + product[at : at + OV]
        whole = lat // LANE * LANE
        total = rows[:, :LANE]
        for at in range(LANE, whole, LANE):
            total = total + rows[:, at : at + LANE]
        if whole < lat:
            blank = jnp.zeros((OV, LANE - lat + whole), F32)
            total = total + jnp.concatenate([rows[:, whole:], blank], axis=1)
        return jnp.sum(total, axis=0, keepdims=True)

    parts = [
        partial(masked, z_own),
        partial(z_own, y_own),
        partial(masked, m),
        partial(y_own, m),
        partial(z_own, x),
        partial(m, x),
        partial(land, land),
        jnp.zeros((1, LANE), F32),
    ]
    sent[...] = jnp.broadcast_to(jnp.concatenate(parts, axis=0)[None], sent.shape)


def send(copies, level, at, u_rows, v_out, w_out, u_new, v_new, w_vel, sems):
    own = slice(at - OV, at)
    for held, rows, result in ((u_rows, slice(at, at + OV), u_new), (v_out, own, v_new), (w_out, own, w_vel)):
        copies.append(
            pltpu.make_async_copy(held.at[level, rows], result.at[level, own], sems.at[len(copies)])
        )
        copies[-1].start()


def finish(came, z, w, edges, source, depth, u_vel, v_vel, solution, u_new, v_new, w_vel,
           s_rows, d_rows, u_rows, v_out, w_out, s_out, sems):
    cells, lat = source.shape
    total = jnp.sum(jnp.sum(came[...], axis=0), axis=1, keepdims=True)
    rz, zy, rw, yw, zx, wx, ll = [total[i : i + 1] for i in range(7)]
    step0 = (rz + ll) / (zy + ll)
    rest = (zy - rz) / (zy + ll)
    new = rz - step0 * (zy + rw) + step0 * step0 * yw + rest * rest * ll
    beta = new / (rz + ll)
    grown = 1.0 + beta
    bent = grown * grown * zy - grown * step0 * (zx + yw) + step0 * step0 * wx
    step1 = new / (bent + (rest + beta) * (rest + beta) * ll)
    of_z = jnp.broadcast_to(step0 + step1 * grown, (OV, lat))
    of_w = jnp.broadcast_to(-step1 * step0, (OV, lat))
    of_land = jnp.broadcast_to(step0 + step1 * (rest + beta), (OV, lat))

    copies = []
    d_rows[:OV] = jnp.broadcast_to(edges[1:2], (OV, lat))
    d_rows[OV : OV + cells] = depth[...]
    d_rows[OV + cells :] = jnp.broadcast_to(edges[OV + 1 : OV + 2], (OV, lat))
    for at in range(0, cells + 2 * OV, OV):
        s = of_z * z[at : at + OV] + of_w * w[at : at + OV]
        if OV <= at < OV + cells:
            d = d_rows[at : at + OV]
            s = jnp.where(d > 0, s, of_land * source[at - OV : at])
            s_out[at - OV : at] = s
        s_rows[at : at + OV] = s
    copies.append(pltpu.make_async_copy(s_out, solution, sems.at[0]))
    copies[-1].start()

    s_west = s_rows[OV - 1 : OV]
    s_first = s_rows[OV : OV + 1]
    d_west = jnp.minimum(d_rows[OV - 1 : OV], d_rows[OV : OV + 1])
    for level in range(KL):
        left = edges[level + 2 : level + 3] - gravity_step * (s_first - s_west)
        u_rows[level, :OV] = jnp.broadcast_to(jnp.where(d_west > level, left, 0.0), (OV, lat))
    zero = jnp.zeros((OV, 1), F32)
    for block in range(cells // OV):
        at = OV + block * OV
        own = slice(at - OV, at)
        s = s_rows[at : at + OV]
        d = d_rows[at : at + OV]
        slope_e = gravity_step * (s_rows[at + 1 : at + OV + 1] - s)
        depth_e = jnp.minimum(d, d_rows[at + 1 : at + OV + 1])
        slope_n = gravity_step * (jnp.concatenate([s[:, 1:], zero], axis=1) - s)
        depth_n = jnp.minimum(d, jnp.concatenate([d[:, 1:], zero], axis=1))
        w_sum = jnp.zeros((OV, lat), F32)
        for level in range(KL - 1, -1, -1):
            u = jnp.where(depth_e > level, u_vel[level, own] - slope_e, 0.0)
            u_rows[level, at : at + OV] = u
            v = jnp.where(depth_n > level, v_vel[level, own] - slope_n, 0.0)
            v_out[level, own] = v
            south = jnp.concatenate([zero, v[:, :-1]], axis=1)
            flow = (u - u_rows[level, at - 1 : at + OV - 1]) + (v - south)
            w_sum = w_sum + jnp.where(d > level, flow, 0.0)
            w_out[level, own] = w_sum
            if block == 0:
                send(copies, level, at, u_rows, v_out, w_out, u_new, v_new, w_vel, sems)
        if block > 0:
            send(copies, slice(None), at, u_rows, v_out, w_out, u_new, v_new, w_vel, sems)
    for copy in copies:
        copy.wait()


def swap_pairs(block, outward):
    devices = lax.axis_size("lon")
    if outward:
        route = [(i, (i - 1 if i % 2 == 0 else i + 1) % devices) for i in range(devices)]
    else:
        route = [(i, i ^ 1) for i in range(devices)]
    return lax.ppermute(block, "lon", route)


def shape(*dims):
    return jax.ShapeDtypeStruct(dims, F32)


def body(source, diagonal, u_vel, v_vel, bottom):
    cells, lat = source.shape
    span = cells + 2 * OV
    devices = lax.axis_size("lon")
    parity = (lax.axis_index("lon") % 2).astype(jnp.int32).reshape(1)
    consts = [jnp.asarray(table) for table in tables(span)]
    hbm = {name: pltpu.with_memory_space_constraint(x, pltpu.HBM) for name, x in (
        ("source", source), ("diagonal", diagonal), ("u", u_vel), ("v", v_vel), ("bottom", bottom))}
    consts = [pltpu.with_memory_space_constraint(x, pltpu.HBM) for x in consts]

    inner, outer = pl.pallas_call(
        first_edges,
        in_specs=[SM, HB, HB],
        out_specs=[VM] * 2,
        out_shape=[pltpu.VMEM((OV, lat), F32)] * 2,
        scratch_shapes=[pltpu.VMEM((OV, lat), F32)] * 2
        + [pltpu.VMEM((OV, lat), jnp.int32)] * 2
        + [pltpu.SemaphoreType.DMA((4,))],
        compiler_params=PARAMS,
        name="first_edges",
    )(parity, hbm["source"], hbm["bottom"])
    near = swap_pairs(inner, False), swap_pairs(outer, True)

    masked, coef_own, depth, source_v, *held = pl.pallas_call(
        prepare,
        in_specs=[HB] * 9,
        out_specs=[VM] * 8,
        out_shape=[pltpu.VMEM((cells, lat), F32)] * 4
        + [pltpu.VMEM(table.shape, table.dtype) for table in consts],
        scratch_shapes=[
            pltpu.VMEM((cells, lat), F32),
            pltpu.VMEM((cells, lat), jnp.int32),
            pltpu.SemaphoreType.DMA((7,)),
        ],
        compiler_params=PARAMS,
        cost_estimate=pl.CostEstimate(flops=10**6, bytes_accessed=7 * 10**6, transcendentals=0),
        name="prepare",
    )(inner, outer, hbm["source"], hbm["diagonal"], hbm["bottom"], *consts)

    blocks = -(-lat // LANE)
    first, inner, outer, u_v, v_v = pl.pallas_call(
        first_solve,
        in_specs=[SM] + [VM] * 4 + [HB] * 2 + [VM] * 4,
        out_specs=[VM] * 5,
        out_shape=[pltpu.VMEM((span, lat), F32)]
        + [pltpu.VMEM(((3 * OV + 2) * blocks, LANE), F32)] * 2
        + [pltpu.VMEM((KL, cells, lat), F32)] * 2,
        scratch_shapes=solve_scratch(span, lat) + [pltpu.SemaphoreType.DMA((2,))],
        compiler_params=PARAMS,
        name="first_solve",
    )(parity, *near, masked, coef_own, hbm["u"], hbm["v"], *held)
    near = swap_pairs(inner, False), swap_pairs(outer, True)

    z, y, coef, second, inner, outer = pl.pallas_call(
        second_solve,
        in_specs=[SM] + [VM] * 10,
        out_specs=[VM] * 6,
        out_shape=[pltpu.VMEM((span, lat), F32)] * 4 + [pltpu.VMEM((2 * OV, lat), F32)] * 2,
        scratch_shapes=solve_scratch(span, lat) + [pltpu.VMEM((span + 2 * OV, lat), F32)] * 2,
        compiler_params=PARAMS,
        name="second_solve",
    )(parity, *near, first, coef_own, depth, u_v, *held)
    near = swap_pairs(inner, False), swap_pairs(outer, True)

    w, edges, sent = pl.pallas_call(
        sums,
        in_specs=[SM] + [VM] * 7,
        out_specs=[VM] * 3,
        out_shape=[pltpu.VMEM((span, lat), F32), pltpu.VMEM((2 * OV, lat), F32),
                   pltpu.VMEM((devices, 8, LANE), F32)],
        compiler_params=PARAMS,
        name="sums",
    )(parity, *near, second, z, y, coef, source_v)
    came = lax.all_to_all(sent, "lon", 0, 0)

    return pl.pallas_call(
        finish,
        in_specs=[VM] * 8,
        out_specs=[HB] * 4,
        out_shape=[shape(cells, lat)] + [shape(KL, cells, lat)] * 3,
        scratch_shapes=[
            pltpu.VMEM((span, lat), F32),
            pltpu.VMEM((span, lat), F32),
            pltpu.VMEM((KL, OV + cells, lat), F32),
            pltpu.VMEM((KL, cells, lat), F32),
            pltpu.VMEM((KL, cells, lat), F32),
            pltpu.VMEM((cells, lat), F32),
            pltpu.SemaphoreType.DMA((1 + 3 * (KL + cells // OV - 1),)),
        ],
        compiler_params=PARAMS,
        name="finish",
    )(came, z, w, edges, source_v, depth, u_v, v_v)


def solution(mesh):
    return jax.shard_map(
        body,
        mesh=mesh,
        in_specs=(
            P(("members", "lon"), None),
            P(("members", "lon"), None),
            P(None, ("members", "lon"), None),
            P(None, ("members", "lon"), None),
            P(("members", "lon"), None),
        ),
        out_specs=(
            P(("members", "lon"), None),
            P(None, ("members", "lon"), None),
            P(None, ("members", "lon"), None),
            P(None, ("members", "lon"), None),
        ),
        check_vma=False,
    )
```

```python
import math

import jax
import jax.numpy as jnp
import ml_dtypes
import numpy as np
from jax import lax
from jax.experimental import pallas as pl
from jax.experimental.pallas import tpu as pltpu
from jax.sharding import PartitionSpec as P

LT = 112
OV = 8
KL = 6
LANE = 128

tile_shift = 0.1
gravity_step = 0.5

F32 = jnp.float32
BF16 = jnp.bfloat16
VM = pl.BlockSpec(memory_space=pltpu.VMEM)
SM = pl.BlockSpec(memory_space=pltpu.SMEM)
HB = pl.BlockSpec(memory_space=pl.ANY)
PARAMS = pltpu.CompilerParams(vmem_limit_bytes=32 * 1024 * 1024)


def sine_basis(length):
    ordinal = np.arange(length, dtype=np.float64) + 1.0
    angles = math.pi * ordinal[:, None] * ordinal[None, :] / (length + 1)
    basis_matrix = np.sqrt(2.0 / (length + 1)) * np.sin(angles)
    eigen_value = 2.0 - 2.0 * np.cos(math.pi * ordinal / (length + 1))
    return basis_matrix, eigen_value


def halves(matrix):
    high = matrix.astype(ml_dtypes.bfloat16)
    low = (matrix - high.astype(np.float64)).astype(ml_dtypes.bfloat16)
    return high, low


def window_at(tile):
    return divmod(tile * LT - OV + LANE, LANE)


def tables(span):
    lon_basis, lon_value = sine_basis(span)
    lat_basis, lat_value = sine_basis(LT + 2 * OV)
    high, low = halves(lat_basis)
    forward = np.zeros((8, 2 * LANE, 2 * LANE), ml_dtypes.bfloat16)
    inverse = np.zeros((8, 2 * LANE, 2 * LANE), ml_dtypes.bfloat16)
    for kind in range(8):
        lane = window_at(kind)[1]
        forward[kind, lane : lane + LANE, :LANE] = high
        forward[kind, lane : lane + LANE, LANE:] = low
        inverse[kind, :LANE, lane : lane + LANE] = high.T
        inverse[kind, LANE:, lane : lane + LANE] = low.T
    high, low = halves(lon_basis)
    lon = np.concatenate([high, low, high], axis=1)
    scale = 1.0 / (lon_value[:, None] + lat_value[None, :] + tile_shift)
    return forward, inverse, lon, scale.astype(np.float32)


def split(x):
    high = x.astype(BF16)
    return high, (x - high.astype(F32)).astype(BF16)


def tile_solve(x, forward, inverse, lon, scale, wide, spectral, restored, out):
    span, lat = x.shape
    tiles = lat // LT
    high, low = split(x)
    wide[:, :LANE] = jnp.zeros((2 * span, LANE), BF16)
    wide[:, LANE + lat :] = jnp.zeros((2 * span, wide.shape[1] - LANE - lat), BF16)
    wide[:span, LANE : LANE + lat] = high
    wide[span:, LANE : LANE + lat] = low
    for kind in range(8):
        group = range(kind, tiles, 8)
        starts = [window_at(t)[0] * LANE for t in group]
        rows = jnp.concatenate([wide[:, s : s + 2 * LANE] for s in starts], axis=0)
        product = jnp.dot(rows, forward[kind], preferred_element_type=F32)
        for i, t in enumerate(group):
            part = product[2 * span * i : 2 * span * (i + 1)]
            part = part[:, :LANE] + part[:, LANE:]
            high, low = split(part[:span] + part[span:])
            at = pl.ds(t * LANE, LANE)
            spectral[:span, at] = high
            spectral[span : 2 * span, at] = high
            spectral[2 * span :, at] = low
    chunk = 4
    for first in range(0, tiles, chunk):
        n = min(chunk, tiles - first)
        c = jnp.dot(lon[...], spectral[:, pl.ds(first * LANE, n * LANE)], preferred_element_type=F32)
        c = c * jnp.concatenate([scale[...]] * n, axis=1)
        high, low = split(c)
        c = jnp.concatenate([high, high, low], axis=0)
        c = jnp.dot(lon[...], c, preferred_element_type=F32)
        high, low = split(c)
        for i in range(n):
            for side in range(2):
                at = pl.ds((2 * (first + i) + side) * LANE, LANE)
                restored[:span, at] = high[:, i * LANE : (i + 1) * LANE]
                restored[span:, at] = low[:, i * LANE : (i + 1) * LANE]
    out[...] = jnp.zeros(out.shape, F32)
    for kind in range(8):
        group = range(kind, tiles, 8)
        rows = jnp.concatenate(
            [restored[:, pl.ds(2 * t * LANE, 2 * LANE)] for t in group], axis=0
        )
        product = jnp.dot(rows, inverse[kind], preferred_element_type=F32)
        for i, t in enumerate(group):
            part = product[2 * span * i : 2 * span * (i + 1)]
            at = pl.ds(window_at(t)[0] * LANE, 2 * LANE)
            out[:, at] += part[:span] + part[span:]


def solve_scratch(span, lat):
    tiles = lat // LT
    lanes = (window_at(tiles - 1)[0] + 2) * LANE
    return [
        pltpu.VMEM((2 * span, lanes), BF16),
        pltpu.VMEM((3 * span, tiles * LANE), BF16),
        pltpu.VMEM((2 * span, 2 * tiles * LANE), BF16),
        pltpu.VMEM((span, lanes), F32),
    ]


def pick(parity, inner, outer):
    even = jnp.full(inner.shape, parity[0], jnp.int32) == 0
    return jnp.where(even, outer, inner), jnp.where(even, inner, outer)


def lat_beside(m):
    zero = jnp.zeros((m.shape[0], 1), m.dtype)
    return jnp.concatenate([m[:, 1:], zero], axis=1) + jnp.concatenate([zero, m[:, :-1]], axis=1)


def pack(message, rows):
    n, lat = rows.shape
    for block, at in enumerate(range(0, lat, LANE)):
        width = min(LANE, lat - at)
        message[block * n : (block + 1) * n, :width] = rows[:, at : at + width]


def unpack(message, n, lat):
    blocks = [message[i * n : (i + 1) * n] for i in range(-(-lat // LANE))]
    return jnp.concatenate(blocks, axis=1)[:, :lat]


def first_edges(parity, source, bottom, outer, rows, depth, sems):
    start = pl.multiple_of(parity[0] * (source.shape[0] - OV), OV)
    at = pl.ds(start, OV)
    copies = [
        pltpu.make_async_copy(source.at[at], rows, sems.at[0]),
        pltpu.make_async_copy(bottom.at[at], depth, sems.at[1]),
    ]
    for copy in copies:
        copy.start()
    for copy in copies:
        copy.wait()
    outer[...] = jnp.where(depth[...] > 0, rows[...], 0.0)


def prepare(parity, after, source_h, diagonal_h, bottom_h, *refs):
    tables_h, (inner, masked, coef, depth, source), held = refs[:4], refs[4:9], refs[9:13]
    diagonal, bottom, sems = refs[13:]
    pairs = [(source_h, source), (bottom_h, bottom), (diagonal_h, diagonal)]
    pairs += list(zip(tables_h, held))
    copies = [pltpu.make_async_copy(a, b, sems.at[i]) for i, (a, b) in enumerate(pairs)]
    for copy in copies:
        copy.start()
    for copy in copies[:3]:
        copy.wait()
    wet = bottom[...] > 0
    masked[...] = jnp.where(wet, source[...], 0.0)
    coef[...] = jnp.where(wet, 4.0 + diagonal[...], 0.0)
    depth[...] = bottom[...].astype(F32)
    inner[...] = pick(parity, masked[:OV], masked[source.shape[0] - OV :])[0]
    for copy in copies[3:]:
        copy.wait()


def first_solve(parity, inner_in, outer_in, masked, coef, forward, inverse, lon, scale,
                first, inner, outer, wide, spectral, restored, out):
    cells, lat = masked.shape
    west, east = pick(parity, inner_in[...], outer_in[...])
    x = jnp.concatenate([west, masked[...], east], axis=0)
    tile_solve(x, forward, inverse, lon, scale, wide, spectral, restored, out)
    first[...] = out[:, LANE : LANE + lat]
    reach, edge = 2 * OV + 1, OV + 1
    to_west = jnp.concatenate([first[:reach], coef[:edge]], axis=0)
    to_east = jnp.concatenate([first[cells - 1 :], coef[cells - edge :]], axis=0)
    to_outer, to_inner = pick(parity, to_east, to_west)
    pack(inner, to_inner)
    pack(outer, to_outer)


def absorb(after, u_h, v_h, u, v, u_before, v_before, sems):
    copies = [pltpu.make_async_copy(a, b, sems.at[i]) for i, (a, b) in enumerate([(u_h, u), (v_h, v)])]
    for copy in copies:
        copy.start()
    levels, cells, lat = u.shape
    copies[0].wait()
    for level in range(levels):
        u_before[level] = jnp.concatenate([jnp.zeros((1, lat), F32), u[level, : cells - 1]], axis=0)
    copies[1].wait()
    for level in range(levels):
        v_before[level] = jnp.concatenate([jnp.zeros((cells, 1), F32), v[level, :, : lat - 1]], axis=1)


def second_solve(parity, inner_in, outer_in, first, coef_own, depth, u, forward, inverse, lon, scale,
                 z, y, coef, second, inner, outer, wide, spectral, restored, out, m_rows, c_rows):
    cells, lat = coef_own.shape
    span = cells + 2 * OV
    reach, edge = 2 * OV + 1, OV + 1
    west, east = pick(
        parity, unpack(inner_in, reach + edge, lat), unpack(outer_in, reach + edge, lat)
    )
    c_rows[:OV] = jnp.zeros((OV, lat), F32)
    c_rows[OV - 1 : 2 * OV] = west[reach:]
    c_rows[2 * OV : 2 * OV + cells] = coef_own[...]
    c_rows[2 * OV + cells + OV :] = jnp.zeros((OV, lat), F32)
    c_rows[2 * OV + cells : 2 * OV + cells + edge] = east[reach:]
    m_rows[:OV] = jnp.zeros((OV, lat), F32)
    m_rows[OV : OV + span] = first[...]
    m_rows[OV + span :] = jnp.zeros((OV, lat), F32)
    m_rows[OV - 1 : OV - 1 + reach] += west[:reach]
    m_rows[OV + cells : OV + cells + reach] += east[:reach]
    m_rows[...] = jnp.where(c_rows[...] > 0, m_rows[...], 0.0)
    inside = slice(OV, OV + span)
    c, m = c_rows[inside], m_rows[inside]
    coef[...] = c
    z[...] = m
    beside = m_rows[OV - 1 : OV - 1 + span] + m_rows[OV + 1 : OV + 1 + span]
    image = jnp.where(c > 0, c * m - (beside + lat_beside(m)), 0.0)
    y[...] = image
    tile_solve(image, forward, inverse, lon, scale, wide, spectral, restored, out)
    second[...] = out[:, LANE : LANE + lat]
    to_west = jnp.concatenate([second[:edge], depth[:1], jnp.zeros((KL, lat), F32)], axis=0)
    u_rows = [u[level, cells - 1 : cells] for level in range(KL)]
    to_east = jnp.concatenate([second[span - edge :], depth[cells - 1 :]] + u_rows, axis=0)
    outer[...], inner[...] = pick(parity, to_east, to_west)


def sums(parity, inner_in, outer_in, second, z, y, coef, source, w, edges, sent):
    cells, lat = source.shape
    west, east = pick(parity, inner_in[...], outer_in[...])
    edges[:OV] = west[OV:]
    edges[OV:] = east[OV:]
    w[...] = second[...]
    w[OV - 1 : 2 * OV] += west[: OV + 1]
    w[cells : cells + OV + 1] += east[: OV + 1]
    w[...] = jnp.where(coef[...] > 0, w[...], 0.0)
    own = slice(OV, OV + cells)
    c, m = coef[own], w[own]
    wet = c > 0
    beside = w[OV - 1 : OV - 1 + cells] + w[OV + 1 : OV + 1 + cells]
    x = jnp.where(wet, c * m - (beside + lat_beside(m)), 0.0)
    masked = jnp.where(wet, source[...], 0.0)
    land = jnp.where(wet, 0.0, source[...])
    z_own, y_own = z[own], y[own]

    def partial(a, b):
        product = a * b
        rows = product[:OV]
        for at in range(OV, cells, OV):
            rows = rows + product[at : at + OV]
        whole = lat // LANE * LANE
        total = rows[:, :LANE]
        for at in range(LANE, whole, LANE):
            total = total + rows[:, at : at + LANE]
        if whole < lat:
            blank = jnp.zeros((OV, LANE - lat + whole), F32)
            total = total + jnp.concatenate([rows[:, whole:], blank], axis=1)
        return jnp.sum(jnp.sum(total, axis=0, keepdims=True), axis=1, keepdims=True)

    pairs = [(masked, z_own), (z_own, y_own), (masked, m), (y_own, m), (z_own, x), (m, x), (land, land)]
    lane = lax.broadcasted_iota(jnp.int32, (1, LANE), 1)
    row = jnp.zeros((1, LANE), F32)
    for i, (a, b) in enumerate(pairs):
        row = jnp.where(lane == i, partial(a, b), row)
    sent[...] = jnp.broadcast_to(row[None], sent.shape)


def finish(came, z, w, edges, source, depth, u_vel, v_vel, u_before, v_before, solution, u_new, v_new, w_vel,
           s_rows, d_rows, u_out, v_out, w_out, s_out, sems):
    cells, lat = source.shape
    total = jnp.sum(came[...], axis=0)
    rz, zy, rw, yw, zx, wx, ll = [total[:, i : i + 1] for i in range(7)]
    step0 = (rz + ll) / (zy + ll)
    rest = (zy - rz) / (zy + ll)
    new = rz - step0 * (zy + rw) + step0 * step0 * yw + rest * rest * ll
    beta = new / (rz + ll)
    grown = 1.0 + beta
    bent = grown * grown * zy - grown * step0 * (zx + yw) + step0 * step0 * wx
    step1 = new / (bent + (rest + beta) * (rest + beta) * ll)
    of_z = jnp.broadcast_to(step0 + step1 * grown, (OV, lat))
    of_w = jnp.broadcast_to(-step1 * step0, (OV, lat))
    of_land = jnp.broadcast_to(step0 + step1 * (rest + beta), (OV, lat))

    d_rows[:OV] = jnp.broadcast_to(edges[1:2], (OV, lat))
    d_rows[OV : OV + cells] = depth[...]
    d_rows[OV + cells :] = jnp.broadcast_to(edges[OV + 1 : OV + 2], (OV, lat))
    first_row = lax.broadcasted_iota(jnp.int32, (OV, 3 * LANE), 0) == 0
    copies = []

    def rows_of_surface(at):
        s = of_z * z[at : at + OV] + of_w * w[at : at + OV]
        if OV <= at < OV + cells:
            s = jnp.where(d_rows[at : at + OV] > 0, s, of_land * source[at - OV : at])
            s_out[at - OV : at] = s
        s_rows[at : at + OV] = s

    def send(held, result):
        copies.append(pltpu.make_async_copy(held, result, sems.at[len(copies)]))
        copies[-1].start()

    rows_of_surface(0)
    rows_of_surface(OV)
    zero = jnp.zeros((OV, 1), F32)
    for at in range(OV, OV + cells, OV):
        rows_of_surface(at + OV)
        own = slice(at - OV, at)
        s, d = s_rows[at : at + OV], d_rows[at : at + OV]
        slope_e = gravity_step * (s_rows[at + 1 : at + OV + 1] - s)
        depth_e = jnp.minimum(d, d_rows[at + 1 : at + OV + 1])
        slope_w = gravity_step * (s - s_rows[at - 1 : at + OV - 1])
        depth_w = jnp.minimum(d, d_rows[at - 1 : at + OV - 1])
        slope_n = gravity_step * (jnp.concatenate([s[:, 1:], zero], axis=1) - s)
        depth_n = jnp.minimum(d, jnp.concatenate([d[:, 1:], zero], axis=1))
        slope_s = jnp.concatenate([zero, slope_n[:, :-1]], axis=1)
        depth_s = jnp.concatenate([zero, depth_n[:, :-1]], axis=1)
        for first in range(0, lat, 3 * LANE):
            part = slice(first, min(first + 3 * LANE, lat))
            d_p, de, dw, dn, ds = [x[:, part] for x in (d, depth_e, depth_w, depth_n, depth_s)]
            se, sw, sn, ss = [x[:, part] for x in (slope_e, slope_w, slope_n, slope_s)]
            w_sum = jnp.zeros(d_p.shape, F32)
            for level in range(KL - 1, -1, -1):
                u = jnp.where(de > level, u_vel[level, own, part] - se, 0.0)
                v = jnp.where(dn > level, v_vel[level, own, part] - sn, 0.0)
                before = u_before[level, own, part]
                if at == OV:
                    edge = jnp.broadcast_to(edges[level + 2 : level + 3, part], before.shape)
                    before = jnp.where(first_row[:, : before.shape[1]], edge, before)
                u_west = jnp.where(dw > level, before - sw, 0.0)
                v_south = jnp.where(ds > level, v_before[level, own, part] - ss, 0.0)
                w_sum = w_sum + jnp.where(d_p > level, (u - u_west) + (v - v_south), 0.0)
                u_out[level, own, part] = u
                v_out[level, own, part] = v
                w_out[level, own, part] = w_sum
        for held, result in ((u_out, u_new), (v_out, v_new), (w_out, w_vel)):
            send(held.at[:, own], result.at[:, own])
        if at == cells:
            send(s_out, solution)
    for copy in copies:
        copy.wait()


def swap_pairs(block, outward):
    devices = lax.axis_size("lon")
    if outward:
        route = [(i, (i - 1 if i % 2 == 0 else i + 1) % devices) for i in range(devices)]
    else:
        route = [(i, i ^ 1) for i in range(devices)]
    return lax.ppermute(block, "lon", route)


def shape(*dims):
    return jax.ShapeDtypeStruct(dims, F32)


def body(source, diagonal, u_vel, v_vel, bottom):
    cells, lat = source.shape
    span = cells + 2 * OV
    devices = lax.axis_size("lon")
    parity = (lax.axis_index("lon") % 2).astype(jnp.int32).reshape(1)
    consts = [jnp.asarray(table) for table in tables(span)]
    hbm = {name: pltpu.with_memory_space_constraint(x, pltpu.HBM) for name, x in (
        ("source", source), ("diagonal", diagonal), ("u", u_vel), ("v", v_vel), ("bottom", bottom))}
    consts = [pltpu.with_memory_space_constraint(x, pltpu.HBM) for x in consts]

    outer = pl.pallas_call(
        first_edges,
        in_specs=[SM, HB, HB],
        out_specs=VM,
        out_shape=pltpu.VMEM((OV, lat), F32),
        scratch_shapes=[pltpu.VMEM((OV, lat), F32), pltpu.VMEM((OV, lat), jnp.int32),
                        pltpu.SemaphoreType.DMA((2,))],
        compiler_params=PARAMS,
        name="first_edges",
    )(parity, hbm["source"], hbm["bottom"])
    outer_in = swap_pairs(outer, True)

    inner, masked, coef_own, depth, source_v, *held = pl.pallas_call(
        prepare,
        in_specs=[SM] + [HB] * 8,
        out_specs=[VM] * 9,
        out_shape=[pltpu.VMEM((OV, lat), F32)]
        + [pltpu.VMEM((cells, lat), F32)] * 4
        + [pltpu.VMEM(table.shape, table.dtype) for table in consts],
        scratch_shapes=[
            pltpu.VMEM((cells, lat), F32),
            pltpu.VMEM((cells, lat), jnp.int32),
            pltpu.SemaphoreType.DMA((7,)),
        ],
        compiler_params=PARAMS,
        cost_estimate=pl.CostEstimate(flops=10**6, bytes_accessed=7 * 10**6, transcendentals=0),
        name="prepare",
    )(parity, outer, hbm["source"], hbm["diagonal"], hbm["bottom"], *consts)
    near = swap_pairs(inner, False), outer_in

    blocks = -(-lat // LANE)
    first, inner, outer = pl.pallas_call(
        first_solve,
        in_specs=[SM] + [VM] * 8,
        out_specs=[VM] * 3,
        out_shape=[pltpu.VMEM((span, lat), F32)]
        + [pltpu.VMEM(((3 * OV + 2) * blocks, LANE), F32)] * 2,
        scratch_shapes=solve_scratch(span, lat),
        compiler_params=PARAMS,
        name="first_solve",
    )(parity, *near, masked, coef_own, *held)
    near = swap_pairs(inner, False), swap_pairs(outer, True)

    u_v, v_v, u_shift, v_shift = pl.pallas_call(
        absorb,
        in_specs=[HB] * 3,
        out_specs=[VM] * 4,
        out_shape=[pltpu.VMEM((KL, cells, lat), F32)] * 4,
        scratch_shapes=[pltpu.SemaphoreType.DMA((2,))],
        compiler_params=PARAMS,
        cost_estimate=pl.CostEstimate(flops=10**6, bytes_accessed=7 * 10**6, transcendentals=0),
        name="absorb",
    )(first, hbm["u"], hbm["v"])

    z, y, coef, second, inner, outer = pl.pallas_call(
        second_solve,
        in_specs=[SM] + [VM] * 10,
        out_specs=[VM] * 6,
        out_shape=[pltpu.VMEM((span, lat), F32)] * 4 + [pltpu.VMEM((2 * OV, lat), F32)] * 2,
        scratch_shapes=solve_scratch(span, lat) + [pltpu.VMEM((span + 2 * OV, lat), F32)] * 2,
        compiler_params=PARAMS,
        name="second_solve",
    )(parity, *near, first, coef_own, depth, u_v, *held)
    near = swap_pairs(inner, False), swap_pairs(outer, True)

    w, edges, sent = pl.pallas_call(
        sums,
        in_specs=[SM] + [VM] * 7,
        out_specs=[VM] * 3,
        out_shape=[pltpu.VMEM((span, lat), F32), pltpu.VMEM((2 * OV, lat), F32),
                   pltpu.VMEM((devices, 1, LANE), F32)],
        compiler_params=PARAMS,
        name="sums",
    )(parity, *near, second, z, y, coef, source_v)
    came = lax.all_to_all(sent, "lon", 0, 0)

    return pl.pallas_call(
        finish,
        in_specs=[VM] * 10,
        out_specs=[HB] * 4,
        out_shape=[shape(cells, lat)] + [shape(KL, cells, lat)] * 3,
        scratch_shapes=[pltpu.VMEM((span, lat), F32)] * 2
        + [pltpu.VMEM((KL, cells, lat), F32)] * 3
        + [pltpu.VMEM((cells, lat), F32), pltpu.SemaphoreType.DMA((1 + 3 * (cells // OV),))],
        compiler_params=PARAMS,
        name="finish",
    )(came, z, w, edges, source_v, depth, u_v, v_v, u_shift, v_shift)


def solution(mesh):
    return jax.shard_map(
        body,
        mesh=mesh,
        in_specs=(
            P(("members", "lon"), None),
            P(("members", "lon"), None),
            P(None, ("members", "lon"), None),
            P(None, ("members", "lon"), None),
            P(("members", "lon"), None),
        ),
        out_specs=(
            P(("members", "lon"), None),
            P(None, ("members", "lon"), None),
            P(None, ("members", "lon"), None),
            P(None, ("members", "lon"), None),
        ),
        check_vma=False,
    )
```

```python
import math

import jax
import jax.numpy as jnp
import ml_dtypes
import numpy as np
from jax import lax
from jax.experimental import pallas as pl
from jax.experimental.pallas import tpu as pltpu
from jax.sharding import PartitionSpec as P

LT = 112
OV = 8
KL = 6
LANE = 128

tile_shift = 0.1
gravity_step = 0.5

F32 = jnp.float32
BF16 = jnp.bfloat16
VM = pl.BlockSpec(memory_space=pltpu.VMEM)
SM = pl.BlockSpec(memory_space=pltpu.SMEM)
HB = pl.BlockSpec(memory_space=pl.ANY)
PARAMS = pltpu.CompilerParams(vmem_limit_bytes=32 * 1024 * 1024)


def sine_basis(length):
    ordinal = np.arange(length, dtype=np.float64) + 1.0
    angles = math.pi * ordinal[:, None] * ordinal[None, :] / (length + 1)
    basis_matrix = np.sqrt(2.0 / (length + 1)) * np.sin(angles)
    eigen_value = 2.0 - 2.0 * np.cos(math.pi * ordinal / (length + 1))
    return basis_matrix, eigen_value


def halves(matrix):
    high = matrix.astype(ml_dtypes.bfloat16)
    low = (matrix - high.astype(np.float64)).astype(ml_dtypes.bfloat16)
    return high, low


def tables(span):
    lon_basis, lon_value = sine_basis(span)
    lat_basis, lat_value = sine_basis(LT + 2 * OV)
    high, low = halves(lat_basis)
    lat = np.block([[high, low], [high, np.zeros_like(low)]])
    high, low = halves(lon_basis)
    lon = np.concatenate([high, low, high], axis=1)
    scale = 1.0 / (lon_value[:, None] + lat_value[None, :] + tile_shift)
    return lat, lon, scale.astype(np.float32)


def split(x):
    high = x.astype(BF16)
    return high, (x - high.astype(F32)).astype(BF16)


def tile_solve(x, lat_basis, lon, scale, wide, rows, spectral, out):
    span, lat = x.shape
    tiles = lat // LT
    high, low = split(x)
    for at, part in ((0, high), (span, low)):
        wide[at : at + span, :LANE] = jnp.zeros((span, LANE), BF16)
        wide[at : at + span, LANE : LANE + lat] = part
        wide[at : at + span, LANE + lat :] = jnp.zeros((span, wide.shape[1] - LANE - lat), BF16)
    for t in range(tiles):
        block, lane = divmod(LANE + t * LT - OV, LANE)
        window = wide[:, block * LANE : (block + 2) * LANE][:, lane : lane + LANE]
        rows[t * span : (t + 1) * span, :LANE] = window[:span]
        rows[t * span : (t + 1) * span, LANE:] = window[span:]
    chunk = 4
    for first in range(0, tiles, chunk):
        n = min(chunk, tiles - first)
        product = jnp.dot(
            rows[first * span : (first + n) * span], lat_basis[...], preferred_element_type=F32
        )
        high, low = split(product[:, :LANE] + product[:, LANE:])
        for i in range(n):
            at = slice((first + i) * LANE, (first + i + 1) * LANE)
            spectral[:span, at] = high[i * span : (i + 1) * span]
            spectral[span : 2 * span, at] = high[i * span : (i + 1) * span]
            spectral[2 * span :, at] = low[i * span : (i + 1) * span]
    for first in range(0, tiles, chunk):
        n = min(chunk, tiles - first)
        c = jnp.dot(lon[...], spectral[:, first * LANE : (first + n) * LANE], preferred_element_type=F32)
        c = c * jnp.concatenate([scale[...]] * n, axis=1)
        high, low = split(c)
        c = jnp.concatenate([high, high, low], axis=0)
        c = jnp.dot(lon[...], c, preferred_element_type=F32)
        high, low = split(c)
        for i in range(n):
            at = slice((first + i) * span, (first + i + 1) * span)
            rows[at, :LANE] = high[:, i * LANE : (i + 1) * LANE]
            rows[at, LANE:] = low[:, i * LANE : (i + 1) * LANE]
    out[...] = jnp.zeros(out.shape, F32)
    for first in range(0, tiles, chunk):
        n = min(chunk, tiles - first)
        product = jnp.dot(
            rows[first * span : (first + n) * span], lat_basis[...], preferred_element_type=F32
        )
        product = product[:, :LANE] + product[:, LANE:]
        for i in range(n):
            at = (first + i) * LT
            out[:, at : at + LANE] += product[i * span : (i + 1) * span]


def solve_scratch(span, lat):
    tiles = lat // LT
    lanes = -(-(LANE + lat + OV) // LANE) * LANE
    return [
        pltpu.VMEM((2 * span, lanes), BF16),
        pltpu.VMEM((tiles * span, 2 * LANE), BF16),
        pltpu.VMEM((3 * span, tiles * LANE), BF16),
        pltpu.VMEM((span, lanes), F32),
    ]


def pick(parity, inner, outer):
    even = jnp.full(inner.shape, parity[0], jnp.int32) == 0
    return jnp.where(even, outer, inner), jnp.where(even, inner, outer)


def lat_beside(m):
    zero = jnp.zeros((m.shape[0], 1), m.dtype)
    return jnp.concatenate([m[:, 1:], zero], axis=1) + jnp.concatenate([zero, m[:, :-1]], axis=1)


def pack(message, rows):
    n, lat = rows.shape
    for block, at in enumerate(range(0, lat, LANE)):
        width = min(LANE, lat - at)
        message[block * n : (block + 1) * n, :width] = rows[:, at : at + width]


def unpack(message, n, lat):
    blocks = [message[i * n : (i + 1) * n] for i in range(-(-lat // LANE))]
    return jnp.concatenate(blocks, axis=1)[:, :lat]


def first_edges(parity, source, bottom, outer, rows, depth, sems):
    start = pl.multiple_of(parity[0] * (source.shape[0] - OV), OV)
    at = pl.ds(start, OV)
    copies = [
        pltpu.make_async_copy(source.at[at], rows, sems.at[0]),
        pltpu.make_async_copy(bottom.at[at], depth, sems.at[1]),
    ]
    for copy in copies:
        copy.start()
    for copy in copies:
        copy.wait()
    outer[...] = jnp.where(depth[...] > 0, rows[...], 0.0)


def prepare(parity, after, source_h, diagonal_h, bottom_h, *refs):
    tables_h, (inner, masked, coef, depth, source), held = refs[:3], refs[3:8], refs[8:11]
    diagonal, bottom, sems = refs[11:]
    pairs = [(source_h, source), (bottom_h, bottom), (diagonal_h, diagonal)]
    pairs += list(zip(tables_h, held))
    copies = [pltpu.make_async_copy(a, b, sems.at[i]) for i, (a, b) in enumerate(pairs)]
    for copy in copies:
        copy.start()
    for copy in copies[:3]:
        copy.wait()
    wet = bottom[...] > 0
    masked[...] = jnp.where(wet, source[...], 0.0)
    coef[...] = jnp.where(wet, 4.0 + diagonal[...], 0.0)
    depth[...] = bottom[...].astype(F32)
    inner[...] = pick(parity, masked[:OV], masked[source.shape[0] - OV :])[0]
    for copy in copies[3:]:
        copy.wait()


def first_solve(parity, inner_in, outer_in, masked, coef, lat_basis, lon, scale,
                first, inner, outer, wide, rows, spectral, out):
    cells, lat = masked.shape
    west, east = pick(parity, inner_in[...], outer_in[...])
    x = jnp.concatenate([west, masked[...], east], axis=0)
    tile_solve(x, lat_basis, lon, scale, wide, rows, spectral, out)
    first[...] = out[:, OV : OV + lat]
    reach, edge = 2 * OV + 1, OV + 1
    to_west = jnp.concatenate([first[:reach], coef[:edge]], axis=0)
    to_east = jnp.concatenate([first[cells - 1 :], coef[cells - edge :]], axis=0)
    to_outer, to_inner = pick(parity, to_east, to_west)
    pack(inner, to_inner)
    pack(outer, to_outer)


def absorb(after, u_h, v_h, u, v, sems):
    copies = [pltpu.make_async_copy(a, b, sems.at[i]) for i, (a, b) in enumerate([(u_h, u), (v_h, v)])]
    for copy in copies:
        copy.start()
    for copy in copies:
        copy.wait()


def second_solve(parity, inner_in, outer_in, first, coef_own, depth, u, lat_basis, lon, scale,
                 z, y, coef, second, inner, outer, wide, rows, spectral, out, m_rows, c_rows):
    cells, lat = coef_own.shape
    span = cells + 2 * OV
    reach, edge = 2 * OV + 1, OV + 1
    west, east = pick(
        parity, unpack(inner_in, reach + edge, lat), unpack(outer_in, reach + edge, lat)
    )
    c_rows[:OV] = jnp.zeros((OV, lat), F32)
    c_rows[OV - 1 : 2 * OV] = west[reach:]
    c_rows[2 * OV : 2 * OV + cells] = coef_own[...]
    c_rows[2 * OV + cells + OV :] = jnp.zeros((OV, lat), F32)
    c_rows[2 * OV + cells : 2 * OV + cells + edge] = east[reach:]
    m_rows[:OV] = jnp.zeros((OV, lat), F32)
    m_rows[OV : OV + span] = first[...]
    m_rows[OV + span :] = jnp.zeros((OV, lat), F32)
    m_rows[OV - 1 : OV - 1 + reach] += west[:reach]
    m_rows[OV + cells : OV + cells + reach] += east[:reach]
    m_rows[...] = jnp.where(c_rows[...] > 0, m_rows[...], 0.0)
    inside = slice(OV, OV + span)
    c, m = c_rows[inside], m_rows[inside]
    coef[...] = c
    z[...] = m
    beside = m_rows[OV - 1 : OV - 1 + span] + m_rows[OV + 1 : OV + 1 + span]
    image = jnp.where(c > 0, c * m - (beside + lat_beside(m)), 0.0)
    y[...] = image
    tile_solve(image, lat_basis, lon, scale, wide, rows, spectral, out)
    second[...] = out[:, OV : OV + lat]
    to_west = jnp.concatenate([second[:edge], depth[:1], jnp.zeros((KL, lat), F32)], axis=0)
    u_rows = [u[level, cells - 1 : cells] for level in range(KL)]
    to_east = jnp.concatenate([second[span - edge :], depth[cells - 1 :]] + u_rows, axis=0)
    outer[...], inner[...] = pick(parity, to_east, to_west)


def sums(parity, inner_in, outer_in, second, z, y, coef, source, w, edges, sent):
    cells, lat = source.shape
    west, east = pick(parity, inner_in[...], outer_in[...])
    edges[:OV] = west[OV:]
    edges[OV:] = east[OV:]
    w[...] = second[...]
    w[OV - 1 : 2 * OV] += west[: OV + 1]
    w[cells : cells + OV + 1] += east[: OV + 1]
    w[...] = jnp.where(coef[...] > 0, w[...], 0.0)
    own = slice(OV, OV + cells)
    c, m = coef[own], w[own]
    wet = c > 0
    beside = w[OV - 1 : OV - 1 + cells] + w[OV + 1 : OV + 1 + cells]
    x = jnp.where(wet, c * m - (beside + lat_beside(m)), 0.0)
    masked = jnp.where(wet, source[...], 0.0)
    land = jnp.where(wet, 0.0, source[...])
    z_own, y_own = z[own], y[own]

    def partial(a, b):
        product = a * b
        rows = product[:OV]
        for at in range(OV, cells, OV):
            rows = rows + product[at : at + OV]
        whole = lat // LANE * LANE
        total = rows[:, :LANE]
        for at in range(LANE, whole, LANE):
            total = total + rows[:, at : at + LANE]
        if whole < lat:
            blank = jnp.zeros((OV, LANE - lat + whole), F32)
            total = total + jnp.concatenate([rows[:, whole:], blank], axis=1)
        return jnp.sum(jnp.sum(total, axis=0, keepdims=True), axis=1, keepdims=True)

    pairs = [(masked, z_own), (z_own, y_own), (masked, m), (y_own, m), (z_own, x), (m, x), (land, land)]
    lane = lax.broadcasted_iota(jnp.int32, (1, LANE), 1)
    row = jnp.zeros((1, LANE), F32)
    for i, (a, b) in enumerate(pairs):
        row = jnp.where(lane == i, partial(a, b), row)
    sent[...] = jnp.broadcast_to(row[None], sent.shape)


def finish(came, z, w, edges, source, depth, u_vel, v_vel, solution, u_new, v_new, w_vel,
           s_rows, d_rows, u_rows, v_out, w_out, s_out, sems):
    cells, lat = source.shape
    total = jnp.sum(came[...], axis=0)
    rz, zy, rw, yw, zx, wx, ll = [total[:, i : i + 1] for i in range(7)]
    step0 = (rz + ll) / (zy + ll)
    rest = (zy - rz) / (zy + ll)
    new = rz - step0 * (zy + rw) + step0 * step0 * yw + rest * rest * ll
    beta = new / (rz + ll)
    grown = 1.0 + beta
    bent = grown * grown * zy - grown * step0 * (zx + yw) + step0 * step0 * wx
    step1 = new / (bent + (rest + beta) * (rest + beta) * ll)
    of_z = jnp.broadcast_to(step0 + step1 * grown, (OV, lat))
    of_w = jnp.broadcast_to(-step1 * step0, (OV, lat))
    of_land = jnp.broadcast_to(step0 + step1 * (rest + beta), (OV, lat))

    copies = []
    d_rows[:OV] = jnp.broadcast_to(edges[1:2], (OV, lat))
    d_rows[OV : OV + cells] = depth[...]
    d_rows[OV + cells :] = jnp.broadcast_to(edges[OV + 1 : OV + 2], (OV, lat))
    for at in range(0, cells + 2 * OV, OV):
        s = of_z * z[at : at + OV] + of_w * w[at : at + OV]
        if OV <= at < OV + cells:
            d = d_rows[at : at + OV]
            s = jnp.where(d > 0, s, of_land * source[at - OV : at])
            s_out[at - OV : at] = s
        s_rows[at : at + OV] = s
    copies.append(pltpu.make_async_copy(s_out, solution, sems.at[0]))
    copies[-1].start()

    s_west = s_rows[OV - 1 : OV]
    s_first = s_rows[OV : OV + 1]
    d_west = jnp.minimum(d_rows[OV - 1 : OV], d_rows[OV : OV + 1])
    for level in range(KL):
        left = edges[level + 2 : level + 3] - gravity_step * (s_first - s_west)
        u_rows[level, :OV] = jnp.broadcast_to(jnp.where(d_west > level, left, 0.0), (OV, lat))
    zero = jnp.zeros((OV, 1), F32)
    for block in range(cells // OV):
        at = OV + block * OV
        own = slice(at - OV, at)
        s = s_rows[at : at + OV]
        d = d_rows[at : at + OV]
        slope_e = gravity_step * (s_rows[at + 1 : at + OV + 1] - s)
        depth_e = jnp.minimum(d, d_rows[at + 1 : at + OV + 1])
        slope_n = gravity_step * (jnp.concatenate([s[:, 1:], zero], axis=1) - s)
        depth_n = jnp.minimum(d, jnp.concatenate([d[:, 1:], zero], axis=1))
        w_sum = jnp.zeros((OV, lat), F32)
        for level in range(KL - 1, -1, -1):
            u = jnp.where(depth_e > level, u_vel[level, own] - slope_e, 0.0)
            u_rows[level, at : at + OV] = u
            v = jnp.where(depth_n > level, v_vel[level, own] - slope_n, 0.0)
            v_out[level, own] = v
            south = jnp.concatenate([zero, v[:, :-1]], axis=1)
            flow = (u - u_rows[level, at - 1 : at + OV - 1]) + (v - south)
            w_sum = w_sum + jnp.where(d > level, flow, 0.0)
            w_out[level, own] = w_sum
        for held, result in ((u_rows.at[:, at : at + OV], u_new), (v_out.at[:, own], v_new), (w_out.at[:, own], w_vel)):
            copies.append(pltpu.make_async_copy(held, result.at[:, own], sems.at[len(copies)]))
            copies[-1].start()
    for copy in copies:
        copy.wait()


def swap_pairs(block, outward):
    devices = lax.axis_size("lon")
    if outward:
        route = [(i, (i - 1 if i % 2 == 0 else i + 1) % devices) for i in range(devices)]
    else:
        route = [(i, i ^ 1) for i in range(devices)]
    return lax.ppermute(block, "lon", route)


def shape(*dims):
    return jax.ShapeDtypeStruct(dims, F32)


def body(source, diagonal, u_vel, v_vel, bottom):
    cells, lat = source.shape
    span = cells + 2 * OV
    devices = lax.axis_size("lon")
    parity = (lax.axis_index("lon") % 2).astype(jnp.int32).reshape(1)
    consts = [jnp.asarray(table) for table in tables(span)]
    hbm = {name: pltpu.with_memory_space_constraint(x, pltpu.HBM) for name, x in (
        ("source", source), ("diagonal", diagonal), ("u", u_vel), ("v", v_vel), ("bottom", bottom))}
    consts = [pltpu.with_memory_space_constraint(x, pltpu.HBM) for x in consts]

    outer = pl.pallas_call(
        first_edges,
        in_specs=[SM, HB, HB],
        out_specs=VM,
        out_shape=pltpu.VMEM((OV, lat), F32),
        scratch_shapes=[pltpu.VMEM((OV, lat), F32), pltpu.VMEM((OV, lat), jnp.int32),
                        pltpu.SemaphoreType.DMA((2,))],
        compiler_params=PARAMS,
        name="first_edges",
    )(parity, hbm["source"], hbm["bottom"])
    outer_in = swap_pairs(outer, True)

    inner, masked, coef_own, depth, source_v, *held = pl.pallas_call(
        prepare,
        in_specs=[SM] + [HB] * 7,
        out_specs=[VM] * 8,
        out_shape=[pltpu.VMEM((OV, lat), F32)]
        + [pltpu.VMEM((cells, lat), F32)] * 4
        + [pltpu.VMEM(table.shape, table.dtype) for table in consts],
        scratch_shapes=[
            pltpu.VMEM((cells, lat), F32),
            pltpu.VMEM((cells, lat), jnp.int32),
            pltpu.SemaphoreType.DMA((6,)),
        ],
        compiler_params=PARAMS,
        cost_estimate=pl.CostEstimate(flops=10**6, bytes_accessed=7 * 10**6, transcendentals=0),
        name="prepare",
    )(parity, outer, hbm["source"], hbm["diagonal"], hbm["bottom"], *consts)
    near = swap_pairs(inner, False), outer_in

    blocks = -(-lat // LANE)
    first, inner, outer = pl.pallas_call(
        first_solve,
        in_specs=[SM] + [VM] * 7,
        out_specs=[VM] * 3,
        out_shape=[pltpu.VMEM((span, lat), F32)]
        + [pltpu.VMEM(((3 * OV + 2) * blocks, LANE), F32)] * 2,
        scratch_shapes=solve_scratch(span, lat),
        compiler_params=PARAMS,
        name="first_solve",
    )(parity, *near, masked, coef_own, *held)
    near = swap_pairs(inner, False), swap_pairs(outer, True)

    u_v, v_v = pl.pallas_call(
        absorb,
        in_specs=[HB] * 3,
        out_specs=[VM] * 2,
        out_shape=[pltpu.VMEM((KL, cells, lat), F32)] * 2,
        scratch_shapes=[pltpu.SemaphoreType.DMA((2,))],
        compiler_params=PARAMS,
        cost_estimate=pl.CostEstimate(flops=10**6, bytes_accessed=7 * 10**6, transcendentals=0),
        name="absorb",
    )(first, hbm["u"], hbm["v"])

    z, y, coef, second, inner, outer = pl.pallas_call(
        second_solve,
        in_specs=[SM] + [VM] * 9,
        out_specs=[VM] * 6,
        out_shape=[pltpu.VMEM((span, lat), F32)] * 4 + [pltpu.VMEM((2 * OV, lat), F32)] * 2,
        scratch_shapes=solve_scratch(span, lat) + [pltpu.VMEM((span + 2 * OV, lat), F32)] * 2,
        compiler_params=PARAMS,
        name="second_solve",
    )(parity, *near, first, coef_own, depth, u_v, *held)
    near = swap_pairs(inner, False), swap_pairs(outer, True)

    w, edges, sent = pl.pallas_call(
        sums,
        in_specs=[SM] + [VM] * 7,
        out_specs=[VM] * 3,
        out_shape=[pltpu.VMEM((span, lat), F32), pltpu.VMEM((2 * OV, lat), F32),
                   pltpu.VMEM((devices, 1, LANE), F32)],
        compiler_params=PARAMS,
        name="sums",
    )(parity, *near, second, z, y, coef, source_v)
    came = lax.all_to_all(sent, "lon", 0, 0)

    return pl.pallas_call(
        finish,
        in_specs=[VM] * 8,
        out_specs=[HB] * 4,
        out_shape=[shape(cells, lat)] + [shape(KL, cells, lat)] * 3,
        scratch_shapes=[pltpu.VMEM((span, lat), F32)] * 2
        + [pltpu.VMEM((KL, OV + cells, lat), F32)]
        + [pltpu.VMEM((KL, cells, lat), F32)] * 2
        + [pltpu.VMEM((cells, lat), F32), pltpu.SemaphoreType.DMA((1 + 3 * (cells // OV),))],
        compiler_params=PARAMS,
        name="finish",
    )(came, z, w, edges, source_v, depth, u_v, v_v)


def solution(mesh):
    return jax.shard_map(
        body,
        mesh=mesh,
        in_specs=(
            P(("members", "lon"), None),
            P(("members", "lon"), None),
            P(None, ("members", "lon"), None),
            P(None, ("members", "lon"), None),
            P(("members", "lon"), None),
        ),
        out_specs=(
            P(("members", "lon"), None),
            P(None, ("members", "lon"), None),
            P(None, ("members", "lon"), None),
            P(None, ("members", "lon"), None),
        ),
        check_vma=False,
    )
```

```python
import math

import jax
import jax.numpy as jnp
import ml_dtypes
import numpy as np
from jax import lax
from jax.experimental import pallas as pl
from jax.experimental.pallas import tpu as pltpu
from jax.sharding import PartitionSpec as P

LT = 112
OV = 8
KL = 6
LANE = 128

tile_shift = 0.1
gravity_step = 0.5

F32 = jnp.float32
BF16 = jnp.bfloat16
VM = pl.BlockSpec(memory_space=pltpu.VMEM)
SM = pl.BlockSpec(memory_space=pltpu.SMEM)
HB = pl.BlockSpec(memory_space=pl.ANY)
PARAMS = pltpu.CompilerParams(vmem_limit_bytes=32 * 1024 * 1024)


def sine_basis(length):
    ordinal = np.arange(length, dtype=np.float64) + 1.0
    angles = math.pi * ordinal[:, None] * ordinal[None, :] / (length + 1)
    basis_matrix = np.sqrt(2.0 / (length + 1)) * np.sin(angles)
    eigen_value = 2.0 - 2.0 * np.cos(math.pi * ordinal / (length + 1))
    return basis_matrix, eigen_value


def halves(matrix):
    high = matrix.astype(ml_dtypes.bfloat16)
    low = (matrix - high.astype(np.float64)).astype(ml_dtypes.bfloat16)
    return high, low


def tables(span):
    lon_basis, lon_value = sine_basis(span)
    lat_basis, lat_value = sine_basis(LT + 2 * OV)
    high, low = halves(lat_basis)
    lat = np.block([[high, low], [high, np.zeros_like(low)]])
    high, low = halves(lon_basis)
    lon = np.concatenate([high, low, high], axis=1)
    scale = 1.0 / (lon_value[:, None] + lat_value[None, :] + tile_shift)
    return lat, lon, scale.astype(np.float32)


def split(x):
    high = x.astype(BF16)
    return high, (x - high.astype(F32)).astype(BF16)


def tile_solve(x, lat_basis, lon, scale, rows, spectral, out):
    span, lat = out.shape
    tiles = lat // LT
    lane = lax.broadcasted_iota(jnp.int32, (span, LANE), 1)

    def block_of(b):
        if b < 0:
            return jnp.zeros((span, LANE), F32)
        return x[:, b * LANE : (b + 1) * LANE]

    for t in range(tiles):
        block, start = divmod(t * LT - OV, LANE)
        left, right = [pltpu.roll(block_of(b), LANE - start, 1) for b in (block, block + 1)]
        high, low = split(jnp.where(lane < LANE - start, left, right))
        rows[t * span : (t + 1) * span, :LANE] = high
        rows[t * span : (t + 1) * span, LANE:] = low
    chunk = 4
    for first in range(0, tiles, chunk):
        n = min(chunk, tiles - first)
        product = jnp.dot(
            rows[first * span : (first + n) * span], lat_basis[...], preferred_element_type=F32
        )
        high, low = split(product[:, :LANE] + product[:, LANE:])
        for i in range(n):
            at = slice((first + i) * LANE, (first + i + 1) * LANE)
            spectral[:span, at] = high[i * span : (i + 1) * span]
            spectral[span : 2 * span, at] = high[i * span : (i + 1) * span]
            spectral[2 * span :, at] = low[i * span : (i + 1) * span]
    for first in range(0, tiles, chunk):
        n = min(chunk, tiles - first)
        c = jnp.dot(lon[...], spectral[:, first * LANE : (first + n) * LANE], preferred_element_type=F32)
        c = c * jnp.concatenate([scale[...]] * n, axis=1)
        high, low = split(c)
        c = jnp.concatenate([high, high, low], axis=0)
        c = jnp.dot(lon[...], c, preferred_element_type=F32)
        high, low = split(c)
        for i in range(n):
            at = slice((first + i) * span, (first + i + 1) * span)
            rows[at, :LANE] = high[:, i * LANE : (i + 1) * LANE]
            rows[at, LANE:] = low[:, i * LANE : (i + 1) * LANE]
    sums_of = {}
    for first in range(0, tiles, chunk):
        n = min(chunk, tiles - first)
        product = jnp.dot(
            rows[first * span : (first + n) * span], lat_basis[...], preferred_element_type=F32
        )
        product = product[:, :LANE] + product[:, LANE:]
        for i in range(n):
            block, start = divmod((first + i) * LT - OV, LANE)
            part = pltpu.roll(product[i * span : (i + 1) * span], start, 1)
            for b, inside in ((block, lane >= start), (block + 1, lane < start)):
                if 0 <= b * LANE < lat:
                    piece = jnp.where(inside, part, 0.0)
                    sums_of[b] = sums_of[b] + piece if b in sums_of else piece
        done = (first + n) * LT - OV if first + n < tiles else lat + LANE
        for b in [b for b in sums_of if (b + 1) * LANE <= done]:
            width = min(LANE, lat - b * LANE)
            out[:, b * LANE : b * LANE + width] = sums_of.pop(b)[:, :width]


def wide_lanes(lat):
    return -(-(lat + OV) // LANE) * LANE


def solve_scratch(span, lat):
    tiles = lat // LT
    return [
        pltpu.VMEM((span, wide_lanes(lat)), F32),
        pltpu.VMEM((tiles * span, 2 * LANE), BF16),
        pltpu.VMEM((3 * span, tiles * LANE), BF16),
    ]


def pick(parity, inner, outer):
    even = jnp.full(inner.shape, parity[0], jnp.int32) == 0
    return jnp.where(even, outer, inner), jnp.where(even, inner, outer)


def lat_beside(m):
    zero = jnp.zeros((m.shape[0], 1), m.dtype)
    return jnp.concatenate([m[:, 1:], zero], axis=1) + jnp.concatenate([zero, m[:, :-1]], axis=1)


def pack(message, rows):
    n, lat = rows.shape
    for block, at in enumerate(range(0, lat, LANE)):
        width = min(LANE, lat - at)
        message[block * n : (block + 1) * n, :width] = rows[:, at : at + width]


def unpack(message, n, lat):
    blocks = [message[i * n : (i + 1) * n] for i in range(-(-lat // LANE))]
    return jnp.concatenate(blocks, axis=1)[:, :lat]


def first_edges(parity, source, bottom, outer, rows, depth, sems):
    start = pl.multiple_of(parity[0] * (source.shape[0] - OV), OV)
    at = pl.ds(start, OV)
    copies = [
        pltpu.make_async_copy(source.at[at], rows, sems.at[0]),
        pltpu.make_async_copy(bottom.at[at], depth, sems.at[1]),
    ]
    for copy in copies:
        copy.start()
    for copy in copies:
        copy.wait()
    outer[...] = jnp.where(depth[...] > 0, rows[...], 0.0)


def prepare(parity, after, source_h, diagonal_h, bottom_h, *refs):
    tables_h, (inner, masked, coef, depth, source), held = refs[:3], refs[3:8], refs[8:11]
    diagonal, bottom, sems = refs[11:]
    pairs = [(source_h, source), (bottom_h, bottom), (diagonal_h, diagonal)]
    pairs += list(zip(tables_h, held))
    copies = [pltpu.make_async_copy(a, b, sems.at[i]) for i, (a, b) in enumerate(pairs)]
    for copy in copies:
        copy.start()
    for copy in copies[:3]:
        copy.wait()
    wet = bottom[...] > 0
    masked[...] = jnp.where(wet, source[...], 0.0)
    coef[...] = jnp.where(wet, 4.0 + diagonal[...], 0.0)
    depth[...] = bottom[...].astype(F32)
    inner[...] = pick(parity, masked[:OV], masked[source.shape[0] - OV :])[0]
    for copy in copies[3:]:
        copy.wait()


def first_solve(parity, inner_in, outer_in, masked, coef, lat_basis, lon, scale,
                first, inner, outer, wide, rows, spectral):
    cells, lat = masked.shape
    west, east = pick(parity, inner_in[...], outer_in[...])
    wide[:OV, :lat] = west
    wide[OV : OV + cells, :lat] = masked[...]
    wide[OV + cells :, :lat] = east
    wide[:, lat:] = jnp.zeros((cells + 2 * OV, wide.shape[1] - lat), F32)
    tile_solve(wide, lat_basis, lon, scale, rows, spectral, first)
    reach, edge = 2 * OV + 1, OV + 1
    to_west = jnp.concatenate([first[:reach], coef[:edge]], axis=0)
    to_east = jnp.concatenate([first[cells - 1 :], coef[cells - edge :]], axis=0)
    to_outer, to_inner = pick(parity, to_east, to_west)
    pack(inner, to_inner)
    pack(outer, to_outer)


def absorb(after, u_h, v_h, u, v, sems):
    copies = [pltpu.make_async_copy(a, b, sems.at[i]) for i, (a, b) in enumerate([(u_h, u), (v_h, v)])]
    for copy in copies:
        copy.start()
    for copy in copies:
        copy.wait()


def second_solve(parity, inner_in, outer_in, first, coef_own, depth, u, lat_basis, lon, scale,
                 z, y, coef, second, inner, outer, wide, rows, spectral, m_rows, c_rows):
    cells, lat = coef_own.shape
    span = cells + 2 * OV
    reach, edge = 2 * OV + 1, OV + 1
    west, east = pick(
        parity, unpack(inner_in, reach + edge, lat), unpack(outer_in, reach + edge, lat)
    )
    c_rows[:OV] = jnp.zeros((OV, lat), F32)
    c_rows[OV - 1 : 2 * OV] = west[reach:]
    c_rows[2 * OV : 2 * OV + cells] = coef_own[...]
    c_rows[2 * OV + cells + OV :] = jnp.zeros((OV, lat), F32)
    c_rows[2 * OV + cells : 2 * OV + cells + edge] = east[reach:]
    m_rows[:OV] = jnp.zeros((OV, lat), F32)
    m_rows[OV : OV + span] = first[...]
    m_rows[OV + span :] = jnp.zeros((OV, lat), F32)
    m_rows[OV - 1 : OV - 1 + reach] += west[:reach]
    m_rows[OV + cells : OV + cells + reach] += east[:reach]
    m_rows[...] = jnp.where(c_rows[...] > 0, m_rows[...], 0.0)
    inside = slice(OV, OV + span)
    c, m = c_rows[inside], m_rows[inside]
    coef[...] = c
    z[...] = m
    beside = m_rows[OV - 1 : OV - 1 + span] + m_rows[OV + 1 : OV + 1 + span]
    image = jnp.where(c > 0, c * m - (beside + lat_beside(m)), 0.0)
    y[...] = image
    wide[:, :lat] = image
    wide[:, lat:] = jnp.zeros((span, wide.shape[1] - lat), F32)
    tile_solve(wide, lat_basis, lon, scale, rows, spectral, second)
    to_west = jnp.concatenate([second[:edge], depth[:1], jnp.zeros((KL, lat), F32)], axis=0)
    u_rows = [u[level, cells - 1 : cells] for level in range(KL)]
    to_east = jnp.concatenate([second[span - edge :], depth[cells - 1 :]] + u_rows, axis=0)
    outer[...], inner[...] = pick(parity, to_east, to_west)


def sums(parity, inner_in, outer_in, second, z, y, coef, source, w, edges, sent):
    cells, lat = source.shape
    west, east = pick(parity, inner_in[...], outer_in[...])
    edges[:OV] = west[OV:]
    edges[OV:] = east[OV:]
    w[...] = second[...]
    w[OV - 1 : 2 * OV] += west[: OV + 1]
    w[cells : cells + OV + 1] += east[: OV + 1]
    w[...] = jnp.where(coef[...] > 0, w[...], 0.0)
    own = slice(OV, OV + cells)
    c, m = coef[own], w[own]
    wet = c > 0
    beside = w[OV - 1 : OV - 1 + cells] + w[OV + 1 : OV + 1 + cells]
    x = jnp.where(wet, c * m - (beside + lat_beside(m)), 0.0)
    masked = jnp.where(wet, source[...], 0.0)
    land = jnp.where(wet, 0.0, source[...])
    z_own, y_own = z[own], y[own]

    def partial(a, b):
        product = a * b
        rows = product[:OV]
        for at in range(OV, cells, OV):
            rows = rows + product[at : at + OV]
        whole = lat // LANE * LANE
        total = rows[:, :LANE]
        for at in range(LANE, whole, LANE):
            total = total + rows[:, at : at + LANE]
        if whole < lat:
            blank = jnp.zeros((OV, LANE - lat + whole), F32)
            total = total + jnp.concatenate([rows[:, whole:], blank], axis=1)
        return jnp.sum(jnp.sum(total, axis=0, keepdims=True), axis=1, keepdims=True)

    pairs = [(masked, z_own), (z_own, y_own), (masked, m), (y_own, m), (z_own, x), (m, x), (land, land)]
    lane = lax.broadcasted_iota(jnp.int32, (1, LANE), 1)
    row = jnp.zeros((1, LANE), F32)
    for i, (a, b) in enumerate(pairs):
        row = jnp.where(lane == i, partial(a, b), row)
    sent[...] = jnp.broadcast_to(row[None], sent.shape)


def finish(came, z, w, edges, source, depth, u_vel, v_vel, solution, u_new, v_new, w_vel,
           s_rows, d_rows, u_rows, v_out, w_out, s_out, sems):
    cells, lat = source.shape
    total = jnp.broadcast_to(jnp.sum(came[...], axis=0), (8, LANE))
    place = [lax.broadcasted_iota(jnp.int32, (8, LANE), axis) for axis in range(2)]
    total = jnp.sum(jnp.where(place[0] == place[1], total, 0.0), axis=1, keepdims=True)
    rz, zy, rw, yw, zx, wx, ll = [total[i : i + 1] for i in range(7)]
    step0 = (rz + ll) / (zy + ll)
    rest = (zy - rz) / (zy + ll)
    new = rz - step0 * (zy + rw) + step0 * step0 * yw + rest * rest * ll
    beta = new / (rz + ll)
    grown = 1.0 + beta
    bent = grown * grown * zy - grown * step0 * (zx + yw) + step0 * step0 * wx
    step1 = new / (bent + (rest + beta) * (rest + beta) * ll)
    of_z = jnp.broadcast_to(step0 + step1 * grown, (OV, lat))
    of_w = jnp.broadcast_to(-step1 * step0, (OV, lat))
    of_land = jnp.broadcast_to(step0 + step1 * (rest + beta), (OV, lat))

    copies = []
    d_rows[:OV] = jnp.broadcast_to(edges[1:2], (OV, lat))
    d_rows[OV : OV + cells] = depth[...]
    d_rows[OV + cells :] = jnp.broadcast_to(edges[OV + 1 : OV + 2], (OV, lat))
    for at in range(0, cells + 2 * OV, OV):
        s = of_z * z[at : at + OV] + of_w * w[at : at + OV]
        if OV <= at < OV + cells:
            d = d_rows[at : at + OV]
            s = jnp.where(d > 0, s, of_land * source[at - OV : at])
            s_out[at - OV : at] = s
        s_rows[at : at + OV] = s
    copies.append(pltpu.make_async_copy(s_out, solution, sems.at[0]))
    copies[-1].start()

    s_west = s_rows[OV - 1 : OV]
    s_first = s_rows[OV : OV + 1]
    d_west = jnp.minimum(d_rows[OV - 1 : OV], d_rows[OV : OV + 1])
    for level in range(KL):
        left = edges[level + 2 : level + 3] - gravity_step * (s_first - s_west)
        u_rows[level, :OV] = jnp.broadcast_to(jnp.where(d_west > level, left, 0.0), (OV, lat))
    zero = jnp.zeros((OV, 1), F32)
    for block in range(cells // OV):
        at = OV + block * OV
        own = slice(at - OV, at)
        s = s_rows[at : at + OV]
        d = d_rows[at : at + OV]
        slope_e = gravity_step * (s_rows[at + 1 : at + OV + 1] - s)
        depth_e = jnp.minimum(d, d_rows[at + 1 : at + OV + 1])
        slope_n = gravity_step * (jnp.concatenate([s[:, 1:], zero], axis=1) - s)
        depth_n = jnp.minimum(d, jnp.concatenate([d[:, 1:], zero], axis=1))
        w_sum = jnp.zeros((OV, lat), F32)
        for level in range(KL - 1, -1, -1):
            u = jnp.where(depth_e > level, u_vel[level, own] - slope_e, 0.0)
            u_rows[level, at : at + OV] = u
            v = jnp.where(depth_n > level, v_vel[level, own] - slope_n, 0.0)
            v_out[level, own] = v
            south = jnp.concatenate([zero, v[:, :-1]], axis=1)
            flow = (u - u_rows[level, at - 1 : at + OV - 1]) + (v - south)
            w_sum = w_sum + jnp.where(d > level, flow, 0.0)
            w_out[level, own] = w_sum
        for held, result in ((u_rows.at[:, at : at + OV], u_new), (v_out.at[:, own], v_new), (w_out.at[:, own], w_vel)):
            copies.append(pltpu.make_async_copy(held, result.at[:, own], sems.at[len(copies)]))
            copies[-1].start()
    for copy in copies:
        copy.wait()


def swap_pairs(block, outward):
    devices = lax.axis_size("lon")
    if outward:
        route = [(i, (i - 1 if i % 2 == 0 else i + 1) % devices) for i in range(devices)]
    else:
        route = [(i, i ^ 1) for i in range(devices)]
    return lax.ppermute(block, "lon", route)


def shape(*dims):
    return jax.ShapeDtypeStruct(dims, F32)


def body(source, diagonal, u_vel, v_vel, bottom):
    cells, lat = source.shape
    span = cells + 2 * OV
    devices = lax.axis_size("lon")
    parity = (lax.axis_index("lon") % 2).astype(jnp.int32).reshape(1)
    consts = [jnp.asarray(table) for table in tables(span)]
    hbm = {name: pltpu.with_memory_space_constraint(x, pltpu.HBM) for name, x in (
        ("source", source), ("diagonal", diagonal), ("u", u_vel), ("v", v_vel), ("bottom", bottom))}
    consts = [pltpu.with_memory_space_constraint(x, pltpu.HBM) for x in consts]

    outer = pl.pallas_call(
        first_edges,
        in_specs=[SM, HB, HB],
        out_specs=VM,
        out_shape=pltpu.VMEM((OV, lat), F32),
        scratch_shapes=[pltpu.VMEM((OV, lat), F32), pltpu.VMEM((OV, lat), jnp.int32),
                        pltpu.SemaphoreType.DMA((2,))],
        compiler_params=PARAMS,
        name="first_edges",
    )(parity, hbm["source"], hbm["bottom"])
    outer_in = swap_pairs(outer, True)

    inner, masked, coef_own, depth, source_v, *held = pl.pallas_call(
        prepare,
        in_specs=[SM] + [HB] * 7,
        out_specs=[VM] * 8,
        out_shape=[pltpu.VMEM((OV, lat), F32)]
        + [pltpu.VMEM((cells, lat), F32)] * 4
        + [pltpu.VMEM(table.shape, table.dtype) for table in consts],
        scratch_shapes=[
            pltpu.VMEM((cells, lat), F32),
            pltpu.VMEM((cells, lat), jnp.int32),
            pltpu.SemaphoreType.DMA((6,)),
        ],
        compiler_params=PARAMS,
        cost_estimate=pl.CostEstimate(flops=10**6, bytes_accessed=7 * 10**6, transcendentals=0),
        name="prepare",
    )(parity, outer, hbm["source"], hbm["diagonal"], hbm["bottom"], *consts)
    near = swap_pairs(inner, False), outer_in

    blocks = -(-lat // LANE)
    first, inner, outer = pl.pallas_call(
        first_solve,
        in_specs=[SM] + [VM] * 7,
        out_specs=[VM] * 3,
        out_shape=[pltpu.VMEM((span, lat), F32)]
        + [pltpu.VMEM(((3 * OV + 2) * blocks, LANE), F32)] * 2,
        scratch_shapes=solve_scratch(span, lat),
        compiler_params=PARAMS,
        name="first_solve",
    )(parity, *near, masked, coef_own, *held)
    near = swap_pairs(inner, False), swap_pairs(outer, True)

    u_v, v_v = pl.pallas_call(
        absorb,
        in_specs=[HB] * 3,
        out_specs=[VM] * 2,
        out_shape=[pltpu.VMEM((KL, cells, lat), F32)] * 2,
        scratch_shapes=[pltpu.SemaphoreType.DMA((2,))],
        compiler_params=PARAMS,
        cost_estimate=pl.CostEstimate(flops=10**6, bytes_accessed=7 * 10**6, transcendentals=0),
        name="absorb",
    )(first, hbm["u"], hbm["v"])

    z, y, coef, second, inner, outer = pl.pallas_call(
        second_solve,
        in_specs=[SM] + [VM] * 9,
        out_specs=[VM] * 6,
        out_shape=[pltpu.VMEM((span, lat), F32)] * 4 + [pltpu.VMEM((2 * OV, lat), F32)] * 2,
        scratch_shapes=solve_scratch(span, lat) + [pltpu.VMEM((span + 2 * OV, lat), F32)] * 2,
        compiler_params=PARAMS,
        name="second_solve",
    )(parity, *near, first, coef_own, depth, u_v, *held)
    near = swap_pairs(inner, False), swap_pairs(outer, True)

    w, edges, sent = pl.pallas_call(
        sums,
        in_specs=[SM] + [VM] * 7,
        out_specs=[VM] * 3,
        out_shape=[pltpu.VMEM((span, lat), F32), pltpu.VMEM((2 * OV, lat), F32),
                   pltpu.VMEM((devices, 1, LANE), F32)],
        compiler_params=PARAMS,
        name="sums",
    )(parity, *near, second, z, y, coef, source_v)
    came = lax.all_to_all(sent, "lon", 0, 0)

    return pl.pallas_call(
        finish,
        in_specs=[VM] * 8,
        out_specs=[HB] * 4,
        out_shape=[shape(cells, lat)] + [shape(KL, cells, lat)] * 3,
        scratch_shapes=[pltpu.VMEM((span, lat), F32)] * 2
        + [pltpu.VMEM((KL, OV + cells, lat), F32)]
        + [pltpu.VMEM((KL, cells, lat), F32)] * 2
        + [pltpu.VMEM((cells, lat), F32), pltpu.SemaphoreType.DMA((1 + 3 * (cells // OV),))],
        compiler_params=PARAMS,
        name="finish",
    )(came, z, w, edges, source_v, depth, u_v, v_v)


def solution(mesh):
    return jax.shard_map(
        body,
        mesh=mesh,
        in_specs=(
            P(("members", "lon"), None),
            P(("members", "lon"), None),
            P(None, ("members", "lon"), None),
            P(None, ("members", "lon"), None),
            P(("members", "lon"), None),
        ),
        out_specs=(
            P(("members", "lon"), None),
            P(None, ("members", "lon"), None),
            P(None, ("members", "lon"), None),
            P(None, ("members", "lon"), None),
        ),
        check_vma=False,
    )
```

```python
import math

import jax
import jax.numpy as jnp
import ml_dtypes
import numpy as np
from jax import lax
from jax.experimental import pallas as pl
from jax.experimental.pallas import tpu as pltpu
from jax.sharding import PartitionSpec as P

LT = 112
OV = 8
KL = 6
LANE = 128
FAR = 24

tile_shift = 0.1
gravity_step = 0.5

F32 = jnp.float32
BF16 = jnp.bfloat16
VM = pl.BlockSpec(memory_space=pltpu.VMEM)
SM = pl.BlockSpec(memory_space=pltpu.SMEM)
HB = pl.BlockSpec(memory_space=pl.ANY)
PARAMS = pltpu.CompilerParams(vmem_limit_bytes=32 * 1024 * 1024)


def sine_basis(length):
    ordinal = np.arange(length, dtype=np.float64) + 1.0
    angles = math.pi * ordinal[:, None] * ordinal[None, :] / (length + 1)
    basis_matrix = np.sqrt(2.0 / (length + 1)) * np.sin(angles)
    eigen_value = 2.0 - 2.0 * np.cos(math.pi * ordinal / (length + 1))
    return basis_matrix, eigen_value


def halves(matrix):
    high = matrix.astype(ml_dtypes.bfloat16)
    low = (matrix - high.astype(np.float64)).astype(ml_dtypes.bfloat16)
    return high, low


def tables(span):
    lon_basis, lon_value = sine_basis(span)
    lat_basis, lat_value = sine_basis(LT + 2 * OV)
    high, low = halves(lat_basis)
    lat = np.block([[high, low], [high, np.zeros_like(low)]])
    high, low = halves(lon_basis)
    lon = np.concatenate([high, low, high], axis=1)
    scale = 1.0 / (lon_value[:, None] + lat_value[None, :] + tile_shift)
    return lat, lon, scale.astype(np.float32)


def split(x):
    high = x.astype(BF16)
    return high, (x - high.astype(F32)).astype(BF16)


def tile_solve(x, lat_basis, lon, scale, rows, spectral, out):
    span, lat = out.shape
    tiles = lat // LT
    lane = lax.broadcasted_iota(jnp.int32, (span, LANE), 1)

    def block_of(b):
        if b < 0:
            return jnp.zeros((span, LANE), F32)
        return x[:, b * LANE : (b + 1) * LANE]

    for t in range(tiles):
        block, start = divmod(t * LT - OV, LANE)
        left, right = [pltpu.roll(block_of(b), LANE - start, 1) for b in (block, block + 1)]
        high, low = split(jnp.where(lane < LANE - start, left, right))
        rows[t * span : (t + 1) * span, :LANE] = high
        rows[t * span : (t + 1) * span, LANE:] = low
    chunk = 4
    for first in range(0, tiles, chunk):
        n = min(chunk, tiles - first)
        product = jnp.dot(
            rows[first * span : (first + n) * span], lat_basis[...], preferred_element_type=F32
        )
        high, low = split(product[:, :LANE] + product[:, LANE:])
        for i in range(n):
            at = slice((first + i) * LANE, (first + i + 1) * LANE)
            spectral[:span, at] = high[i * span : (i + 1) * span]
            spectral[span : 2 * span, at] = high[i * span : (i + 1) * span]
            spectral[2 * span :, at] = low[i * span : (i + 1) * span]
    for first in range(0, tiles, chunk):
        n = min(chunk, tiles - first)
        c = jnp.dot(lon[...], spectral[:, first * LANE : (first + n) * LANE], preferred_element_type=F32)
        c = c * jnp.concatenate([scale[...]] * n, axis=1)
        high, low = split(c)
        c = jnp.concatenate([high, high, low], axis=0)
        c = jnp.dot(lon[...], c, preferred_element_type=F32)
        high, low = split(c)
        for i in range(n):
            at = slice((first + i) * span, (first + i + 1) * span)
            rows[at, :LANE] = high[:, i * LANE : (i + 1) * LANE]
            rows[at, LANE:] = low[:, i * LANE : (i + 1) * LANE]
    sums_of = {}
    for first in range(0, tiles, chunk):
        n = min(chunk, tiles - first)
        product = jnp.dot(
            rows[first * span : (first + n) * span], lat_basis[...], preferred_element_type=F32
        )
        product = product[:, :LANE] + product[:, LANE:]
        for i in range(n):
            block, start = divmod((first + i) * LT - OV, LANE)
            part = pltpu.roll(product[i * span : (i + 1) * span], start, 1)
            for b, inside in ((block, lane >= start), (block + 1, lane < start)):
                if 0 <= b * LANE < lat:
                    piece = jnp.where(inside, part, 0.0)
                    sums_of[b] = sums_of[b] + piece if b in sums_of else piece
        done = (first + n) * LT - OV if first + n < tiles else lat + LANE
        for b in [b for b in sums_of if (b + 1) * LANE <= done]:
            width = min(LANE, lat - b * LANE)
            out[:, b * LANE : b * LANE + width] = sums_of.pop(b)[:, :width]


def wide_lanes(lat):
    return -(-(lat + OV) // LANE) * LANE


def solve_scratch(span, lat):
    tiles = lat // LT
    return [
        pltpu.VMEM((span, wide_lanes(lat)), F32),
        pltpu.VMEM((tiles * span, 2 * LANE), BF16),
        pltpu.VMEM((3 * span, tiles * LANE), BF16),
    ]


def pick(parity, inner, outer):
    even = jnp.full(inner.shape, parity[0], jnp.int32) == 0
    return jnp.where(even, outer, inner), jnp.where(even, inner, outer)


def lat_beside(m):
    zero = jnp.zeros((m.shape[0], 1), m.dtype)
    return jnp.concatenate([m[:, 1:], zero], axis=1) + jnp.concatenate([zero, m[:, :-1]], axis=1)


def pack(message, rows):
    n, lat = rows.shape
    for block, at in enumerate(range(0, lat, LANE)):
        width = min(LANE, lat - at)
        message[block * n : (block + 1) * n, :width] = rows[:, at : at + width]


def unpack(message, n, lat):
    blocks = [message[i * n : (i + 1) * n] for i in range(-(-lat // LANE))]
    return jnp.concatenate(blocks, axis=1)[:, :lat]


def first_edges(parity, source, bottom, outer, rows, depth, sems):
    start = pl.multiple_of(parity[0] * (source.shape[0] - OV), OV)
    at = pl.ds(start, OV)
    copies = [
        pltpu.make_async_copy(source.at[at], rows, sems.at[0]),
        pltpu.make_async_copy(bottom.at[at], depth, sems.at[1]),
    ]
    for copy in copies:
        copy.start()
    for copy in copies:
        copy.wait()
    outer[...] = jnp.where(depth[...] > 0, rows[...], 0.0)


def prepare(parity, after, source_h, diagonal_h, bottom_h, u_h, *refs):
    tables_h, (inner, far_inner, far_outer, masked, coef, depth, source), held = refs[:3], refs[3:10], refs[10:13]
    diagonal, bottom, u_strip, sems = refs[13:]
    cells, lat = source.shape
    pairs = [(source_h, source), (bottom_h, bottom), (diagonal_h, diagonal)]
    pairs += [(u_h.at[:, pl.ds(cells - OV, OV)], u_strip)]
    pairs += list(zip(tables_h, held))
    copies = [pltpu.make_async_copy(a, b, sems.at[i]) for i, (a, b) in enumerate(pairs)]
    for copy in copies:
        copy.start()
    for copy in copies[:4]:
        copy.wait()
    wet = bottom[...] > 0
    masked[...] = jnp.where(wet, source[...], 0.0)
    coef[...] = jnp.where(wet, 4.0 + diagonal[...], 0.0)
    depth[...] = bottom[...].astype(F32)
    edge = OV + 1
    blank = jnp.zeros((2 * OV - edge - 1, lat), F32)
    to_west = jnp.concatenate([coef[:edge], blank, depth[:1]], axis=0)
    u_rows = [u_strip[level, OV - 1 : OV] for level in range(KL)]
    to_east = jnp.concatenate(u_rows + [depth[cells - 1 :], coef[cells - edge :]], axis=0)
    far_outer[: 2 * OV], far_inner[: 2 * OV] = pick(parity, to_east, to_west)
    for message in (far_outer, far_inner):
        message[2 * OV :] = jnp.zeros((FAR - 2 * OV, lat), F32)
    inner[...] = pick(parity, masked[:OV], masked[cells - OV :])[0]
    for copy in copies[4:]:
        copy.wait()


def first_solve(parity, inner_in, outer_in, masked, lat_basis, lon, scale,
                first, inner, outer, wide, rows, spectral):
    cells, lat = masked.shape
    west, east = pick(parity, inner_in[...], outer_in[...])
    wide[:OV, :lat] = west
    wide[OV : OV + cells, :lat] = masked[...]
    wide[OV + cells :, :lat] = east
    wide[:, lat:] = jnp.zeros((cells + 2 * OV, wide.shape[1] - lat), F32)
    tile_solve(wide, lat_basis, lon, scale, rows, spectral, first)
    to_outer, to_inner = pick(parity, first[cells - 1 :], first[: 2 * OV + 1])
    pack(inner, to_inner)
    pack(outer, to_outer)


def absorb(parity, after, inner_in, outer_in, coef, u_h, v_h, c_rows, edges, u, v, sems):
    cells, lat = coef.shape
    copies = [pltpu.make_async_copy(a, b, sems.at[i]) for i, (a, b) in enumerate([(u_h, u), (v_h, v)])]
    for copy in copies:
        copy.start()
    west, east = pick(parity, inner_in[: 2 * OV], outer_in[: 2 * OV])
    edges[:OV] = west[:OV]
    edges[OV:] = east[OV:]
    c_rows[: 2 * OV] = west
    c_rows[: OV - 1] = jnp.zeros((OV - 1, lat), F32)
    c_rows[2 * OV : 2 * OV + cells] = coef[...]
    c_rows[2 * OV + cells :] = east
    c_rows[3 * OV + cells + 1 :] = jnp.zeros((OV - 1, lat), F32)
    for copy in copies:
        copy.wait()


def second_solve(parity, inner_in, outer_in, first, c_rows, lat_basis, lon, scale,
                 z, y, second, inner, outer, wide, rows, spectral, m_rows):
    span, lat = first.shape
    cells = span - 2 * OV
    reach = 2 * OV + 1
    west, east = pick(parity, unpack(inner_in, reach, lat), unpack(outer_in, reach, lat))
    m_rows[:OV] = jnp.zeros((OV, lat), F32)
    m_rows[OV : OV + span] = first[...]
    m_rows[OV + span :] = jnp.zeros((OV, lat), F32)
    m_rows[OV - 1 : OV - 1 + reach] += west
    m_rows[OV + cells : OV + cells + reach] += east
    m_rows[...] = jnp.where(c_rows[...] > 0, m_rows[...], 0.0)
    inside = slice(OV, OV + span)
    c, m = c_rows[inside], m_rows[inside]
    z[...] = m
    beside = m_rows[OV - 1 : OV - 1 + span] + m_rows[OV + 1 : OV + 1 + span]
    image = jnp.where(c > 0, c * m - (beside + lat_beside(m)), 0.0)
    y[...] = image
    wide[:, :lat] = image
    wide[:, lat:] = jnp.zeros((span, wide.shape[1] - lat), F32)
    tile_solve(wide, lat_basis, lon, scale, rows, spectral, second)
    to_outer, to_inner = pick(parity, second[span - OV - 1 :], second[: OV + 1])
    pack(inner, to_inner)
    pack(outer, to_outer)


def sums(parity, inner_in, outer_in, second, z, y, c_rows, source, w, sent):
    cells, lat = source.shape
    west, east = pick(parity, unpack(inner_in, OV + 1, lat), unpack(outer_in, OV + 1, lat))
    w[...] = second[...]
    w[OV - 1 : 2 * OV] += west
    w[cells : cells + OV + 1] += east
    w[...] = jnp.where(c_rows[OV : 3 * OV + cells] > 0, w[...], 0.0)
    own = slice(OV, OV + cells)
    c, m = c_rows[2 * OV : 2 * OV + cells], w[own]
    wet = c > 0
    beside = w[OV - 1 : OV - 1 + cells] + w[OV + 1 : OV + 1 + cells]
    x = jnp.where(wet, c * m - (beside + lat_beside(m)), 0.0)
    masked = jnp.where(wet, source[...], 0.0)
    land = jnp.where(wet, 0.0, source[...])
    z_own, y_own = z[own], y[own]

    def partial(a, b):
        product = a * b
        rows = product[:OV]
        for at in range(OV, cells, OV):
            rows = rows + product[at : at + OV]
        whole = lat // LANE * LANE
        total = rows[:, :LANE]
        for at in range(LANE, whole, LANE):
            total = total + rows[:, at : at + LANE]
        if whole < lat:
            blank = jnp.zeros((OV, LANE - lat + whole), F32)
            total = total + jnp.concatenate([rows[:, whole:], blank], axis=1)
        return jnp.sum(jnp.sum(total, axis=0, keepdims=True), axis=1, keepdims=True)

    pairs = [(masked, z_own), (z_own, y_own), (masked, m), (y_own, m), (z_own, x), (m, x), (land, land)]
    lane = lax.broadcasted_iota(jnp.int32, (1, LANE), 1)
    row = jnp.zeros((1, LANE), F32)
    for i, (a, b) in enumerate(pairs):
        row = jnp.where(lane == i, partial(a, b), row)
    sent[...] = jnp.broadcast_to(row[None], sent.shape)


def finish(came, z, w, edges, source, depth, u_vel, v_vel, solution, u_new, v_new, w_vel,
           s_rows, d_rows, u_rows, v_out, w_out, s_out, sems):
    cells, lat = source.shape
    total = jnp.broadcast_to(jnp.sum(came[...], axis=0), (8, LANE))
    place = [lax.broadcasted_iota(jnp.int32, (8, LANE), axis) for axis in range(2)]
    total = jnp.sum(jnp.where(place[0] == place[1], total, 0.0), axis=1, keepdims=True)
    rz, zy, rw, yw, zx, wx, ll = [total[i : i + 1] for i in range(7)]
    step0 = (rz + ll) / (zy + ll)
    rest = (zy - rz) / (zy + ll)
    new = rz - step0 * (zy + rw) + step0 * step0 * yw + rest * rest * ll
    beta = new / (rz + ll)
    grown = 1.0 + beta
    bent = grown * grown * zy - grown * step0 * (zx + yw) + step0 * step0 * wx
    step1 = new / (bent + (rest + beta) * (rest + beta) * ll)
    of_z = jnp.broadcast_to(step0 + step1 * grown, (OV, lat))
    of_w = jnp.broadcast_to(-step1 * step0, (OV, lat))
    of_land = jnp.broadcast_to(step0 + step1 * (rest + beta), (OV, lat))

    copies = []
    d_rows[:OV] = jnp.broadcast_to(edges[KL : KL + 1], (OV, lat))
    d_rows[OV : OV + cells] = depth[...]
    d_rows[OV + cells :] = jnp.broadcast_to(edges[2 * OV - 1 :], (OV, lat))
    for at in range(0, cells + 2 * OV, OV):
        s = of_z * z[at : at + OV] + of_w * w[at : at + OV]
        if OV <= at < OV + cells:
            d = d_rows[at : at + OV]
            s = jnp.where(d > 0, s, of_land * source[at - OV : at])
            s_out[at - OV : at] = s
        s_rows[at : at + OV] = s
    copies.append(pltpu.make_async_copy(s_out, solution, sems.at[0]))
    copies[-1].start()

    s_west = s_rows[OV - 1 : OV]
    s_first = s_rows[OV : OV + 1]
    d_west = jnp.minimum(d_rows[OV - 1 : OV], d_rows[OV : OV + 1])
    for level in range(KL):
        left = edges[level : level + 1] - gravity_step * (s_first - s_west)
        u_rows[level, :OV] = jnp.broadcast_to(jnp.where(d_west > level, left, 0.0), (OV, lat))
    zero = jnp.zeros((OV, 1), F32)
    for block in range(cells // OV):
        at = OV + block * OV
        own = slice(at - OV, at)
        s = s_rows[at : at + OV]
        d = d_rows[at : at + OV]
        slope_e = gravity_step * (s_rows[at + 1 : at + OV + 1] - s)
        depth_e = jnp.minimum(d, d_rows[at + 1 : at + OV + 1])
        slope_n = gravity_step * (jnp.concatenate([s[:, 1:], zero], axis=1) - s)
        depth_n = jnp.minimum(d, jnp.concatenate([d[:, 1:], zero], axis=1))
        w_sum = jnp.zeros((OV, lat), F32)
        for level in range(KL - 1, -1, -1):
            u = jnp.where(depth_e > level, u_vel[level, own] - slope_e, 0.0)
            u_rows[level, at : at + OV] = u
            v = jnp.where(depth_n > level, v_vel[level, own] - slope_n, 0.0)
            v_out[level, own] = v
            south = jnp.concatenate([zero, v[:, :-1]], axis=1)
            flow = (u - u_rows[level, at - 1 : at + OV - 1]) + (v - south)
            w_sum = w_sum + jnp.where(d > level, flow, 0.0)
            w_out[level, own] = w_sum
        for held, result in ((u_rows.at[:, at : at + OV], u_new), (v_out.at[:, own], v_new), (w_out.at[:, own], w_vel)):
            copies.append(pltpu.make_async_copy(held, result.at[:, own], sems.at[len(copies)]))
            copies[-1].start()
    for copy in copies:
        copy.wait()


def swap_pairs(block, outward):
    devices = lax.axis_size("lon")
    if outward:
        route = [(i, (i - 1 if i % 2 == 0 else i + 1) % devices) for i in range(devices)]
    else:
        route = [(i, i ^ 1) for i in range(devices)]
    return lax.ppermute(block, "lon", route)


def shape(*dims):
    return jax.ShapeDtypeStruct(dims, F32)


def body(source, diagonal, u_vel, v_vel, bottom):
    cells, lat = source.shape
    span = cells + 2 * OV
    devices = lax.axis_size("lon")
    parity = (lax.axis_index("lon") % 2).astype(jnp.int32).reshape(1)
    consts = [jnp.asarray(table) for table in tables(span)]
    hbm = {name: pltpu.with_memory_space_constraint(x, pltpu.HBM) for name, x in (
        ("source", source), ("diagonal", diagonal), ("u", u_vel), ("v", v_vel), ("bottom", bottom))}
    consts = [pltpu.with_memory_space_constraint(x, pltpu.HBM) for x in consts]

    outer = pl.pallas_call(
        first_edges,
        in_specs=[SM, HB, HB],
        out_specs=VM,
        out_shape=pltpu.VMEM((OV, lat), F32),
        scratch_shapes=[pltpu.VMEM((OV, lat), F32), pltpu.VMEM((OV, lat), jnp.int32),
                        pltpu.SemaphoreType.DMA((2,))],
        compiler_params=PARAMS,
        name="first_edges",
    )(parity, hbm["source"], hbm["bottom"])
    outer_in = swap_pairs(outer, True)

    inner, far_inner, far_outer, masked, coef, depth, source_v, *held = pl.pallas_call(
        prepare,
        in_specs=[SM] + [HB] * 8,
        out_specs=[VM] * 10,
        out_shape=[pltpu.VMEM((OV, lat), F32)]
        + [pltpu.VMEM((FAR, lat), F32)] * 2
        + [pltpu.VMEM((cells, lat), F32)] * 4
        + [pltpu.VMEM(table.shape, table.dtype) for table in consts],
        scratch_shapes=[
            pltpu.VMEM((cells, lat), F32),
            pltpu.VMEM((cells, lat), jnp.int32),
            pltpu.VMEM((KL, OV, lat), F32),
            pltpu.SemaphoreType.DMA((7,)),
        ],
        compiler_params=PARAMS,
        cost_estimate=pl.CostEstimate(flops=10**6, bytes_accessed=7 * 10**6, transcendentals=0),
        name="prepare",
    )(parity, outer, hbm["source"], hbm["diagonal"], hbm["bottom"], hbm["u"], *consts)
    near = swap_pairs(inner, False), outer_in
    far = swap_pairs(far_inner, False), swap_pairs(far_outer, True)

    blocks = -(-lat // LANE)
    first, inner, outer = pl.pallas_call(
        first_solve,
        in_specs=[SM] + [VM] * 6,
        out_specs=[VM] * 3,
        out_shape=[pltpu.VMEM((span, lat), F32)] + [pltpu.VMEM(((2 * OV + 1) * blocks, LANE), F32)] * 2,
        scratch_shapes=solve_scratch(span, lat),
        compiler_params=PARAMS,
        name="first_solve",
    )(parity, *near, masked, *held)
    near = swap_pairs(inner, False), swap_pairs(outer, True)

    c_rows, edges, u_v, v_v = pl.pallas_call(
        absorb,
        in_specs=[SM, HB] + [VM] * 3 + [HB] * 2,
        out_specs=[VM] * 4,
        out_shape=[pltpu.VMEM((span + 2 * OV, lat), F32), pltpu.VMEM((2 * OV, lat), F32)]
        + [pltpu.VMEM((KL, cells, lat), F32)] * 2,
        scratch_shapes=[pltpu.SemaphoreType.DMA((2,))],
        compiler_params=PARAMS,
        cost_estimate=pl.CostEstimate(flops=10**6, bytes_accessed=7 * 10**6, transcendentals=0),
        name="absorb",
    )(parity, first, *far, coef, hbm["u"], hbm["v"])

    z, y, second, inner, outer = pl.pallas_call(
        second_solve,
        in_specs=[SM] + [VM] * 7,
        out_specs=[VM] * 5,
        out_shape=[pltpu.VMEM((span, lat), F32)] * 3 + [pltpu.VMEM(((OV + 1) * blocks, LANE), F32)] * 2,
        scratch_shapes=solve_scratch(span, lat) + [pltpu.VMEM((span + 2 * OV, lat), F32)],
        compiler_params=PARAMS,
        name="second_solve",
    )(parity, *near, first, c_rows, *held)
    near = swap_pairs(inner, False), swap_pairs(outer, True)

    w, sent = pl.pallas_call(
        sums,
        in_specs=[SM] + [VM] * 7,
        out_specs=[VM] * 2,
        out_shape=[pltpu.VMEM((span, lat), F32), pltpu.VMEM((devices, 1, LANE), F32)],
        compiler_params=PARAMS,
        name="sums",
    )(parity, *near, second, z, y, c_rows, source_v)
    came = lax.all_to_all(sent, "lon", 0, 0)

    return pl.pallas_call(
        finish,
        in_specs=[VM] * 8,
        out_specs=[HB] * 4,
        out_shape=[shape(cells, lat)] + [shape(KL, cells, lat)] * 3,
        scratch_shapes=[pltpu.VMEM((span, lat), F32)] * 2
        + [pltpu.VMEM((KL, OV + cells, lat), F32)]
        + [pltpu.VMEM((KL, cells, lat), F32)] * 2
        + [pltpu.VMEM((cells, lat), F32), pltpu.SemaphoreType.DMA((1 + 3 * (cells // OV),))],
        compiler_params=PARAMS,
        name="finish",
    )(came, z, w, edges, source_v, depth, u_v, v_v)


def solution(mesh):
    return jax.shard_map(
        body,
        mesh=mesh,
        in_specs=(
            P(("members", "lon"), None),
            P(("members", "lon"), None),
            P(None, ("members", "lon"), None),
            P(None, ("members", "lon"), None),
            P(("members", "lon"), None),
        ),
        out_specs=(
            P(("members", "lon"), None),
            P(None, ("members", "lon"), None),
            P(None, ("members", "lon"), None),
            P(None, ("members", "lon"), None),
        ),
        check_vma=False,
    )
```

```python
import math

import jax
import jax.numpy as jnp
import ml_dtypes
import numpy as np
from jax import lax
from jax.experimental import pallas as pl
from jax.experimental.pallas import tpu as pltpu
from jax.sharding import PartitionSpec as P

LT = 112
OV = 8
KL = 6
LANE = 128
FAR = 24

tile_shift = 0.1
gravity_step = 0.5

F32 = jnp.float32
BF16 = jnp.bfloat16
VM = pl.BlockSpec(memory_space=pltpu.VMEM)
SM = pl.BlockSpec(memory_space=pltpu.SMEM)
HB = pl.BlockSpec(memory_space=pl.ANY)
PARAMS = pltpu.CompilerParams(vmem_limit_bytes=32 * 1024 * 1024)


def sine_basis(length):
    ordinal = np.arange(length, dtype=np.float64) + 1.0
    angles = math.pi * ordinal[:, None] * ordinal[None, :] / (length + 1)
    basis_matrix = np.sqrt(2.0 / (length + 1)) * np.sin(angles)
    eigen_value = 2.0 - 2.0 * np.cos(math.pi * ordinal / (length + 1))
    return basis_matrix, eigen_value


def halves(matrix):
    high = matrix.astype(ml_dtypes.bfloat16)
    low = (matrix - high.astype(np.float64)).astype(ml_dtypes.bfloat16)
    return high, low


def tables(span):
    lon_basis, lon_value = sine_basis(span)
    lat_basis, lat_value = sine_basis(LT + 2 * OV)
    high, low = halves(lat_basis)
    lat = np.block([[high, low], [high, np.zeros_like(low)]])
    high, low = halves(lon_basis)
    lon = np.concatenate([high, low, high], axis=1)
    scale = 1.0 / (lon_value[:, None] + lat_value[None, :] + tile_shift)
    return lat, lon, scale.astype(np.float32)


def split(x):
    high = x.astype(BF16)
    return high, (x - high.astype(F32)).astype(BF16)


def tile_solve(x, lat_basis, lon, scale, rows, spectral, out):
    span, lat = out.shape
    tiles = lat // LT
    lane = lax.broadcasted_iota(jnp.int32, (span, LANE), 1)

    def block_of(b):
        if b < 0:
            return jnp.zeros((span, LANE), F32)
        return x[:, b * LANE : (b + 1) * LANE]

    for t in range(tiles):
        block, start = divmod(t * LT - OV, LANE)
        left, right = [pltpu.roll(block_of(b), LANE - start, 1) for b in (block, block + 1)]
        high, low = split(jnp.where(lane < LANE - start, left, right))
        rows[t * span : (t + 1) * span, :LANE] = high
        rows[t * span : (t + 1) * span, LANE:] = low
    chunk = 4
    for first in range(0, tiles, chunk):
        n = min(chunk, tiles - first)
        product = jnp.dot(
            rows[first * span : (first + n) * span], lat_basis[...], preferred_element_type=F32
        )
        high, low = split(product[:, :LANE] + product[:, LANE:])
        for i in range(n):
            at = slice((first + i) * LANE, (first + i + 1) * LANE)
            spectral[:span, at] = high[i * span : (i + 1) * span]
            spectral[span : 2 * span, at] = high[i * span : (i + 1) * span]
            spectral[2 * span :, at] = low[i * span : (i + 1) * span]
    for first in range(0, tiles, chunk):
        n = min(chunk, tiles - first)
        c = jnp.dot(lon[...], spectral[:, first * LANE : (first + n) * LANE], preferred_element_type=F32)
        c = c * jnp.concatenate([scale[...]] * n, axis=1)
        high, low = split(c)
        c = jnp.concatenate([high, high, low], axis=0)
        c = jnp.dot(lon[...], c, preferred_element_type=F32)
        high, low = split(c)
        for i in range(n):
            at = slice((first + i) * span, (first + i + 1) * span)
            rows[at, :LANE] = high[:, i * LANE : (i + 1) * LANE]
            rows[at, LANE:] = low[:, i * LANE : (i + 1) * LANE]
    sums_of = {}
    for first in range(0, tiles, chunk):
        n = min(chunk, tiles - first)
        product = jnp.dot(
            rows[first * span : (first + n) * span], lat_basis[...], preferred_element_type=F32
        )
        product = product[:, :LANE] + product[:, LANE:]
        for i in range(n):
            block, start = divmod((first + i) * LT - OV, LANE)
            part = pltpu.roll(product[i * span : (i + 1) * span], start, 1)
            for b, inside in ((block, lane >= start), (block + 1, lane < start)):
                if 0 <= b * LANE < lat:
                    piece = jnp.where(inside, part, 0.0)
                    sums_of[b] = sums_of[b] + piece if b in sums_of else piece
        done = (first + n) * LT - OV if first + n < tiles else lat + LANE
        for b in [b for b in sums_of if (b + 1) * LANE <= done]:
            width = min(LANE, lat - b * LANE)
            out[:, b * LANE : b * LANE + width] = sums_of.pop(b)[:, :width]


def wide_lanes(lat):
    return -(-(lat + OV) // LANE) * LANE


def solve_scratch(span, lat):
    tiles = lat // LT
    return [
        pltpu.VMEM((span, wide_lanes(lat)), F32),
        pltpu.VMEM((tiles * span, 2 * LANE), BF16),
        pltpu.VMEM((3 * span, tiles * LANE), BF16),
    ]


def pick(parity, inner, outer):
    even = jnp.full(inner.shape, parity[0], jnp.int32) == 0
    return jnp.where(even, outer, inner), jnp.where(even, inner, outer)


def lat_beside(m):
    zero = jnp.zeros((m.shape[0], 1), m.dtype)
    return jnp.concatenate([m[:, 1:], zero], axis=1) + jnp.concatenate([zero, m[:, :-1]], axis=1)


def pack(message, rows):
    n, lat = rows.shape
    for block, at in enumerate(range(0, lat, LANE)):
        width = min(LANE, lat - at)
        message[block * n : (block + 1) * n, :width] = rows[:, at : at + width]


def unpack(message, n, lat):
    blocks = [message[i * n : (i + 1) * n] for i in range(-(-lat // LANE))]
    return jnp.concatenate(blocks, axis=1)[:, :lat]


def first_edges(parity, source, bottom, outer, rows, depth, sems):
    start = pl.multiple_of(parity[0] * (source.shape[0] - OV), OV)
    at = pl.ds(start, OV)
    copies = [
        pltpu.make_async_copy(source.at[at], rows, sems.at[0]),
        pltpu.make_async_copy(bottom.at[at], depth, sems.at[1]),
    ]
    for copy in copies:
        copy.start()
    for copy in copies:
        copy.wait()
    outer[...] = jnp.where(depth[...] > 0, rows[...], 0.0)


def prepare(parity, after, source_h, diagonal_h, bottom_h, u_h, *refs):
    tables_h, (inner, far_inner, far_outer, masked, coef, depth, source), held = refs[:3], refs[3:10], refs[10:13]
    diagonal, bottom, u_strip, sems = refs[13:]
    cells, lat = source.shape
    pairs = [(source_h, source), (bottom_h, bottom), (diagonal_h, diagonal)]
    pairs += [(u_h.at[:, pl.ds(cells - OV, OV)], u_strip)]
    pairs += list(zip(tables_h, held))
    copies = [pltpu.make_async_copy(a, b, sems.at[i]) for i, (a, b) in enumerate(pairs)]
    for copy in copies:
        copy.start()
    for copy in copies[:4]:
        copy.wait()
    wet = bottom[...] > 0
    masked[...] = jnp.where(wet, source[...], 0.0)
    coef[...] = jnp.where(wet, 4.0 + diagonal[...], 0.0)
    depth[...] = bottom[...].astype(F32)
    edge = OV + 1
    blank = jnp.zeros((2 * OV - edge - 1, lat), F32)
    to_west = jnp.concatenate([coef[:edge], blank, depth[:1]], axis=0)
    u_rows = [u_strip[level, OV - 1 : OV] for level in range(KL)]
    to_east = jnp.concatenate(u_rows + [depth[cells - 1 :], coef[cells - edge :]], axis=0)
    far_outer[: 2 * OV], far_inner[: 2 * OV] = pick(parity, to_east, to_west)
    for message in (far_outer, far_inner):
        message[2 * OV :] = jnp.zeros((FAR - 2 * OV, lat), F32)
    inner[...] = pick(parity, masked[:OV], masked[cells - OV :])[0]
    for copy in copies[4:]:
        copy.wait()


def first_solve(parity, inner_in, outer_in, masked, lat_basis, lon, scale,
                first, inner, outer, wide, rows, spectral):
    cells, lat = masked.shape
    west, east = pick(parity, inner_in[...], outer_in[...])
    wide[:OV, :lat] = west
    wide[OV : OV + cells, :lat] = masked[...]
    wide[OV + cells :, :lat] = east
    wide[:, lat:] = jnp.zeros((cells + 2 * OV, wide.shape[1] - lat), F32)
    tile_solve(wide, lat_basis, lon, scale, rows, spectral, first)
    to_outer, to_inner = pick(parity, first[cells - 1 :], first[: 2 * OV + 1])
    pack(inner, to_inner)
    pack(outer, to_outer)


def absorb(parity, after, inner_in, outer_in, coef, u_h, v_h, c_rows, edges, u, v, sems):
    cells, lat = coef.shape
    copies = [pltpu.make_async_copy(a, b, sems.at[i]) for i, (a, b) in enumerate([(u_h, u), (v_h, v)])]
    for copy in copies:
        copy.start()
    west, east = pick(parity, inner_in[: 2 * OV], outer_in[: 2 * OV])
    edges[:OV] = west[:OV]
    edges[OV:] = east[OV:]
    c_rows[: 2 * OV] = west
    c_rows[: OV - 1] = jnp.zeros((OV - 1, lat), F32)
    c_rows[2 * OV : 2 * OV + cells] = coef[...]
    c_rows[2 * OV + cells :] = east
    c_rows[3 * OV + cells + 1 :] = jnp.zeros((OV - 1, lat), F32)
    for copy in copies:
        copy.wait()


def second_solve(parity, inner_in, outer_in, first, c_rows, lat_basis, lon, scale,
                 z, y, second, inner, outer, wide, rows, spectral, m_rows):
    span, lat = first.shape
    cells = span - 2 * OV
    reach = 2 * OV + 1
    west, east = pick(parity, unpack(inner_in, reach, lat), unpack(outer_in, reach, lat))
    m_rows[:OV] = jnp.zeros((OV, lat), F32)
    m_rows[OV : OV + span] = first[...]
    m_rows[OV + span :] = jnp.zeros((OV, lat), F32)
    m_rows[OV - 1 : OV - 1 + reach] += west
    m_rows[OV + cells : OV + cells + reach] += east
    m_rows[...] = jnp.where(c_rows[...] > 0, m_rows[...], 0.0)
    inside = slice(OV, OV + span)
    c, m = c_rows[inside], m_rows[inside]
    z[...] = m
    beside = m_rows[OV - 1 : OV - 1 + span] + m_rows[OV + 1 : OV + 1 + span]
    image = jnp.where(c > 0, c * m - (beside + lat_beside(m)), 0.0)
    y[...] = image
    wide[:, :lat] = image
    wide[:, lat:] = jnp.zeros((span, wide.shape[1] - lat), F32)
    tile_solve(wide, lat_basis, lon, scale, rows, spectral, second)
    to_outer, to_inner = pick(parity, second[span - OV - 1 :], second[: OV + 1])
    pack(inner, to_inner)
    pack(outer, to_outer)


def sums(parity, inner_in, outer_in, second, z, y, c_rows, source, w, sent, held, sem):
    cells, lat = source.shape
    west, east = pick(parity, unpack(inner_in, OV + 1, lat), unpack(outer_in, OV + 1, lat))
    w[...] = second[...]
    w[OV - 1 : 2 * OV] += west
    w[cells : cells + OV + 1] += east
    w[...] = jnp.where(c_rows[OV : 3 * OV + cells] > 0, w[...], 0.0)
    own = slice(OV, OV + cells)
    c, m = c_rows[2 * OV : 2 * OV + cells], w[own]
    wet = c > 0
    beside = w[OV - 1 : OV - 1 + cells] + w[OV + 1 : OV + 1 + cells]
    x = jnp.where(wet, c * m - (beside + lat_beside(m)), 0.0)
    masked = jnp.where(wet, source[...], 0.0)
    land = jnp.where(wet, 0.0, source[...])
    z_own, y_own = z[own], y[own]

    def partial(a, b):
        product = a * b
        rows = product[:OV]
        for at in range(OV, cells, OV):
            rows = rows + product[at : at + OV]
        whole = lat // LANE * LANE
        total = rows[:, :LANE]
        for at in range(LANE, whole, LANE):
            total = total + rows[:, at : at + LANE]
        if whole < lat:
            blank = jnp.zeros((OV, LANE - lat + whole), F32)
            total = total + jnp.concatenate([rows[:, whole:], blank], axis=1)
        return jnp.sum(jnp.sum(total, axis=0, keepdims=True), axis=1, keepdims=True)

    pairs = [(masked, z_own), (z_own, y_own), (masked, m), (y_own, m), (z_own, x), (m, x), (land, land)]
    lane = lax.broadcasted_iota(jnp.int32, (1, LANE), 1)
    row = jnp.zeros((1, LANE), F32)
    for i, (a, b) in enumerate(pairs):
        row = jnp.where(lane == i, partial(a, b), row)
    held[...] = row
    copy = pltpu.make_async_copy(held, sent, sem)
    copy.start()
    copy.wait()


def finish(came_h, z, w, edges, source, depth, u_vel, v_vel, solution, u_new, v_new, w_vel,
           s_rows, d_rows, u_rows, v_out, w_out, s_out, came, sems):
    cells, lat = source.shape
    fetch = pltpu.make_async_copy(came_h, came, sems.at[0])
    fetch.start()
    fetch.wait()
    total = jnp.broadcast_to(jnp.sum(came[...], axis=0), (8, LANE))
    place = [lax.broadcasted_iota(jnp.int32, (8, LANE), axis) for axis in range(2)]
    total = jnp.sum(jnp.where(place[0] == place[1], total, 0.0), axis=1, keepdims=True)
    rz, zy, rw, yw, zx, wx, ll = [total[i : i + 1] for i in range(7)]
    step0 = (rz + ll) / (zy + ll)
    rest = (zy - rz) / (zy + ll)
    new = rz - step0 * (zy + rw) + step0 * step0 * yw + rest * rest * ll
    beta = new / (rz + ll)
    grown = 1.0 + beta
    bent = grown * grown * zy - grown * step0 * (zx + yw) + step0 * step0 * wx
    step1 = new / (bent + (rest + beta) * (rest + beta) * ll)
    of_z = jnp.broadcast_to(step0 + step1 * grown, (OV, lat))
    of_w = jnp.broadcast_to(-step1 * step0, (OV, lat))
    of_land = jnp.broadcast_to(step0 + step1 * (rest + beta), (OV, lat))

    copies = []
    d_rows[:OV] = jnp.broadcast_to(edges[KL : KL + 1], (OV, lat))
    d_rows[OV : OV + cells] = depth[...]
    d_rows[OV + cells :] = jnp.broadcast_to(edges[2 * OV - 1 :], (OV, lat))
    for at in range(0, cells + 2 * OV, OV):
        s = of_z * z[at : at + OV] + of_w * w[at : at + OV]
        if OV <= at < OV + cells:
            d = d_rows[at : at + OV]
            s = jnp.where(d > 0, s, of_land * source[at - OV : at])
            s_out[at - OV : at] = s
        s_rows[at : at + OV] = s
    copies.append(pltpu.make_async_copy(s_out, solution, sems.at[0]))
    copies[-1].start()

    s_west = s_rows[OV - 1 : OV]
    s_first = s_rows[OV : OV + 1]
    d_west = jnp.minimum(d_rows[OV - 1 : OV], d_rows[OV : OV + 1])
    for level in range(KL):
        left = edges[level : level + 1] - gravity_step * (s_first - s_west)
        u_rows[level, :OV] = jnp.broadcast_to(jnp.where(d_west > level, left, 0.0), (OV, lat))
    zero = jnp.zeros((OV, 1), F32)
    for block in range(cells // OV):
        at = OV + block * OV
        own = slice(at - OV, at)
        s = s_rows[at : at + OV]
        d = d_rows[at : at + OV]
        slope_e = gravity_step * (s_rows[at + 1 : at + OV + 1] - s)
        depth_e = jnp.minimum(d, d_rows[at + 1 : at + OV + 1])
        slope_n = gravity_step * (jnp.concatenate([s[:, 1:], zero], axis=1) - s)
        depth_n = jnp.minimum(d, jnp.concatenate([d[:, 1:], zero], axis=1))
        w_sum = jnp.zeros((OV, lat), F32)
        for level in range(KL - 1, -1, -1):
            u = jnp.where(depth_e > level, u_vel[level, own] - slope_e, 0.0)
            u_rows[level, at : at + OV] = u
            v = jnp.where(depth_n > level, v_vel[level, own] - slope_n, 0.0)
            v_out[level, own] = v
            south = jnp.concatenate([zero, v[:, :-1]], axis=1)
            flow = (u - u_rows[level, at - 1 : at + OV - 1]) + (v - south)
            w_sum = w_sum + jnp.where(d > level, flow, 0.0)
            w_out[level, own] = w_sum
        for held, result in ((u_rows.at[:, at : at + OV], u_new), (v_out.at[:, own], v_new), (w_out.at[:, own], w_vel)):
            copies.append(pltpu.make_async_copy(held, result.at[:, own], sems.at[len(copies)]))
            copies[-1].start()
    for copy in copies:
        copy.wait()


def swap_pairs(block, outward):
    devices = lax.axis_size("lon")
    if outward:
        route = [(i, (i - 1 if i % 2 == 0 else i + 1) % devices) for i in range(devices)]
    else:
        route = [(i, i ^ 1) for i in range(devices)]
    return lax.ppermute(block, "lon", route)


def shape(*dims):
    return jax.ShapeDtypeStruct(dims, F32)


def body(source, diagonal, u_vel, v_vel, bottom):
    cells, lat = source.shape
    span = cells + 2 * OV
    devices = lax.axis_size("lon")
    parity = (lax.axis_index("lon") % 2).astype(jnp.int32).reshape(1)
    consts = [jnp.asarray(table) for table in tables(span)]
    hbm = {name: pltpu.with_memory_space_constraint(x, pltpu.HBM) for name, x in (
        ("source", source), ("diagonal", diagonal), ("u", u_vel), ("v", v_vel), ("bottom", bottom))}
    consts = [pltpu.with_memory_space_constraint(x, pltpu.HBM) for x in consts]

    outer = pl.pallas_call(
        first_edges,
        in_specs=[SM, HB, HB],
        out_specs=VM,
        out_shape=pltpu.VMEM((OV, lat), F32),
        scratch_shapes=[pltpu.VMEM((OV, lat), F32), pltpu.VMEM((OV, lat), jnp.int32),
                        pltpu.SemaphoreType.DMA((2,))],
        compiler_params=PARAMS,
        name="first_edges",
    )(parity, hbm["source"], hbm["bottom"])
    outer_in = swap_pairs(outer, True)

    inner, far_inner, far_outer, masked, coef, depth, source_v, *held = pl.pallas_call(
        prepare,
        in_specs=[SM] + [HB] * 8,
        out_specs=[VM] * 10,
        out_shape=[pltpu.VMEM((OV, lat), F32)]
        + [pltpu.VMEM((FAR, lat), F32)] * 2
        + [pltpu.VMEM((cells, lat), F32)] * 4
        + [pltpu.VMEM(table.shape, table.dtype) for table in consts],
        scratch_shapes=[
            pltpu.VMEM((cells, lat), F32),
            pltpu.VMEM((cells, lat), jnp.int32),
            pltpu.VMEM((KL, OV, lat), F32),
            pltpu.SemaphoreType.DMA((7,)),
        ],
        compiler_params=PARAMS,
        cost_estimate=pl.CostEstimate(flops=10**6, bytes_accessed=7 * 10**6, transcendentals=0),
        name="prepare",
    )(parity, outer, hbm["source"], hbm["diagonal"], hbm["bottom"], hbm["u"], *consts)
    near = swap_pairs(inner, False), outer_in
    far = swap_pairs(far_inner, False), swap_pairs(far_outer, True)

    blocks = -(-lat // LANE)
    first, inner, outer = pl.pallas_call(
        first_solve,
        in_specs=[SM] + [VM] * 6,
        out_specs=[VM] * 3,
        out_shape=[pltpu.VMEM((span, lat), F32)] + [pltpu.VMEM(((2 * OV + 1) * blocks, LANE), F32)] * 2,
        scratch_shapes=solve_scratch(span, lat),
        compiler_params=PARAMS,
        name="first_solve",
    )(parity, *near, masked, *held)
    near = swap_pairs(inner, False), swap_pairs(outer, True)

    c_rows, edges, u_v, v_v = pl.pallas_call(
        absorb,
        in_specs=[SM, HB] + [VM] * 3 + [HB] * 2,
        out_specs=[VM] * 4,
        out_shape=[pltpu.VMEM((span + 2 * OV, lat), F32), pltpu.VMEM((2 * OV, lat), F32)]
        + [pltpu.VMEM((KL, cells, lat), F32)] * 2,
        scratch_shapes=[pltpu.SemaphoreType.DMA((2,))],
        compiler_params=PARAMS,
        cost_estimate=pl.CostEstimate(flops=10**6, bytes_accessed=7 * 10**6, transcendentals=0),
        name="absorb",
    )(parity, first, *far, coef, hbm["u"], hbm["v"])

    z, y, second, inner, outer = pl.pallas_call(
        second_solve,
        in_specs=[SM] + [VM] * 7,
        out_specs=[VM] * 5,
        out_shape=[pltpu.VMEM((span, lat), F32)] * 3 + [pltpu.VMEM(((OV + 1) * blocks, LANE), F32)] * 2,
        scratch_shapes=solve_scratch(span, lat) + [pltpu.VMEM((span + 2 * OV, lat), F32)],
        compiler_params=PARAMS,
        name="second_solve",
    )(parity, *near, first, c_rows, *held)
    near = swap_pairs(inner, False), swap_pairs(outer, True)

    w, sent = pl.pallas_call(
        sums,
        in_specs=[SM] + [VM] * 7,
        out_specs=[VM, HB],
        out_shape=[pltpu.VMEM((span, lat), F32), pltpu.HBM((1, LANE), F32)],
        scratch_shapes=[pltpu.VMEM((1, LANE), F32), pltpu.SemaphoreType.DMA],
        compiler_params=PARAMS,
        name="sums",
    )(parity, *near, second, z, y, c_rows, source_v)
    came = pltpu.with_memory_space_constraint(lax.all_gather(sent, "lon"), pltpu.HBM)

    return pl.pallas_call(
        finish,
        in_specs=[HB] + [VM] * 7,
        out_specs=[HB] * 4,
        out_shape=[shape(cells, lat)] + [shape(KL, cells, lat)] * 3,
        scratch_shapes=[pltpu.VMEM((span, lat), F32)] * 2
        + [pltpu.VMEM((KL, OV + cells, lat), F32)]
        + [pltpu.VMEM((KL, cells, lat), F32)] * 2
        + [pltpu.VMEM((cells, lat), F32), pltpu.VMEM((devices, 1, LANE), F32)]
        + [pltpu.SemaphoreType.DMA((1 + 3 * (cells // OV),))],
        compiler_params=PARAMS,
        name="finish",
    )(came, z, w, edges, source_v, depth, u_v, v_v)


def solution(mesh):
    return jax.shard_map(
        body,
        mesh=mesh,
        in_specs=(
            P(("members", "lon"), None),
            P(("members", "lon"), None),
            P(None, ("members", "lon"), None),
            P(None, ("members", "lon"), None),
            P(("members", "lon"), None),
        ),
        out_specs=(
            P(("members", "lon"), None),
            P(None, ("members", "lon"), None),
            P(None, ("members", "lon"), None),
            P(None, ("members", "lon"), None),
        ),
        check_vma=False,
    )
```

```python
import math

import jax
import jax.numpy as jnp
import ml_dtypes
import numpy as np
from jax import lax
from jax.experimental import pallas as pl
from jax.experimental.pallas import tpu as pltpu
from jax.sharding import PartitionSpec as P

LT = 112
OV = 8
KL = 6
LANE = 128
FAR = 24

tile_shift = 0.1
gravity_step = 0.5

F32 = jnp.float32
BF16 = jnp.bfloat16
VM = pl.BlockSpec(memory_space=pltpu.VMEM)
SM = pl.BlockSpec(memory_space=pltpu.SMEM)
HB = pl.BlockSpec(memory_space=pl.ANY)
PARAMS = pltpu.CompilerParams(vmem_limit_bytes=32 * 1024 * 1024)


def sine_basis(length):
    ordinal = np.arange(length, dtype=np.float64) + 1.0
    angles = math.pi * ordinal[:, None] * ordinal[None, :] / (length + 1)
    basis_matrix = np.sqrt(2.0 / (length + 1)) * np.sin(angles)
    eigen_value = 2.0 - 2.0 * np.cos(math.pi * ordinal / (length + 1))
    return basis_matrix, eigen_value


def halves(matrix):
    high = matrix.astype(ml_dtypes.bfloat16)
    low = (matrix - high.astype(np.float64)).astype(ml_dtypes.bfloat16)
    return high, low


def tables(span):
    lon_basis, lon_value = sine_basis(span)
    lat_basis, lat_value = sine_basis(LT + 2 * OV)
    high, low = halves(lat_basis)
    lat = np.block([[high, low], [high, np.zeros_like(low)]])
    high, low = halves(lon_basis)
    lon = np.concatenate([high, low, high], axis=1)
    scale = 1.0 / (lon_value[:, None] + lat_value[None, :] + tile_shift)
    return lat, lon, scale.astype(np.float32)


def split(x):
    high = x.astype(BF16)
    return high, (x - high.astype(F32)).astype(BF16)


def tile_solve(x, lat_basis, lon, scale, rows, spectral, out):
    span, lat = out.shape
    tiles = lat // LT
    lane = lax.broadcasted_iota(jnp.int32, (span, LANE), 1)

    def block_of(b):
        if b < 0:
            return jnp.zeros((span, LANE), F32)
        return x[:, b * LANE : (b + 1) * LANE]

    chunk = 4
    groups = [range(first, min(first + chunk, tiles)) for first in range(0, tiles, chunk)]
    held = {}

    def lanes_of(group):
        return slice(group[0] * LANE, (group[-1] + 1) * LANE)

    def cut(group):
        for t in group:
            block, start = divmod(t * LT - OV, LANE)
            left, right = [pltpu.roll(block_of(b), LANE - start, 1) for b in (block, block + 1)]
            high, low = split(jnp.where(lane < LANE - start, left, right))
            rows[t * span : (t + 1) * span, :LANE] = high
            rows[t * span : (t + 1) * span, LANE:] = low

    def along_lat(group):
        product = jnp.dot(
            rows[group[0] * span : (group[-1] + 1) * span], lat_basis[...], preferred_element_type=F32
        )
        return product[:, :LANE] + product[:, LANE:]

    def lat_there(group):
        high, low = split(along_lat(group))
        for i, t in enumerate(group):
            at = slice(t * LANE, (t + 1) * LANE)
            spectral[:span, at] = high[i * span : (i + 1) * span]
            spectral[span : 2 * span, at] = high[i * span : (i + 1) * span]
            spectral[2 * span :, at] = low[i * span : (i + 1) * span]

    def lon_there(group):
        c = jnp.dot(lon[...], spectral[:, lanes_of(group)], preferred_element_type=F32)
        high, low = split(c * jnp.concatenate([scale[...]] * len(group), axis=1))
        spectral[:, lanes_of(group)] = jnp.concatenate([high, high, low], axis=0)

    def lon_back(group):
        c = jnp.dot(lon[...], spectral[:, lanes_of(group)], preferred_element_type=F32)
        high, low = split(c)
        for i, t in enumerate(group):
            at = slice(t * span, (t + 1) * span)
            rows[at, :LANE] = high[:, i * LANE : (i + 1) * LANE]
            rows[at, LANE:] = low[:, i * LANE : (i + 1) * LANE]

    def lat_back(group):
        product = along_lat(group)
        for i, t in enumerate(group):
            block, start = divmod(t * LT - OV, LANE)
            part = pltpu.roll(product[i * span : (i + 1) * span], start, 1)
            for b, inside in ((block, lane >= start), (block + 1, lane < start)):
                if 0 <= b * LANE < lat:
                    piece = jnp.where(inside, part, 0.0)
                    held[b] = held[b] + piece if b in held else piece
        done = (group[-1] + 1) * LT - OV if group[-1] + 1 < tiles else lat + LANE
        for b in [b for b in held if (b + 1) * LANE <= done]:
            width = min(LANE, lat - b * LANE)
            out[:, b * LANE : b * LANE + width] = held.pop(b)[:, :width]

    stages = [cut, lat_there, lon_there, lon_back, lat_back]
    for step in range(len(groups) + len(stages) - 1):
        for i in reversed(range(len(stages))):
            if 0 <= step - i < len(groups):
                stages[i](groups[step - i])


def wide_lanes(lat):
    return -(-(lat + OV) // LANE) * LANE


def solve_scratch(span, lat):
    tiles = lat // LT
    return [
        pltpu.VMEM((span, wide_lanes(lat)), F32),
        pltpu.VMEM((tiles * span, 2 * LANE), BF16),
        pltpu.VMEM((3 * span, tiles * LANE), BF16),
    ]


def pick(parity, inner, outer):
    even = jnp.full(inner.shape, parity[0], jnp.int32) == 0
    return jnp.where(even, outer, inner), jnp.where(even, inner, outer)


def lat_beside(m):
    zero = jnp.zeros((m.shape[0], 1), m.dtype)
    return jnp.concatenate([m[:, 1:], zero], axis=1) + jnp.concatenate([zero, m[:, :-1]], axis=1)


def pack(message, rows):
    n, lat = rows.shape
    for block, at in enumerate(range(0, lat, LANE)):
        width = min(LANE, lat - at)
        message[block * n : (block + 1) * n, :width] = rows[:, at : at + width]


def unpack(message, n, lat):
    blocks = [message[i * n : (i + 1) * n] for i in range(-(-lat // LANE))]
    return jnp.concatenate(blocks, axis=1)[:, :lat]


def first_edges(parity, source, bottom, outer, rows, depth, sems):
    start = pl.multiple_of(parity[0] * (source.shape[0] - OV), OV)
    at = pl.ds(start, OV)
    copies = [
        pltpu.make_async_copy(source.at[at], rows, sems.at[0]),
        pltpu.make_async_copy(bottom.at[at], depth, sems.at[1]),
    ]
    for copy in copies:
        copy.start()
    for copy in copies:
        copy.wait()
    outer[...] = jnp.where(depth[...] > 0, rows[...], 0.0)


def prepare(parity, after, source_h, diagonal_h, bottom_h, u_h, *refs):
    tables_h, (inner, far_inner, far_outer, masked, coef, depth, source), held = refs[:3], refs[3:10], refs[10:13]
    diagonal, bottom, u_strip, sems = refs[13:]
    cells, lat = source.shape
    pairs = [(source_h, source), (bottom_h, bottom), (diagonal_h, diagonal)]
    pairs += [(u_h.at[:, pl.ds(cells - OV, OV)], u_strip)]
    pairs += list(zip(tables_h, held))
    copies = [pltpu.make_async_copy(a, b, sems.at[i]) for i, (a, b) in enumerate(pairs)]
    for copy in copies:
        copy.start()
    for copy in copies[:4]:
        copy.wait()
    wet = bottom[...] > 0
    masked[...] = jnp.where(wet, source[...], 0.0)
    coef[...] = jnp.where(wet, 4.0 + diagonal[...], 0.0)
    depth[...] = bottom[...].astype(F32)
    edge = OV + 1
    blank = jnp.zeros((2 * OV - edge - 1, lat), F32)
    to_west = jnp.concatenate([coef[:edge], blank, depth[:1]], axis=0)
    u_rows = [u_strip[level, OV - 1 : OV] for level in range(KL)]
    to_east = jnp.concatenate(u_rows + [depth[cells - 1 :], coef[cells - edge :]], axis=0)
    far_outer[: 2 * OV], far_inner[: 2 * OV] = pick(parity, to_east, to_west)
    for message in (far_outer, far_inner):
        message[2 * OV :] = jnp.zeros((FAR - 2 * OV, lat), F32)
    inner[...] = pick(parity, masked[:OV], masked[cells - OV :])[0]
    for copy in copies[4:]:
        copy.wait()


def first_solve(parity, inner_in, outer_in, masked, lat_basis, lon, scale,
                first, inner, outer, wide, rows, spectral):
    cells, lat = masked.shape
    west, east = pick(parity, inner_in[...], outer_in[...])
    wide[:OV, :lat] = west
    wide[OV : OV + cells, :lat] = masked[...]
    wide[OV + cells :, :lat] = east
    wide[:, lat:] = jnp.zeros((cells + 2 * OV, wide.shape[1] - lat), F32)
    tile_solve(wide, lat_basis, lon, scale, rows, spectral, first)
    to_outer, to_inner = pick(parity, first[cells - 1 :], first[: 2 * OV + 1])
    pack(inner, to_inner)
    pack(outer, to_outer)


def absorb(parity, after, inner_in, outer_in, coef, depth, u_h, v_h, c_rows, d_rows, edge, u, v, sems):
    cells, lat = coef.shape
    copies = [pltpu.make_async_copy(a, b, sems.at[i]) for i, (a, b) in enumerate([(u_h, u), (v_h, v)])]
    for copy in copies:
        copy.start()
    west, east = pick(parity, inner_in[: 2 * OV], outer_in[: 2 * OV])
    edge[...] = west[:OV]
    d_rows[:OV] = jnp.broadcast_to(west[KL : KL + 1], (OV, lat))
    d_rows[OV : OV + cells] = depth[...]
    d_rows[OV + cells :] = jnp.broadcast_to(east[2 * OV - 1 :], (OV, lat))
    c_rows[: 2 * OV] = west
    c_rows[: OV - 1] = jnp.zeros((OV - 1, lat), F32)
    c_rows[2 * OV : 2 * OV + cells] = coef[...]
    c_rows[2 * OV + cells :] = east
    c_rows[3 * OV + cells + 1 :] = jnp.zeros((OV - 1, lat), F32)
    for copy in copies:
        copy.wait()


def second_solve(parity, inner_in, outer_in, first, c_rows, lat_basis, lon, scale,
                 z, y, second, inner, outer, wide, rows, spectral, m_rows):
    span, lat = first.shape
    cells = span - 2 * OV
    reach = 2 * OV + 1
    west, east = pick(parity, unpack(inner_in, reach, lat), unpack(outer_in, reach, lat))
    m_rows[:OV] = jnp.zeros((OV, lat), F32)
    m_rows[OV : OV + span] = first[...]
    m_rows[OV + span :] = jnp.zeros((OV, lat), F32)
    m_rows[OV - 1 : OV - 1 + reach] += west
    m_rows[OV + cells : OV + cells + reach] += east
    m_rows[...] = jnp.where(c_rows[...] > 0, m_rows[...], 0.0)
    inside = slice(OV, OV + span)
    c, m = c_rows[inside], m_rows[inside]
    z[...] = m
    beside = m_rows[OV - 1 : OV - 1 + span] + m_rows[OV + 1 : OV + 1 + span]
    image = jnp.where(c > 0, c * m - (beside + lat_beside(m)), 0.0)
    y[...] = image
    wide[:, :lat] = image
    wide[:, lat:] = jnp.zeros((span, wide.shape[1] - lat), F32)
    tile_solve(wide, lat_basis, lon, scale, rows, spectral, second)
    to_outer, to_inner = pick(parity, second[span - OV - 1 :], second[: OV + 1])
    pack(inner, to_inner)
    pack(outer, to_outer)


def sums(parity, inner_in, outer_in, second, z, y, c_rows, source, w, sent):
    cells, lat = source.shape
    west, east = pick(parity, unpack(inner_in, OV + 1, lat), unpack(outer_in, OV + 1, lat))
    w[...] = second[...]
    w[OV - 1 : 2 * OV] += west
    w[cells : cells + OV + 1] += east
    w[...] = jnp.where(c_rows[OV : 3 * OV + cells] > 0, w[...], 0.0)
    own = slice(OV, OV + cells)
    c, m = c_rows[2 * OV : 2 * OV + cells], w[own]
    wet = c > 0
    beside = w[OV - 1 : OV - 1 + cells] + w[OV + 1 : OV + 1 + cells]
    x = jnp.where(wet, c * m - (beside + lat_beside(m)), 0.0)
    masked = jnp.where(wet, source[...], 0.0)
    land = jnp.where(wet, 0.0, source[...])
    z_own, y_own = z[own], y[own]

    def partial(a, b):
        product = a * b
        rows = product[:OV]
        for at in range(OV, cells, OV):
            rows = rows + product[at : at + OV]
        whole = lat // LANE * LANE
        total = rows[:, :LANE]
        for at in range(LANE, whole, LANE):
            total = total + rows[:, at : at + LANE]
        if whole < lat:
            blank = jnp.zeros((OV, LANE - lat + whole), F32)
            total = total + jnp.concatenate([rows[:, whole:], blank], axis=1)
        return jnp.sum(jnp.sum(total, axis=0, keepdims=True), axis=1, keepdims=True)

    pairs = [(masked, z_own), (z_own, y_own), (masked, m), (y_own, m), (z_own, x), (m, x), (land, land)]
    lane = lax.broadcasted_iota(jnp.int32, (1, LANE), 1)
    row = jnp.zeros((1, LANE), F32)
    for i, (a, b) in enumerate(pairs):
        row = jnp.where(lane == i, partial(a, b), row)
    sent[...] = jnp.broadcast_to(row[None], sent.shape)


def finish(came, z, w, d_rows, edge, source, u_vel, v_vel, solution, u_new, v_new, w_vel,
           s_rows, u_rows, v_out, w_out, s_out, sems):
    cells, lat = source.shape
    total = jnp.broadcast_to(jnp.sum(came[...], axis=0), (8, LANE))
    place = [lax.broadcasted_iota(jnp.int32, (8, LANE), axis) for axis in range(2)]
    total = jnp.sum(jnp.where(place[0] == place[1], total, 0.0), axis=1, keepdims=True)
    rz, zy, rw, yw, zx, wx, ll = [total[i : i + 1] for i in range(7)]
    step0 = (rz + ll) / (zy + ll)
    rest = (zy - rz) / (zy + ll)
    new = rz - step0 * (zy + rw) + step0 * step0 * yw + rest * rest * ll
    beta = new / (rz + ll)
    grown = 1.0 + beta
    bent = grown * grown * zy - grown * step0 * (zx + yw) + step0 * step0 * wx
    step1 = new / (bent + (rest + beta) * (rest + beta) * ll)
    of_z = jnp.broadcast_to(step0 + step1 * grown, (OV, lat))
    of_w = jnp.broadcast_to(-step1 * step0, (OV, lat))
    of_land = jnp.broadcast_to(step0 + step1 * (rest + beta), (OV, lat))

    copies = []

    def send(held, result):
        copies.append(pltpu.make_async_copy(held, result, sems.at[len(copies)]))
        copies[-1].start()

    def surface_rows(at):
        s = of_z * z[at : at + OV] + of_w * w[at : at + OV]
        if OV <= at < OV + cells:
            s = jnp.where(d_rows[at : at + OV] > 0, s, of_land * source[at - OV : at])
            s_out[at - OV : at] = s
        s_rows[at : at + OV] = s

    surface_rows(0)
    surface_rows(OV)
    slope = gravity_step * (s_rows[OV : OV + 1] - s_rows[OV - 1 : OV])
    d_west = jnp.minimum(d_rows[OV - 1 : OV], d_rows[OV : OV + 1])
    for level in range(KL):
        u = jnp.where(d_west > level, edge[level : level + 1] - slope, 0.0)
        u_rows[level, :OV] = jnp.broadcast_to(u, (OV, lat))
    zero = jnp.zeros((OV, 1), F32)
    for at in range(OV, OV + cells, OV):
        own = slice(at - OV, at)
        surface_rows(at + OV)
        s = s_rows[at : at + OV]
        d = d_rows[at : at + OV]
        slope = gravity_step * (s_rows[at + 1 : at + OV + 1] - s)
        face = jnp.minimum(d, d_rows[at + 1 : at + OV + 1])
        for level in range(KL):
            u_rows[level, at : at + OV] = jnp.where(face > level, u_vel[level, own] - slope, 0.0)
        send(u_rows.at[:, at : at + OV], u_new.at[:, own])
        slope = gravity_step * (jnp.concatenate([s[:, 1:], zero], axis=1) - s)
        face = jnp.minimum(d, jnp.concatenate([d[:, 1:], zero], axis=1))
        for level in range(KL):
            v_out[level, own] = jnp.where(face > level, v_vel[level, own] - slope, 0.0)
        send(v_out.at[:, own], v_new.at[:, own])
        w_sum = jnp.zeros((OV, lat), F32)
        for level in range(KL - 1, -1, -1):
            v = v_out[level, own]
            flow = u_rows[level, at : at + OV] - u_rows[level, at - 1 : at + OV - 1]
            flow = flow + (v - jnp.concatenate([zero, v[:, :-1]], axis=1))
            w_sum = w_sum + jnp.where(d > level, flow, 0.0)
            w_out[level, own] = w_sum
        send(w_out.at[:, own], w_vel.at[:, own])
        if at == cells:
            send(s_out, solution)
    for copy in copies:
        copy.wait()


def swap_pairs(block, outward):
    devices = lax.axis_size("lon")
    if outward:
        route = [(i, (i - 1 if i % 2 == 0 else i + 1) % devices) for i in range(devices)]
    else:
        route = [(i, i ^ 1) for i in range(devices)]
    return lax.ppermute(block, "lon", route)


def shape(*dims):
    return jax.ShapeDtypeStruct(dims, F32)


def body(source, diagonal, u_vel, v_vel, bottom):
    cells, lat = source.shape
    span = cells + 2 * OV
    devices = lax.axis_size("lon")
    parity = (lax.axis_index("lon") % 2).astype(jnp.int32).reshape(1)
    consts = [jnp.asarray(table) for table in tables(span)]
    hbm = {name: pltpu.with_memory_space_constraint(x, pltpu.HBM) for name, x in (
        ("source", source), ("diagonal", diagonal), ("u", u_vel), ("v", v_vel), ("bottom", bottom))}
    consts = [pltpu.with_memory_space_constraint(x, pltpu.HBM) for x in consts]

    outer = pl.pallas_call(
        first_edges,
        in_specs=[SM, HB, HB],
        out_specs=VM,
        out_shape=pltpu.VMEM((OV, lat), F32),
        scratch_shapes=[pltpu.VMEM((OV, lat), F32), pltpu.VMEM((OV, lat), jnp.int32),
                        pltpu.SemaphoreType.DMA((2,))],
        compiler_params=PARAMS,
        name="first_edges",
    )(parity, hbm["source"], hbm["bottom"])
    outer_in = swap_pairs(outer, True)

    inner, far_inner, far_outer, masked, coef, depth, source_v, *held = pl.pallas_call(
        prepare,
        in_specs=[SM] + [HB] * 8,
        out_specs=[VM] * 10,
        out_shape=[pltpu.VMEM((OV, lat), F32)]
        + [pltpu.VMEM((FAR, lat), F32)] * 2
        + [pltpu.VMEM((cells, lat), F32)] * 4
        + [pltpu.VMEM(table.shape, table.dtype) for table in consts],
        scratch_shapes=[
            pltpu.VMEM((cells, lat), F32),
            pltpu.VMEM((cells, lat), jnp.int32),
            pltpu.VMEM((KL, OV, lat), F32),
            pltpu.SemaphoreType.DMA((7,)),
        ],
        compiler_params=PARAMS,
        cost_estimate=pl.CostEstimate(flops=10**6, bytes_accessed=7 * 10**6, transcendentals=0),
        name="prepare",
    )(parity, outer, hbm["source"], hbm["diagonal"], hbm["bottom"], hbm["u"], *consts)
    near = swap_pairs(inner, False), outer_in
    far = swap_pairs(far_inner, False), swap_pairs(far_outer, True)

    blocks = -(-lat // LANE)
    first, inner, outer = pl.pallas_call(
        first_solve,
        in_specs=[SM] + [VM] * 6,
        out_specs=[VM] * 3,
        out_shape=[pltpu.VMEM((span, lat), F32)] + [pltpu.VMEM(((2 * OV + 1) * blocks, LANE), F32)] * 2,
        scratch_shapes=solve_scratch(span, lat),
        compiler_params=PARAMS,
        name="first_solve",
    )(parity, *near, masked, *held)
    near = swap_pairs(inner, False), swap_pairs(outer, True)

    c_rows, d_rows, edge, u_v, v_v = pl.pallas_call(
        absorb,
        in_specs=[SM, HB] + [VM] * 4 + [HB] * 2,
        out_specs=[VM] * 5,
        out_shape=[pltpu.VMEM((span + 2 * OV, lat), F32), pltpu.VMEM((span, lat), F32), pltpu.VMEM((OV, lat), F32)]
        + [pltpu.VMEM((KL, cells, lat), F32)] * 2,
        scratch_shapes=[pltpu.SemaphoreType.DMA((2,))],
        compiler_params=PARAMS,
        cost_estimate=pl.CostEstimate(flops=10**6, bytes_accessed=7 * 10**6, transcendentals=0),
        name="absorb",
    )(parity, first, *far, coef, depth, hbm["u"], hbm["v"])

    z, y, second, inner, outer = pl.pallas_call(
        second_solve,
        in_specs=[SM] + [VM] * 7,
        out_specs=[VM] * 5,
        out_shape=[pltpu.VMEM((span, lat), F32)] * 3 + [pltpu.VMEM(((OV + 1) * blocks, LANE), F32)] * 2,
        scratch_shapes=solve_scratch(span, lat) + [pltpu.VMEM((span + 2 * OV, lat), F32)],
        compiler_params=PARAMS,
        name="second_solve",
    )(parity, *near, first, c_rows, *held)
    near = swap_pairs(inner, False), swap_pairs(outer, True)

    w, sent = pl.pallas_call(
        sums,
        in_specs=[SM] + [VM] * 7,
        out_specs=[VM] * 2,
        out_shape=[pltpu.VMEM((span, lat), F32), pltpu.VMEM((devices, 1, LANE), F32)],
        compiler_params=PARAMS,
        name="sums",
    )(parity, *near, second, z, y, c_rows, source_v)
    came = lax.all_to_all(sent, "lon", 0, 0)

    return pl.pallas_call(
        finish,
        in_specs=[VM] * 8,
        out_specs=[HB] * 4,
        out_shape=[shape(cells, lat)] + [shape(KL, cells, lat)] * 3,
        scratch_shapes=[pltpu.VMEM((span, lat), F32)]
        + [pltpu.VMEM((KL, OV + cells, lat), F32)]
        + [pltpu.VMEM((KL, cells, lat), F32)] * 2
        + [pltpu.VMEM((cells, lat), F32), pltpu.SemaphoreType.DMA((1 + 3 * (cells // OV),))],
        compiler_params=PARAMS,
        name="finish",
    )(came, z, w, d_rows, edge, source_v, u_v, v_v)


def solution(mesh):
    return jax.shard_map(
        body,
        mesh=mesh,
        in_specs=(
            P(("members", "lon"), None),
            P(("members", "lon"), None),
            P(None, ("members", "lon"), None),
            P(None, ("members", "lon"), None),
            P(("members", "lon"), None),
        ),
        out_specs=(
            P(("members", "lon"), None),
            P(None, ("members", "lon"), None),
            P(None, ("members", "lon"), None),
            P(None, ("members", "lon"), None),
        ),
        check_vma=False,
    )
```

```python
import math

import jax
import jax.numpy as jnp
import ml_dtypes
import numpy as np
from jax import lax
from jax.experimental import pallas as pl
from jax.experimental.pallas import tpu as pltpu
from jax.sharding import PartitionSpec as P

LT = 112
OV = 8
KL = 6
LANE = 128
FAR = 24

tile_shift = 0.1
gravity_step = 0.5

F32 = jnp.float32
BF16 = jnp.bfloat16
VM = pl.BlockSpec(memory_space=pltpu.VMEM)
SM = pl.BlockSpec(memory_space=pltpu.SMEM)
HB = pl.BlockSpec(memory_space=pl.ANY)
PARAMS = pltpu.CompilerParams(vmem_limit_bytes=32 * 1024 * 1024)


def sine_basis(length):
    ordinal = np.arange(length, dtype=np.float64) + 1.0
    angles = math.pi * ordinal[:, None] * ordinal[None, :] / (length + 1)
    basis_matrix = np.sqrt(2.0 / (length + 1)) * np.sin(angles)
    eigen_value = 2.0 - 2.0 * np.cos(math.pi * ordinal / (length + 1))
    return basis_matrix, eigen_value


def halves(matrix):
    high = matrix.astype(ml_dtypes.bfloat16)
    low = (matrix - high.astype(np.float64)).astype(ml_dtypes.bfloat16)
    return high, low


def tables(span):
    lon_basis, lon_value = sine_basis(span)
    lat_basis, lat_value = sine_basis(LT + 2 * OV)
    high, low = halves(lat_basis)
    lat = np.block([[high, low], [high, np.zeros_like(low)]])
    high, low = halves(lon_basis)
    lon = np.concatenate([high, low, high], axis=1)
    scale = 1.0 / (lon_value[:, None] + lat_value[None, :] + tile_shift)
    return lat, lon, scale.astype(np.float32)


def split(x):
    high = x.astype(BF16)
    return high, (x - high.astype(F32)).astype(BF16)


def tile_solve(x, lat_basis, lon, scale, rows, spectral, out):
    span, lat = out.shape
    tiles = lat // LT
    lane = lax.broadcasted_iota(jnp.int32, (span, LANE), 1)

    def block_of(b):
        if b < 0:
            return jnp.zeros((span, LANE), F32)
        return x[:, b * LANE : (b + 1) * LANE]

    chunk = 4
    groups = [range(first, min(first + chunk, tiles)) for first in range(0, tiles, chunk)]
    held = {}

    def lanes_of(group):
        return slice(group[0] * LANE, (group[-1] + 1) * LANE)

    def cut(group):
        for t in group:
            block, start = divmod(t * LT - OV, LANE)
            left, right = [pltpu.roll(block_of(b), LANE - start, 1) for b in (block, block + 1)]
            high, low = split(jnp.where(lane < LANE - start, left, right))
            rows[t * span : (t + 1) * span, :LANE] = high
            rows[t * span : (t + 1) * span, LANE:] = low

    def along_lat(group):
        product = jnp.dot(
            rows[group[0] * span : (group[-1] + 1) * span], lat_basis[...], preferred_element_type=F32
        )
        return product[:, :LANE] + product[:, LANE:]

    def lat_there(group):
        high, low = split(along_lat(group))
        for i, t in enumerate(group):
            at = slice(t * LANE, (t + 1) * LANE)
            spectral[:span, at] = high[i * span : (i + 1) * span]
            spectral[span : 2 * span, at] = high[i * span : (i + 1) * span]
            spectral[2 * span :, at] = low[i * span : (i + 1) * span]

    def lon_there(group):
        c = jnp.dot(lon[...], spectral[:, lanes_of(group)], preferred_element_type=F32)
        high, low = split(c * jnp.concatenate([scale[...]] * len(group), axis=1))
        spectral[:, lanes_of(group)] = jnp.concatenate([high, high, low], axis=0)

    def lon_back(group):
        c = jnp.dot(lon[...], spectral[:, lanes_of(group)], preferred_element_type=F32)
        high, low = split(c)
        for i, t in enumerate(group):
            at = slice(t * span, (t + 1) * span)
            rows[at, :LANE] = high[:, i * LANE : (i + 1) * LANE]
            rows[at, LANE:] = low[:, i * LANE : (i + 1) * LANE]

    def lat_back(group):
        product = along_lat(group)
        for i, t in enumerate(group):
            block, start = divmod(t * LT - OV, LANE)
            part = pltpu.roll(product[i * span : (i + 1) * span], start, 1)
            for b, inside in ((block, lane >= start), (block + 1, lane < start)):
                if 0 <= b * LANE < lat:
                    piece = jnp.where(inside, part, 0.0)
                    held[b] = held[b] + piece if b in held else piece
        done = (group[-1] + 1) * LT - OV if group[-1] + 1 < tiles else lat + LANE
        for b in [b for b in held if (b + 1) * LANE <= done]:
            width = min(LANE, lat - b * LANE)
            out[:, b * LANE : b * LANE + width] = held.pop(b)[:, :width]

    stages = [cut, lat_there, lon_there, lon_back, lat_back]
    for step in range(len(groups) + len(stages) - 1):
        for i in reversed(range(len(stages))):
            if 0 <= step - i < len(groups):
                stages[i](groups[step - i])


def wide_lanes(lat):
    return -(-(lat + OV) // LANE) * LANE


def solve_scratch(span, lat):
    tiles = lat // LT
    return [
        pltpu.VMEM((span, wide_lanes(lat)), F32),
        pltpu.VMEM((tiles * span, 2 * LANE), BF16),
        pltpu.VMEM((3 * span, tiles * LANE), BF16),
    ]


def pick(parity, inner, outer):
    even = jnp.full(inner.shape, parity[0], jnp.int32) == 0
    return jnp.where(even, outer, inner), jnp.where(even, inner, outer)


def lat_beside(m):
    zero = jnp.zeros((m.shape[0], 1), m.dtype)
    return jnp.concatenate([m[:, 1:], zero], axis=1) + jnp.concatenate([zero, m[:, :-1]], axis=1)


def pack(message, rows):
    n, lat = rows.shape
    for block, at in enumerate(range(0, lat, LANE)):
        width = min(LANE, lat - at)
        message[block * n : (block + 1) * n, :width] = rows[:, at : at + width]


def unpack(message, n, lat):
    blocks = [message[i * n : (i + 1) * n] for i in range(-(-lat // LANE))]
    return jnp.concatenate(blocks, axis=1)[:, :lat]


def first_edges(parity, source, bottom, outer, rows, depth, sems):
    start = pl.multiple_of(parity[0] * (source.shape[0] - OV), OV)
    at = pl.ds(start, OV)
    copies = [
        pltpu.make_async_copy(source.at[at], rows, sems.at[0]),
        pltpu.make_async_copy(bottom.at[at], depth, sems.at[1]),
    ]
    for copy in copies:
        copy.start()
    for copy in copies:
        copy.wait()
    outer[...] = jnp.where(depth[...] > 0, rows[...], 0.0)


def prepare(parity, after, source_h, diagonal_h, bottom_h, u_h, *refs):
    tables_h, (inner, far_inner, far_outer, masked, coef, depth, source), held = refs[:3], refs[3:10], refs[10:13]
    diagonal, bottom, u_strip, sems = refs[13:]
    cells, lat = source.shape
    pairs = [(source_h, source), (bottom_h, bottom), (diagonal_h, diagonal)]
    pairs += [(u_h.at[:, pl.ds(cells - OV, OV)], u_strip)]
    pairs += list(zip(tables_h, held))
    copies = [pltpu.make_async_copy(a, b, sems.at[i]) for i, (a, b) in enumerate(pairs)]
    for copy in copies:
        copy.start()
    for copy in copies[:4]:
        copy.wait()
    wet = bottom[...] > 0
    masked[...] = jnp.where(wet, source[...], 0.0)
    coef[...] = jnp.where(wet, 4.0 + diagonal[...], 0.0)
    depth[...] = bottom[...].astype(F32)
    edge = OV + 1
    blank = jnp.zeros((2 * OV - edge - 1, lat), F32)
    to_west = jnp.concatenate([coef[:edge], blank, depth[:1]], axis=0)
    u_rows = [u_strip[level, OV - 1 : OV] for level in range(KL)]
    to_east = jnp.concatenate(u_rows + [depth[cells - 1 :], coef[cells - edge :]], axis=0)
    far_outer[: 2 * OV], far_inner[: 2 * OV] = pick(parity, to_east, to_west)
    for message in (far_outer, far_inner):
        message[2 * OV :] = jnp.zeros((FAR - 2 * OV, lat), F32)
    inner[...] = pick(parity, masked[:OV], masked[cells - OV :])[0]
    for copy in copies[4:]:
        copy.wait()


def first_solve(parity, inner_in, outer_in, masked, lat_basis, lon, scale,
                first, inner, outer, wide, rows, spectral):
    cells, lat = masked.shape
    west, east = pick(parity, inner_in[...], outer_in[...])
    wide[:OV, :lat] = west
    wide[OV : OV + cells, :lat] = masked[...]
    wide[OV + cells :, :lat] = east
    wide[:, lat:] = jnp.zeros((cells + 2 * OV, wide.shape[1] - lat), F32)
    tile_solve(wide, lat_basis, lon, scale, rows, spectral, first)
    to_outer, to_inner = pick(parity, first[cells - 1 :], first[: 2 * OV + 1])
    pack(inner, to_inner)
    pack(outer, to_outer)


def absorb(parity, after, inner_in, outer_in, coef, depth, u_h, v_h, c_rows, d_rows, edge, u, v, sems):
    cells, lat = coef.shape
    copies = [pltpu.make_async_copy(a, b, sems.at[i]) for i, (a, b) in enumerate([(u_h, u), (v_h, v)])]
    for copy in copies:
        copy.start()
    west, east = pick(parity, inner_in[: 2 * OV], outer_in[: 2 * OV])
    edge[...] = west[:OV]
    d_rows[:OV] = jnp.broadcast_to(west[KL : KL + 1], (OV, lat))
    d_rows[OV : OV + cells] = depth[...]
    d_rows[OV + cells :] = jnp.broadcast_to(east[2 * OV - 1 :], (OV, lat))
    c_rows[: 2 * OV] = west
    c_rows[: OV - 1] = jnp.zeros((OV - 1, lat), F32)
    c_rows[2 * OV : 2 * OV + cells] = coef[...]
    c_rows[2 * OV + cells :] = east
    c_rows[3 * OV + cells + 1 :] = jnp.zeros((OV - 1, lat), F32)
    for copy in copies:
        copy.wait()


def second_solve(parity, inner_in, outer_in, first, c_rows, lat_basis, lon, scale,
                 z, y, second, inner, outer, wide, rows, spectral, m_rows):
    span, lat = first.shape
    cells = span - 2 * OV
    reach = 2 * OV + 1
    west, east = pick(parity, unpack(inner_in, reach, lat), unpack(outer_in, reach, lat))
    m_rows[:OV] = jnp.zeros((OV, lat), F32)
    m_rows[OV : OV + span] = first[...]
    m_rows[OV + span :] = jnp.zeros((OV, lat), F32)
    m_rows[OV - 1 : OV - 1 + reach] += west
    m_rows[OV + cells : OV + cells + reach] += east
    m_rows[...] = jnp.where(c_rows[...] > 0, m_rows[...], 0.0)
    inside = slice(OV, OV + span)
    c, m = c_rows[inside], m_rows[inside]
    z[...] = m
    beside = m_rows[OV - 1 : OV - 1 + span] + m_rows[OV + 1 : OV + 1 + span]
    image = jnp.where(c > 0, c * m - (beside + lat_beside(m)), 0.0)
    y[...] = image
    wide[:, :lat] = image
    wide[:, lat:] = jnp.zeros((span, wide.shape[1] - lat), F32)
    tile_solve(wide, lat_basis, lon, scale, rows, spectral, second)
    to_outer, to_inner = pick(parity, second[span - OV - 1 :], second[: OV + 1])
    pack(inner, to_inner)
    pack(outer, to_outer)


def sums(parity, inner_in, outer_in, second, z, y, c_rows, source, w, sent):
    cells, lat = source.shape
    west, east = pick(parity, unpack(inner_in, OV + 1, lat), unpack(outer_in, OV + 1, lat))
    w[...] = second[...]
    w[OV - 1 : 2 * OV] += west
    w[cells : cells + OV + 1] += east
    w[...] = jnp.where(c_rows[OV : 3 * OV + cells] > 0, w[...], 0.0)
    own = slice(OV, OV + cells)
    c, m = c_rows[2 * OV : 2 * OV + cells], w[own]
    wet = c > 0
    beside = w[OV - 1 : OV - 1 + cells] + w[OV + 1 : OV + 1 + cells]
    x = jnp.where(wet, c * m - (beside + lat_beside(m)), 0.0)
    masked = jnp.where(wet, source[...], 0.0)
    land = jnp.where(wet, 0.0, source[...])
    z_own, y_own = z[own], y[own]

    def partial(a, b):
        product = a * b
        rows = product[:OV]
        for at in range(OV, cells, OV):
            rows = rows + product[at : at + OV]
        whole = lat // LANE * LANE
        total = rows[:, :LANE]
        for at in range(LANE, whole, LANE):
            total = total + rows[:, at : at + LANE]
        if whole < lat:
            blank = jnp.zeros((OV, LANE - lat + whole), F32)
            total = total + jnp.concatenate([rows[:, whole:], blank], axis=1)
        return jnp.sum(jnp.sum(total, axis=0, keepdims=True), axis=1, keepdims=True)

    pairs = [(masked, z_own), (z_own, y_own), (masked, m), (y_own, m), (z_own, x), (m, x), (land, land)]
    lane = lax.broadcasted_iota(jnp.int32, (1, LANE), 1)
    row = jnp.zeros((1, LANE), F32)
    for i, (a, b) in enumerate(pairs):
        row = jnp.where(lane == i, partial(a, b), row)
    sent[...] = jnp.broadcast_to(row[None], sent.shape)


def finish(came, z, w, d_rows, edge, source, u_vel, v_vel, solution, u_new, v_new, w_vel,
           s_rows, u_rows, v_out, w_out, s_out, sems):
    cells, lat = source.shape
    total = jnp.broadcast_to(jnp.sum(came[...], axis=0), (8, LANE))
    place = [lax.broadcasted_iota(jnp.int32, (8, LANE), axis) for axis in range(2)]
    total = jnp.sum(jnp.where(place[0] == place[1], total, 0.0), axis=1, keepdims=True)
    rz, zy, rw, yw, zx, wx, ll = [total[i : i + 1] for i in range(7)]
    step0 = (rz + ll) / (zy + ll)
    rest = (zy - rz) / (zy + ll)
    new = rz - step0 * (zy + rw) + step0 * step0 * yw + rest * rest * ll
    beta = new / (rz + ll)
    grown = 1.0 + beta
    bent = grown * grown * zy - grown * step0 * (zx + yw) + step0 * step0 * wx
    step1 = new / (bent + (rest + beta) * (rest + beta) * ll)
    of_z = jnp.broadcast_to(step0 + step1 * grown, (OV, lat))
    of_w = jnp.broadcast_to(-step1 * step0, (OV, lat))
    of_land = jnp.broadcast_to(step0 + step1 * (rest + beta), (OV, lat))

    for at in (0, OV + cells):
        s_rows[at : at + OV] = of_z * z[at : at + OV] + of_w * w[at : at + OV]

    def rows_at(start):
        return pl.ds(pl.multiple_of(start, OV), OV)

    def surface_rows(block, _):
        own, at = rows_at(block * OV), rows_at(block * OV + OV)
        s = of_z * z[at] + of_w * w[at]
        s = jnp.where(d_rows[at] > 0, s, of_land * source[own])
        s_out[own] = s
        s_rows[at] = s
        return 0

    lax.fori_loop(0, cells // OV, surface_rows, 0)
    send_s = pltpu.make_async_copy(s_out, solution, sems.at[0])
    send_s.start()
    slope = gravity_step * (s_rows[OV : OV + 1] - s_rows[OV - 1 : OV])
    d_west = jnp.minimum(d_rows[OV - 1 : OV], d_rows[OV : OV + 1])
    for level in range(KL):
        u = jnp.where(d_west > level, edge[level : level + 1] - slope, 0.0)
        u_rows[level, :OV] = jnp.broadcast_to(u, (OV, lat))
    zero = jnp.zeros((OV, 1), F32)
    last = lax.broadcasted_iota(jnp.int32, (OV, lat), 0) == OV - 1
    first = lax.broadcasted_iota(jnp.int32, (OV, lat), 0) == 0

    def sends(block):
        own, at = rows_at(block * OV), rows_at(block * OV + OV)
        pairs = [(u_rows.at[:, at], u_new), (v_out.at[:, own], v_new), (w_out.at[:, own], w_vel)]
        return [
            pltpu.make_async_copy(held, result.at[:, own], sems.at[1 + 3 * block + i])
            for i, (held, result) in enumerate(pairs)
        ]

    def next_row(rows, after):
        return jnp.where(last, after[:1], pltpu.roll(rows, OV - 1, 0))

    def faces(block, _):
        own, at = rows_at(block * OV), rows_at(block * OV + OV)
        before, after = rows_at(block * OV), rows_at(block * OV + 2 * OV)
        to_u, to_v, to_w = sends(block)
        s, d = s_rows[at], d_rows[at]
        slope_e = gravity_step * (next_row(s, s_rows[after]) - s)
        face_e = jnp.minimum(d, next_row(d, d_rows[after]))
        slope_n = gravity_step * (jnp.concatenate([s[:, 1:], zero], axis=1) - s)
        face_n = jnp.minimum(d, jnp.concatenate([d[:, 1:], zero], axis=1))
        w_sum = jnp.zeros((OV, lat), F32)
        for level in range(KL - 1, -1, -1):
            u = jnp.where(face_e > level, u_vel[level, own] - slope_e, 0.0)
            u_rows[level, at] = u
            v = jnp.where(face_n > level, v_vel[level, own] - slope_n, 0.0)
            v_out[level, own] = v
            west = jnp.where(first, u_rows[level, before][OV - 1 :], pltpu.roll(u, 1, 0))
            south = jnp.concatenate([zero, v[:, :-1]], axis=1)
            w_sum = w_sum + jnp.where(d > level, (u - west) + (v - south), 0.0)
            w_out[level, own] = w_sum
        for copy in (to_u, to_v, to_w):
            copy.start()
        return 0

    lax.fori_loop(0, cells // OV, faces, 0)
    send_s.wait()
    for block in range(cells // OV):
        for copy in sends(block):
            copy.wait()


def swap_pairs(block, outward):
    devices = lax.axis_size("lon")
    if outward:
        route = [(i, (i - 1 if i % 2 == 0 else i + 1) % devices) for i in range(devices)]
    else:
        route = [(i, i ^ 1) for i in range(devices)]
    return lax.ppermute(block, "lon", route)


def shape(*dims):
    return jax.ShapeDtypeStruct(dims, F32)


def body(source, diagonal, u_vel, v_vel, bottom):
    cells, lat = source.shape
    span = cells + 2 * OV
    devices = lax.axis_size("lon")
    parity = (lax.axis_index("lon") % 2).astype(jnp.int32).reshape(1)
    consts = [jnp.asarray(table) for table in tables(span)]
    hbm = {name: pltpu.with_memory_space_constraint(x, pltpu.HBM) for name, x in (
        ("source", source), ("diagonal", diagonal), ("u", u_vel), ("v", v_vel), ("bottom", bottom))}
    consts = [pltpu.with_memory_space_constraint(x, pltpu.HBM) for x in consts]

    outer = pl.pallas_call(
        first_edges,
        in_specs=[SM, HB, HB],
        out_specs=VM,
        out_shape=pltpu.VMEM((OV, lat), F32),
        scratch_shapes=[pltpu.VMEM((OV, lat), F32), pltpu.VMEM((OV, lat), jnp.int32),
                        pltpu.SemaphoreType.DMA((2,))],
        compiler_params=PARAMS,
        name="first_edges",
    )(parity, hbm["source"], hbm["bottom"])
    outer_in = swap_pairs(outer, True)

    inner, far_inner, far_outer, masked, coef, depth, source_v, *held = pl.pallas_call(
        prepare,
        in_specs=[SM] + [HB] * 8,
        out_specs=[VM] * 10,
        out_shape=[pltpu.VMEM((OV, lat), F32)]
        + [pltpu.VMEM((FAR, lat), F32)] * 2
        + [pltpu.VMEM((cells, lat), F32)] * 4
        + [pltpu.VMEM(table.shape, table.dtype) for table in consts],
        scratch_shapes=[
            pltpu.VMEM((cells, lat), F32),
            pltpu.VMEM((cells, lat), jnp.int32),
            pltpu.VMEM((KL, OV, lat), F32),
            pltpu.SemaphoreType.DMA((7,)),
        ],
        compiler_params=PARAMS,
        cost_estimate=pl.CostEstimate(flops=10**6, bytes_accessed=7 * 10**6, transcendentals=0),
        name="prepare",
    )(parity, outer, hbm["source"], hbm["diagonal"], hbm["bottom"], hbm["u"], *consts)
    near = swap_pairs(inner, False), outer_in
    far = swap_pairs(far_inner, False), swap_pairs(far_outer, True)

    blocks = -(-lat // LANE)
    first, inner, outer = pl.pallas_call(
        first_solve,
        in_specs=[SM] + [VM] * 6,
        out_specs=[VM] * 3,
        out_shape=[pltpu.VMEM((span, lat), F32)] + [pltpu.VMEM(((2 * OV + 1) * blocks, LANE), F32)] * 2,
        scratch_shapes=solve_scratch(span, lat),
        compiler_params=PARAMS,
        name="first_solve",
    )(parity, *near, masked, *held)
    near = swap_pairs(inner, False), swap_pairs(outer, True)

    c_rows, d_rows, edge, u_v, v_v = pl.pallas_call(
        absorb,
        in_specs=[SM, HB] + [VM] * 4 + [HB] * 2,
        out_specs=[VM] * 5,
        out_shape=[pltpu.VMEM((span + 2 * OV, lat), F32), pltpu.VMEM((span, lat), F32), pltpu.VMEM((OV, lat), F32)]
        + [pltpu.VMEM((KL, cells, lat), F32)] * 2,
        scratch_shapes=[pltpu.SemaphoreType.DMA((2,))],
        compiler_params=PARAMS,
        cost_estimate=pl.CostEstimate(flops=10**6, bytes_accessed=7 * 10**6, transcendentals=0),
        name="absorb",
    )(parity, first, *far, coef, depth, hbm["u"], hbm["v"])

    z, y, second, inner, outer = pl.pallas_call(
        second_solve,
        in_specs=[SM] + [VM] * 7,
        out_specs=[VM] * 5,
        out_shape=[pltpu.VMEM((span, lat), F32)] * 3 + [pltpu.VMEM(((OV + 1) * blocks, LANE), F32)] * 2,
        scratch_shapes=solve_scratch(span, lat) + [pltpu.VMEM((span + 2 * OV, lat), F32)],
        compiler_params=PARAMS,
        name="second_solve",
    )(parity, *near, first, c_rows, *held)
    near = swap_pairs(inner, False), swap_pairs(outer, True)

    w, sent = pl.pallas_call(
        sums,
        in_specs=[SM] + [VM] * 7,
        out_specs=[VM] * 2,
        out_shape=[pltpu.VMEM((span, lat), F32), pltpu.VMEM((devices, 1, LANE), F32)],
        compiler_params=PARAMS,
        name="sums",
    )(parity, *near, second, z, y, c_rows, source_v)
    came = lax.all_to_all(sent, "lon", 0, 0)

    return pl.pallas_call(
        finish,
        in_specs=[VM] * 8,
        out_specs=[HB] * 4,
        out_shape=[shape(cells, lat)] + [shape(KL, cells, lat)] * 3,
        scratch_shapes=[pltpu.VMEM((span, lat), F32)]
        + [pltpu.VMEM((KL, OV + cells, lat), F32)]
        + [pltpu.VMEM((KL, cells, lat), F32)] * 2
        + [pltpu.VMEM((cells, lat), F32), pltpu.SemaphoreType.DMA((1 + 3 * (cells // OV),))],
        compiler_params=PARAMS,
        name="finish",
    )(came, z, w, d_rows, edge, source_v, u_v, v_v)


def solution(mesh):
    return jax.shard_map(
        body,
        mesh=mesh,
        in_specs=(
            P(("members", "lon"), None),
            P(("members", "lon"), None),
            P(None, ("members", "lon"), None),
            P(None, ("members", "lon"), None),
            P(("members", "lon"), None),
        ),
        out_specs=(
            P(("members", "lon"), None),
            P(None, ("members", "lon"), None),
            P(None, ("members", "lon"), None),
            P(None, ("members", "lon"), None),
        ),
        check_vma=False,
    )
```

```python
import math

import jax
import jax.numpy as jnp
import ml_dtypes
import numpy as np
from jax import lax
from jax.experimental import pallas as pl
from jax.experimental.pallas import tpu as pltpu
from jax.sharding import PartitionSpec as P

LT = 112
OV = 8
KL = 6
LANE = 128
FAR = 24

tile_shift = 0.1
gravity_step = 0.5

F32 = jnp.float32
BF16 = jnp.bfloat16
VM = pl.BlockSpec(memory_space=pltpu.VMEM)
SM = pl.BlockSpec(memory_space=pltpu.SMEM)
HB = pl.BlockSpec(memory_space=pl.ANY)
PARAMS = pltpu.CompilerParams(vmem_limit_bytes=32 * 1024 * 1024)


def sine_basis(length):
    ordinal = np.arange(length, dtype=np.float64) + 1.0
    angles = math.pi * ordinal[:, None] * ordinal[None, :] / (length + 1)
    basis_matrix = np.sqrt(2.0 / (length + 1)) * np.sin(angles)
    eigen_value = 2.0 - 2.0 * np.cos(math.pi * ordinal / (length + 1))
    return basis_matrix, eigen_value


def halves(matrix):
    high = matrix.astype(ml_dtypes.bfloat16)
    low = (matrix - high.astype(np.float64)).astype(ml_dtypes.bfloat16)
    return high, low


def tables(span):
    lon_basis, lon_value = sine_basis(span)
    lat_basis, lat_value = sine_basis(LT + 2 * OV)
    high, low = halves(lat_basis)
    lat = np.block([[high, low], [high, np.zeros_like(low)]])
    high, low = halves(lon_basis)
    lon = np.concatenate([high, low, high], axis=1)
    scale = 1.0 / (lon_value[:, None] + lat_value[None, :] + tile_shift)
    return lat, lon, scale.astype(np.float32)


def split(x):
    high = x.astype(BF16)
    return high, (x - high.astype(F32)).astype(BF16)


def tile_solve(x, lat_basis, lon, scale, rows, spectral, out):
    span, lat = out.shape
    tiles = lat // LT
    lane = lax.broadcasted_iota(jnp.int32, (span, LANE), 1)

    def block_of(b):
        if b < 0:
            return jnp.zeros((span, LANE), F32)
        return x[:, b * LANE : (b + 1) * LANE]

    chunk = 4
    groups = [range(first, min(first + chunk, tiles)) for first in range(0, tiles, chunk)]
    held = {}

    def lanes_of(group):
        return slice(group[0] * LANE, (group[-1] + 1) * LANE)

    def cut(group):
        for t in group:
            block, start = divmod(t * LT - OV, LANE)
            left, right = [pltpu.roll(block_of(b), LANE - start, 1) for b in (block, block + 1)]
            high, low = split(jnp.where(lane < LANE - start, left, right))
            rows[t * span : (t + 1) * span, :LANE] = high
            rows[t * span : (t + 1) * span, LANE:] = low

    def along_lat(group):
        product = jnp.dot(
            rows[group[0] * span : (group[-1] + 1) * span], lat_basis[...], preferred_element_type=F32
        )
        return product[:, :LANE] + product[:, LANE:]

    def lat_there(group):
        high, low = split(along_lat(group))
        for i, t in enumerate(group):
            at = slice(t * LANE, (t + 1) * LANE)
            spectral[:span, at] = high[i * span : (i + 1) * span]
            spectral[span : 2 * span, at] = high[i * span : (i + 1) * span]
            spectral[2 * span :, at] = low[i * span : (i + 1) * span]

    def lon_there(group):
        c = jnp.dot(lon[...], spectral[:, lanes_of(group)], preferred_element_type=F32)
        high, low = split(c * jnp.concatenate([scale[...]] * len(group), axis=1))
        spectral[:, lanes_of(group)] = jnp.concatenate([high, high, low], axis=0)

    def lon_back(group):
        c = jnp.dot(lon[...], spectral[:, lanes_of(group)], preferred_element_type=F32)
        high, low = split(c)
        for i, t in enumerate(group):
            at = slice(t * span, (t + 1) * span)
            rows[at, :LANE] = high[:, i * LANE : (i + 1) * LANE]
            rows[at, LANE:] = low[:, i * LANE : (i + 1) * LANE]

    def lat_back(group):
        product = along_lat(group)
        for i, t in enumerate(group):
            block, start = divmod(t * LT - OV, LANE)
            part = pltpu.roll(product[i * span : (i + 1) * span], start, 1)
            for b, inside in ((block, lane >= start), (block + 1, lane < start)):
                if 0 <= b * LANE < lat:
                    piece = jnp.where(inside, part, 0.0)
                    held[b] = held[b] + piece if b in held else piece
        done = (group[-1] + 1) * LT - OV if group[-1] + 1 < tiles else lat + LANE
        for b in [b for b in held if (b + 1) * LANE <= done]:
            width = min(LANE, lat - b * LANE)
            out[:, b * LANE : b * LANE + width] = held.pop(b)[:, :width]

    stages = [cut, lat_there, lon_there, lon_back, lat_back]
    for step in range(len(groups) + len(stages) - 1):
        for i in reversed(range(len(stages))):
            if 0 <= step - i < len(groups):
                stages[i](groups[step - i])


def wide_lanes(lat):
    return -(-(lat + OV) // LANE) * LANE


def solve_scratch(span, lat):
    tiles = lat // LT
    return [
        pltpu.VMEM((span, wide_lanes(lat)), F32),
        pltpu.VMEM((tiles * span, 2 * LANE), BF16),
        pltpu.VMEM((3 * span, tiles * LANE), BF16),
    ]


def pick(parity, inner, outer):
    even = jnp.full(inner.shape, parity[0], jnp.int32) == 0
    return jnp.where(even, outer, inner), jnp.where(even, inner, outer)


def lat_beside(m):
    zero = jnp.zeros((m.shape[0], 1), m.dtype)
    return jnp.concatenate([m[:, 1:], zero], axis=1) + jnp.concatenate([zero, m[:, :-1]], axis=1)


def pack(message, rows):
    n, lat = rows.shape
    for block, at in enumerate(range(0, lat, LANE)):
        width = min(LANE, lat - at)
        message[block * n : (block + 1) * n, :width] = rows[:, at : at + width]


def unpack(message, n, lat):
    blocks = [message[i * n : (i + 1) * n] for i in range(-(-lat // LANE))]
    return jnp.concatenate(blocks, axis=1)[:, :lat]


def first_edges(parity, source, bottom, outer, rows, depth, sems):
    start = pl.multiple_of(parity[0] * (source.shape[0] - OV), OV)
    at = pl.ds(start, OV)
    copies = [
        pltpu.make_async_copy(source.at[at], rows, sems.at[0]),
        pltpu.make_async_copy(bottom.at[at], depth, sems.at[1]),
    ]
    for copy in copies:
        copy.start()
    for copy in copies:
        copy.wait()
    outer[...] = jnp.where(depth[...] > 0, rows[...], 0.0)


def prepare(parity, after, source_h, diagonal_h, bottom_h, u_h, *refs):
    tables_h, (inner, far_inner, far_outer, masked, coef, depth, source), held = refs[:3], refs[3:10], refs[10:13]
    diagonal, bottom, u_strip, sems = refs[13:]
    cells, lat = source.shape
    pairs = [(source_h, source), (bottom_h, bottom), (diagonal_h, diagonal)]
    pairs += [(u_h.at[:, pl.ds(cells - OV, OV)], u_strip)]
    pairs += list(zip(tables_h, held))
    copies = [pltpu.make_async_copy(a, b, sems.at[i]) for i, (a, b) in enumerate(pairs)]
    for copy in copies:
        copy.start()
    for copy in copies[:4]:
        copy.wait()
    wet = bottom[...] > 0
    masked[...] = jnp.where(wet, source[...], 0.0)
    coef[...] = jnp.where(wet, 4.0 + diagonal[...], 0.0)
    depth[...] = bottom[...].astype(F32)
    edge = OV + 1
    blank = jnp.zeros((2 * OV - edge - 1, lat), F32)
    to_west = jnp.concatenate([coef[:edge], blank, depth[:1]], axis=0)
    u_rows = [u_strip[level, OV - 1 : OV] for level in range(KL)]
    to_east = jnp.concatenate(u_rows + [depth[cells - 1 :], coef[cells - edge :]], axis=0)
    far_outer[: 2 * OV], far_inner[: 2 * OV] = pick(parity, to_east, to_west)
    for message in (far_outer, far_inner):
        message[2 * OV :] = jnp.zeros((FAR - 2 * OV, lat), F32)
    inner[...] = pick(parity, masked[:OV], masked[cells - OV :])[0]
    for copy in copies[4:]:
        copy.wait()


def first_solve(parity, inner_in, outer_in, masked, lat_basis, lon, scale,
                first, inner, outer, wide, rows, spectral):
    cells, lat = masked.shape
    west, east = pick(parity, inner_in[...], outer_in[...])
    wide[:OV, :lat] = west
    wide[OV : OV + cells, :lat] = masked[...]
    wide[OV + cells :, :lat] = east
    wide[:, lat:] = jnp.zeros((cells + 2 * OV, wide.shape[1] - lat), F32)
    tile_solve(wide, lat_basis, lon, scale, rows, spectral, first)
    to_outer, to_inner = pick(parity, first[cells - 1 :], first[: 2 * OV + 1])
    pack(inner, to_inner)
    pack(outer, to_outer)


def absorb(parity, after, inner_in, outer_in, coef, depth, u_h, v_h, c_rows, d_rows, edge, u, v, sems):
    cells, lat = coef.shape
    copies = [pltpu.make_async_copy(a, b, sems.at[i]) for i, (a, b) in enumerate([(u_h, u), (v_h, v)])]
    for copy in copies:
        copy.start()
    west, east = pick(parity, inner_in[: 2 * OV], outer_in[: 2 * OV])
    edge[...] = west[:OV]
    d_rows[:OV] = jnp.broadcast_to(west[KL : KL + 1], (OV, lat))
    d_rows[OV : OV + cells] = depth[...]
    d_rows[OV + cells :] = jnp.broadcast_to(east[2 * OV - 1 :], (OV, lat))
    c_rows[: 2 * OV] = west
    c_rows[: OV - 1] = jnp.zeros((OV - 1, lat), F32)
    c_rows[2 * OV : 2 * OV + cells] = coef[...]
    c_rows[2 * OV + cells :] = east
    c_rows[3 * OV + cells + 1 :] = jnp.zeros((OV - 1, lat), F32)
    for copy in copies:
        copy.wait()


def second_solve(parity, inner_in, outer_in, first, c_rows, lat_basis, lon, scale,
                 z, y, second, inner, outer, wide, rows, spectral, m_rows):
    span, lat = first.shape
    cells = span - 2 * OV
    reach = 2 * OV + 1
    west, east = pick(parity, unpack(inner_in, reach, lat), unpack(outer_in, reach, lat))
    m_rows[:OV] = jnp.zeros((OV, lat), F32)
    m_rows[OV : OV + span] = first[...]
    m_rows[OV + span :] = jnp.zeros((OV, lat), F32)
    m_rows[OV - 1 : OV - 1 + reach] += west
    m_rows[OV + cells : OV + cells + reach] += east
    m_rows[...] = jnp.where(c_rows[...] > 0, m_rows[...], 0.0)
    inside = slice(OV, OV + span)
    c, m = c_rows[inside], m_rows[inside]
    z[...] = m
    beside = m_rows[OV - 1 : OV - 1 + span] + m_rows[OV + 1 : OV + 1 + span]
    image = jnp.where(c > 0, c * m - (beside + lat_beside(m)), 0.0)
    y[...] = image
    wide[:, :lat] = image
    wide[:, lat:] = jnp.zeros((span, wide.shape[1] - lat), F32)
    tile_solve(wide, lat_basis, lon, scale, rows, spectral, second)
    to_outer, to_inner = pick(parity, second[span - OV - 1 :], second[: OV + 1])
    pack(inner, to_inner)
    pack(outer, to_outer)


def sums(parity, inner_in, outer_in, second, z, y, c_rows, source, w, sent):
    cells, lat = source.shape
    west, east = pick(parity, unpack(inner_in, OV + 1, lat), unpack(outer_in, OV + 1, lat))
    w[...] = second[...]
    w[OV - 1 : 2 * OV] += west
    w[cells : cells + OV + 1] += east
    w[...] = jnp.where(c_rows[OV : 3 * OV + cells] > 0, w[...], 0.0)
    own = slice(OV, OV + cells)
    c, m = c_rows[2 * OV : 2 * OV + cells], w[own]
    wet = c > 0
    beside = w[OV - 1 : OV - 1 + cells] + w[OV + 1 : OV + 1 + cells]
    x = jnp.where(wet, c * m - (beside + lat_beside(m)), 0.0)
    masked = jnp.where(wet, source[...], 0.0)
    land = jnp.where(wet, 0.0, source[...])
    z_own, y_own = z[own], y[own]

    def partial(a, b):
        product = a * b
        rows = product[:OV]
        for at in range(OV, cells, OV):
            rows = rows + product[at : at + OV]
        whole = lat // LANE * LANE
        total = rows[:, :LANE]
        for at in range(LANE, whole, LANE):
            total = total + rows[:, at : at + LANE]
        if whole < lat:
            blank = jnp.zeros((OV, LANE - lat + whole), F32)
            total = total + jnp.concatenate([rows[:, whole:], blank], axis=1)
        return jnp.sum(jnp.sum(total, axis=0, keepdims=True), axis=1, keepdims=True)

    pairs = [(masked, z_own), (z_own, y_own), (masked, m), (y_own, m), (z_own, x), (m, x), (land, land)]
    lane = lax.broadcasted_iota(jnp.int32, (1, LANE), 1)
    row = jnp.zeros((1, LANE), F32)
    for i, (a, b) in enumerate(pairs):
        row = jnp.where(lane == i, partial(a, b), row)
    sent[...] = jnp.broadcast_to(row[None], sent.shape)


def finish(came, z, w, d_rows, edge, source, u_vel, v_vel, solution, u_new, v_new, w_vel,
           s_rows, u_rows, v_out, w_out, s_out, sems):
    cells, lat = source.shape
    total = jnp.broadcast_to(jnp.sum(came[...], axis=0), (8, LANE))
    place = [lax.broadcasted_iota(jnp.int32, (8, LANE), axis) for axis in range(2)]
    total = jnp.sum(jnp.where(place[0] == place[1], total, 0.0), axis=1, keepdims=True)
    rz, zy, rw, yw, zx, wx, ll = [total[i : i + 1] for i in range(7)]
    step0 = (rz + ll) / (zy + ll)
    rest = (zy - rz) / (zy + ll)
    new = rz - step0 * (zy + rw) + step0 * step0 * yw + rest * rest * ll
    beta = new / (rz + ll)
    grown = 1.0 + beta
    bent = grown * grown * zy - grown * step0 * (zx + yw) + step0 * step0 * wx
    step1 = new / (bent + (rest + beta) * (rest + beta) * ll)
    of_z = jnp.broadcast_to(step0 + step1 * grown, (OV, lat))
    of_w = jnp.broadcast_to(-step1 * step0, (OV, lat))
    of_land = jnp.broadcast_to(step0 + step1 * (rest + beta), (OV, lat))

    copies = []

    def send(held, result):
        copies.append(pltpu.make_async_copy(held, result, sems.at[len(copies)]))
        copies[-1].start()

    def surface_rows(at):
        s = of_z * z[at : at + OV] + of_w * w[at : at + OV]
        if OV <= at < OV + cells:
            s = jnp.where(d_rows[at : at + OV] > 0, s, of_land * source[at - OV : at])
            s_out[at - OV : at] = s
        s_rows[at : at + OV] = s

    surface_rows(0)
    surface_rows(OV)
    slope = gravity_step * (s_rows[OV : OV + 1] - s_rows[OV - 1 : OV])
    d_west = jnp.minimum(d_rows[OV - 1 : OV], d_rows[OV : OV + 1])
    for level in range(KL):
        u = jnp.where(d_west > level, edge[level : level + 1] - slope, 0.0)
        u_rows[level, :OV] = jnp.broadcast_to(u, (OV, lat))
    zero = jnp.zeros((OV, 1), F32)
    for at in range(OV, OV + cells, OV):
        own = slice(at - OV, at)
        surface_rows(at + OV)
        s = s_rows[at : at + OV]
        d = d_rows[at : at + OV]
        slope = gravity_step * (s_rows[at + 1 : at + OV + 1] - s)
        face = jnp.minimum(d, d_rows[at + 1 : at + OV + 1])
        for level in range(KL):
            u_rows[level, at : at + OV] = jnp.where(face > level, u_vel[level, own] - slope, 0.0)
        send(u_rows.at[:, at : at + OV], u_new.at[:, own])
        slope = gravity_step * (jnp.concatenate([s[:, 1:], zero], axis=1) - s)
        face = jnp.minimum(d, jnp.concatenate([d[:, 1:], zero], axis=1))
        for level in range(KL):
            v_out[level, own] = jnp.where(face > level, v_vel[level, own] - slope, 0.0)
        send(v_out.at[:, own], v_new.at[:, own])
        w_sum = jnp.zeros((OV, lat), F32)
        for level in range(KL - 1, -1, -1):
            v = v_out[level, own]
            flow = u_rows[level, at : at + OV] - u_rows[level, at - 1 : at + OV - 1]
            flow = flow + (v - jnp.concatenate([zero, v[:, :-1]], axis=1))
            w_sum = w_sum + jnp.where(d > level, flow, 0.0)
            w_out[level, own] = w_sum
        send(w_out.at[:, own], w_vel.at[:, own])
        if at == cells:
            send(s_out, solution)
    for copy in copies:
        copy.wait()


def swap_pairs(block, outward):
    devices = lax.axis_size("lon")
    if outward:
        route = [(i, (i - 1 if i % 2 == 0 else i + 1) % devices) for i in range(devices)]
    else:
        route = [(i, i ^ 1) for i in range(devices)]
    return lax.ppermute(block, "lon", route)


def shape(*dims):
    return jax.ShapeDtypeStruct(dims, F32)


def body(source, diagonal, u_vel, v_vel, bottom):
    cells, lat = source.shape
    span = cells + 2 * OV
    devices = lax.axis_size("lon")
    parity = (lax.axis_index("lon") % 2).astype(jnp.int32).reshape(1)
    consts = [jnp.asarray(table) for table in tables(span)]
    hbm = {name: pltpu.with_memory_space_constraint(x, pltpu.HBM) for name, x in (
        ("source", source), ("diagonal", diagonal), ("u", u_vel), ("v", v_vel), ("bottom", bottom))}
    consts = [pltpu.with_memory_space_constraint(x, pltpu.HBM) for x in consts]

    outer = pl.pallas_call(
        first_edges,
        in_specs=[SM, HB, HB],
        out_specs=VM,
        out_shape=pltpu.VMEM((OV, lat), F32),
        scratch_shapes=[pltpu.VMEM((OV, lat), F32), pltpu.VMEM((OV, lat), jnp.int32),
                        pltpu.SemaphoreType.DMA((2,))],
        compiler_params=PARAMS,
        name="first_edges",
    )(parity, hbm["source"], hbm["bottom"])
    outer_in = swap_pairs(outer, True)

    inner, far_inner, far_outer, masked, coef, depth, source_v, *held = pl.pallas_call(
        prepare,
        in_specs=[SM] + [HB] * 8,
        out_specs=[VM] * 10,
        out_shape=[pltpu.VMEM((OV, lat), F32)]
        + [pltpu.VMEM((FAR, lat), F32)] * 2
        + [pltpu.VMEM((cells, lat), F32)] * 4
        + [pltpu.VMEM(table.shape, table.dtype) for table in consts],
        scratch_shapes=[
            pltpu.VMEM((cells, lat), F32),
            pltpu.VMEM((cells, lat), jnp.int32),
            pltpu.VMEM((KL, OV, lat), F32),
            pltpu.SemaphoreType.DMA((7,)),
        ],
        compiler_params=PARAMS,
        cost_estimate=pl.CostEstimate(flops=10**6, bytes_accessed=7 * 10**6, transcendentals=0),
        name="prepare",
    )(parity, outer, hbm["source"], hbm["diagonal"], hbm["bottom"], hbm["u"], *consts)
    near = swap_pairs(inner, False), outer_in
    far = swap_pairs(far_inner, False), swap_pairs(far_outer, True)

    blocks = -(-lat // LANE)
    first, inner, outer = pl.pallas_call(
        first_solve,
        in_specs=[SM] + [VM] * 6,
        out_specs=[VM] * 3,
        out_shape=[pltpu.VMEM((span, lat), F32)] + [pltpu.VMEM(((2 * OV + 1) * blocks, LANE), F32)] * 2,
        scratch_shapes=solve_scratch(span, lat),
        compiler_params=PARAMS,
        name="first_solve",
    )(parity, *near, masked, *held)
    near = swap_pairs(inner, False), swap_pairs(outer, True)

    c_rows, d_rows, edge, u_v, v_v = pl.pallas_call(
        absorb,
        in_specs=[SM, HB] + [VM] * 4 + [HB] * 2,
        out_specs=[VM] * 5,
        out_shape=[pltpu.VMEM((span + 2 * OV, lat), F32), pltpu.VMEM((span, lat), F32), pltpu.VMEM((OV, lat), F32)]
        + [pltpu.VMEM((KL, cells, lat), F32)] * 2,
        scratch_shapes=[pltpu.SemaphoreType.DMA((2,))],
        compiler_params=PARAMS,
        cost_estimate=pl.CostEstimate(flops=10**6, bytes_accessed=7 * 10**6, transcendentals=0),
        name="absorb",
    )(parity, first, *far, coef, depth, hbm["u"], hbm["v"])

    z, y, second, inner, outer = pl.pallas_call(
        second_solve,
        in_specs=[SM] + [VM] * 7,
        out_specs=[VM] * 5,
        out_shape=[pltpu.VMEM((span, lat), F32)] * 3 + [pltpu.VMEM(((OV + 1) * blocks, LANE), F32)] * 2,
        scratch_shapes=solve_scratch(span, lat) + [pltpu.VMEM((span + 2 * OV, lat), F32)],
        compiler_params=PARAMS,
        name="second_solve",
    )(parity, *near, first, c_rows, *held)
    near = swap_pairs(inner, False), swap_pairs(outer, True)

    w, sent = pl.pallas_call(
        sums,
        in_specs=[SM] + [VM] * 7,
        out_specs=[VM] * 2,
        out_shape=[pltpu.VMEM((span, lat), F32), pltpu.VMEM((devices, 1, LANE), F32)],
        compiler_params=PARAMS,
        name="sums",
    )(parity, *near, second, z, y, c_rows, source_v)
    ring = [list(reversed(range(devices)))]
    came = lax.all_to_all(sent, "lon", 0, 0, axis_index_groups=ring)

    return pl.pallas_call(
        finish,
        in_specs=[VM] * 8,
        out_specs=[HB] * 4,
        out_shape=[shape(cells, lat)] + [shape(KL, cells, lat)] * 3,
        scratch_shapes=[pltpu.VMEM((span, lat), F32)]
        + [pltpu.VMEM((KL, OV + cells, lat), F32)]
        + [pltpu.VMEM((KL, cells, lat), F32)] * 2
        + [pltpu.VMEM((cells, lat), F32), pltpu.SemaphoreType.DMA((1 + 3 * (cells // OV),))],
        compiler_params=PARAMS,
        name="finish",
    )(came, z, w, d_rows, edge, source_v, u_v, v_v)


def solution(mesh):
    return jax.shard_map(
        body,
        mesh=mesh,
        in_specs=(
            P(("members", "lon"), None),
            P(("members", "lon"), None),
            P(None, ("members", "lon"), None),
            P(None, ("members", "lon"), None),
            P(("members", "lon"), None),
        ),
        out_specs=(
            P(("members", "lon"), None),
            P(None, ("members", "lon"), None),
            P(None, ("members", "lon"), None),
            P(None, ("members", "lon"), None),
        ),
        check_vma=False,
    )
```

```python
import math

import jax
import jax.numpy as jnp
import ml_dtypes
import numpy as np
from jax import lax
from jax.experimental import pallas as pl
from jax.experimental.pallas import tpu as pltpu
from jax.sharding import PartitionSpec as P

LT = 112
OV = 8
KL = 6
LANE = 128
FAR = 24

tile_shift = 0.1
gravity_step = 0.5

F32 = jnp.float32
BF16 = jnp.bfloat16
VM = pl.BlockSpec(memory_space=pltpu.VMEM)
SM = pl.BlockSpec(memory_space=pltpu.SMEM)
HB = pl.BlockSpec(memory_space=pl.ANY)
PARAMS = pltpu.CompilerParams(vmem_limit_bytes=32 * 1024 * 1024)


def sine_basis(length):
    ordinal = np.arange(length, dtype=np.float64) + 1.0
    angles = math.pi * ordinal[:, None] * ordinal[None, :] / (length + 1)
    basis_matrix = np.sqrt(2.0 / (length + 1)) * np.sin(angles)
    eigen_value = 2.0 - 2.0 * np.cos(math.pi * ordinal / (length + 1))
    return basis_matrix, eigen_value


def halves(matrix):
    high = matrix.astype(ml_dtypes.bfloat16)
    low = (matrix - high.astype(np.float64)).astype(ml_dtypes.bfloat16)
    return high, low


def tables(span):
    lon_basis, lon_value = sine_basis(span)
    lat_basis, lat_value = sine_basis(LT + 2 * OV)
    high, low = halves(lat_basis)
    lat = np.block([[high, low], [high, np.zeros_like(low)]])
    high, low = halves(lon_basis)
    lon = np.concatenate([high, low, high], axis=1)
    scale = 1.0 / (lon_value[:, None] + lat_value[None, :] + tile_shift)
    return lat, lon, scale.astype(np.float32)


def split(x):
    high = x.astype(BF16)
    return high, (x - high.astype(F32)).astype(BF16)


def tile_solve(x, lat_basis, lon, scale, rows, spectral, out):
    span, lat = out.shape
    tiles = lat // LT
    lane = lax.broadcasted_iota(jnp.int32, (span, LANE), 1)

    def block_of(b):
        if b < 0:
            return jnp.zeros((span, LANE), F32)
        return x[:, b * LANE : (b + 1) * LANE]

    chunk = 4
    groups = [range(first, min(first + chunk, tiles)) for first in range(0, tiles, chunk)]
    held = {}

    def lanes_of(group):
        return slice(group[0] * LANE, (group[-1] + 1) * LANE)

    def cut(group):
        for t in group:
            block, start = divmod(t * LT - OV, LANE)
            left, right = [pltpu.roll(block_of(b), LANE - start, 1) for b in (block, block + 1)]
            high, low = split(jnp.where(lane < LANE - start, left, right))
            rows[t * span : (t + 1) * span, :LANE] = high
            rows[t * span : (t + 1) * span, LANE:] = low

    def along_lat(group):
        product = jnp.dot(
            rows[group[0] * span : (group[-1] + 1) * span], lat_basis[...], preferred_element_type=F32
        )
        return product[:, :LANE] + product[:, LANE:]

    def lat_there(group):
        high, low = split(along_lat(group))
        for i, t in enumerate(group):
            at = slice(t * LANE, (t + 1) * LANE)
            spectral[:span, at] = high[i * span : (i + 1) * span]
            spectral[span : 2 * span, at] = high[i * span : (i + 1) * span]
            spectral[2 * span :, at] = low[i * span : (i + 1) * span]

    def lon_there(group):
        c = jnp.dot(lon[...], spectral[:, lanes_of(group)], preferred_element_type=F32)
        high, low = split(c * jnp.concatenate([scale[...]] * len(group), axis=1))
        spectral[:, lanes_of(group)] = jnp.concatenate([high, high, low], axis=0)

    def lon_back(group):
        c = jnp.dot(lon[...], spectral[:, lanes_of(group)], preferred_element_type=F32)
        high, low = split(c)
        for i, t in enumerate(group):
            at = slice(t * span, (t + 1) * span)
            rows[at, :LANE] = high[:, i * LANE : (i + 1) * LANE]
            rows[at, LANE:] = low[:, i * LANE : (i + 1) * LANE]

    def lat_back(group):
        product = along_lat(group)
        for i, t in enumerate(group):
            block, start = divmod(t * LT - OV, LANE)
            part = pltpu.roll(product[i * span : (i + 1) * span], start, 1)
            for b, inside in ((block, lane >= start), (block + 1, lane < start)):
                if 0 <= b * LANE < lat:
                    piece = jnp.where(inside, part, 0.0)
                    held[b] = held[b] + piece if b in held else piece
        done = (group[-1] + 1) * LT - OV if group[-1] + 1 < tiles else lat + LANE
        for b in [b for b in held if (b + 1) * LANE <= done]:
            width = min(LANE, lat - b * LANE)
            out[:, b * LANE : b * LANE + width] = held.pop(b)[:, :width]

    stages = [cut, lat_there, lon_there, lon_back, lat_back]
    for step in range(len(groups) + len(stages) - 1):
        for i in reversed(range(len(stages))):
            if 0 <= step - i < len(groups):
                stages[i](groups[step - i])


def wide_lanes(lat):
    return -(-(lat + OV) // LANE) * LANE


def solve_scratch(span, lat):
    tiles = lat // LT
    return [
        pltpu.VMEM((span, wide_lanes(lat)), F32),
        pltpu.VMEM((tiles * span, 2 * LANE), BF16),
        pltpu.VMEM((3 * span, tiles * LANE), BF16),
    ]


def pick(parity, inner, outer):
    even = jnp.full(inner.shape, parity[0], jnp.int32) == 0
    return jnp.where(even, outer, inner), jnp.where(even, inner, outer)


def lat_beside(m):
    zero = jnp.zeros((m.shape[0], 1), m.dtype)
    return jnp.concatenate([m[:, 1:], zero], axis=1) + jnp.concatenate([zero, m[:, :-1]], axis=1)


def pack(message, rows):
    n, lat = rows.shape
    for block, at in enumerate(range(0, lat, LANE)):
        width = min(LANE, lat - at)
        message[block * n : (block + 1) * n, :width] = rows[:, at : at + width]


def unpack(message, n, lat):
    blocks = [message[i * n : (i + 1) * n] for i in range(-(-lat // LANE))]
    return jnp.concatenate(blocks, axis=1)[:, :lat]


def first_edges(parity, source, bottom, outer, rows, depth, sems):
    start = pl.multiple_of(parity[0] * (source.shape[0] - OV), OV)
    at = pl.ds(start, OV)
    copies = [
        pltpu.make_async_copy(source.at[at], rows, sems.at[0]),
        pltpu.make_async_copy(bottom.at[at], depth, sems.at[1]),
    ]
    for copy in copies:
        copy.start()
    for copy in copies:
        copy.wait()
    outer[...] = jnp.where(depth[...] > 0, rows[...], 0.0)


def prepare(parity, after, source_h, diagonal_h, bottom_h, u_h, *refs):
    tables_h, (inner, far_inner, far_outer, masked, coef, depth, source), held = refs[:3], refs[3:10], refs[10:13]
    diagonal, bottom, u_strip, sems = refs[13:]
    cells, lat = source.shape
    pairs = [(source_h, source), (bottom_h, bottom), (diagonal_h, diagonal)]
    pairs += [(u_h.at[:, pl.ds(cells - OV, OV)], u_strip)]
    pairs += list(zip(tables_h, held))
    copies = [pltpu.make_async_copy(a, b, sems.at[i]) for i, (a, b) in enumerate(pairs)]
    for copy in copies:
        copy.start()
    for copy in copies[:4]:
        copy.wait()
    wet = bottom[...] > 0
    masked[...] = jnp.where(wet, source[...], 0.0)
    coef[...] = jnp.where(wet, 4.0 + diagonal[...], 0.0)
    depth[...] = bottom[...].astype(F32)
    edge = OV + 1
    blank = jnp.zeros((2 * OV - edge - 1, lat), F32)
    to_west = jnp.concatenate([coef[:edge], blank, depth[:1]], axis=0)
    u_rows = [u_strip[level, OV - 1 : OV] for level in range(KL)]
    to_east = jnp.concatenate(u_rows + [depth[cells - 1 :], coef[cells - edge :]], axis=0)
    far_outer[: 2 * OV], far_inner[: 2 * OV] = pick(parity, to_east, to_west)
    for message in (far_outer, far_inner):
        message[2 * OV :] = jnp.zeros((FAR - 2 * OV, lat), F32)
    inner[...] = pick(parity, masked[:OV], masked[cells - OV :])[0]
    for copy in copies[4:]:
        copy.wait()


def first_solve(parity, inner_in, outer_in, masked, lat_basis, lon, scale,
                first, inner, outer, wide, rows, spectral):
    cells, lat = masked.shape
    west, east = pick(parity, inner_in[...], outer_in[...])
    wide[:OV, :lat] = west
    wide[OV : OV + cells, :lat] = masked[...]
    wide[OV + cells :, :lat] = east
    wide[:, lat:] = jnp.zeros((cells + 2 * OV, wide.shape[1] - lat), F32)
    tile_solve(wide, lat_basis, lon, scale, rows, spectral, first)
    to_outer, to_inner = pick(parity, first[cells - 1 :], first[: 2 * OV + 1])
    pack(inner, to_inner)
    pack(outer, to_outer)


def absorb(parity, first, inner_in, outer_in, coef, depth, u_h, v_h, c_rows, z_rows, d_rows, edge, u, v, sems):
    cells, lat = coef.shape
    copies = [pltpu.make_async_copy(a, b, sems.at[i]) for i, (a, b) in enumerate([(u_h, u), (v_h, v)])]
    for copy in copies:
        copy.start()
    west, east = pick(parity, inner_in[: 2 * OV], outer_in[: 2 * OV])
    edge[...] = west[:OV]
    d_rows[:OV] = jnp.broadcast_to(west[KL : KL + 1], (OV, lat))
    d_rows[OV : OV + cells] = depth[...]
    d_rows[OV + cells :] = jnp.broadcast_to(east[2 * OV - 1 :], (OV, lat))
    c_rows[: 2 * OV] = west
    c_rows[: OV - 1] = jnp.zeros((OV - 1, lat), F32)
    c_rows[2 * OV : 2 * OV + cells] = coef[...]
    c_rows[2 * OV + cells :] = east
    c_rows[3 * OV + cells + 1 :] = jnp.zeros((OV - 1, lat), F32)
    z_rows[:OV] = jnp.zeros((OV, lat), F32)
    z_rows[3 * OV + cells :] = jnp.zeros((OV, lat), F32)
    inside = slice(OV, 3 * OV + cells)
    z_rows[inside] = jnp.where(c_rows[inside] > 0, first[...], 0.0)
    for copy in copies:
        copy.wait()


def second_solve(parity, outer_in, inner_in, z_rows, c_rows, lat_basis, lon, scale,
                 z, y, second, inner, outer, wide, rows, spectral):
    span, lat = y.shape
    cells = span - 2 * OV
    reach = 2 * OV + 1
    west, east = pick(parity, unpack(inner_in, reach, lat), unpack(outer_in, reach, lat))
    z[...] = z_rows[...]
    for came, start in ((west, OV - 1), (east, OV + cells)):
        at = slice(start, start + reach)
        z[at] += jnp.where(c_rows[at] > 0, came, 0.0)
    inside = slice(OV, OV + span)
    c, m = c_rows[inside], z[inside]
    beside = z[OV - 1 : OV - 1 + span] + z[OV + 1 : OV + 1 + span]
    image = jnp.where(c > 0, c * m - (beside + lat_beside(m)), 0.0)
    y[...] = image
    wide[:, :lat] = image
    wide[:, lat:] = jnp.zeros((span, wide.shape[1] - lat), F32)
    tile_solve(wide, lat_basis, lon, scale, rows, spectral, second)
    to_outer, to_inner = pick(parity, second[span - OV - 1 :], second[: OV + 1])
    pack(inner, to_inner)
    pack(outer, to_outer)


def dot(a, b):
    cells, lat = a.shape
    product = a * b
    rows = product[:OV]
    for at in range(OV, cells, OV):
        rows = rows + product[at : at + OV]
    whole = lat // LANE * LANE
    total = rows[:, :LANE]
    for at in range(LANE, whole, LANE):
        total = total + rows[:, at : at + LANE]
    if whole < lat:
        blank = jnp.zeros((OV, LANE - lat + whole), F32)
        total = total + jnp.concatenate([rows[:, whole:], blank], axis=1)
    return jnp.sum(jnp.sum(total, axis=0, keepdims=True), axis=1, keepdims=True)


def in_lanes(row, sums):
    lane = lax.broadcasted_iota(jnp.int32, row.shape, 1)
    for i, value in sums.items():
        row = jnp.where(lane == i, value, row)
    return row


def early_sums(z, y, c_rows, second, source, w_rows, masked, row):
    cells, lat = source.shape
    inside = slice(OV, 3 * OV + cells)
    w_rows[...] = jnp.where(c_rows[inside] > 0, second[...], 0.0)
    own = slice(2 * OV, 2 * OV + cells)
    wet = c_rows[own] > 0
    masked[...] = jnp.where(wet, source[...], 0.0)
    land = jnp.where(wet, 0.0, source[...])
    z_own = z[own]
    sums_of = {0: dot(masked[...], z_own), 1: dot(z_own, y[OV : OV + cells]), 6: dot(land, land)}
    row[...] = in_lanes(jnp.zeros((1, LANE), F32), sums_of)


def sums(parity, outer_in, inner_in, w_rows, z, y, c_rows, masked, row, w, sent):
    cells, lat = masked.shape
    west, east = pick(parity, unpack(inner_in, OV + 1, lat), unpack(outer_in, OV + 1, lat))
    w[...] = w_rows[...]
    for came, start in ((west, OV - 1), (east, cells)):
        wet = c_rows[OV + start : 2 * OV + start + 1] > 0
        w[start : start + OV + 1] += jnp.where(wet, came, 0.0)
    own = slice(OV, OV + cells)
    c, m = c_rows[2 * OV : 2 * OV + cells], w[own]
    beside = w[OV - 1 : OV - 1 + cells] + w[OV + 1 : OV + 1 + cells]
    x = jnp.where(c > 0, c * m - (beside + lat_beside(m)), 0.0)
    sums_of = {2: dot(masked[...], m), 3: dot(y[own], m), 4: dot(z[2 * OV : 2 * OV + cells], x), 5: dot(m, x)}
    sent[...] = jnp.broadcast_to(in_lanes(row[...], sums_of)[None], sent.shape)


def finish(came, z, w, d_rows, edge, source, u_vel, v_vel, solution, u_new, v_new, w_vel,
           s_rows, u_rows, v_out, w_out, s_out, sems):
    cells, lat = source.shape
    total = jnp.broadcast_to(jnp.sum(came[...], axis=0), (8, LANE))
    place = [lax.broadcasted_iota(jnp.int32, (8, LANE), axis) for axis in range(2)]
    total = jnp.sum(jnp.where(place[0] == place[1], total, 0.0), axis=1, keepdims=True)
    rz, zy, rw, yw, zx, wx, ll = [total[i : i + 1] for i in range(7)]
    step0 = (rz + ll) / (zy + ll)
    rest = (zy - rz) / (zy + ll)
    new = rz - step0 * (zy + rw) + step0 * step0 * yw + rest * rest * ll
    beta = new / (rz + ll)
    grown = 1.0 + beta
    bent = grown * grown * zy - grown * step0 * (zx + yw) + step0 * step0 * wx
    step1 = new / (bent + (rest + beta) * (rest + beta) * ll)
    of_z = jnp.broadcast_to(step0 + step1 * grown, (OV, lat))
    of_w = jnp.broadcast_to(-step1 * step0, (OV, lat))
    of_land = jnp.broadcast_to(step0 + step1 * (rest + beta), (OV, lat))

    copies = []

    def send(held, result):
        copies.append(pltpu.make_async_copy(held, result, sems.at[len(copies)]))
        copies[-1].start()

    def surface_rows(at):
        s = of_z * z[at + OV : at + 2 * OV] + of_w * w[at : at + OV]
        if OV <= at < OV + cells:
            s = jnp.where(d_rows[at : at + OV] > 0, s, of_land * source[at - OV : at])
            s_out[at - OV : at] = s
        s_rows[at : at + OV] = s

    surface_rows(0)
    surface_rows(OV)
    slope = gravity_step * (s_rows[OV : OV + 1] - s_rows[OV - 1 : OV])
    d_west = jnp.minimum(d_rows[OV - 1 : OV], d_rows[OV : OV + 1])
    for level in range(KL):
        u = jnp.where(d_west > level, edge[level : level + 1] - slope, 0.0)
        u_rows[level, :OV] = jnp.broadcast_to(u, (OV, lat))
    zero = jnp.zeros((OV, 1), F32)
    for at in range(OV, OV + cells, OV):
        own = slice(at - OV, at)
        surface_rows(at + OV)
        s = s_rows[at : at + OV]
        d = d_rows[at : at + OV]
        slope = gravity_step * (s_rows[at + 1 : at + OV + 1] - s)
        face = jnp.minimum(d, d_rows[at + 1 : at + OV + 1])
        for level in range(KL):
            u_rows[level, at : at + OV] = jnp.where(face > level, u_vel[level, own] - slope, 0.0)
        send(u_rows.at[:, at : at + OV], u_new.at[:, own])
        slope = gravity_step * (jnp.concatenate([s[:, 1:], zero], axis=1) - s)
        face = jnp.minimum(d, jnp.concatenate([d[:, 1:], zero], axis=1))
        for level in range(KL):
            v_out[level, own] = jnp.where(face > level, v_vel[level, own] - slope, 0.0)
        send(v_out.at[:, own], v_new.at[:, own])
        w_sum = jnp.zeros((OV, lat), F32)
        for level in range(KL - 1, -1, -1):
            v = v_out[level, own]
            flow = u_rows[level, at : at + OV] - u_rows[level, at - 1 : at + OV - 1]
            flow = flow + (v - jnp.concatenate([zero, v[:, :-1]], axis=1))
            w_sum = w_sum + jnp.where(d > level, flow, 0.0)
            w_out[level, own] = w_sum
        send(w_out.at[:, own], w_vel.at[:, own])
        if at == cells:
            send(s_out, solution)
    for copy in copies:
        copy.wait()


def swap_pairs(block, outward):
    devices = lax.axis_size("lon")
    if outward:
        route = [(i, (i - 1 if i % 2 == 0 else i + 1) % devices) for i in range(devices)]
    else:
        route = [(i, i ^ 1) for i in range(devices)]
    return lax.ppermute(block, "lon", route)


def swap(inner, outer):
    outer = swap_pairs(outer, True)
    return outer, swap_pairs(inner, False)


def shape(*dims):
    return jax.ShapeDtypeStruct(dims, F32)


def body(source, diagonal, u_vel, v_vel, bottom):
    cells, lat = source.shape
    span = cells + 2 * OV
    devices = lax.axis_size("lon")
    parity = (lax.axis_index("lon") % 2).astype(jnp.int32).reshape(1)
    consts = [jnp.asarray(table) for table in tables(span)]
    hbm = {name: pltpu.with_memory_space_constraint(x, pltpu.HBM) for name, x in (
        ("source", source), ("diagonal", diagonal), ("u", u_vel), ("v", v_vel), ("bottom", bottom))}
    consts = [pltpu.with_memory_space_constraint(x, pltpu.HBM) for x in consts]

    outer = pl.pallas_call(
        first_edges,
        in_specs=[SM, HB, HB],
        out_specs=VM,
        out_shape=pltpu.VMEM((OV, lat), F32),
        scratch_shapes=[pltpu.VMEM((OV, lat), F32), pltpu.VMEM((OV, lat), jnp.int32),
                        pltpu.SemaphoreType.DMA((2,))],
        compiler_params=PARAMS,
        name="first_edges",
    )(parity, hbm["source"], hbm["bottom"])
    outer_in = swap_pairs(outer, True)

    inner, far_inner, far_outer, masked, coef, depth, source_v, *held = pl.pallas_call(
        prepare,
        in_specs=[SM] + [HB] * 8,
        out_specs=[VM] * 10,
        out_shape=[pltpu.VMEM((OV, lat), F32)]
        + [pltpu.VMEM((FAR, lat), F32)] * 2
        + [pltpu.VMEM((cells, lat), F32)] * 4
        + [pltpu.VMEM(table.shape, table.dtype) for table in consts],
        scratch_shapes=[
            pltpu.VMEM((cells, lat), F32),
            pltpu.VMEM((cells, lat), jnp.int32),
            pltpu.VMEM((KL, OV, lat), F32),
            pltpu.SemaphoreType.DMA((7,)),
        ],
        compiler_params=PARAMS,
        cost_estimate=pl.CostEstimate(flops=10**6, bytes_accessed=7 * 10**6, transcendentals=0),
        name="prepare",
    )(parity, outer, hbm["source"], hbm["diagonal"], hbm["bottom"], hbm["u"], *consts)
    near = swap_pairs(inner, False), outer_in
    far = swap(far_inner, far_outer)[::-1]

    blocks = -(-lat // LANE)
    first, inner, outer = pl.pallas_call(
        first_solve,
        in_specs=[SM] + [VM] * 6,
        out_specs=[VM] * 3,
        out_shape=[pltpu.VMEM((span, lat), F32)] + [pltpu.VMEM(((2 * OV + 1) * blocks, LANE), F32)] * 2,
        scratch_shapes=solve_scratch(span, lat),
        compiler_params=PARAMS,
        name="first_solve",
    )(parity, *near, masked, *held)
    near = swap(inner, outer)

    c_rows, z_rows, d_rows, edge, u_v, v_v = pl.pallas_call(
        absorb,
        in_specs=[SM] + [VM] * 5 + [HB] * 2,
        out_specs=[VM] * 6,
        out_shape=[pltpu.VMEM((span + 2 * OV, lat), F32)] * 2
        + [pltpu.VMEM((span, lat), F32), pltpu.VMEM((OV, lat), F32)]
        + [pltpu.VMEM((KL, cells, lat), F32)] * 2,
        scratch_shapes=[pltpu.SemaphoreType.DMA((2,))],
        compiler_params=PARAMS,
        cost_estimate=pl.CostEstimate(flops=10**6, bytes_accessed=7 * 10**6, transcendentals=0),
        name="absorb",
    )(parity, first, *far, coef, depth, hbm["u"], hbm["v"])

    z, y, second, inner, outer = pl.pallas_call(
        second_solve,
        in_specs=[SM] + [VM] * 7,
        out_specs=[VM] * 5,
        out_shape=[pltpu.VMEM((span + 2 * OV, lat), F32)]
        + [pltpu.VMEM((span, lat), F32)] * 2
        + [pltpu.VMEM(((OV + 1) * blocks, LANE), F32)] * 2,
        scratch_shapes=solve_scratch(span, lat),
        compiler_params=PARAMS,
        name="second_solve",
    )(parity, *near, z_rows, c_rows, *held)
    near = swap(inner, outer)

    w_rows, masked, row = pl.pallas_call(
        early_sums,
        in_specs=[VM] * 5,
        out_specs=[VM] * 3,
        out_shape=[pltpu.VMEM((span, lat), F32), pltpu.VMEM((cells, lat), F32), pltpu.VMEM((1, LANE), F32)],
        compiler_params=PARAMS,
        cost_estimate=pl.CostEstimate(flops=10**6, bytes_accessed=7 * 10**6, transcendentals=0),
        name="early_sums",
    )(z, y, c_rows, second, source_v)

    w, sent = pl.pallas_call(
        sums,
        in_specs=[SM] + [VM] * 8,
        out_specs=[VM] * 2,
        out_shape=[pltpu.VMEM((span, lat), F32), pltpu.VMEM((devices, 1, LANE), F32)],
        compiler_params=PARAMS,
        name="sums",
    )(parity, *near, w_rows, z, y, c_rows, masked, row)
    ring = [[(i + devices // 2) % devices for i in range(devices)]]
    came = lax.all_to_all(sent, "lon", 0, 0, axis_index_groups=ring)

    return pl.pallas_call(
        finish,
        in_specs=[VM] * 8,
        out_specs=[HB] * 4,
        out_shape=[shape(cells, lat)] + [shape(KL, cells, lat)] * 3,
        scratch_shapes=[pltpu.VMEM((span, lat), F32)]
        + [pltpu.VMEM((KL, OV + cells, lat), F32)]
        + [pltpu.VMEM((KL, cells, lat), F32)] * 2
        + [pltpu.VMEM((cells, lat), F32), pltpu.SemaphoreType.DMA((1 + 3 * (cells // OV),))],
        compiler_params=PARAMS,
        name="finish",
    )(came, z, w, d_rows, edge, source_v, u_v, v_v)


def solution(mesh):
    return jax.shard_map(
        body,
        mesh=mesh,
        in_specs=(
            P(("members", "lon"), None),
            P(("members", "lon"), None),
            P(None, ("members", "lon"), None),
            P(None, ("members", "lon"), None),
            P(("members", "lon"), None),
        ),
        out_specs=(
            P(("members", "lon"), None),
            P(None, ("members", "lon"), None),
            P(None, ("members", "lon"), None),
            P(None, ("members", "lon"), None),
        ),
        check_vma=False,
    )
```

```python
import math

import jax
import jax.numpy as jnp
import ml_dtypes
import numpy as np
from jax import lax
from jax.experimental import pallas as pl
from jax.experimental.pallas import tpu as pltpu
from jax.sharding import PartitionSpec as P

LT = 112
OV = 8
KL = 6
LANE = 128
FAR = 24

tile_shift = 0.1
gravity_step = 0.5

F32 = jnp.float32
BF16 = jnp.bfloat16
VM = pl.BlockSpec(memory_space=pltpu.VMEM)
SM = pl.BlockSpec(memory_space=pltpu.SMEM)
HB = pl.BlockSpec(memory_space=pl.ANY)
PARAMS = pltpu.CompilerParams(vmem_limit_bytes=32 * 1024 * 1024)


def sine_basis(length):
    ordinal = np.arange(length, dtype=np.float64) + 1.0
    angles = math.pi * ordinal[:, None] * ordinal[None, :] / (length + 1)
    basis_matrix = np.sqrt(2.0 / (length + 1)) * np.sin(angles)
    eigen_value = 2.0 - 2.0 * np.cos(math.pi * ordinal / (length + 1))
    return basis_matrix, eigen_value


def halves(matrix):
    high = matrix.astype(ml_dtypes.bfloat16)
    low = (matrix - high.astype(np.float64)).astype(ml_dtypes.bfloat16)
    return high, low


def tables(span):
    lon_basis, lon_value = sine_basis(span)
    lat_basis, lat_value = sine_basis(LT + 2 * OV)
    high, low = halves(lat_basis)
    lat = np.block([[high, low], [high, np.zeros_like(low)]])
    high, low = halves(lon_basis)
    lon = np.concatenate([high, low, high], axis=1)
    scale = 1.0 / (lon_value[:, None] + lat_value[None, :] + tile_shift)
    return lat, lon, scale.astype(np.float32)


def split(x):
    high = x.astype(BF16)
    return high, (x - high.astype(F32)).astype(BF16)


def tile_solve(x, lat_basis, lon, scale, rows, spectral, out):
    span, lat = out.shape
    tiles = lat // LT
    lane = lax.broadcasted_iota(jnp.int32, (span, LANE), 1)

    def block_of(b):
        if b < 0:
            return jnp.zeros((span, LANE), F32)
        return x[:, b * LANE : (b + 1) * LANE]

    chunk = 4
    groups = [range(first, min(first + chunk, tiles)) for first in range(0, tiles, chunk)]
    held = {}

    def lanes_of(group):
        return slice(group[0] * LANE, (group[-1] + 1) * LANE)

    def cut(group):
        for t in group:
            block, start = divmod(t * LT - OV, LANE)
            left, right = [pltpu.roll(block_of(b), LANE - start, 1) for b in (block, block + 1)]
            high, low = split(jnp.where(lane < LANE - start, left, right))
            rows[t * span : (t + 1) * span, :LANE] = high
            rows[t * span : (t + 1) * span, LANE:] = low

    def along_lat(group):
        product = jnp.dot(
            rows[group[0] * span : (group[-1] + 1) * span], lat_basis[...], preferred_element_type=F32
        )
        return product[:, :LANE] + product[:, LANE:]

    def lat_there(group):
        high, low = split(along_lat(group))
        for i, t in enumerate(group):
            at = slice(t * LANE, (t + 1) * LANE)
            spectral[:span, at] = high[i * span : (i + 1) * span]
            spectral[span : 2 * span, at] = high[i * span : (i + 1) * span]
            spectral[2 * span :, at] = low[i * span : (i + 1) * span]

    def lon_there(group):
        c = jnp.dot(lon[...], spectral[:, lanes_of(group)], preferred_element_type=F32)
        high, low = split(c * jnp.concatenate([scale[...]] * len(group), axis=1))
        spectral[:, lanes_of(group)] = jnp.concatenate([high, high, low], axis=0)

    def lon_back(group):
        c = jnp.dot(lon[...], spectral[:, lanes_of(group)], preferred_element_type=F32)
        high, low = split(c)
        for i, t in enumerate(group):
            at = slice(t * span, (t + 1) * span)
            rows[at, :LANE] = high[:, i * LANE : (i + 1) * LANE]
            rows[at, LANE:] = low[:, i * LANE : (i + 1) * LANE]

    def lat_back(group):
        product = along_lat(group)
        for i, t in enumerate(group):
            block, start = divmod(t * LT - OV, LANE)
            part = pltpu.roll(product[i * span : (i + 1) * span], start, 1)
            for b, inside in ((block, lane >= start), (block + 1, lane < start)):
                if 0 <= b * LANE < lat:
                    piece = jnp.where(inside, part, 0.0)
                    held[b] = held[b] + piece if b in held else piece
        done = (group[-1] + 1) * LT - OV if group[-1] + 1 < tiles else lat + LANE
        for b in [b for b in held if (b + 1) * LANE <= done]:
            width = min(LANE, lat - b * LANE)
            out[:, b * LANE : b * LANE + width] = held.pop(b)[:, :width]

    stages = [cut, lat_there, lon_there, lon_back, lat_back]
    for step in range(len(groups) + len(stages) - 1):
        for i in reversed(range(len(stages))):
            if 0 <= step - i < len(groups):
                stages[i](groups[step - i])


def wide_lanes(lat):
    return -(-(lat + OV) // LANE) * LANE


def solve_scratch(span, lat):
    tiles = lat // LT
    return [
        pltpu.VMEM((span, wide_lanes(lat)), F32),
        pltpu.VMEM((tiles * span, 2 * LANE), BF16),
        pltpu.VMEM((3 * span, tiles * LANE), BF16),
    ]


def pick(parity, inner, outer):
    even = jnp.full(inner.shape, parity[0], jnp.int32) == 0
    return jnp.where(even, outer, inner), jnp.where(even, inner, outer)


def lat_beside(m):
    zero = jnp.zeros((m.shape[0], 1), m.dtype)
    return jnp.concatenate([m[:, 1:], zero], axis=1) + jnp.concatenate([zero, m[:, :-1]], axis=1)


def pack(message, rows):
    n, lat = rows.shape
    for block, at in enumerate(range(0, lat, LANE)):
        width = min(LANE, lat - at)
        message[block * n : (block + 1) * n, :width] = rows[:, at : at + width]


def unpack(message, n, lat):
    blocks = [message[i * n : (i + 1) * n] for i in range(-(-lat // LANE))]
    return jnp.concatenate(blocks, axis=1)[:, :lat]


def first_edges(parity, source, bottom, outer, rows, depth, sems):
    start = pl.multiple_of(parity[0] * (source.shape[0] - OV), OV)
    at = pl.ds(start, OV)
    copies = [
        pltpu.make_async_copy(source.at[at], rows, sems.at[0]),
        pltpu.make_async_copy(bottom.at[at], depth, sems.at[1]),
    ]
    for copy in copies:
        copy.start()
    for copy in copies:
        copy.wait()
    outer[...] = jnp.where(depth[...] > 0, rows[...], 0.0)


def prepare(parity, after, source_h, diagonal_h, bottom_h, u_h, *refs):
    tables_h, (inner, far_inner, far_outer, masked, coef, depth, source), held = refs[:3], refs[3:10], refs[10:13]
    diagonal, bottom, u_strip, sems = refs[13:]
    cells, lat = source.shape
    pairs = [(source_h, source), (bottom_h, bottom), (diagonal_h, diagonal)]
    pairs += [(u_h.at[:, pl.ds(cells - OV, OV)], u_strip)]
    pairs += list(zip(tables_h, held))
    copies = [pltpu.make_async_copy(a, b, sems.at[i]) for i, (a, b) in enumerate(pairs)]
    for copy in copies:
        copy.start()
    for copy in copies[:4]:
        copy.wait()
    wet = bottom[...] > 0
    masked[...] = jnp.where(wet, source[...], 0.0)
    coef[...] = jnp.where(wet, 4.0 + diagonal[...], 0.0)
    depth[...] = bottom[...].astype(F32)
    edge = OV + 1
    blank = jnp.zeros((2 * OV - edge - 1, lat), F32)
    to_west = jnp.concatenate([coef[:edge], blank, depth[:1]], axis=0)
    u_rows = [u_strip[level, OV - 1 : OV] for level in range(KL)]
    to_east = jnp.concatenate(u_rows + [depth[cells - 1 :], coef[cells - edge :]], axis=0)
    far_outer[: 2 * OV], far_inner[: 2 * OV] = pick(parity, to_east, to_west)
    for message in (far_outer, far_inner):
        message[2 * OV :] = jnp.zeros((FAR - 2 * OV, lat), F32)
    inner[...] = pick(parity, masked[:OV], masked[cells - OV :])[0]
    for copy in copies[4:]:
        copy.wait()


def first_solve(parity, inner_in, outer_in, masked, lat_basis, lon, scale,
                first, inner, outer, wide, rows, spectral):
    cells, lat = masked.shape
    west, east = pick(parity, inner_in[...], outer_in[...])
    wide[:OV, :lat] = west
    wide[OV : OV + cells, :lat] = masked[...]
    wide[OV + cells :, :lat] = east
    wide[:, lat:] = jnp.zeros((cells + 2 * OV, wide.shape[1] - lat), F32)
    tile_solve(wide, lat_basis, lon, scale, rows, spectral, first)
    to_outer, to_inner = pick(parity, first[cells - 1 :], first[: 2 * OV + 1])
    pack(inner, to_inner)
    pack(outer, to_outer)


def absorb(parity, first, inner_in, outer_in, coef, depth, u_h, v_h, c_rows, z_rows, d_rows, edge, u, v, sems):
    cells, lat = coef.shape
    copies = [pltpu.make_async_copy(a, b, sems.at[i]) for i, (a, b) in enumerate([(u_h, u), (v_h, v)])]
    for copy in copies:
        copy.start()
    west, east = pick(parity, inner_in[: 2 * OV], outer_in[: 2 * OV])
    edge[...] = west[:OV]
    d_rows[:OV] = jnp.broadcast_to(west[KL : KL + 1], (OV, lat))
    d_rows[OV : OV + cells] = depth[...]
    d_rows[OV + cells :] = jnp.broadcast_to(east[2 * OV - 1 :], (OV, lat))
    c_rows[: 2 * OV] = west
    c_rows[: OV - 1] = jnp.zeros((OV - 1, lat), F32)
    c_rows[2 * OV : 2 * OV + cells] = coef[...]
    c_rows[2 * OV + cells :] = east
    c_rows[3 * OV + cells + 1 :] = jnp.zeros((OV - 1, lat), F32)
    z_rows[:OV] = jnp.zeros((OV, lat), F32)
    z_rows[3 * OV + cells :] = jnp.zeros((OV, lat), F32)
    inside = slice(OV, 3 * OV + cells)
    z_rows[inside] = jnp.where(c_rows[inside] > 0, first[...], 0.0)
    for copy in copies:
        copy.wait()


def second_solve(parity, outer_in, inner_in, z_rows, c_rows, lat_basis, lon, scale,
                 z, y, second, inner, outer, wide, rows, spectral):
    span, lat = y.shape
    cells = span - 2 * OV
    reach = 2 * OV + 1
    west, east = pick(parity, unpack(inner_in, reach, lat), unpack(outer_in, reach, lat))
    z[...] = z_rows[...]
    for came, start in ((west, OV - 1), (east, OV + cells)):
        at = slice(start, start + reach)
        z[at] += jnp.where(c_rows[at] > 0, came, 0.0)
    inside = slice(OV, OV + span)
    c, m = c_rows[inside], z[inside]
    beside = z[OV - 1 : OV - 1 + span] + z[OV + 1 : OV + 1 + span]
    image = jnp.where(c > 0, c * m - (beside + lat_beside(m)), 0.0)
    y[...] = image
    wide[:, :lat] = image
    wide[:, lat:] = jnp.zeros((span, wide.shape[1] - lat), F32)
    tile_solve(wide, lat_basis, lon, scale, rows, spectral, second)
    to_outer, to_inner = pick(parity, second[span - OV - 1 :], second[: OV + 1])
    pack(inner, to_inner)
    pack(outer, to_outer)


def dot(a, b):
    cells, lat = a.shape
    product = a * b
    rows = product[:OV]
    for at in range(OV, cells, OV):
        rows = rows + product[at : at + OV]
    whole = lat // LANE * LANE
    total = rows[:, :LANE]
    for at in range(LANE, whole, LANE):
        total = total + rows[:, at : at + LANE]
    if whole < lat:
        blank = jnp.zeros((OV, LANE - lat + whole), F32)
        total = total + jnp.concatenate([rows[:, whole:], blank], axis=1)
    return jnp.sum(jnp.sum(total, axis=0, keepdims=True), axis=1, keepdims=True)


def in_lanes(row, sums):
    lane = lax.broadcasted_iota(jnp.int32, row.shape, 1)
    for i, value in sums.items():
        row = jnp.where(lane == i, value, row)
    return row


def early_sums(z, y, c_rows, second, source, w_rows, masked, row):
    cells, lat = source.shape
    inside = slice(OV, 3 * OV + cells)
    w_rows[...] = jnp.where(c_rows[inside] > 0, second[...], 0.0)
    own = slice(2 * OV, 2 * OV + cells)
    wet = c_rows[own] > 0
    masked[...] = jnp.where(wet, source[...], 0.0)
    land = jnp.where(wet, 0.0, source[...])
    z_own = z[own]
    sums_of = {0: dot(masked[...], z_own), 1: dot(z_own, y[OV : OV + cells]), 6: dot(land, land)}
    row[...] = in_lanes(jnp.zeros((1, LANE), F32), sums_of)


def sums(parity, outer_in, inner_in, w_rows, z, y, c_rows, masked, row, w, sent):
    cells, lat = masked.shape
    west, east = pick(parity, unpack(inner_in, OV + 1, lat), unpack(outer_in, OV + 1, lat))
    w[...] = w_rows[...]
    for came, start in ((west, OV - 1), (east, cells)):
        wet = c_rows[OV + start : 2 * OV + start + 1] > 0
        w[start : start + OV + 1] += jnp.where(wet, came, 0.0)
    own = slice(OV, OV + cells)
    c, m = c_rows[2 * OV : 2 * OV + cells], w[own]
    beside = w[OV - 1 : OV - 1 + cells] + w[OV + 1 : OV + 1 + cells]
    x = jnp.where(c > 0, c * m - (beside + lat_beside(m)), 0.0)
    sums_of = {2: dot(masked[...], m), 3: dot(y[own], m), 4: dot(z[2 * OV : 2 * OV + cells], x), 5: dot(m, x)}
    sent[...] = jnp.broadcast_to(in_lanes(row[...], sums_of)[None], sent.shape)


def finish(came, z, w, d_rows, edge, source, u_vel, v_vel, solution, u_new, v_new, w_vel,
           s_rows, u_rows, v_out, w_out, s_out, sems):
    cells, lat = source.shape
    total = jnp.broadcast_to(jnp.sum(came[...], axis=0), (8, LANE))
    place = [lax.broadcasted_iota(jnp.int32, (8, LANE), axis) for axis in range(2)]
    total = jnp.sum(jnp.where(place[0] == place[1], total, 0.0), axis=1, keepdims=True)
    rz, zy, rw, yw, zx, wx, ll = [total[i : i + 1] for i in range(7)]
    step0 = (rz + ll) / (zy + ll)
    rest = (zy - rz) / (zy + ll)
    new = rz - step0 * (zy + rw) + step0 * step0 * yw + rest * rest * ll
    beta = new / (rz + ll)
    grown = 1.0 + beta
    bent = grown * grown * zy - grown * step0 * (zx + yw) + step0 * step0 * wx
    step1 = new / (bent + (rest + beta) * (rest + beta) * ll)
    of_z = jnp.broadcast_to(step0 + step1 * grown, (OV, lat))
    of_w = jnp.broadcast_to(-step1 * step0, (OV, lat))
    of_land = jnp.broadcast_to(step0 + step1 * (rest + beta), (OV, lat))

    copies = []

    def send(held, result):
        copies.append(pltpu.make_async_copy(held, result, sems.at[len(copies)]))
        copies[-1].start()

    def surface_rows(at):
        s = of_z * z[at + OV : at + 2 * OV] + of_w * w[at : at + OV]
        if OV <= at < OV + cells:
            s = jnp.where(d_rows[at : at + OV] > 0, s, of_land * source[at - OV : at])
            s_out[at - OV : at] = s
        s_rows[at : at + OV] = s

    surface_rows(0)
    surface_rows(OV)
    slope = gravity_step * (s_rows[OV : OV + 1] - s_rows[OV - 1 : OV])
    d_west = jnp.minimum(d_rows[OV - 1 : OV], d_rows[OV : OV + 1])
    for level in range(KL):
        u = jnp.where(d_west > level, edge[level : level + 1] - slope, 0.0)
        u_rows[level, :OV] = jnp.broadcast_to(u, (OV, lat))
    zero = jnp.zeros((OV, 1), F32)
    for at in range(OV, OV + cells, OV):
        own = slice(at - OV, at)
        surface_rows(at + OV)
        s = s_rows[at : at + OV]
        d = d_rows[at : at + OV]
        slope = gravity_step * (s_rows[at + 1 : at + OV + 1] - s)
        face = jnp.minimum(d, d_rows[at + 1 : at + OV + 1])
        for level in range(KL):
            u_rows[level, at : at + OV] = jnp.where(face > level, u_vel[level, own] - slope, 0.0)
        send(u_rows.at[:, at : at + OV], u_new.at[:, own])
        slope = gravity_step * (jnp.concatenate([s[:, 1:], zero], axis=1) - s)
        face = jnp.minimum(d, jnp.concatenate([d[:, 1:], zero], axis=1))
        for level in range(KL):
            v_out[level, own] = jnp.where(face > level, v_vel[level, own] - slope, 0.0)
        send(v_out.at[:, own], v_new.at[:, own])
        w_sum = jnp.zeros((OV, lat), F32)
        for level in range(KL - 1, -1, -1):
            v = v_out[level, own]
            flow = u_rows[level, at : at + OV] - u_rows[level, at - 1 : at + OV - 1]
            flow = flow + (v - jnp.concatenate([zero, v[:, :-1]], axis=1))
            w_sum = w_sum + jnp.where(d > level, flow, 0.0)
            w_out[level, own] = w_sum
        send(w_out.at[:, own], w_vel.at[:, own])
        if at == cells:
            send(s_out, solution)
    for copy in copies:
        copy.wait()


def swap_pairs(block, outward):
    devices = lax.axis_size("lon")
    if outward:
        route = [(i, (i - 1 if i % 2 == 0 else i + 1) % devices) for i in range(devices)]
    else:
        route = [(i, i ^ 1) for i in range(devices)]
    return lax.ppermute(block, "lon", route)


def swap(inner, outer):
    outer = swap_pairs(outer, True)
    return outer, swap_pairs(inner, False)


def shape(*dims):
    return jax.ShapeDtypeStruct(dims, F32)


def body(source, diagonal, u_vel, v_vel, bottom):
    cells, lat = source.shape
    span = cells + 2 * OV
    devices = lax.axis_size("lon")
    parity = (lax.axis_index("lon") % 2).astype(jnp.int32).reshape(1)
    consts = [jnp.asarray(table) for table in tables(span)]
    hbm = {name: pltpu.with_memory_space_constraint(x, pltpu.HBM) for name, x in (
        ("source", source), ("diagonal", diagonal), ("u", u_vel), ("v", v_vel), ("bottom", bottom))}
    consts = [pltpu.with_memory_space_constraint(x, pltpu.HBM) for x in consts]

    outer = pl.pallas_call(
        first_edges,
        in_specs=[SM, HB, HB],
        out_specs=VM,
        out_shape=pltpu.VMEM((OV, lat), F32),
        scratch_shapes=[pltpu.VMEM((OV, lat), F32), pltpu.VMEM((OV, lat), jnp.int32),
                        pltpu.SemaphoreType.DMA((2,))],
        compiler_params=PARAMS,
        name="first_edges",
    )(parity, hbm["source"], hbm["bottom"])
    outer_in = swap_pairs(outer, True)

    inner, far_inner, far_outer, masked, coef, depth, source_v, *held = pl.pallas_call(
        prepare,
        in_specs=[SM] + [HB] * 8,
        out_specs=[VM] * 10,
        out_shape=[pltpu.VMEM((OV, lat), F32)]
        + [pltpu.VMEM((FAR, lat), F32)] * 2
        + [pltpu.VMEM((cells, lat), F32)] * 4
        + [pltpu.VMEM(table.shape, table.dtype) for table in consts],
        scratch_shapes=[
            pltpu.VMEM((cells, lat), F32),
            pltpu.VMEM((cells, lat), jnp.int32),
            pltpu.VMEM((KL, OV, lat), F32),
            pltpu.SemaphoreType.DMA((7,)),
        ],
        compiler_params=PARAMS,
        cost_estimate=pl.CostEstimate(flops=10**6, bytes_accessed=7 * 10**6, transcendentals=0),
        name="prepare",
    )(parity, outer, hbm["source"], hbm["diagonal"], hbm["bottom"], hbm["u"], *consts)
    near = swap_pairs(inner, False), outer_in
    far = swap(far_inner, far_outer)[::-1]

    blocks = -(-lat // LANE)
    first, inner, outer = pl.pallas_call(
        first_solve,
        in_specs=[SM] + [VM] * 6,
        out_specs=[VM] * 3,
        out_shape=[pltpu.VMEM((span, lat), F32)] + [pltpu.VMEM(((2 * OV + 1) * blocks, LANE), F32)] * 2,
        scratch_shapes=solve_scratch(span, lat),
        compiler_params=PARAMS,
        name="first_solve",
    )(parity, *near, masked, *held)
    near = swap(inner, outer)

    c_rows, z_rows, d_rows, edge, u_v, v_v = pl.pallas_call(
        absorb,
        in_specs=[SM] + [VM] * 5 + [HB] * 2,
        out_specs=[VM] * 6,
        out_shape=[pltpu.VMEM((span + 2 * OV, lat), F32)] * 2
        + [pltpu.VMEM((span, lat), F32), pltpu.VMEM((OV, lat), F32)]
        + [pltpu.VMEM((KL, cells, lat), F32)] * 2,
        scratch_shapes=[pltpu.SemaphoreType.DMA((2,))],
        compiler_params=PARAMS,
        cost_estimate=pl.CostEstimate(flops=10**6, bytes_accessed=7 * 10**6, transcendentals=0),
        name="absorb",
    )(parity, first, *far, coef, depth, hbm["u"], hbm["v"])

    z, y, second, inner, outer = pl.pallas_call(
        second_solve,
        in_specs=[SM] + [VM] * 7,
        out_specs=[VM] * 5,
        out_shape=[pltpu.VMEM((span + 2 * OV, lat), F32)]
        + [pltpu.VMEM((span, lat), F32)] * 2
        + [pltpu.VMEM(((OV + 1) * blocks, LANE), F32)] * 2,
        scratch_shapes=solve_scratch(span, lat),
        compiler_params=PARAMS,
        name="second_solve",
    )(parity, *near, z_rows, c_rows, *held)
    near = swap(inner, outer)

    w_rows, masked, row = pl.pallas_call(
        early_sums,
        in_specs=[VM] * 5,
        out_specs=[VM] * 3,
        out_shape=[pltpu.VMEM((span, lat), F32), pltpu.VMEM((cells, lat), F32), pltpu.VMEM((1, LANE), F32)],
        compiler_params=PARAMS,
        cost_estimate=pl.CostEstimate(flops=10**6, bytes_accessed=7 * 10**6, transcendentals=0),
        name="early_sums",
    )(z, y, c_rows, second, source_v)

    w, sent = pl.pallas_call(
        sums,
        in_specs=[SM] + [VM] * 8,
        out_specs=[VM] * 2,
        out_shape=[pltpu.VMEM((span, lat), F32), pltpu.VMEM((devices, 1, LANE), F32)],
        compiler_params=PARAMS,
        name="sums",
    )(parity, *near, w_rows, z, y, c_rows, masked, row)
    ring = [list(reversed(range(devices)))]
    came = lax.all_to_all(sent, "lon", 0, 0, axis_index_groups=ring)

    return pl.pallas_call(
        finish,
        in_specs=[VM] * 8,
        out_specs=[HB] * 4,
        out_shape=[shape(cells, lat)] + [shape(KL, cells, lat)] * 3,
        scratch_shapes=[pltpu.VMEM((span, lat), F32)]
        + [pltpu.VMEM((KL, OV + cells, lat), F32)]
        + [pltpu.VMEM((KL, cells, lat), F32)] * 2
        + [pltpu.VMEM((cells, lat), F32), pltpu.SemaphoreType.DMA((1 + 3 * (cells // OV),))],
        compiler_params=PARAMS,
        name="finish",
    )(came, z, w, d_rows, edge, source_v, u_v, v_v)


def solution(mesh):
    return jax.shard_map(
        body,
        mesh=mesh,
        in_specs=(
            P(("members", "lon"), None),
            P(("members", "lon"), None),
            P(None, ("members", "lon"), None),
            P(None, ("members", "lon"), None),
            P(("members", "lon"), None),
        ),
        out_specs=(
            P(("members", "lon"), None),
            P(None, ("members", "lon"), None),
            P(None, ("members", "lon"), None),
            P(None, ("members", "lon"), None),
        ),
        check_vma=False,
    )
```

```python
import math

import jax
import jax.numpy as jnp
import ml_dtypes
import numpy as np
from jax import lax
from jax.experimental import pallas as pl
from jax.experimental.pallas import tpu as pltpu
from jax.sharding import PartitionSpec as P

LT = 112
OV = 8
KL = 6
LANE = 128
FAR = 24

tile_shift = 0.1
gravity_step = 0.5

F32 = jnp.float32
BF16 = jnp.bfloat16
VM = pl.BlockSpec(memory_space=pltpu.VMEM)
SM = pl.BlockSpec(memory_space=pltpu.SMEM)
HB = pl.BlockSpec(memory_space=pl.ANY)
PARAMS = pltpu.CompilerParams(vmem_limit_bytes=32 * 1024 * 1024)


def sine_basis(length):
    ordinal = np.arange(length, dtype=np.float64) + 1.0
    angles = math.pi * ordinal[:, None] * ordinal[None, :] / (length + 1)
    basis_matrix = np.sqrt(2.0 / (length + 1)) * np.sin(angles)
    eigen_value = 2.0 - 2.0 * np.cos(math.pi * ordinal / (length + 1))
    return basis_matrix, eigen_value


def halves(matrix):
    high = matrix.astype(ml_dtypes.bfloat16)
    low = (matrix - high.astype(np.float64)).astype(ml_dtypes.bfloat16)
    return high, low


def tables(span):
    lon_basis, lon_value = sine_basis(span)
    lat_basis, lat_value = sine_basis(LT + 2 * OV)
    high, low = halves(lat_basis)
    lat = np.block([[high, low], [high, np.zeros_like(low)]])
    high, low = halves(lon_basis)
    lon = np.concatenate([high, low, high], axis=1)
    scale = 1.0 / (lon_value[:, None] + lat_value[None, :] + tile_shift)
    return lat, lon, scale.astype(np.float32)


def split(x):
    high = x.astype(BF16)
    return high, (x - high.astype(F32)).astype(BF16)


def tile_solve(x, lat_basis, lon, scale, rows, spectral, out):
    span, lat = out.shape
    tiles = lat // LT
    lane = lax.broadcasted_iota(jnp.int32, (span, LANE), 1)

    def block_of(b):
        if b < 0:
            return jnp.zeros((span, LANE), F32)
        return x[:, b * LANE : (b + 1) * LANE]

    chunk = 4
    groups = [range(first, min(first + chunk, tiles)) for first in range(0, tiles, chunk)]
    held = {}

    def lanes_of(group):
        return slice(group[0] * LANE, (group[-1] + 1) * LANE)

    def cut(group):
        for t in group:
            block, start = divmod(t * LT - OV, LANE)
            left, right = [pltpu.roll(block_of(b), LANE - start, 1) for b in (block, block + 1)]
            high, low = split(jnp.where(lane < LANE - start, left, right))
            rows[t * span : (t + 1) * span, :LANE] = high
            rows[t * span : (t + 1) * span, LANE:] = low

    def along_lat(group):
        product = jnp.dot(
            rows[group[0] * span : (group[-1] + 1) * span], lat_basis[...], preferred_element_type=F32
        )
        return product[:, :LANE] + product[:, LANE:]

    def lat_there(group):
        high, low = split(along_lat(group))
        for i, t in enumerate(group):
            at = slice(t * LANE, (t + 1) * LANE)
            spectral[:span, at] = high[i * span : (i + 1) * span]
            spectral[span : 2 * span, at] = high[i * span : (i + 1) * span]
            spectral[2 * span :, at] = low[i * span : (i + 1) * span]

    def lon_there(group):
        c = jnp.dot(lon[...], spectral[:, lanes_of(group)], preferred_element_type=F32)
        high, low = split(c * jnp.concatenate([scale[...]] * len(group), axis=1))
        spectral[:, lanes_of(group)] = jnp.concatenate([high, high, low], axis=0)

    def lon_back(group):
        c = jnp.dot(lon[...], spectral[:, lanes_of(group)], preferred_element_type=F32)
        high, low = split(c)
        for i, t in enumerate(group):
            at = slice(t * span, (t + 1) * span)
            rows[at, :LANE] = high[:, i * LANE : (i + 1) * LANE]
            rows[at, LANE:] = low[:, i * LANE : (i + 1) * LANE]

    def lat_back(group):
        product = along_lat(group)
        for i, t in enumerate(group):
            block, start = divmod(t * LT - OV, LANE)
            part = pltpu.roll(product[i * span : (i + 1) * span], start, 1)
            for b, inside in ((block, lane >= start), (block + 1, lane < start)):
                if 0 <= b * LANE < lat:
                    piece = jnp.where(inside, part, 0.0)
                    held[b] = held[b] + piece if b in held else piece
        done = (group[-1] + 1) * LT - OV if group[-1] + 1 < tiles else lat + LANE
        for b in [b for b in held if (b + 1) * LANE <= done]:
            width = min(LANE, lat - b * LANE)
            out[:, b * LANE : b * LANE + width] = held.pop(b)[:, :width]

    stages = [cut, lat_there, lon_there, lon_back, lat_back]
    for step in range(len(groups) + len(stages) - 1):
        for i in reversed(range(len(stages))):
            if 0 <= step - i < len(groups):
                stages[i](groups[step - i])


def wide_lanes(lat):
    return -(-(lat + OV) // LANE) * LANE


def solve_scratch(span, lat):
    tiles = lat // LT
    return [
        pltpu.VMEM((span, wide_lanes(lat)), F32),
        pltpu.VMEM((tiles * span, 2 * LANE), BF16),
        pltpu.VMEM((3 * span, tiles * LANE), BF16),
    ]


def pick(parity, inner, outer):
    even = jnp.full(inner.shape, parity[0], jnp.int32) == 0
    return jnp.where(even, outer, inner), jnp.where(even, inner, outer)


def lat_beside(m):
    zero = jnp.zeros((m.shape[0], 1), m.dtype)
    return jnp.concatenate([m[:, 1:], zero], axis=1) + jnp.concatenate([zero, m[:, :-1]], axis=1)


def pack(message, rows):
    n, lat = rows.shape
    for block, at in enumerate(range(0, lat, LANE)):
        width = min(LANE, lat - at)
        message[block * n : (block + 1) * n, :width] = rows[:, at : at + width]


def unpack(message, n, lat):
    blocks = [message[i * n : (i + 1) * n] for i in range(-(-lat // LANE))]
    return jnp.concatenate(blocks, axis=1)[:, :lat]


def first_edges(parity, source, bottom, outer, rows, depth, sems):
    start = pl.multiple_of(parity[0] * (source.shape[0] - OV), OV)
    at = pl.ds(start, OV)
    copies = [
        pltpu.make_async_copy(source.at[at], rows, sems.at[0]),
        pltpu.make_async_copy(bottom.at[at], depth, sems.at[1]),
    ]
    for copy in copies:
        copy.start()
    for copy in copies:
        copy.wait()
    outer[...] = jnp.where(depth[...] > 0, rows[...], 0.0)


def prepare(parity, after, source_h, diagonal_h, bottom_h, u_h, *refs):
    tables_h, (inner, far_inner, far_outer, masked, coef, depth, source), held = refs[:3], refs[3:10], refs[10:13]
    diagonal, bottom, u_strip, sems = refs[13:]
    cells, lat = source.shape
    pairs = [(source_h, source), (bottom_h, bottom), (diagonal_h, diagonal)]
    pairs += [(u_h.at[:, pl.ds(cells - OV, OV)], u_strip)]
    pairs += list(zip(tables_h, held))
    copies = [pltpu.make_async_copy(a, b, sems.at[i]) for i, (a, b) in enumerate(pairs)]
    for copy in copies:
        copy.start()
    for copy in copies[:4]:
        copy.wait()
    wet = bottom[...] > 0
    masked[...] = jnp.where(wet, source[...], 0.0)
    coef[...] = jnp.where(wet, 4.0 + diagonal[...], 0.0)
    depth[...] = bottom[...].astype(F32)
    edge = OV + 1
    blank = jnp.zeros((2 * OV - edge - 1, lat), F32)
    to_west = jnp.concatenate([coef[:edge], blank, depth[:1]], axis=0)
    u_rows = [u_strip[level, OV - 1 : OV] for level in range(KL)]
    to_east = jnp.concatenate(u_rows + [depth[cells - 1 :], coef[cells - edge :]], axis=0)
    far_outer[: 2 * OV], far_inner[: 2 * OV] = pick(parity, to_east, to_west)
    for message in (far_outer, far_inner):
        message[2 * OV :] = jnp.zeros((FAR - 2 * OV, lat), F32)
    inner[...] = pick(parity, masked[:OV], masked[cells - OV :])[0]
    for copy in copies[4:]:
        copy.wait()


def first_solve(parity, inner_in, outer_in, masked, lat_basis, lon, scale,
                first, inner, outer, wide, rows, spectral):
    cells, lat = masked.shape
    west, east = pick(parity, inner_in[...], outer_in[...])
    wide[:OV, :lat] = west
    wide[OV : OV + cells, :lat] = masked[...]
    wide[OV + cells :, :lat] = east
    wide[:, lat:] = jnp.zeros((cells + 2 * OV, wide.shape[1] - lat), F32)
    tile_solve(wide, lat_basis, lon, scale, rows, spectral, first)
    to_outer, to_inner = pick(parity, first[cells - 1 :], first[: 2 * OV + 1])
    pack(inner, to_inner)
    pack(outer, to_outer)


def absorb(parity, first, inner_in, outer_in, coef, depth, c_rows, z_rows, d_rows, edge):
    cells, lat = coef.shape
    west, east = pick(parity, inner_in[: 2 * OV], outer_in[: 2 * OV])
    edge[...] = west[:OV]
    d_rows[:OV] = jnp.broadcast_to(west[KL : KL + 1], (OV, lat))
    d_rows[OV : OV + cells] = depth[...]
    d_rows[OV + cells :] = jnp.broadcast_to(east[2 * OV - 1 :], (OV, lat))
    c_rows[: 2 * OV] = west
    c_rows[: OV - 1] = jnp.zeros((OV - 1, lat), F32)
    c_rows[2 * OV : 2 * OV + cells] = coef[...]
    c_rows[2 * OV + cells :] = east
    c_rows[3 * OV + cells + 1 :] = jnp.zeros((OV - 1, lat), F32)
    z_rows[:OV] = jnp.zeros((OV, lat), F32)
    z_rows[3 * OV + cells :] = jnp.zeros((OV, lat), F32)
    inside = slice(OV, 3 * OV + cells)
    z_rows[inside] = jnp.where(c_rows[inside] > 0, first[...], 0.0)


def second_solve(parity, outer_in, inner_in, z_rows, c_rows, lat_basis, lon, scale,
                 z, y, second, inner, outer, wide, rows, spectral):
    span, lat = y.shape
    cells = span - 2 * OV
    reach = 2 * OV + 1
    west, east = pick(parity, unpack(inner_in, reach, lat), unpack(outer_in, reach, lat))
    z[...] = z_rows[...]
    for came, start in ((west, OV - 1), (east, OV + cells)):
        at = slice(start, start + reach)
        z[at] += jnp.where(c_rows[at] > 0, came, 0.0)
    inside = slice(OV, OV + span)
    c, m = c_rows[inside], z[inside]
    beside = z[OV - 1 : OV - 1 + span] + z[OV + 1 : OV + 1 + span]
    image = jnp.where(c > 0, c * m - (beside + lat_beside(m)), 0.0)
    y[...] = image
    wide[:, :lat] = image
    wide[:, lat:] = jnp.zeros((span, wide.shape[1] - lat), F32)
    tile_solve(wide, lat_basis, lon, scale, rows, spectral, second)
    to_outer, to_inner = pick(parity, second[span - OV - 1 :], second[: OV + 1])
    pack(inner, to_inner)
    pack(outer, to_outer)


def dot(a, b):
    cells, lat = a.shape
    product = a * b
    rows = product[:OV]
    for at in range(OV, cells, OV):
        rows = rows + product[at : at + OV]
    whole = lat // LANE * LANE
    total = rows[:, :LANE]
    for at in range(LANE, whole, LANE):
        total = total + rows[:, at : at + LANE]
    if whole < lat:
        blank = jnp.zeros((OV, LANE - lat + whole), F32)
        total = total + jnp.concatenate([rows[:, whole:], blank], axis=1)
    return jnp.sum(jnp.sum(total, axis=0, keepdims=True), axis=1, keepdims=True)


def in_lanes(row, sums):
    lane = lax.broadcasted_iota(jnp.int32, row.shape, 1)
    for i, value in sums.items():
        row = jnp.where(lane == i, value, row)
    return row


def early_sums(z, y, c_rows, second, source, u_h, v_h, w_rows, masked, row, u, v, sems):
    copies = [pltpu.make_async_copy(a, b, sems.at[i]) for i, (a, b) in enumerate([(u_h, u), (v_h, v)])]
    for copy in copies:
        copy.start()
    cells, lat = source.shape
    inside = slice(OV, 3 * OV + cells)
    w_rows[...] = jnp.where(c_rows[inside] > 0, second[...], 0.0)
    own = slice(2 * OV, 2 * OV + cells)
    wet = c_rows[own] > 0
    masked[...] = jnp.where(wet, source[...], 0.0)
    land = jnp.where(wet, 0.0, source[...])
    z_own = z[own]
    sums_of = {0: dot(masked[...], z_own), 1: dot(z_own, y[OV : OV + cells]), 6: dot(land, land)}
    row[...] = in_lanes(jnp.zeros((1, LANE), F32), sums_of)
    for copy in copies:
        copy.wait()


def sums(parity, outer_in, inner_in, w_rows, z, y, c_rows, masked, row, w, sent):
    cells, lat = masked.shape
    west, east = pick(parity, unpack(inner_in, OV + 1, lat), unpack(outer_in, OV + 1, lat))
    w[...] = w_rows[...]
    for came, start in ((west, OV - 1), (east, cells)):
        wet = c_rows[OV + start : 2 * OV + start + 1] > 0
        w[start : start + OV + 1] += jnp.where(wet, came, 0.0)
    own = slice(OV, OV + cells)
    c, m = c_rows[2 * OV : 2 * OV + cells], w[own]
    beside = w[OV - 1 : OV - 1 + cells] + w[OV + 1 : OV + 1 + cells]
    x = jnp.where(c > 0, c * m - (beside + lat_beside(m)), 0.0)
    sums_of = {2: dot(masked[...], m), 3: dot(y[own], m), 4: dot(z[2 * OV : 2 * OV + cells], x), 5: dot(m, x)}
    sent[...] = jnp.broadcast_to(in_lanes(row[...], sums_of)[None], sent.shape)


def finish(came, z, w, d_rows, edge, source, u_vel, v_vel, solution, u_new, v_new, w_vel,
           s_rows, u_rows, v_out, w_out, s_out, sems):
    cells, lat = source.shape
    total = jnp.broadcast_to(jnp.sum(came[...], axis=0), (8, LANE))
    place = [lax.broadcasted_iota(jnp.int32, (8, LANE), axis) for axis in range(2)]
    total = jnp.sum(jnp.where(place[0] == place[1], total, 0.0), axis=1, keepdims=True)
    rz, zy, rw, yw, zx, wx, ll = [total[i : i + 1] for i in range(7)]
    step0 = (rz + ll) / (zy + ll)
    rest = (zy - rz) / (zy + ll)
    new = rz - step0 * (zy + rw) + step0 * step0 * yw + rest * rest * ll
    beta = new / (rz + ll)
    grown = 1.0 + beta
    bent = grown * grown * zy - grown * step0 * (zx + yw) + step0 * step0 * wx
    step1 = new / (bent + (rest + beta) * (rest + beta) * ll)
    of_z = jnp.broadcast_to(step0 + step1 * grown, (OV, lat))
    of_w = jnp.broadcast_to(-step1 * step0, (OV, lat))
    of_land = jnp.broadcast_to(step0 + step1 * (rest + beta), (OV, lat))

    copies = []

    def send(held, result):
        copies.append(pltpu.make_async_copy(held, result, sems.at[len(copies)]))
        copies[-1].start()

    def surface_rows(at):
        s = of_z * z[at + OV : at + 2 * OV] + of_w * w[at : at + OV]
        if OV <= at < OV + cells:
            s = jnp.where(d_rows[at : at + OV] > 0, s, of_land * source[at - OV : at])
            s_out[at - OV : at] = s
        s_rows[at : at + OV] = s

    surface_rows(0)
    surface_rows(OV)
    slope = gravity_step * (s_rows[OV : OV + 1] - s_rows[OV - 1 : OV])
    d_west = jnp.minimum(d_rows[OV - 1 : OV], d_rows[OV : OV + 1])
    for level in range(KL):
        u = jnp.where(d_west > level, edge[level : level + 1] - slope, 0.0)
        u_rows[level, :OV] = jnp.broadcast_to(u, (OV, lat))
    zero = jnp.zeros((OV, 1), F32)
    for at in range(OV, OV + cells, OV):
        own = slice(at - OV, at)
        surface_rows(at + OV)
        s = s_rows[at : at + OV]
        d = d_rows[at : at + OV]
        slope = gravity_step * (s_rows[at + 1 : at + OV + 1] - s)
        face = jnp.minimum(d, d_rows[at + 1 : at + OV + 1])
        for level in range(KL):
            u_rows[level, at : at + OV] = jnp.where(face > level, u_vel[level, own] - slope, 0.0)
        send(u_rows.at[:, at : at + OV], u_new.at[:, own])
        slope = gravity_step * (jnp.concatenate([s[:, 1:], zero], axis=1) - s)
        face = jnp.minimum(d, jnp.concatenate([d[:, 1:], zero], axis=1))
        for level in range(KL):
            v_out[level, own] = jnp.where(face > level, v_vel[level, own] - slope, 0.0)
        send(v_out.at[:, own], v_new.at[:, own])
        w_sum = jnp.zeros((OV, lat), F32)
        for level in range(KL - 1, -1, -1):
            v = v_out[level, own]
            flow = u_rows[level, at : at + OV] - u_rows[level, at - 1 : at + OV - 1]
            flow = flow + (v - jnp.concatenate([zero, v[:, :-1]], axis=1))
            w_sum = w_sum + jnp.where(d > level, flow, 0.0)
            w_out[level, own] = w_sum
        send(w_out.at[:, own], w_vel.at[:, own])
        if at == cells:
            send(s_out, solution)
    for copy in copies:
        copy.wait()


def swap_pairs(block, outward):
    devices = lax.axis_size("lon")
    if outward:
        route = [(i, (i - 1 if i % 2 == 0 else i + 1) % devices) for i in range(devices)]
    else:
        route = [(i, i ^ 1) for i in range(devices)]
    return lax.ppermute(block, "lon", route)


def swap(inner, outer):
    outer = swap_pairs(outer, True)
    return outer, swap_pairs(inner, False)


def shape(*dims):
    return jax.ShapeDtypeStruct(dims, F32)


def body(source, diagonal, u_vel, v_vel, bottom):
    cells, lat = source.shape
    span = cells + 2 * OV
    devices = lax.axis_size("lon")
    parity = (lax.axis_index("lon") % 2).astype(jnp.int32).reshape(1)
    consts = [jnp.asarray(table) for table in tables(span)]
    hbm = {name: pltpu.with_memory_space_constraint(x, pltpu.HBM) for name, x in (
        ("source", source), ("diagonal", diagonal), ("u", u_vel), ("v", v_vel), ("bottom", bottom))}
    consts = [pltpu.with_memory_space_constraint(x, pltpu.HBM) for x in consts]

    outer = pl.pallas_call(
        first_edges,
        in_specs=[SM, HB, HB],
        out_specs=VM,
        out_shape=pltpu.VMEM((OV, lat), F32),
        scratch_shapes=[pltpu.VMEM((OV, lat), F32), pltpu.VMEM((OV, lat), jnp.int32),
                        pltpu.SemaphoreType.DMA((2,))],
        compiler_params=PARAMS,
        name="first_edges",
    )(parity, hbm["source"], hbm["bottom"])
    outer_in = swap_pairs(outer, True)

    inner, far_inner, far_outer, masked, coef, depth, source_v, *held = pl.pallas_call(
        prepare,
        in_specs=[SM] + [HB] * 8,
        out_specs=[VM] * 10,
        out_shape=[pltpu.VMEM((OV, lat), F32)]
        + [pltpu.VMEM((FAR, lat), F32)] * 2
        + [pltpu.VMEM((cells, lat), F32)] * 4
        + [pltpu.VMEM(table.shape, table.dtype) for table in consts],
        scratch_shapes=[
            pltpu.VMEM((cells, lat), F32),
            pltpu.VMEM((cells, lat), jnp.int32),
            pltpu.VMEM((KL, OV, lat), F32),
            pltpu.SemaphoreType.DMA((7,)),
        ],
        compiler_params=PARAMS,
        cost_estimate=pl.CostEstimate(flops=10**6, bytes_accessed=7 * 10**6, transcendentals=0),
        name="prepare",
    )(parity, outer, hbm["source"], hbm["diagonal"], hbm["bottom"], hbm["u"], *consts)
    near = swap_pairs(inner, False), outer_in
    far = swap(far_inner, far_outer)[::-1]

    blocks = -(-lat // LANE)
    first, inner, outer = pl.pallas_call(
        first_solve,
        in_specs=[SM] + [VM] * 6,
        out_specs=[VM] * 3,
        out_shape=[pltpu.VMEM((span, lat), F32)] + [pltpu.VMEM(((2 * OV + 1) * blocks, LANE), F32)] * 2,
        scratch_shapes=solve_scratch(span, lat),
        compiler_params=PARAMS,
        name="first_solve",
    )(parity, *near, masked, *held)
    near = swap(inner, outer)

    c_rows, z_rows, d_rows, edge = pl.pallas_call(
        absorb,
        in_specs=[SM] + [VM] * 5,
        out_specs=[VM] * 4,
        out_shape=[pltpu.VMEM((span + 2 * OV, lat), F32)] * 2
        + [pltpu.VMEM((span, lat), F32), pltpu.VMEM((OV, lat), F32)],
        compiler_params=PARAMS,
        cost_estimate=pl.CostEstimate(flops=10**6, bytes_accessed=7 * 10**6, transcendentals=0),
        name="absorb",
    )(parity, first, *far, coef, depth)

    z, y, second, inner, outer = pl.pallas_call(
        second_solve,
        in_specs=[SM] + [VM] * 7,
        out_specs=[VM] * 5,
        out_shape=[pltpu.VMEM((span + 2 * OV, lat), F32)]
        + [pltpu.VMEM((span, lat), F32)] * 2
        + [pltpu.VMEM(((OV + 1) * blocks, LANE), F32)] * 2,
        scratch_shapes=solve_scratch(span, lat),
        compiler_params=PARAMS,
        name="second_solve",
    )(parity, *near, z_rows, c_rows, *held)
    near = swap(inner, outer)

    w_rows, masked, row, u_v, v_v = pl.pallas_call(
        early_sums,
        in_specs=[VM] * 5 + [HB] * 2,
        out_specs=[VM] * 5,
        out_shape=[pltpu.VMEM((span, lat), F32), pltpu.VMEM((cells, lat), F32), pltpu.VMEM((1, LANE), F32)]
        + [pltpu.VMEM((KL, cells, lat), F32)] * 2,
        scratch_shapes=[pltpu.SemaphoreType.DMA((2,))],
        compiler_params=PARAMS,
        cost_estimate=pl.CostEstimate(flops=10**6, bytes_accessed=7 * 10**6, transcendentals=0),
        name="early_sums",
    )(z, y, c_rows, second, source_v, hbm["u"], hbm["v"])

    w, sent = pl.pallas_call(
        sums,
        in_specs=[SM] + [VM] * 8,
        out_specs=[VM] * 2,
        out_shape=[pltpu.VMEM((span, lat), F32), pltpu.VMEM((devices, 1, LANE), F32)],
        compiler_params=PARAMS,
        name="sums",
    )(parity, *near, w_rows, z, y, c_rows, masked, row)
    ring = [list(reversed(range(devices)))]
    came = lax.all_to_all(sent, "lon", 0, 0, axis_index_groups=ring)

    return pl.pallas_call(
        finish,
        in_specs=[VM] * 8,
        out_specs=[HB] * 4,
        out_shape=[shape(cells, lat)] + [shape(KL, cells, lat)] * 3,
        scratch_shapes=[pltpu.VMEM((span, lat), F32)]
        + [pltpu.VMEM((KL, OV + cells, lat), F32)]
        + [pltpu.VMEM((KL, cells, lat), F32)] * 2
        + [pltpu.VMEM((cells, lat), F32), pltpu.SemaphoreType.DMA((1 + 3 * (cells // OV),))],
        compiler_params=PARAMS,
        name="finish",
    )(came, z, w, d_rows, edge, source_v, u_v, v_v)


def solution(mesh):
    return jax.shard_map(
        body,
        mesh=mesh,
        in_specs=(
            P(("members", "lon"), None),
            P(("members", "lon"), None),
            P(None, ("members", "lon"), None),
            P(None, ("members", "lon"), None),
            P(("members", "lon"), None),
        ),
        out_specs=(
            P(("members", "lon"), None),
            P(None, ("members", "lon"), None),
            P(None, ("members", "lon"), None),
            P(None, ("members", "lon"), None),
        ),
        check_vma=False,
    )
```

```python
import math

import jax
import jax.numpy as jnp
import ml_dtypes
import numpy as np
from jax import lax
from jax.experimental import pallas as pl
from jax.experimental.pallas import tpu as pltpu
from jax.sharding import PartitionSpec as P

LT = 112
OV = 8
KL = 6
LANE = 128
FAR = 24

tile_shift = 0.1
gravity_step = 0.5

F32 = jnp.float32
BF16 = jnp.bfloat16
VM = pl.BlockSpec(memory_space=pltpu.VMEM)
SM = pl.BlockSpec(memory_space=pltpu.SMEM)
HB = pl.BlockSpec(memory_space=pl.ANY)
PARAMS = pltpu.CompilerParams(vmem_limit_bytes=32 * 1024 * 1024)


def sine_basis(length):
    ordinal = np.arange(length, dtype=np.float64) + 1.0
    angles = math.pi * ordinal[:, None] * ordinal[None, :] / (length + 1)
    basis_matrix = np.sqrt(2.0 / (length + 1)) * np.sin(angles)
    eigen_value = 2.0 - 2.0 * np.cos(math.pi * ordinal / (length + 1))
    return basis_matrix, eigen_value


def halves(matrix):
    high = matrix.astype(ml_dtypes.bfloat16)
    low = (matrix - high.astype(np.float64)).astype(ml_dtypes.bfloat16)
    return high, low


def tables(span):
    lon_basis, lon_value = sine_basis(span)
    lat_basis, lat_value = sine_basis(LT + 2 * OV)
    high, low = halves(lat_basis)
    lat = np.block([[high, low], [high, np.zeros_like(low)]])
    high, low = halves(lon_basis)
    lon = np.concatenate([high, low, high], axis=1)
    scale = 1.0 / (lon_value[:, None] + lat_value[None, :] + tile_shift)
    return lat, lon, scale.astype(np.float32)


def split(x):
    high = x.astype(BF16)
    return high, (x - high.astype(F32)).astype(BF16)


def tile_solve(x, lat_basis, lon, scale, rows, spectral, out):
    span, lat = out.shape
    tiles = lat // LT
    lane = lax.broadcasted_iota(jnp.int32, (span, LANE), 1)

    def block_of(b):
        if b < 0:
            return jnp.zeros((span, LANE), F32)
        return x[:, b * LANE : (b + 1) * LANE]

    chunk = 4
    groups = [range(first, min(first + chunk, tiles)) for first in range(0, tiles, chunk)]
    held = {}

    def lanes_of(group):
        return slice(group[0] * LANE, (group[-1] + 1) * LANE)

    def cut(group):
        for t in group:
            block, start = divmod(t * LT - OV, LANE)
            left, right = [pltpu.roll(block_of(b), LANE - start, 1) for b in (block, block + 1)]
            high, low = split(jnp.where(lane < LANE - start, left, right))
            rows[t * span : (t + 1) * span, :LANE] = high
            rows[t * span : (t + 1) * span, LANE:] = low

    def along_lat(group):
        product = jnp.dot(
            rows[group[0] * span : (group[-1] + 1) * span], lat_basis[...], preferred_element_type=F32
        )
        return product[:, :LANE] + product[:, LANE:]

    def lat_there(group):
        high, low = split(along_lat(group))
        for i, t in enumerate(group):
            at = slice(t * LANE, (t + 1) * LANE)
            spectral[:span, at] = high[i * span : (i + 1) * span]
            spectral[span : 2 * span, at] = high[i * span : (i + 1) * span]
            spectral[2 * span :, at] = low[i * span : (i + 1) * span]

    def lon_there(group):
        c = jnp.dot(lon[...], spectral[:, lanes_of(group)], preferred_element_type=F32)
        high, low = split(c * jnp.concatenate([scale[...]] * len(group), axis=1))
        spectral[:, lanes_of(group)] = jnp.concatenate([high, high, low], axis=0)

    def lon_back(group):
        c = jnp.dot(lon[...], spectral[:, lanes_of(group)], preferred_element_type=F32)
        high, low = split(c)
        for i, t in enumerate(group):
            at = slice(t * span, (t + 1) * span)
            rows[at, :LANE] = high[:, i * LANE : (i + 1) * LANE]
            rows[at, LANE:] = low[:, i * LANE : (i + 1) * LANE]

    def lat_back(group):
        product = along_lat(group)
        for i, t in enumerate(group):
            block, start = divmod(t * LT - OV, LANE)
            part = pltpu.roll(product[i * span : (i + 1) * span], start, 1)
            for b, inside in ((block, lane >= start), (block + 1, lane < start)):
                if 0 <= b * LANE < lat:
                    piece = jnp.where(inside, part, 0.0)
                    held[b] = held[b] + piece if b in held else piece
        done = (group[-1] + 1) * LT - OV if group[-1] + 1 < tiles else lat + LANE
        for b in [b for b in held if (b + 1) * LANE <= done]:
            width = min(LANE, lat - b * LANE)
            out[:, b * LANE : b * LANE + width] = held.pop(b)[:, :width]

    stages = [cut, lat_there, lon_there, lon_back, lat_back]
    for step in range(len(groups) + len(stages) - 1):
        for i in reversed(range(len(stages))):
            if 0 <= step - i < len(groups):
                stages[i](groups[step - i])


def wide_lanes(lat):
    return -(-(lat + OV) // LANE) * LANE


def solve_scratch(span, lat):
    tiles = lat // LT
    return [
        pltpu.VMEM((span, wide_lanes(lat)), F32),
        pltpu.VMEM((tiles * span, 2 * LANE), BF16),
        pltpu.VMEM((3 * span, tiles * LANE), BF16),
    ]


def pick(parity, inner, outer):
    even = jnp.full(inner.shape, parity[0], jnp.int32) == 0
    return jnp.where(even, outer, inner), jnp.where(even, inner, outer)


def lat_beside(m):
    zero = jnp.zeros((m.shape[0], 1), m.dtype)
    return jnp.concatenate([m[:, 1:], zero], axis=1) + jnp.concatenate([zero, m[:, :-1]], axis=1)


def pack(message, rows):
    n, lat = rows.shape
    for block, at in enumerate(range(0, lat, LANE)):
        width = min(LANE, lat - at)
        message[block * n : (block + 1) * n, :width] = rows[:, at : at + width]


def unpack(message, n, lat):
    blocks = [message[i * n : (i + 1) * n] for i in range(-(-lat // LANE))]
    return jnp.concatenate(blocks, axis=1)[:, :lat]


def first_edges(parity, source, bottom, outer, inner, rows, depth, sems):
    last = source.shape[0] - OV
    copies = []
    for i, start in enumerate((parity[0] * last, (1 - parity[0]) * last)):
        at = pl.ds(pl.multiple_of(start, OV), OV)
        copies.append(pltpu.make_async_copy(source.at[at], rows.at[i], sems.at[2 * i]))
        copies.append(pltpu.make_async_copy(bottom.at[at], depth.at[i], sems.at[2 * i + 1]))
    for copy in copies:
        copy.start()
    for copy in copies:
        copy.wait()
    outer[...] = jnp.where(depth[0] > 0, rows[0], 0.0)
    inner[...] = jnp.where(depth[1] > 0, rows[1], 0.0)


def prepare(parity, after, source_h, diagonal_h, bottom_h, u_h, *refs):
    tables_h, (far_inner, far_outer, masked, coef, depth, source), held = refs[:3], refs[3:9], refs[9:12]
    diagonal, bottom, u_strip, sems = refs[12:]
    cells, lat = source.shape
    pairs = [(source_h, source), (bottom_h, bottom), (diagonal_h, diagonal)]
    pairs += [(u_h.at[:, pl.ds(cells - OV, OV)], u_strip)]
    pairs += list(zip(tables_h, held))
    copies = [pltpu.make_async_copy(a, b, sems.at[i]) for i, (a, b) in enumerate(pairs)]
    for copy in copies:
        copy.start()
    for copy in copies[:4]:
        copy.wait()
    wet = bottom[...] > 0
    masked[...] = jnp.where(wet, source[...], 0.0)
    coef[...] = jnp.where(wet, 4.0 + diagonal[...], 0.0)
    depth[...] = bottom[...].astype(F32)
    edge = OV + 1
    blank = jnp.zeros((2 * OV - edge - 1, lat), F32)
    to_west = jnp.concatenate([coef[:edge], blank, depth[:1]], axis=0)
    u_rows = [u_strip[level, OV - 1 : OV] for level in range(KL)]
    to_east = jnp.concatenate(u_rows + [depth[cells - 1 :], coef[cells - edge :]], axis=0)
    far_outer[: 2 * OV], far_inner[: 2 * OV] = pick(parity, to_east, to_west)
    for message in (far_outer, far_inner):
        message[2 * OV :] = jnp.zeros((FAR - 2 * OV, lat), F32)
    for copy in copies[4:]:
        copy.wait()


def first_solve(parity, outer_in, inner_in, masked, lat_basis, lon, scale,
                first, inner, outer, wide, rows, spectral):
    cells, lat = masked.shape
    west, east = pick(parity, inner_in[...], outer_in[...])
    wide[:OV, :lat] = west
    wide[OV : OV + cells, :lat] = masked[...]
    wide[OV + cells :, :lat] = east
    wide[:, lat:] = jnp.zeros((cells + 2 * OV, wide.shape[1] - lat), F32)
    tile_solve(wide, lat_basis, lon, scale, rows, spectral, first)
    to_outer, to_inner = pick(parity, first[cells - 1 :], first[: 2 * OV + 1])
    pack(inner, to_inner)
    pack(outer, to_outer)


def absorb(parity, first, inner_in, outer_in, coef, depth, c_rows, z_rows, d_rows, edge):
    cells, lat = coef.shape
    west, east = pick(parity, inner_in[: 2 * OV], outer_in[: 2 * OV])
    edge[...] = west[:OV]
    d_rows[:OV] = jnp.broadcast_to(west[KL : KL + 1], (OV, lat))
    d_rows[OV : OV + cells] = depth[...]
    d_rows[OV + cells :] = jnp.broadcast_to(east[2 * OV - 1 :], (OV, lat))
    c_rows[: 2 * OV] = west
    c_rows[: OV - 1] = jnp.zeros((OV - 1, lat), F32)
    c_rows[2 * OV : 2 * OV + cells] = coef[...]
    c_rows[2 * OV + cells :] = east
    c_rows[3 * OV + cells + 1 :] = jnp.zeros((OV - 1, lat), F32)
    z_rows[:OV] = jnp.zeros((OV, lat), F32)
    z_rows[3 * OV + cells :] = jnp.zeros((OV, lat), F32)
    inside = slice(OV, 3 * OV + cells)
    z_rows[inside] = jnp.where(c_rows[inside] > 0, first[...], 0.0)


def second_solve(parity, outer_in, inner_in, z_rows, c_rows, lat_basis, lon, scale,
                 z, y, second, inner, outer, wide, rows, spectral):
    span, lat = y.shape
    cells = span - 2 * OV
    reach = 2 * OV + 1
    west, east = pick(parity, unpack(inner_in, reach, lat), unpack(outer_in, reach, lat))
    z[...] = z_rows[...]
    for came, start in ((west, OV - 1), (east, OV + cells)):
        at = slice(start, start + reach)
        z[at] += jnp.where(c_rows[at] > 0, came, 0.0)
    inside = slice(OV, OV + span)
    c, m = c_rows[inside], z[inside]
    beside = z[OV - 1 : OV - 1 + span] + z[OV + 1 : OV + 1 + span]
    image = jnp.where(c > 0, c * m - (beside + lat_beside(m)), 0.0)
    y[...] = image
    wide[:, :lat] = image
    wide[:, lat:] = jnp.zeros((span, wide.shape[1] - lat), F32)
    tile_solve(wide, lat_basis, lon, scale, rows, spectral, second)
    to_outer, to_inner = pick(parity, second[span - OV - 1 :], second[: OV + 1])
    pack(inner, to_inner)
    pack(outer, to_outer)


def dot(a, b):
    cells, lat = a.shape
    product = a * b
    rows = product[:OV]
    for at in range(OV, cells, OV):
        rows = rows + product[at : at + OV]
    whole = lat // LANE * LANE
    total = rows[:, :LANE]
    for at in range(LANE, whole, LANE):
        total = total + rows[:, at : at + LANE]
    if whole < lat:
        blank = jnp.zeros((OV, LANE - lat + whole), F32)
        total = total + jnp.concatenate([rows[:, whole:], blank], axis=1)
    return jnp.sum(jnp.sum(total, axis=0, keepdims=True), axis=1, keepdims=True)


def in_lanes(row, sums):
    lane = lax.broadcasted_iota(jnp.int32, row.shape, 1)
    for i, value in sums.items():
        row = jnp.where(lane == i, value, row)
    return row


def early_sums(z, y, c_rows, second, source, u_h, v_h, w_rows, masked, row, u, v, sems):
    copies = [pltpu.make_async_copy(a, b, sems.at[i]) for i, (a, b) in enumerate([(u_h, u), (v_h, v)])]
    for copy in copies:
        copy.start()
    cells, lat = source.shape
    inside = slice(OV, 3 * OV + cells)
    w_rows[...] = jnp.where(c_rows[inside] > 0, second[...], 0.0)
    own = slice(2 * OV, 2 * OV + cells)
    wet = c_rows[own] > 0
    masked[...] = jnp.where(wet, source[...], 0.0)
    land = jnp.where(wet, 0.0, source[...])
    z_own = z[own]
    sums_of = {0: dot(masked[...], z_own), 1: dot(z_own, y[OV : OV + cells]), 6: dot(land, land)}
    row[...] = in_lanes(jnp.zeros((1, LANE), F32), sums_of)
    for copy in copies:
        copy.wait()


def sums(parity, outer_in, inner_in, w_rows, z, y, c_rows, masked, row, w, sent):
    cells, lat = masked.shape
    west, east = pick(parity, unpack(inner_in, OV + 1, lat), unpack(outer_in, OV + 1, lat))
    w[...] = w_rows[...]
    for came, start in ((west, OV - 1), (east, cells)):
        wet = c_rows[OV + start : 2 * OV + start + 1] > 0
        w[start : start + OV + 1] += jnp.where(wet, came, 0.0)
    own = slice(OV, OV + cells)
    c, m = c_rows[2 * OV : 2 * OV + cells], w[own]
    beside = w[OV - 1 : OV - 1 + cells] + w[OV + 1 : OV + 1 + cells]
    x = jnp.where(c > 0, c * m - (beside + lat_beside(m)), 0.0)
    sums_of = {2: dot(masked[...], m), 3: dot(y[own], m), 4: dot(z[2 * OV : 2 * OV + cells], x), 5: dot(m, x)}
    sent[...] = jnp.broadcast_to(in_lanes(row[...], sums_of)[None], sent.shape)


def finish(came, z, w, d_rows, edge, source, u_vel, v_vel, solution, u_new, v_new, w_vel,
           s_rows, u_rows, v_out, w_out, s_out, sems):
    cells, lat = source.shape
    total = jnp.broadcast_to(jnp.sum(came[...], axis=0), (8, LANE))
    place = [lax.broadcasted_iota(jnp.int32, (8, LANE), axis) for axis in range(2)]
    total = jnp.sum(jnp.where(place[0] == place[1], total, 0.0), axis=1, keepdims=True)
    rz, zy, rw, yw, zx, wx, ll = [total[i : i + 1] for i in range(7)]
    step0 = (rz + ll) / (zy + ll)
    rest = (zy - rz) / (zy + ll)
    new = rz - step0 * (zy + rw) + step0 * step0 * yw + rest * rest * ll
    beta = new / (rz + ll)
    grown = 1.0 + beta
    bent = grown * grown * zy - grown * step0 * (zx + yw) + step0 * step0 * wx
    step1 = new / (bent + (rest + beta) * (rest + beta) * ll)
    of_z = jnp.broadcast_to(step0 + step1 * grown, (OV, lat))
    of_w = jnp.broadcast_to(-step1 * step0, (OV, lat))
    of_land = jnp.broadcast_to(step0 + step1 * (rest + beta), (OV, lat))

    copies = []

    def send(held, result):
        copies.append(pltpu.make_async_copy(held, result, sems.at[len(copies)]))
        copies[-1].start()

    def surface_rows(at):
        s = of_z * z[at + OV : at + 2 * OV] + of_w * w[at : at + OV]
        if OV <= at < OV + cells:
            s = jnp.where(d_rows[at : at + OV] > 0, s, of_land * source[at - OV : at])
            s_out[at - OV : at] = s
        s_rows[at : at + OV] = s

    surface_rows(0)
    surface_rows(OV)
    slope = gravity_step * (s_rows[OV : OV + 1] - s_rows[OV - 1 : OV])
    d_west = jnp.minimum(d_rows[OV - 1 : OV], d_rows[OV : OV + 1])
    for level in range(KL):
        u = jnp.where(d_west > level, edge[level : level + 1] - slope, 0.0)
        u_rows[level, :OV] = jnp.broadcast_to(u, (OV, lat))
    zero = jnp.zeros((OV, 1), F32)
    for at in range(OV, OV + cells, OV):
        own = slice(at - OV, at)
        surface_rows(at + OV)
        s = s_rows[at : at + OV]
        d = d_rows[at : at + OV]
        slope = gravity_step * (s_rows[at + 1 : at + OV + 1] - s)
        face = jnp.minimum(d, d_rows[at + 1 : at + OV + 1])
        for level in range(KL):
            u_rows[level, at : at + OV] = jnp.where(face > level, u_vel[level, own] - slope, 0.0)
        send(u_rows.at[:, at : at + OV], u_new.at[:, own])
        slope = gravity_step * (jnp.concatenate([s[:, 1:], zero], axis=1) - s)
        face = jnp.minimum(d, jnp.concatenate([d[:, 1:], zero], axis=1))
        for level in range(KL):
            v_out[level, own] = jnp.where(face > level, v_vel[level, own] - slope, 0.0)
        send(v_out.at[:, own], v_new.at[:, own])
        w_sum = jnp.zeros((OV, lat), F32)
        for level in range(KL - 1, -1, -1):
            v = v_out[level, own]
            flow = u_rows[level, at : at + OV] - u_rows[level, at - 1 : at + OV - 1]
            flow = flow + (v - jnp.concatenate([zero, v[:, :-1]], axis=1))
            w_sum = w_sum + jnp.where(d > level, flow, 0.0)
            w_out[level, own] = w_sum
        send(w_out.at[:, own], w_vel.at[:, own])
        if at == cells:
            send(s_out, solution)
    for copy in copies:
        copy.wait()


def swap_pairs(block, outward):
    devices = lax.axis_size("lon")
    if outward:
        route = [(i, (i - 1 if i % 2 == 0 else i + 1) % devices) for i in range(devices)]
    else:
        route = [(i, i ^ 1) for i in range(devices)]
    return lax.ppermute(block, "lon", route)


def swap(inner, outer):
    outer = swap_pairs(outer, True)
    return outer, swap_pairs(inner, False)


def shape(*dims):
    return jax.ShapeDtypeStruct(dims, F32)


def body(source, diagonal, u_vel, v_vel, bottom):
    cells, lat = source.shape
    span = cells + 2 * OV
    devices = lax.axis_size("lon")
    parity = (lax.axis_index("lon") % 2).astype(jnp.int32).reshape(1)
    consts = [jnp.asarray(table) for table in tables(span)]
    hbm = {name: pltpu.with_memory_space_constraint(x, pltpu.HBM) for name, x in (
        ("source", source), ("diagonal", diagonal), ("u", u_vel), ("v", v_vel), ("bottom", bottom))}
    consts = [pltpu.with_memory_space_constraint(x, pltpu.HBM) for x in consts]

    outer, inner = pl.pallas_call(
        first_edges,
        in_specs=[SM, HB, HB],
        out_specs=[VM] * 2,
        out_shape=[pltpu.VMEM((OV, lat), F32)] * 2,
        scratch_shapes=[pltpu.VMEM((2, OV, lat), F32), pltpu.VMEM((2, OV, lat), jnp.int32),
                        pltpu.SemaphoreType.DMA((4,))],
        compiler_params=PARAMS,
        name="first_edges",
    )(parity, hbm["source"], hbm["bottom"])
    near = swap(inner, outer)

    far_inner, far_outer, masked, coef, depth, source_v, *held = pl.pallas_call(
        prepare,
        in_specs=[SM] + [HB] * 8,
        out_specs=[VM] * 9,
        out_shape=[pltpu.VMEM((FAR, lat), F32)] * 2
        + [pltpu.VMEM((cells, lat), F32)] * 4
        + [pltpu.VMEM(table.shape, table.dtype) for table in consts],
        scratch_shapes=[
            pltpu.VMEM((cells, lat), F32),
            pltpu.VMEM((cells, lat), jnp.int32),
            pltpu.VMEM((KL, OV, lat), F32),
            pltpu.SemaphoreType.DMA((7,)),
        ],
        compiler_params=PARAMS,
        cost_estimate=pl.CostEstimate(flops=10**6, bytes_accessed=7 * 10**6, transcendentals=0),
        name="prepare",
    )(parity, inner, hbm["source"], hbm["diagonal"], hbm["bottom"], hbm["u"], *consts)
    far = swap(far_inner, far_outer)[::-1]

    blocks = -(-lat // LANE)
    first, inner, outer = pl.pallas_call(
        first_solve,
        in_specs=[SM] + [VM] * 6,
        out_specs=[VM] * 3,
        out_shape=[pltpu.VMEM((span, lat), F32)] + [pltpu.VMEM(((2 * OV + 1) * blocks, LANE), F32)] * 2,
        scratch_shapes=solve_scratch(span, lat),
        compiler_params=PARAMS,
        name="first_solve",
    )(parity, *near, masked, *held)
    near = swap(inner, outer)

    c_rows, z_rows, d_rows, edge = pl.pallas_call(
        absorb,
        in_specs=[SM] + [VM] * 5,
        out_specs=[VM] * 4,
        out_shape=[pltpu.VMEM((span + 2 * OV, lat), F32)] * 2
        + [pltpu.VMEM((span, lat), F32), pltpu.VMEM((OV, lat), F32)],
        compiler_params=PARAMS,
        cost_estimate=pl.CostEstimate(flops=10**6, bytes_accessed=7 * 10**6, transcendentals=0),
        name="absorb",
    )(parity, first, *far, coef, depth)

    z, y, second, inner, outer = pl.pallas_call(
        second_solve,
        in_specs=[SM] + [VM] * 7,
        out_specs=[VM] * 5,
        out_shape=[pltpu.VMEM((span + 2 * OV, lat), F32)]
        + [pltpu.VMEM((span, lat), F32)] * 2
        + [pltpu.VMEM(((OV + 1) * blocks, LANE), F32)] * 2,
        scratch_shapes=solve_scratch(span, lat),
        compiler_params=PARAMS,
        name="second_solve",
    )(parity, *near, z_rows, c_rows, *held)
    near = swap(inner, outer)

    w_rows, masked, row, u_v, v_v = pl.pallas_call(
        early_sums,
        in_specs=[VM] * 5 + [HB] * 2,
        out_specs=[VM] * 5,
        out_shape=[pltpu.VMEM((span, lat), F32), pltpu.VMEM((cells, lat), F32), pltpu.VMEM((1, LANE), F32)]
        + [pltpu.VMEM((KL, cells, lat), F32)] * 2,
        scratch_shapes=[pltpu.SemaphoreType.DMA((2,))],
        compiler_params=PARAMS,
        cost_estimate=pl.CostEstimate(flops=10**6, bytes_accessed=7 * 10**6, transcendentals=0),
        name="early_sums",
    )(z, y, c_rows, second, source_v, hbm["u"], hbm["v"])

    w, sent = pl.pallas_call(
        sums,
        in_specs=[SM] + [VM] * 8,
        out_specs=[VM] * 2,
        out_shape=[pltpu.VMEM((span, lat), F32), pltpu.VMEM((devices, 1, LANE), F32)],
        compiler_params=PARAMS,
        name="sums",
    )(parity, *near, w_rows, z, y, c_rows, masked, row)
    ring = [list(reversed(range(devices)))]
    came = lax.all_to_all(sent, "lon", 0, 0, axis_index_groups=ring)

    return pl.pallas_call(
        finish,
        in_specs=[VM] * 8,
        out_specs=[HB] * 4,
        out_shape=[shape(cells, lat)] + [shape(KL, cells, lat)] * 3,
        scratch_shapes=[pltpu.VMEM((span, lat), F32)]
        + [pltpu.VMEM((KL, OV + cells, lat), F32)]
        + [pltpu.VMEM((KL, cells, lat), F32)] * 2
        + [pltpu.VMEM((cells, lat), F32), pltpu.SemaphoreType.DMA((1 + 3 * (cells // OV),))],
        compiler_params=PARAMS,
        name="finish",
    )(came, z, w, d_rows, edge, source_v, u_v, v_v)


def solution(mesh):
    return jax.shard_map(
        body,
        mesh=mesh,
        in_specs=(
            P(("members", "lon"), None),
            P(("members", "lon"), None),
            P(None, ("members", "lon"), None),
            P(None, ("members", "lon"), None),
            P(("members", "lon"), None),
        ),
        out_specs=(
            P(("members", "lon"), None),
            P(None, ("members", "lon"), None),
            P(None, ("members", "lon"), None),
            P(None, ("members", "lon"), None),
        ),
        check_vma=False,
    )
```

```python
import math

import jax
import jax.numpy as jnp
import ml_dtypes
import numpy as np
from jax import lax
from jax.experimental import pallas as pl
from jax.experimental.pallas import tpu as pltpu
from jax.sharding import PartitionSpec as P

LT = 112
OV = 8
KL = 6
LANE = 128
FAR = 24

tile_shift = 0.1
gravity_step = 0.5

F32 = jnp.float32
BF16 = jnp.bfloat16
VM = pl.BlockSpec(memory_space=pltpu.VMEM)
SM = pl.BlockSpec(memory_space=pltpu.SMEM)
HB = pl.BlockSpec(memory_space=pl.ANY)
PARAMS = pltpu.CompilerParams(vmem_limit_bytes=32 * 1024 * 1024)


def sine_basis(length):
    ordinal = np.arange(length, dtype=np.float64) + 1.0
    angles = math.pi * ordinal[:, None] * ordinal[None, :] / (length + 1)
    basis_matrix = np.sqrt(2.0 / (length + 1)) * np.sin(angles)
    eigen_value = 2.0 - 2.0 * np.cos(math.pi * ordinal / (length + 1))
    return basis_matrix, eigen_value


def halves(matrix):
    high = matrix.astype(ml_dtypes.bfloat16)
    low = (matrix - high.astype(np.float64)).astype(ml_dtypes.bfloat16)
    return high, low


def tables(span):
    lon_basis, lon_value = sine_basis(span)
    lat_basis, lat_value = sine_basis(LT + 2 * OV)
    high, low = halves(lat_basis)
    lat = np.block([[high, low], [high, np.zeros_like(low)]])
    high, low = halves(lon_basis)
    lon = np.concatenate([high, low, high], axis=1)
    scale = 1.0 / (lon_value[:, None] + lat_value[None, :] + tile_shift)
    return lat, lon, scale.astype(np.float32)


def split(x):
    high = x.astype(BF16)
    return high, (x - high.astype(F32)).astype(BF16)


def tile_solve(x, lat_basis, lon, scale, rows, spectral, out):
    span, lat = out.shape
    tiles = lat // LT
    lane = lax.broadcasted_iota(jnp.int32, (span, LANE), 1)

    def block_of(b):
        if b < 0:
            return jnp.zeros((span, LANE), F32)
        return x[:, b * LANE : (b + 1) * LANE]

    chunk = 4
    groups = [range(first, min(first + chunk, tiles)) for first in range(0, tiles, chunk)]
    held = {}

    def lanes_of(group):
        return slice(group[0] * LANE, (group[-1] + 1) * LANE)

    def cut(group):
        for t in group:
            block, start = divmod(t * LT - OV, LANE)
            left, right = [pltpu.roll(block_of(b), LANE - start, 1) for b in (block, block + 1)]
            high, low = split(jnp.where(lane < LANE - start, left, right))
            rows[t * span : (t + 1) * span, :LANE] = high
            rows[t * span : (t + 1) * span, LANE:] = low

    def along_lat(group):
        product = jnp.dot(
            rows[group[0] * span : (group[-1] + 1) * span], lat_basis[...], preferred_element_type=F32
        )
        return product[:, :LANE] + product[:, LANE:]

    def lat_there(group):
        high, low = split(along_lat(group))
        for i, t in enumerate(group):
            at = slice(t * LANE, (t + 1) * LANE)
            spectral[:span, at] = high[i * span : (i + 1) * span]
            spectral[span : 2 * span, at] = high[i * span : (i + 1) * span]
            spectral[2 * span :, at] = low[i * span : (i + 1) * span]

    def lon_there(group):
        c = jnp.dot(lon[...], spectral[:, lanes_of(group)], preferred_element_type=F32)
        high, low = split(c * jnp.concatenate([scale[...]] * len(group), axis=1))
        spectral[:, lanes_of(group)] = jnp.concatenate([high, high, low], axis=0)

    def lon_back(group):
        c = jnp.dot(lon[...], spectral[:, lanes_of(group)], preferred_element_type=F32)
        high, low = split(c)
        for i, t in enumerate(group):
            at = slice(t * span, (t + 1) * span)
            rows[at, :LANE] = high[:, i * LANE : (i + 1) * LANE]
            rows[at, LANE:] = low[:, i * LANE : (i + 1) * LANE]

    def lat_back(group):
        product = along_lat(group)
        for i, t in enumerate(group):
            block, start = divmod(t * LT - OV, LANE)
            part = pltpu.roll(product[i * span : (i + 1) * span], start, 1)
            for b, inside in ((block, lane >= start), (block + 1, lane < start)):
                if 0 <= b * LANE < lat:
                    piece = jnp.where(inside, part, 0.0)
                    held[b] = held[b] + piece if b in held else piece
        done = (group[-1] + 1) * LT - OV if group[-1] + 1 < tiles else lat + LANE
        for b in [b for b in held if (b + 1) * LANE <= done]:
            width = min(LANE, lat - b * LANE)
            out[:, b * LANE : b * LANE + width] = held.pop(b)[:, :width]

    stages = [cut, lat_there, lon_there, lon_back, lat_back]
    for step in range(len(groups) + len(stages) - 1):
        for i in reversed(range(len(stages))):
            if 0 <= step - i < len(groups):
                stages[i](groups[step - i])


def wide_lanes(lat):
    return -(-(lat + OV) // LANE) * LANE


def solve_scratch(span, lat):
    tiles = lat // LT
    return [
        pltpu.VMEM((span, wide_lanes(lat)), F32),
        pltpu.VMEM((tiles * span, 2 * LANE), BF16),
        pltpu.VMEM((3 * span, tiles * LANE), BF16),
    ]


def pick(parity, inner, outer):
    even = jnp.full(inner.shape, parity[0], jnp.int32) == 0
    return jnp.where(even, outer, inner), jnp.where(even, inner, outer)


def lat_beside(m):
    zero = jnp.zeros((m.shape[0], 1), m.dtype)
    return jnp.concatenate([m[:, 1:], zero], axis=1) + jnp.concatenate([zero, m[:, :-1]], axis=1)


def pack(message, rows):
    n, lat = rows.shape
    for block, at in enumerate(range(0, lat, LANE)):
        width = min(LANE, lat - at)
        message[block * n : (block + 1) * n, :width] = rows[:, at : at + width]


def unpack(message, n, lat):
    blocks = [message[i * n : (i + 1) * n] for i in range(-(-lat // LANE))]
    return jnp.concatenate(blocks, axis=1)[:, :lat]


def first_edges(parity, source, bottom, outer, inner, rows, depth, sems):
    last = source.shape[0] - OV
    copies = []
    for i, start in enumerate((parity[0] * last, (1 - parity[0]) * last)):
        at = pl.ds(pl.multiple_of(start, OV), OV)
        copies.append(pltpu.make_async_copy(source.at[at], rows.at[i], sems.at[2 * i]))
        copies.append(pltpu.make_async_copy(bottom.at[at], depth.at[i], sems.at[2 * i + 1]))
    for copy in copies:
        copy.start()
    for copy in copies:
        copy.wait()
    outer[...] = jnp.where(depth[0] > 0, rows[0], 0.0)
    inner[...] = jnp.where(depth[1] > 0, rows[1], 0.0)


def prepare(parity, after, source_h, diagonal_h, bottom_h, u_h, *refs):
    tables_h, (far_inner, far_outer, masked, coef, depth, source), held = refs[:3], refs[3:9], refs[9:12]
    diagonal, bottom, u_strip, sems = refs[12:]
    cells, lat = source.shape
    pairs = [(source_h, source), (bottom_h, bottom), (diagonal_h, diagonal)]
    pairs += [(u_h.at[:, pl.ds(cells - OV, OV)], u_strip)]
    pairs += list(zip(tables_h, held))
    copies = [pltpu.make_async_copy(a, b, sems.at[i]) for i, (a, b) in enumerate(pairs)]
    for copy in copies:
        copy.start()
    for copy in copies[:4]:
        copy.wait()
    wet = bottom[...] > 0
    masked[...] = jnp.where(wet, source[...], 0.0)
    coef[...] = jnp.where(wet, 4.0 + diagonal[...], 0.0)
    depth[...] = bottom[...].astype(F32)
    edge = OV + 1
    blank = jnp.zeros((2 * OV - edge - 1, lat), F32)
    to_west = jnp.concatenate([coef[:edge], blank, depth[:1]], axis=0)
    u_rows = [u_strip[level, OV - 1 : OV] for level in range(KL)]
    to_east = jnp.concatenate(u_rows + [depth[cells - 1 :], coef[cells - edge :]], axis=0)
    far_outer[: 2 * OV], far_inner[: 2 * OV] = pick(parity, to_east, to_west)
    for message in (far_outer, far_inner):
        message[2 * OV :] = jnp.zeros((FAR - 2 * OV, lat), F32)
    for copy in copies[4:]:
        copy.wait()


def first_solve(parity, outer_in, inner_in, masked, lat_basis, lon, scale,
                first, inner, outer, wide, rows, spectral):
    cells, lat = masked.shape
    west, east = pick(parity, inner_in[...], outer_in[...])
    wide[:OV, :lat] = west
    wide[OV : OV + cells, :lat] = masked[...]
    wide[OV + cells :, :lat] = east
    wide[:, lat:] = jnp.zeros((cells + 2 * OV, wide.shape[1] - lat), F32)
    tile_solve(wide, lat_basis, lon, scale, rows, spectral, first)
    to_outer, to_inner = pick(parity, first[cells - 1 :], first[: 2 * OV + 1])
    pack(inner, to_inner)
    pack(outer, to_outer)


def absorb(parity, first, outer_in, inner_in, coef, depth, c_rows, z_rows, d_rows, edge):
    cells, lat = coef.shape
    west, east = pick(parity, inner_in[: 2 * OV], outer_in[: 2 * OV])
    edge[...] = west[:OV]
    d_rows[:OV] = jnp.broadcast_to(west[KL : KL + 1], (OV, lat))
    d_rows[OV : OV + cells] = depth[...]
    d_rows[OV + cells :] = jnp.broadcast_to(east[2 * OV - 1 :], (OV, lat))
    c_rows[: 2 * OV] = west
    c_rows[: OV - 1] = jnp.zeros((OV - 1, lat), F32)
    c_rows[2 * OV : 2 * OV + cells] = coef[...]
    c_rows[2 * OV + cells :] = east
    c_rows[3 * OV + cells + 1 :] = jnp.zeros((OV - 1, lat), F32)
    z_rows[:OV] = jnp.zeros((OV, lat), F32)
    z_rows[3 * OV + cells :] = jnp.zeros((OV, lat), F32)
    inside = slice(OV, 3 * OV + cells)
    z_rows[inside] = jnp.where(c_rows[inside] > 0, first[...], 0.0)


def second_solve(parity, outer_in, inner_in, z_rows, c_rows, lat_basis, lon, scale,
                 z, y, second, inner, outer, wide, rows, spectral):
    span, lat = y.shape
    cells = span - 2 * OV
    reach = 2 * OV + 1
    west, east = pick(parity, unpack(inner_in, reach, lat), unpack(outer_in, reach, lat))
    z[...] = z_rows[...]
    for came, start in ((west, OV - 1), (east, OV + cells)):
        at = slice(start, start + reach)
        z[at] += jnp.where(c_rows[at] > 0, came, 0.0)
    inside = slice(OV, OV + span)
    c, m = c_rows[inside], z[inside]
    beside = z[OV - 1 : OV - 1 + span] + z[OV + 1 : OV + 1 + span]
    image = jnp.where(c > 0, c * m - (beside + lat_beside(m)), 0.0)
    y[...] = image
    wide[:, :lat] = image
    wide[:, lat:] = jnp.zeros((span, wide.shape[1] - lat), F32)
    tile_solve(wide, lat_basis, lon, scale, rows, spectral, second)
    to_outer, to_inner = pick(parity, second[span - OV - 1 :], second[: OV + 1])
    pack(inner, to_inner)
    pack(outer, to_outer)


def dot(a, b):
    cells, lat = a.shape
    product = a * b
    rows = product[:OV]
    for at in range(OV, cells, OV):
        rows = rows + product[at : at + OV]
    whole = lat // LANE * LANE
    total = rows[:, :LANE]
    for at in range(LANE, whole, LANE):
        total = total + rows[:, at : at + LANE]
    if whole < lat:
        blank = jnp.zeros((OV, LANE - lat + whole), F32)
        total = total + jnp.concatenate([rows[:, whole:], blank], axis=1)
    return jnp.sum(jnp.sum(total, axis=0, keepdims=True), axis=1, keepdims=True)


def in_lanes(row, sums):
    lane = lax.broadcasted_iota(jnp.int32, row.shape, 1)
    for i, value in sums.items():
        row = jnp.where(lane == i, value, row)
    return row


def early_sums(z, y, c_rows, second, source, u_h, v_h, w_rows, masked, row, u, v, sems):
    copies = [pltpu.make_async_copy(a, b, sems.at[i]) for i, (a, b) in enumerate([(u_h, u), (v_h, v)])]
    for copy in copies:
        copy.start()
    cells, lat = source.shape
    inside = slice(OV, 3 * OV + cells)
    w_rows[...] = jnp.where(c_rows[inside] > 0, second[...], 0.0)
    own = slice(2 * OV, 2 * OV + cells)
    wet = c_rows[own] > 0
    masked[...] = jnp.where(wet, source[...], 0.0)
    land = jnp.where(wet, 0.0, source[...])
    z_own = z[own]
    sums_of = {0: dot(masked[...], z_own), 1: dot(z_own, y[OV : OV + cells]), 6: dot(land, land)}
    row[...] = in_lanes(jnp.zeros((1, LANE), F32), sums_of)
    for copy in copies:
        copy.wait()


def sums(parity, outer_in, inner_in, w_rows, z, y, c_rows, masked, row, w, sent):
    cells, lat = masked.shape
    west, east = pick(parity, unpack(inner_in, OV + 1, lat), unpack(outer_in, OV + 1, lat))
    w[...] = w_rows[...]
    for came, start in ((west, OV - 1), (east, cells)):
        wet = c_rows[OV + start : 2 * OV + start + 1] > 0
        w[start : start + OV + 1] += jnp.where(wet, came, 0.0)
    own = slice(OV, OV + cells)
    c, m = c_rows[2 * OV : 2 * OV + cells], w[own]
    beside = w[OV - 1 : OV - 1 + cells] + w[OV + 1 : OV + 1 + cells]
    x = jnp.where(c > 0, c * m - (beside + lat_beside(m)), 0.0)
    sums_of = {2: dot(masked[...], m), 3: dot(y[own], m), 4: dot(z[2 * OV : 2 * OV + cells], x), 5: dot(m, x)}
    sent[...] = jnp.broadcast_to(in_lanes(row[...], sums_of)[None], sent.shape)


def finish(came, z, w, d_rows, edge, source, u_vel, v_vel, solution, u_new, v_new, w_vel,
           s_rows, u_rows, v_out, w_out, s_out, sems):
    cells, lat = source.shape
    total = jnp.broadcast_to(jnp.sum(came[...], axis=0), (8, LANE))
    place = [lax.broadcasted_iota(jnp.int32, (8, LANE), axis) for axis in range(2)]
    total = jnp.sum(jnp.where(place[0] == place[1], total, 0.0), axis=1, keepdims=True)
    rz, zy, rw, yw, zx, wx, ll = [total[i : i + 1] for i in range(7)]
    step0 = (rz + ll) / (zy + ll)
    rest = (zy - rz) / (zy + ll)
    new = rz - step0 * (zy + rw) + step0 * step0 * yw + rest * rest * ll
    beta = new / (rz + ll)
    grown = 1.0 + beta
    bent = grown * grown * zy - grown * step0 * (zx + yw) + step0 * step0 * wx
    step1 = new / (bent + (rest + beta) * (rest + beta) * ll)
    of_z = jnp.broadcast_to(step0 + step1 * grown, (OV, lat))
    of_w = jnp.broadcast_to(-step1 * step0, (OV, lat))
    of_land = jnp.broadcast_to(step0 + step1 * (rest + beta), (OV, lat))

    copies = []

    def send(held, result):
        copies.append(pltpu.make_async_copy(held, result, sems.at[len(copies)]))
        copies[-1].start()

    def surface_rows(at):
        s = of_z * z[at + OV : at + 2 * OV] + of_w * w[at : at + OV]
        if OV <= at < OV + cells:
            s = jnp.where(d_rows[at : at + OV] > 0, s, of_land * source[at - OV : at])
            s_out[at - OV : at] = s
        s_rows[at : at + OV] = s

    surface_rows(0)
    surface_rows(OV)
    slope = gravity_step * (s_rows[OV : OV + 1] - s_rows[OV - 1 : OV])
    d_west = jnp.minimum(d_rows[OV - 1 : OV], d_rows[OV : OV + 1])
    for level in range(KL):
        u = jnp.where(d_west > level, edge[level : level + 1] - slope, 0.0)
        u_rows[level, :OV] = jnp.broadcast_to(u, (OV, lat))
    zero = jnp.zeros((OV, 1), F32)
    for at in range(OV, OV + cells, OV):
        own = slice(at - OV, at)
        surface_rows(at + OV)
        s = s_rows[at : at + OV]
        d = d_rows[at : at + OV]
        slope = gravity_step * (s_rows[at + 1 : at + OV + 1] - s)
        face = jnp.minimum(d, d_rows[at + 1 : at + OV + 1])
        for level in range(KL):
            u_rows[level, at : at + OV] = jnp.where(face > level, u_vel[level, own] - slope, 0.0)
        send(u_rows.at[:, at : at + OV], u_new.at[:, own])
        slope = gravity_step * (jnp.concatenate([s[:, 1:], zero], axis=1) - s)
        face = jnp.minimum(d, jnp.concatenate([d[:, 1:], zero], axis=1))
        for level in range(KL):
            v_out[level, own] = jnp.where(face > level, v_vel[level, own] - slope, 0.0)
        send(v_out.at[:, own], v_new.at[:, own])
        w_sum = jnp.zeros((OV, lat), F32)
        for level in range(KL - 1, -1, -1):
            v = v_out[level, own]
            flow = u_rows[level, at : at + OV] - u_rows[level, at - 1 : at + OV - 1]
            flow = flow + (v - jnp.concatenate([zero, v[:, :-1]], axis=1))
            w_sum = w_sum + jnp.where(d > level, flow, 0.0)
            w_out[level, own] = w_sum
        send(w_out.at[:, own], w_vel.at[:, own])
        if at == cells:
            send(s_out, solution)
    for copy in copies:
        copy.wait()


def swap_pairs(block, outward):
    devices = lax.axis_size("lon")
    if outward:
        route = [(i, (i - 1 if i % 2 == 0 else i + 1) % devices) for i in range(devices)]
    else:
        route = [(i, i ^ 1) for i in range(devices)]
    return lax.ppermute(block, "lon", route)


def swap(inner, outer):
    outer = swap_pairs(outer, True)
    return outer, swap_pairs(inner, False)


def shape(*dims):
    return jax.ShapeDtypeStruct(dims, F32)


def body(source, diagonal, u_vel, v_vel, bottom):
    cells, lat = source.shape
    span = cells + 2 * OV
    devices = lax.axis_size("lon")
    parity = (lax.axis_index("lon") % 2).astype(jnp.int32).reshape(1)
    consts = [jnp.asarray(table) for table in tables(span)]
    hbm = {name: pltpu.with_memory_space_constraint(x, pltpu.HBM) for name, x in (
        ("source", source), ("diagonal", diagonal), ("u", u_vel), ("v", v_vel), ("bottom", bottom))}
    consts = [pltpu.with_memory_space_constraint(x, pltpu.HBM) for x in consts]

    outer, inner = pl.pallas_call(
        first_edges,
        in_specs=[SM, HB, HB],
        out_specs=[VM] * 2,
        out_shape=[pltpu.VMEM((OV, lat), F32)] * 2,
        scratch_shapes=[pltpu.VMEM((2, OV, lat), F32), pltpu.VMEM((2, OV, lat), jnp.int32),
                        pltpu.SemaphoreType.DMA((4,))],
        compiler_params=PARAMS,
        name="first_edges",
    )(parity, hbm["source"], hbm["bottom"])
    near = swap(inner, outer)

    far_inner, far_outer, masked, coef, depth, source_v, *held = pl.pallas_call(
        prepare,
        in_specs=[SM] + [HB] * 8,
        out_specs=[VM] * 9,
        out_shape=[pltpu.VMEM((FAR, lat), F32)] * 2
        + [pltpu.VMEM((cells, lat), F32)] * 4
        + [pltpu.VMEM(table.shape, table.dtype) for table in consts],
        scratch_shapes=[
            pltpu.VMEM((cells, lat), F32),
            pltpu.VMEM((cells, lat), jnp.int32),
            pltpu.VMEM((KL, OV, lat), F32),
            pltpu.SemaphoreType.DMA((7,)),
        ],
        compiler_params=PARAMS,
        cost_estimate=pl.CostEstimate(flops=10**6, bytes_accessed=7 * 10**6, transcendentals=0),
        name="prepare",
    )(parity, inner, hbm["source"], hbm["diagonal"], hbm["bottom"], hbm["u"], *consts)
    far = swap(far_inner, far_outer)

    blocks = -(-lat // LANE)
    first, inner, outer = pl.pallas_call(
        first_solve,
        in_specs=[SM] + [VM] * 6,
        out_specs=[VM] * 3,
        out_shape=[pltpu.VMEM((span, lat), F32)] + [pltpu.VMEM(((2 * OV + 1) * blocks, LANE), F32)] * 2,
        scratch_shapes=solve_scratch(span, lat),
        compiler_params=PARAMS,
        name="first_solve",
    )(parity, *near, masked, *held)
    near = swap(inner, outer)

    c_rows, z_rows, d_rows, edge = pl.pallas_call(
        absorb,
        in_specs=[SM] + [VM] * 5,
        out_specs=[VM] * 4,
        out_shape=[pltpu.VMEM((span + 2 * OV, lat), F32)] * 2
        + [pltpu.VMEM((span, lat), F32), pltpu.VMEM((OV, lat), F32)],
        compiler_params=PARAMS,
        cost_estimate=pl.CostEstimate(flops=10**6, bytes_accessed=7 * 10**6, transcendentals=0),
        name="absorb",
    )(parity, first, *far, coef, depth)

    z, y, second, inner, outer = pl.pallas_call(
        second_solve,
        in_specs=[SM] + [VM] * 7,
        out_specs=[VM] * 5,
        out_shape=[pltpu.VMEM((span + 2 * OV, lat), F32)]
        + [pltpu.VMEM((span, lat), F32)] * 2
        + [pltpu.VMEM(((OV + 1) * blocks, LANE), F32)] * 2,
        scratch_shapes=solve_scratch(span, lat),
        compiler_params=PARAMS,
        name="second_solve",
    )(parity, *near, z_rows, c_rows, *held)
    near = swap(inner, outer)

    w_rows, masked, row, u_v, v_v = pl.pallas_call(
        early_sums,
        in_specs=[VM] * 5 + [HB] * 2,
        out_specs=[VM] * 5,
        out_shape=[pltpu.VMEM((span, lat), F32), pltpu.VMEM((cells, lat), F32), pltpu.VMEM((1, LANE), F32)]
        + [pltpu.VMEM((KL, cells, lat), F32)] * 2,
        scratch_shapes=[pltpu.SemaphoreType.DMA((2,))],
        compiler_params=PARAMS,
        cost_estimate=pl.CostEstimate(flops=10**6, bytes_accessed=7 * 10**6, transcendentals=0),
        name="early_sums",
    )(z, y, c_rows, second, source_v, hbm["u"], hbm["v"])

    w, sent = pl.pallas_call(
        sums,
        in_specs=[SM] + [VM] * 8,
        out_specs=[VM] * 2,
        out_shape=[pltpu.VMEM((span, lat), F32), pltpu.VMEM((devices, 1, LANE), F32)],
        compiler_params=PARAMS,
        name="sums",
    )(parity, *near, w_rows, z, y, c_rows, masked, row)
    ring = [list(reversed(range(devices)))]
    came = lax.all_to_all(sent, "lon", 0, 0, axis_index_groups=ring)

    return pl.pallas_call(
        finish,
        in_specs=[VM] * 8,
        out_specs=[HB] * 4,
        out_shape=[shape(cells, lat)] + [shape(KL, cells, lat)] * 3,
        scratch_shapes=[pltpu.VMEM((span, lat), F32)]
        + [pltpu.VMEM((KL, OV + cells, lat), F32)]
        + [pltpu.VMEM((KL, cells, lat), F32)] * 2
        + [pltpu.VMEM((cells, lat), F32), pltpu.SemaphoreType.DMA((1 + 3 * (cells // OV),))],
        compiler_params=PARAMS,
        name="finish",
    )(came, z, w, d_rows, edge, source_v, u_v, v_v)


def solution(mesh):
    return jax.shard_map(
        body,
        mesh=mesh,
        in_specs=(
            P(("members", "lon"), None),
            P(("members", "lon"), None),
            P(None, ("members", "lon"), None),
            P(None, ("members", "lon"), None),
            P(("members", "lon"), None),
        ),
        out_specs=(
            P(("members", "lon"), None),
            P(None, ("members", "lon"), None),
            P(None, ("members", "lon"), None),
            P(None, ("members", "lon"), None),
        ),
        check_vma=False,
    )
```

```python
import math

import jax
import jax.numpy as jnp
import ml_dtypes
import numpy as np
from jax import lax
from jax.experimental import pallas as pl
from jax.experimental.pallas import tpu as pltpu
from jax.sharding import PartitionSpec as P

LT = 112
OV = 8
KL = 6
LANE = 128
FAR = 24

tile_shift = 0.1
gravity_step = 0.5

F32 = jnp.float32
BF16 = jnp.bfloat16
VM = pl.BlockSpec(memory_space=pltpu.VMEM)
SM = pl.BlockSpec(memory_space=pltpu.SMEM)
HB = pl.BlockSpec(memory_space=pl.ANY)
PARAMS = pltpu.CompilerParams(vmem_limit_bytes=32 * 1024 * 1024)


def sine_basis(length):
    ordinal = np.arange(length, dtype=np.float64) + 1.0
    angles = math.pi * ordinal[:, None] * ordinal[None, :] / (length + 1)
    basis_matrix = np.sqrt(2.0 / (length + 1)) * np.sin(angles)
    eigen_value = 2.0 - 2.0 * np.cos(math.pi * ordinal / (length + 1))
    return basis_matrix, eigen_value


def halves(matrix):
    high = matrix.astype(ml_dtypes.bfloat16)
    low = (matrix - high.astype(np.float64)).astype(ml_dtypes.bfloat16)
    return high, low


def tables(span):
    lon_basis, lon_value = sine_basis(span)
    lat_basis, lat_value = sine_basis(LT + 2 * OV)
    high, low = halves(lat_basis)
    lat = np.block([[high, low], [high, np.zeros_like(low)]])
    high, low = halves(lon_basis)
    lon = np.concatenate([high, low, high], axis=1)
    scale = 1.0 / (lon_value[:, None] + lat_value[None, :] + tile_shift)
    return lat, lon, scale.astype(np.float32)


def split(x):
    high = x.astype(BF16)
    return high, (x - high.astype(F32)).astype(BF16)


def tile_solve(x, lat_basis, lon, scale, rows, spectral, out):
    span, lat = out.shape
    tiles = lat // LT
    lane = lax.broadcasted_iota(jnp.int32, (span, LANE), 1)

    def block_of(b):
        if b < 0:
            return jnp.zeros((span, LANE), F32)
        return x[:, b * LANE : (b + 1) * LANE]

    chunk = 4
    groups = [range(first, min(first + chunk, tiles)) for first in range(0, tiles, chunk)]
    held = {}

    def lanes_of(group):
        return slice(group[0] * LANE, (group[-1] + 1) * LANE)

    def cut(group):
        for t in group:
            block, start = divmod(t * LT - OV, LANE)
            left, right = [pltpu.roll(block_of(b), LANE - start, 1) for b in (block, block + 1)]
            high, low = split(jnp.where(lane < LANE - start, left, right))
            rows[t * span : (t + 1) * span, :LANE] = high
            rows[t * span : (t + 1) * span, LANE:] = low

    def along_lat(group):
        product = jnp.dot(
            rows[group[0] * span : (group[-1] + 1) * span], lat_basis[...], preferred_element_type=F32
        )
        return product[:, :LANE] + product[:, LANE:]

    def lat_there(group):
        high, low = split(along_lat(group))
        for i, t in enumerate(group):
            at = slice(t * LANE, (t + 1) * LANE)
            spectral[:span, at] = high[i * span : (i + 1) * span]
            spectral[span : 2 * span, at] = high[i * span : (i + 1) * span]
            spectral[2 * span :, at] = low[i * span : (i + 1) * span]

    def lon_there(group):
        c = jnp.dot(lon[...], spectral[:, lanes_of(group)], preferred_element_type=F32)
        high, low = split(c * jnp.concatenate([scale[...]] * len(group), axis=1))
        spectral[:, lanes_of(group)] = jnp.concatenate([high, high, low], axis=0)

    def lon_back(group):
        c = jnp.dot(lon[...], spectral[:, lanes_of(group)], preferred_element_type=F32)
        high, low = split(c)
        for i, t in enumerate(group):
            at = slice(t * span, (t + 1) * span)
            rows[at, :LANE] = high[:, i * LANE : (i + 1) * LANE]
            rows[at, LANE:] = low[:, i * LANE : (i + 1) * LANE]

    def lat_back(group):
        product = along_lat(group)
        for i, t in enumerate(group):
            block, start = divmod(t * LT - OV, LANE)
            part = pltpu.roll(product[i * span : (i + 1) * span], start, 1)
            for b, inside in ((block, lane >= start), (block + 1, lane < start)):
                if 0 <= b * LANE < lat:
                    piece = jnp.where(inside, part, 0.0)
                    held[b] = held[b] + piece if b in held else piece
        done = (group[-1] + 1) * LT - OV if group[-1] + 1 < tiles else lat + LANE
        for b in [b for b in held if (b + 1) * LANE <= done]:
            width = min(LANE, lat - b * LANE)
            out[:, b * LANE : b * LANE + width] = held.pop(b)[:, :width]

    stages = [cut, lat_there, lon_there, lon_back, lat_back]
    for step in range(len(groups) + len(stages) - 1):
        for i in reversed(range(len(stages))):
            if 0 <= step - i < len(groups):
                stages[i](groups[step - i])


def wide_lanes(lat):
    return -(-(lat + OV) // LANE) * LANE


def solve_scratch(span, lat):
    tiles = lat // LT
    return [
        pltpu.VMEM((span, wide_lanes(lat)), F32),
        pltpu.VMEM((tiles * span, 2 * LANE), BF16),
        pltpu.VMEM((3 * span, tiles * LANE), BF16),
    ]


def pick(parity, inner, outer):
    even = jnp.full(inner.shape, parity[0], jnp.int32) == 0
    return jnp.where(even, outer, inner), jnp.where(even, inner, outer)


def lat_beside(m):
    zero = jnp.zeros((m.shape[0], 1), m.dtype)
    return jnp.concatenate([m[:, 1:], zero], axis=1) + jnp.concatenate([zero, m[:, :-1]], axis=1)


def pack(message, rows):
    n, lat = rows.shape
    for block, at in enumerate(range(0, lat, LANE)):
        width = min(LANE, lat - at)
        message[block * n : (block + 1) * n, :width] = rows[:, at : at + width]


def unpack(message, n, lat):
    blocks = [message[i * n : (i + 1) * n] for i in range(-(-lat // LANE))]
    return jnp.concatenate(blocks, axis=1)[:, :lat]


def first_edges(parity, source, bottom, outer, inner, rows, depth, sems):
    last = source.shape[0] - OV
    copies = []
    for i, start in enumerate((parity[0] * last, (1 - parity[0]) * last)):
        at = pl.ds(pl.multiple_of(start, OV), OV)
        copies.append(pltpu.make_async_copy(source.at[at], rows.at[i], sems.at[2 * i]))
        copies.append(pltpu.make_async_copy(bottom.at[at], depth.at[i], sems.at[2 * i + 1]))
    for copy in copies:
        copy.start()
    for copy in copies:
        copy.wait()
    outer[...] = jnp.where(depth[0] > 0, rows[0], 0.0)
    inner[...] = jnp.where(depth[1] > 0, rows[1], 0.0)


def prepare(parity, after, source_h, diagonal_h, bottom_h, u_h, *refs):
    tables_h, (far_inner, far_outer, masked, coef, depth, source), held = refs[:3], refs[3:9], refs[9:12]
    diagonal, bottom, u_strip, sems = refs[12:]
    cells, lat = source.shape
    pairs = [(source_h, source), (bottom_h, bottom), (diagonal_h, diagonal)]
    pairs += [(u_h.at[:, pl.ds(cells - OV, OV)], u_strip)]
    pairs += list(zip(tables_h, held))
    copies = [pltpu.make_async_copy(a, b, sems.at[i]) for i, (a, b) in enumerate(pairs)]
    for copy in copies:
        copy.start()
    for copy in copies[:4]:
        copy.wait()
    wet = bottom[...] > 0
    masked[...] = jnp.where(wet, source[...], 0.0)
    coef[...] = jnp.where(wet, 4.0 + diagonal[...], 0.0)
    depth[...] = bottom[...].astype(F32)
    edge = OV + 1
    blank = jnp.zeros((2 * OV - edge - 1, lat), F32)
    to_west = jnp.concatenate([coef[:edge], blank, depth[:1]], axis=0)
    u_rows = [u_strip[level, OV - 1 : OV] for level in range(KL)]
    to_east = jnp.concatenate(u_rows + [depth[cells - 1 :], coef[cells - edge :]], axis=0)
    far_outer[: 2 * OV], far_inner[: 2 * OV] = pick(parity, to_east, to_west)
    for message in (far_outer, far_inner):
        message[2 * OV :] = jnp.zeros((FAR - 2 * OV, lat), F32)
    for copy in copies[4:]:
        copy.wait()


def first_solve(parity, outer_in, inner_in, masked, lat_basis, lon, scale,
                first, inner, outer, wide, rows, spectral):
    cells, lat = masked.shape
    west, east = pick(parity, inner_in[...], outer_in[...])
    wide[:OV, :lat] = west
    wide[OV : OV + cells, :lat] = masked[...]
    wide[OV + cells :, :lat] = east
    wide[:, lat:] = jnp.zeros((cells + 2 * OV, wide.shape[1] - lat), F32)
    tile_solve(wide, lat_basis, lon, scale, rows, spectral, first)
    to_outer, to_inner = pick(parity, first[cells - 1 :], first[: 2 * OV + 1])
    pack(inner, to_inner)
    pack(outer, to_outer)


def absorb(parity, first, inner_in, outer_in, coef, depth, u_h, c_rows, z_rows, d_rows, face_e, face_n, edge, u, sem):
    cells, lat = coef.shape
    copy = pltpu.make_async_copy(u_h, u, sem)
    copy.start()
    west, east = pick(parity, inner_in[: 2 * OV], outer_in[: 2 * OV])
    edge[...] = west[:OV]
    d_rows[:OV] = jnp.broadcast_to(west[KL : KL + 1], (OV, lat))
    d_rows[OV : OV + cells] = depth[...]
    d_rows[OV + cells :] = jnp.broadcast_to(east[2 * OV - 1 :], (OV, lat))
    c_rows[: 2 * OV] = west
    c_rows[: OV - 1] = jnp.zeros((OV - 1, lat), F32)
    c_rows[2 * OV : 2 * OV + cells] = coef[...]
    c_rows[2 * OV + cells :] = east
    c_rows[3 * OV + cells + 1 :] = jnp.zeros((OV - 1, lat), F32)
    z_rows[:OV] = jnp.zeros((OV, lat), F32)
    z_rows[3 * OV + cells :] = jnp.zeros((OV, lat), F32)
    inside = slice(OV, 3 * OV + cells)
    z_rows[inside] = jnp.where(c_rows[inside] > 0, first[...], 0.0)
    own = slice(OV, OV + cells)
    face_e[...] = jnp.minimum(d_rows[own], d_rows[OV + 1 : OV + cells + 1])
    zero = jnp.zeros((cells, 1), F32)
    face_n[...] = jnp.minimum(d_rows[own], jnp.concatenate([d_rows[own][:, 1:], zero], axis=1))
    copy.wait()


def second_solve(parity, outer_in, inner_in, z_rows, c_rows, lat_basis, lon, scale,
                 z, y, second, inner, outer, wide, rows, spectral):
    span, lat = y.shape
    cells = span - 2 * OV
    reach = 2 * OV + 1
    west, east = pick(parity, unpack(inner_in, reach, lat), unpack(outer_in, reach, lat))
    z[...] = z_rows[...]
    for came, start in ((west, OV - 1), (east, OV + cells)):
        at = slice(start, start + reach)
        z[at] += jnp.where(c_rows[at] > 0, came, 0.0)
    inside = slice(OV, OV + span)
    c, m = c_rows[inside], z[inside]
    beside = z[OV - 1 : OV - 1 + span] + z[OV + 1 : OV + 1 + span]
    image = jnp.where(c > 0, c * m - (beside + lat_beside(m)), 0.0)
    y[...] = image
    wide[:, :lat] = image
    wide[:, lat:] = jnp.zeros((span, wide.shape[1] - lat), F32)
    tile_solve(wide, lat_basis, lon, scale, rows, spectral, second)
    to_outer, to_inner = pick(parity, second[span - OV - 1 :], second[: OV + 1])
    pack(inner, to_inner)
    pack(outer, to_outer)


def dot(a, b):
    cells, lat = a.shape
    product = a * b
    rows = product[:OV]
    for at in range(OV, cells, OV):
        rows = rows + product[at : at + OV]
    whole = lat // LANE * LANE
    total = rows[:, :LANE]
    for at in range(LANE, whole, LANE):
        total = total + rows[:, at : at + LANE]
    if whole < lat:
        blank = jnp.zeros((OV, LANE - lat + whole), F32)
        total = total + jnp.concatenate([rows[:, whole:], blank], axis=1)
    return jnp.sum(jnp.sum(total, axis=0, keepdims=True), axis=1, keepdims=True)


def in_lanes(row, sums):
    lane = lax.broadcasted_iota(jnp.int32, row.shape, 1)
    for i, value in sums.items():
        row = jnp.where(lane == i, value, row)
    return row


def early_sums(z, y, c_rows, second, source, v_h, w_rows, masked, row, v, sem):
    copy = pltpu.make_async_copy(v_h, v, sem)
    copy.start()
    cells, lat = source.shape
    inside = slice(OV, 3 * OV + cells)
    w_rows[...] = jnp.where(c_rows[inside] > 0, second[...], 0.0)
    own = slice(2 * OV, 2 * OV + cells)
    wet = c_rows[own] > 0
    masked[...] = jnp.where(wet, source[...], 0.0)
    land = jnp.where(wet, 0.0, source[...])
    z_own = z[own]
    sums_of = {0: dot(masked[...], z_own), 1: dot(z_own, y[OV : OV + cells]), 6: dot(land, land)}
    row[...] = in_lanes(jnp.zeros((1, LANE), F32), sums_of)
    copy.wait()


def sums(parity, outer_in, inner_in, w_rows, z, y, c_rows, masked, row, w, sent):
    cells, lat = masked.shape
    west, east = pick(parity, unpack(inner_in, OV + 1, lat), unpack(outer_in, OV + 1, lat))
    w[...] = w_rows[...]
    for came, start in ((west, OV - 1), (east, cells)):
        wet = c_rows[OV + start : 2 * OV + start + 1] > 0
        w[start : start + OV + 1] += jnp.where(wet, came, 0.0)
    own = slice(OV, OV + cells)
    c, m = c_rows[2 * OV : 2 * OV + cells], w[own]
    beside = w[OV - 1 : OV - 1 + cells] + w[OV + 1 : OV + 1 + cells]
    x = jnp.where(c > 0, c * m - (beside + lat_beside(m)), 0.0)
    sums_of = {2: dot(masked[...], m), 3: dot(y[own], m), 4: dot(z[2 * OV : 2 * OV + cells], x), 5: dot(m, x)}
    sent[...] = jnp.broadcast_to(in_lanes(row[...], sums_of)[None], sent.shape)


def finish(came, z, w, d_rows, face_e, face_n, edge, source, u_vel, v_vel, solution, u_new, v_new, w_vel,
           s_rows, u_rows, v_out, w_out, s_out, sems):
    cells, lat = source.shape
    total = jnp.broadcast_to(jnp.sum(came[...], axis=0), (8, LANE))
    place = [lax.broadcasted_iota(jnp.int32, (8, LANE), axis) for axis in range(2)]
    total = jnp.sum(jnp.where(place[0] == place[1], total, 0.0), axis=1, keepdims=True)
    rz, zy, rw, yw, zx, wx, ll = [total[i : i + 1] for i in range(7)]
    step0 = (rz + ll) / (zy + ll)
    rest = (zy - rz) / (zy + ll)
    new = rz - step0 * (zy + rw) + step0 * step0 * yw + rest * rest * ll
    beta = new / (rz + ll)
    grown = 1.0 + beta
    bent = grown * grown * zy - grown * step0 * (zx + yw) + step0 * step0 * wx
    step1 = new / (bent + (rest + beta) * (rest + beta) * ll)
    of_z = jnp.broadcast_to(step0 + step1 * grown, (OV, lat))
    of_w = jnp.broadcast_to(-step1 * step0, (OV, lat))
    of_land = jnp.broadcast_to(step0 + step1 * (rest + beta), (OV, lat))

    copies = []

    def send(held, result):
        copies.append(pltpu.make_async_copy(held, result, sems.at[len(copies)]))
        copies[-1].start()

    def surface_rows(at):
        s = of_z * z[at + OV : at + 2 * OV] + of_w * w[at : at + OV]
        if OV <= at < OV + cells:
            s = jnp.where(d_rows[at : at + OV] > 0, s, of_land * source[at - OV : at])
            s_out[at - OV : at] = s
        s_rows[at : at + OV] = s

    surface_rows(0)
    surface_rows(OV)
    slope = jnp.broadcast_to(gravity_step * (s_rows[OV : OV + 1] - s_rows[OV - 1 : OV]), (OV, lat))
    d_west = jnp.broadcast_to(jnp.minimum(d_rows[OV - 1 : OV], d_rows[OV : OV + 1]), (OV, lat))
    levels = lax.broadcasted_iota(jnp.int32, (OV, lat), 0).astype(F32)
    left = jnp.where(d_west > levels, edge[...] - slope, 0.0)
    for level in range(KL):
        u_rows[level, OV - 1 : OV] = left[level : level + 1]
    zero = jnp.zeros((OV, 1), F32)
    for at in range(OV, OV + cells, OV):
        own = slice(at - OV, at)
        surface_rows(at + OV)
        s = s_rows[at : at + OV]
        d = d_rows[at : at + OV]
        slope = gravity_step * (s_rows[at + 1 : at + OV + 1] - s)
        face = face_e[own]
        for level in range(KL):
            u_rows[level, at : at + OV] = jnp.where(face > level, u_vel[level, own] - slope, 0.0)
        send(u_rows.at[:, at : at + OV], u_new.at[:, own])
        slope = gravity_step * (jnp.concatenate([s[:, 1:], zero], axis=1) - s)
        face = face_n[own]
        for level in range(KL):
            v_out[level, own] = jnp.where(face > level, v_vel[level, own] - slope, 0.0)
        send(v_out.at[:, own], v_new.at[:, own])
        w_sum = jnp.zeros((OV, lat), F32)
        for level in range(KL - 1, -1, -1):
            v = v_out[level, own]
            flow = u_rows[level, at : at + OV] - u_rows[level, at - 1 : at + OV - 1]
            flow = flow + (v - jnp.concatenate([zero, v[:, :-1]], axis=1))
            w_sum = w_sum + jnp.where(d > level, flow, 0.0)
            w_out[level, own] = w_sum
        send(w_out.at[:, own], w_vel.at[:, own])
        if at == cells:
            send(s_out, solution)
    for copy in copies:
        copy.wait()


def swap_pairs(block, outward):
    devices = lax.axis_size("lon")
    if outward:
        route = [(i, (i - 1 if i % 2 == 0 else i + 1) % devices) for i in range(devices)]
    else:
        route = [(i, i ^ 1) for i in range(devices)]
    return lax.ppermute(block, "lon", route)


def swap(inner, outer):
    outer = swap_pairs(outer, True)
    return outer, swap_pairs(inner, False)


def shape(*dims):
    return jax.ShapeDtypeStruct(dims, F32)


def body(source, diagonal, u_vel, v_vel, bottom):
    cells, lat = source.shape
    span = cells + 2 * OV
    devices = lax.axis_size("lon")
    parity = (lax.axis_index("lon") % 2).astype(jnp.int32).reshape(1)
    consts = [jnp.asarray(table) for table in tables(span)]
    hbm = {name: pltpu.with_memory_space_constraint(x, pltpu.HBM) for name, x in (
        ("source", source), ("diagonal", diagonal), ("u", u_vel), ("v", v_vel), ("bottom", bottom))}
    consts = [pltpu.with_memory_space_constraint(x, pltpu.HBM) for x in consts]

    outer, inner = pl.pallas_call(
        first_edges,
        in_specs=[SM, HB, HB],
        out_specs=[VM] * 2,
        out_shape=[pltpu.VMEM((OV, lat), F32)] * 2,
        scratch_shapes=[pltpu.VMEM((2, OV, lat), F32), pltpu.VMEM((2, OV, lat), jnp.int32),
                        pltpu.SemaphoreType.DMA((4,))],
        compiler_params=PARAMS,
        name="first_edges",
    )(parity, hbm["source"], hbm["bottom"])
    near = swap(inner, outer)

    far_inner, far_outer, masked, coef, depth, source_v, *held = pl.pallas_call(
        prepare,
        in_specs=[SM] + [HB] * 8,
        out_specs=[VM] * 9,
        out_shape=[pltpu.VMEM((FAR, lat), F32)] * 2
        + [pltpu.VMEM((cells, lat), F32)] * 4
        + [pltpu.VMEM(table.shape, table.dtype) for table in consts],
        scratch_shapes=[
            pltpu.VMEM((cells, lat), F32),
            pltpu.VMEM((cells, lat), jnp.int32),
            pltpu.VMEM((KL, OV, lat), F32),
            pltpu.SemaphoreType.DMA((7,)),
        ],
        compiler_params=PARAMS,
        cost_estimate=pl.CostEstimate(flops=10**6, bytes_accessed=7 * 10**6, transcendentals=0),
        name="prepare",
    )(parity, inner, hbm["source"], hbm["diagonal"], hbm["bottom"], hbm["u"], *consts)
    far = swap(far_inner, far_outer)[::-1]

    blocks = -(-lat // LANE)
    first, inner, outer = pl.pallas_call(
        first_solve,
        in_specs=[SM] + [VM] * 6,
        out_specs=[VM] * 3,
        out_shape=[pltpu.VMEM((span, lat), F32)] + [pltpu.VMEM(((2 * OV + 1) * blocks, LANE), F32)] * 2,
        scratch_shapes=solve_scratch(span, lat),
        compiler_params=PARAMS,
        name="first_solve",
    )(parity, *near, masked, *held)
    near = swap(inner, outer)

    c_rows, z_rows, d_rows, face_e, face_n, edge, u_v = pl.pallas_call(
        absorb,
        in_specs=[SM] + [VM] * 5 + [HB],
        out_specs=[VM] * 7,
        out_shape=[pltpu.VMEM((span + 2 * OV, lat), F32)] * 2
        + [pltpu.VMEM((span, lat), F32)]
        + [pltpu.VMEM((cells, lat), F32)] * 2
        + [pltpu.VMEM((OV, lat), F32), pltpu.VMEM((KL, cells, lat), F32)],
        scratch_shapes=[pltpu.SemaphoreType.DMA],
        compiler_params=PARAMS,
        cost_estimate=pl.CostEstimate(flops=10**6, bytes_accessed=7 * 10**6, transcendentals=0),
        name="absorb",
    )(parity, first, *far, coef, depth, hbm["u"])

    z, y, second, inner, outer = pl.pallas_call(
        second_solve,
        in_specs=[SM] + [VM] * 7,
        out_specs=[VM] * 5,
        out_shape=[pltpu.VMEM((span + 2 * OV, lat), F32)]
        + [pltpu.VMEM((span, lat), F32)] * 2
        + [pltpu.VMEM(((OV + 1) * blocks, LANE), F32)] * 2,
        scratch_shapes=solve_scratch(span, lat),
        compiler_params=PARAMS,
        name="second_solve",
    )(parity, *near, z_rows, c_rows, *held)
    near = swap(inner, outer)

    w_rows, masked, row, v_v = pl.pallas_call(
        early_sums,
        in_specs=[VM] * 5 + [HB],
        out_specs=[VM] * 4,
        out_shape=[pltpu.VMEM((span, lat), F32), pltpu.VMEM((cells, lat), F32), pltpu.VMEM((1, LANE), F32)]
        + [pltpu.VMEM((KL, cells, lat), F32)],
        scratch_shapes=[pltpu.SemaphoreType.DMA],
        compiler_params=PARAMS,
        cost_estimate=pl.CostEstimate(flops=10**6, bytes_accessed=7 * 10**6, transcendentals=0),
        name="early_sums",
    )(z, y, c_rows, second, source_v, hbm["v"])

    w, sent = pl.pallas_call(
        sums,
        in_specs=[SM] + [VM] * 8,
        out_specs=[VM] * 2,
        out_shape=[pltpu.VMEM((span, lat), F32), pltpu.VMEM((devices, 1, LANE), F32)],
        compiler_params=PARAMS,
        name="sums",
    )(parity, *near, w_rows, z, y, c_rows, masked, row)
    ring = [list(reversed(range(devices)))]
    came = lax.all_to_all(sent, "lon", 0, 0, axis_index_groups=ring)

    return pl.pallas_call(
        finish,
        in_specs=[VM] * 10,
        out_specs=[HB] * 4,
        out_shape=[shape(cells, lat)] + [shape(KL, cells, lat)] * 3,
        scratch_shapes=[pltpu.VMEM((span, lat), F32)]
        + [pltpu.VMEM((KL, OV + cells, lat), F32)]
        + [pltpu.VMEM((KL, cells, lat), F32)] * 2
        + [pltpu.VMEM((cells, lat), F32), pltpu.SemaphoreType.DMA((1 + 3 * (cells // OV),))],
        compiler_params=PARAMS,
        name="finish",
    )(came, z, w, d_rows, face_e, face_n, edge, source_v, u_v, v_v)


def solution(mesh):
    return jax.shard_map(
        body,
        mesh=mesh,
        in_specs=(
            P(("members", "lon"), None),
            P(("members", "lon"), None),
            P(None, ("members", "lon"), None),
            P(None, ("members", "lon"), None),
            P(("members", "lon"), None),
        ),
        out_specs=(
            P(("members", "lon"), None),
            P(None, ("members", "lon"), None),
            P(None, ("members", "lon"), None),
            P(None, ("members", "lon"), None),
        ),
        check_vma=False,
    )
```

```python
import math

import jax
import jax.numpy as jnp
import ml_dtypes
import numpy as np
from jax import lax
from jax.experimental import pallas as pl
from jax.experimental.pallas import tpu as pltpu
from jax.sharding import PartitionSpec as P

LT = 112
OV = 8
KL = 6
LANE = 128
FAR = 24

tile_shift = 0.1
gravity_step = 0.5

F32 = jnp.float32
BF16 = jnp.bfloat16
VM = pl.BlockSpec(memory_space=pltpu.VMEM)
SM = pl.BlockSpec(memory_space=pltpu.SMEM)
HB = pl.BlockSpec(memory_space=pl.ANY)
PARAMS = pltpu.CompilerParams(vmem_limit_bytes=32 * 1024 * 1024)


def sine_basis(length):
    ordinal = np.arange(length, dtype=np.float64) + 1.0
    angles = math.pi * ordinal[:, None] * ordinal[None, :] / (length + 1)
    basis_matrix = np.sqrt(2.0 / (length + 1)) * np.sin(angles)
    eigen_value = 2.0 - 2.0 * np.cos(math.pi * ordinal / (length + 1))
    return basis_matrix, eigen_value


def halves(matrix):
    high = matrix.astype(ml_dtypes.bfloat16)
    low = (matrix - high.astype(np.float64)).astype(ml_dtypes.bfloat16)
    return high, low


def tables(span):
    lon_basis, lon_value = sine_basis(span)
    lat_basis, lat_value = sine_basis(LT + 2 * OV)
    high, low = halves(lat_basis)
    lat = np.block([[high, low], [high, np.zeros_like(low)]])
    high, low = halves(lon_basis)
    lon = np.concatenate([high, low, high], axis=1)
    scale = 1.0 / (lon_value[:, None] + lat_value[None, :] + tile_shift)
    return lat, lon, scale.astype(np.float32)


def split(x):
    high = x.astype(BF16)
    return high, (x - high.astype(F32)).astype(BF16)


def tile_solve(x, lat_basis, lon, scale, rows, spectral, out):
    span, lat = out.shape
    tiles = lat // LT
    lane = lax.broadcasted_iota(jnp.int32, (span, LANE), 1)

    def block_of(b):
        if b < 0:
            return jnp.zeros((span, LANE), F32)
        return x[:, b * LANE : (b + 1) * LANE]

    chunk = 10
    groups = [range(first, min(first + chunk, tiles)) for first in range(0, tiles, chunk)]
    held = {}

    def lanes_of(group):
        return slice(group[0] * LANE, (group[-1] + 1) * LANE)

    def cut(group):
        for t in group:
            block, start = divmod(t * LT - OV, LANE)
            left, right = [pltpu.roll(block_of(b), LANE - start, 1) for b in (block, block + 1)]
            high, low = split(jnp.where(lane < LANE - start, left, right))
            rows[t * span : (t + 1) * span, :LANE] = high
            rows[t * span : (t + 1) * span, LANE:] = low

    def along_lat(group):
        product = jnp.dot(
            rows[group[0] * span : (group[-1] + 1) * span], lat_basis[...], preferred_element_type=F32
        )
        return product[:, :LANE] + product[:, LANE:]

    def lat_there(group):
        high, low = split(along_lat(group))
        for i, t in enumerate(group):
            at = slice(t * LANE, (t + 1) * LANE)
            spectral[:span, at] = high[i * span : (i + 1) * span]
            spectral[span : 2 * span, at] = high[i * span : (i + 1) * span]
            spectral[2 * span :, at] = low[i * span : (i + 1) * span]

    def lon_there(group):
        c = jnp.dot(lon[...], spectral[:, lanes_of(group)], preferred_element_type=F32)
        high, low = split(c * jnp.concatenate([scale[...]] * len(group), axis=1))
        spectral[:, lanes_of(group)] = jnp.concatenate([high, high, low], axis=0)

    def lon_back(group):
        c = jnp.dot(lon[...], spectral[:, lanes_of(group)], preferred_element_type=F32)
        high, low = split(c)
        for i, t in enumerate(group):
            at = slice(t * span, (t + 1) * span)
            rows[at, :LANE] = high[:, i * LANE : (i + 1) * LANE]
            rows[at, LANE:] = low[:, i * LANE : (i + 1) * LANE]

    def lat_back(group):
        product = along_lat(group)
        for i, t in enumerate(group):
            block, start = divmod(t * LT - OV, LANE)
            part = pltpu.roll(product[i * span : (i + 1) * span], start, 1)
            for b, inside in ((block, lane >= start), (block + 1, lane < start)):
                if 0 <= b * LANE < lat:
                    piece = jnp.where(inside, part, 0.0)
                    held[b] = held[b] + piece if b in held else piece
        done = (group[-1] + 1) * LT - OV if group[-1] + 1 < tiles else lat + LANE
        for b in [b for b in held if (b + 1) * LANE <= done]:
            width = min(LANE, lat - b * LANE)
            out[:, b * LANE : b * LANE + width] = held.pop(b)[:, :width]

    stages = [cut, lat_there, lon_there, lon_back, lat_back]
    for step in range(len(groups) + len(stages) - 1):
        for i in reversed(range(len(stages))):
            if 0 <= step - i < len(groups):
                stages[i](groups[step - i])


def wide_lanes(lat):
    return -(-(lat + OV) // LANE) * LANE


def solve_scratch(span, lat):
    tiles = lat // LT
    return [
        pltpu.VMEM((span, wide_lanes(lat)), F32),
        pltpu.VMEM((tiles * span, 2 * LANE), BF16),
        pltpu.VMEM((3 * span, tiles * LANE), BF16),
    ]


def pick(parity, inner, outer):
    even = jnp.full(inner.shape, parity[0], jnp.int32) == 0
    return jnp.where(even, outer, inner), jnp.where(even, inner, outer)


def lat_beside(m):
    zero = jnp.zeros((m.shape[0], 1), m.dtype)
    return jnp.concatenate([m[:, 1:], zero], axis=1) + jnp.concatenate([zero, m[:, :-1]], axis=1)


def pack(message, rows):
    n, lat = rows.shape
    for block, at in enumerate(range(0, lat, LANE)):
        width = min(LANE, lat - at)
        message[block * n : (block + 1) * n, :width] = rows[:, at : at + width]


def unpack(message, n, lat):
    blocks = [message[i * n : (i + 1) * n] for i in range(-(-lat // LANE))]
    return jnp.concatenate(blocks, axis=1)[:, :lat]


def first_edges(parity, source, bottom, outer, inner, rows, depth, sems):
    last = source.shape[0] - OV
    copies = []
    for i, start in enumerate((parity[0] * last, (1 - parity[0]) * last)):
        at = pl.ds(pl.multiple_of(start, OV), OV)
        copies.append(pltpu.make_async_copy(source.at[at], rows.at[i], sems.at[2 * i]))
        copies.append(pltpu.make_async_copy(bottom.at[at], depth.at[i], sems.at[2 * i + 1]))
    for copy in copies:
        copy.start()
    for copy in copies:
        copy.wait()
    outer[...] = jnp.where(depth[0] > 0, rows[0], 0.0)
    inner[...] = jnp.where(depth[1] > 0, rows[1], 0.0)


def prepare(parity, after, source_h, diagonal_h, bottom_h, u_h, *refs):
    tables_h, (far_inner, far_outer, masked, coef, depth, source), held = refs[:3], refs[3:9], refs[9:12]
    diagonal, bottom, u_strip, sems = refs[12:]
    cells, lat = source.shape
    pairs = [(source_h, source), (bottom_h, bottom), (diagonal_h, diagonal)]
    pairs += [(u_h.at[:, pl.ds(cells - OV, OV)], u_strip)]
    pairs += list(zip(tables_h, held))
    copies = [pltpu.make_async_copy(a, b, sems.at[i]) for i, (a, b) in enumerate(pairs)]
    for copy in copies:
        copy.start()
    for copy in copies[:4]:
        copy.wait()
    wet = bottom[...] > 0
    masked[...] = jnp.where(wet, source[...], 0.0)
    coef[...] = jnp.where(wet, 4.0 + diagonal[...], 0.0)
    depth[...] = bottom[...].astype(F32)
    edge = OV + 1
    blank = jnp.zeros((2 * OV - edge - 1, lat), F32)
    to_west = jnp.concatenate([coef[:edge], blank, depth[:1]], axis=0)
    u_rows = [u_strip[level, OV - 1 : OV] for level in range(KL)]
    to_east = jnp.concatenate(u_rows + [depth[cells - 1 :], coef[cells - edge :]], axis=0)
    far_outer[: 2 * OV], far_inner[: 2 * OV] = pick(parity, to_east, to_west)
    for message in (far_outer, far_inner):
        message[2 * OV :] = jnp.zeros((FAR - 2 * OV, lat), F32)
    for copy in copies[4:]:
        copy.wait()


def first_solve(parity, outer_in, inner_in, masked, lat_basis, lon, scale,
                first, inner, outer, wide, rows, spectral):
    cells, lat = masked.shape
    west, east = pick(parity, inner_in[...], outer_in[...])
    wide[:OV, :lat] = west
    wide[OV : OV + cells, :lat] = masked[...]
    wide[OV + cells :, :lat] = east
    wide[:, lat:] = jnp.zeros((cells + 2 * OV, wide.shape[1] - lat), F32)
    tile_solve(wide, lat_basis, lon, scale, rows, spectral, first)
    to_outer, to_inner = pick(parity, first[cells - 1 :], first[: 2 * OV + 1])
    pack(inner, to_inner)
    pack(outer, to_outer)


def absorb(parity, first, inner_in, outer_in, coef, depth, u_h, c_rows, z_rows, d_rows, face_e, face_n, edge, u, sem):
    cells, lat = coef.shape
    copy = pltpu.make_async_copy(u_h, u, sem)
    copy.start()
    west, east = pick(parity, inner_in[: 2 * OV], outer_in[: 2 * OV])
    edge[...] = west[:OV]
    d_rows[:OV] = jnp.broadcast_to(west[KL : KL + 1], (OV, lat))
    d_rows[OV : OV + cells] = depth[...]
    d_rows[OV + cells :] = jnp.broadcast_to(east[2 * OV - 1 :], (OV, lat))
    c_rows[: 2 * OV] = west
    c_rows[: OV - 1] = jnp.zeros((OV - 1, lat), F32)
    c_rows[2 * OV : 2 * OV + cells] = coef[...]
    c_rows[2 * OV + cells :] = east
    c_rows[3 * OV + cells + 1 :] = jnp.zeros((OV - 1, lat), F32)
    z_rows[:OV] = jnp.zeros((OV, lat), F32)
    z_rows[3 * OV + cells :] = jnp.zeros((OV, lat), F32)
    inside = slice(OV, 3 * OV + cells)
    z_rows[inside] = jnp.where(c_rows[inside] > 0, first[...], 0.0)
    own = slice(OV, OV + cells)
    face_e[...] = jnp.minimum(d_rows[own], d_rows[OV + 1 : OV + cells + 1])
    zero = jnp.zeros((cells, 1), F32)
    face_n[...] = jnp.minimum(d_rows[own], jnp.concatenate([d_rows[own][:, 1:], zero], axis=1))
    copy.wait()


def second_solve(parity, outer_in, inner_in, z_rows, c_rows, lat_basis, lon, scale,
                 z, y, second, inner, outer, wide, rows, spectral):
    span, lat = y.shape
    cells = span - 2 * OV
    reach = 2 * OV + 1
    west, east = pick(parity, unpack(inner_in, reach, lat), unpack(outer_in, reach, lat))
    z[...] = z_rows[...]
    for came, start in ((west, OV - 1), (east, OV + cells)):
        at = slice(start, start + reach)
        z[at] += jnp.where(c_rows[at] > 0, came, 0.0)
    inside = slice(OV, OV + span)
    c, m = c_rows[inside], z[inside]
    beside = z[OV - 1 : OV - 1 + span] + z[OV + 1 : OV + 1 + span]
    image = jnp.where(c > 0, c * m - (beside + lat_beside(m)), 0.0)
    y[...] = image
    wide[:, :lat] = image
    wide[:, lat:] = jnp.zeros((span, wide.shape[1] - lat), F32)
    tile_solve(wide, lat_basis, lon, scale, rows, spectral, second)
    to_outer, to_inner = pick(parity, second[span - OV - 1 :], second[: OV + 1])
    pack(inner, to_inner)
    pack(outer, to_outer)


def dot(a, b):
    cells, lat = a.shape
    product = a * b
    rows = product[:OV]
    for at in range(OV, cells, OV):
        rows = rows + product[at : at + OV]
    whole = lat // LANE * LANE
    total = rows[:, :LANE]
    for at in range(LANE, whole, LANE):
        total = total + rows[:, at : at + LANE]
    if whole < lat:
        blank = jnp.zeros((OV, LANE - lat + whole), F32)
        total = total + jnp.concatenate([rows[:, whole:], blank], axis=1)
    return jnp.sum(jnp.sum(total, axis=0, keepdims=True), axis=1, keepdims=True)


def in_lanes(row, sums):
    lane = lax.broadcasted_iota(jnp.int32, row.shape, 1)
    for i, value in sums.items():
        row = jnp.where(lane == i, value, row)
    return row


def early_sums(z, y, c_rows, second, source, v_h, w_rows, masked, row, v, sem):
    copy = pltpu.make_async_copy(v_h, v, sem)
    copy.start()
    cells, lat = source.shape
    inside = slice(OV, 3 * OV + cells)
    w_rows[...] = jnp.where(c_rows[inside] > 0, second[...], 0.0)
    own = slice(2 * OV, 2 * OV + cells)
    wet = c_rows[own] > 0
    masked[...] = jnp.where(wet, source[...], 0.0)
    land = jnp.where(wet, 0.0, source[...])
    z_own = z[own]
    sums_of = {0: dot(masked[...], z_own), 1: dot(z_own, y[OV : OV + cells]), 6: dot(land, land)}
    row[...] = in_lanes(jnp.zeros((1, LANE), F32), sums_of)
    copy.wait()


def sums(parity, outer_in, inner_in, w_rows, z, y, c_rows, masked, row, w, sent):
    cells, lat = masked.shape
    west, east = pick(parity, unpack(inner_in, OV + 1, lat), unpack(outer_in, OV + 1, lat))
    w[...] = w_rows[...]
    for came, start in ((west, OV - 1), (east, cells)):
        wet = c_rows[OV + start : 2 * OV + start + 1] > 0
        w[start : start + OV + 1] += jnp.where(wet, came, 0.0)
    own = slice(OV, OV + cells)
    c, m = c_rows[2 * OV : 2 * OV + cells], w[own]
    beside = w[OV - 1 : OV - 1 + cells] + w[OV + 1 : OV + 1 + cells]
    x = jnp.where(c > 0, c * m - (beside + lat_beside(m)), 0.0)
    sums_of = {2: dot(masked[...], m), 3: dot(y[own], m), 4: dot(z[2 * OV : 2 * OV + cells], x), 5: dot(m, x)}
    sent[...] = jnp.broadcast_to(in_lanes(row[...], sums_of)[None], sent.shape)


def finish(came, z, w, d_rows, face_e, face_n, edge, source, u_vel, v_vel, solution, u_new, v_new, w_vel,
           s_rows, u_rows, v_out, w_out, s_out, sems):
    cells, lat = source.shape
    total = jnp.broadcast_to(jnp.sum(came[...], axis=0), (8, LANE))
    place = [lax.broadcasted_iota(jnp.int32, (8, LANE), axis) for axis in range(2)]
    total = jnp.sum(jnp.where(place[0] == place[1], total, 0.0), axis=1, keepdims=True)
    rz, zy, rw, yw, zx, wx, ll = [total[i : i + 1] for i in range(7)]
    step0 = (rz + ll) / (zy + ll)
    rest = (zy - rz) / (zy + ll)
    new = rz - step0 * (zy + rw) + step0 * step0 * yw + rest * rest * ll
    beta = new / (rz + ll)
    grown = 1.0 + beta
    bent = grown * grown * zy - grown * step0 * (zx + yw) + step0 * step0 * wx
    step1 = new / (bent + (rest + beta) * (rest + beta) * ll)
    of_z = jnp.broadcast_to(step0 + step1 * grown, (OV, lat))
    of_w = jnp.broadcast_to(-step1 * step0, (OV, lat))
    of_land = jnp.broadcast_to(step0 + step1 * (rest + beta), (OV, lat))

    copies = []

    def send(held, result):
        copies.append(pltpu.make_async_copy(held, result, sems.at[len(copies)]))
        copies[-1].start()

    def surface_rows(at):
        s = of_z * z[at + OV : at + 2 * OV] + of_w * w[at : at + OV]
        if OV <= at < OV + cells:
            s = jnp.where(d_rows[at : at + OV] > 0, s, of_land * source[at - OV : at])
            s_out[at - OV : at] = s
        s_rows[at : at + OV] = s

    surface_rows(0)
    surface_rows(OV)
    slope = jnp.broadcast_to(gravity_step * (s_rows[OV : OV + 1] - s_rows[OV - 1 : OV]), (OV, lat))
    d_west = jnp.broadcast_to(jnp.minimum(d_rows[OV - 1 : OV], d_rows[OV : OV + 1]), (OV, lat))
    levels = lax.broadcasted_iota(jnp.int32, (OV, lat), 0).astype(F32)
    left = jnp.where(d_west > levels, edge[...] - slope, 0.0)
    for level in range(KL):
        u_rows[level, OV - 1 : OV] = left[level : level + 1]
    zero = jnp.zeros((OV, 1), F32)
    for at in range(OV, OV + cells, OV):
        own = slice(at - OV, at)
        surface_rows(at + OV)
        s = s_rows[at : at + OV]
        d = d_rows[at : at + OV]
        slope = gravity_step * (s_rows[at + 1 : at + OV + 1] - s)
        face = face_e[own]
        for level in range(KL):
            u_rows[level, at : at + OV] = jnp.where(face > level, u_vel[level, own] - slope, 0.0)
        send(u_rows.at[:, at : at + OV], u_new.at[:, own])
        slope = gravity_step * (jnp.concatenate([s[:, 1:], zero], axis=1) - s)
        face = face_n[own]
        for level in range(KL):
            v_out[level, own] = jnp.where(face > level, v_vel[level, own] - slope, 0.0)
        send(v_out.at[:, own], v_new.at[:, own])
        w_sum = jnp.zeros((OV, lat), F32)
        for level in range(KL - 1, -1, -1):
            v = v_out[level, own]
            flow = u_rows[level, at : at + OV] - u_rows[level, at - 1 : at + OV - 1]
            flow = flow + (v - jnp.concatenate([zero, v[:, :-1]], axis=1))
            w_sum = w_sum + jnp.where(d > level, flow, 0.0)
            w_out[level, own] = w_sum
        send(w_out.at[:, own], w_vel.at[:, own])
        if at == cells:
            send(s_out, solution)
    for copy in copies:
        copy.wait()


def swap_pairs(block, outward):
    devices = lax.axis_size("lon")
    if outward:
        route = [(i, (i - 1 if i % 2 == 0 else i + 1) % devices) for i in range(devices)]
    else:
        route = [(i, i ^ 1) for i in range(devices)]
    return lax.ppermute(block, "lon", route)


def swap(inner, outer):
    outer = swap_pairs(outer, True)
    return outer, swap_pairs(inner, False)


def shape(*dims):
    return jax.ShapeDtypeStruct(dims, F32)


def body(source, diagonal, u_vel, v_vel, bottom):
    cells, lat = source.shape
    span = cells + 2 * OV
    devices = lax.axis_size("lon")
    parity = (lax.axis_index("lon") % 2).astype(jnp.int32).reshape(1)
    consts = [jnp.asarray(table) for table in tables(span)]
    hbm = {name: pltpu.with_memory_space_constraint(x, pltpu.HBM) for name, x in (
        ("source", source), ("diagonal", diagonal), ("u", u_vel), ("v", v_vel), ("bottom", bottom))}
    consts = [pltpu.with_memory_space_constraint(x, pltpu.HBM) for x in consts]

    outer, inner = pl.pallas_call(
        first_edges,
        in_specs=[SM, HB, HB],
        out_specs=[VM] * 2,
        out_shape=[pltpu.VMEM((OV, lat), F32)] * 2,
        scratch_shapes=[pltpu.VMEM((2, OV, lat), F32), pltpu.VMEM((2, OV, lat), jnp.int32),
                        pltpu.SemaphoreType.DMA((4,))],
        compiler_params=PARAMS,
        name="first_edges",
    )(parity, hbm["source"], hbm["bottom"])
    near = swap(inner, outer)

    far_inner, far_outer, masked, coef, depth, source_v, *held = pl.pallas_call(
        prepare,
        in_specs=[SM] + [HB] * 8,
        out_specs=[VM] * 9,
        out_shape=[pltpu.VMEM((FAR, lat), F32)] * 2
        + [pltpu.VMEM((cells, lat), F32)] * 4
        + [pltpu.VMEM(table.shape, table.dtype) for table in consts],
        scratch_shapes=[
            pltpu.VMEM((cells, lat), F32),
            pltpu.VMEM((cells, lat), jnp.int32),
            pltpu.VMEM((KL, OV, lat), F32),
            pltpu.SemaphoreType.DMA((7,)),
        ],
        compiler_params=PARAMS,
        cost_estimate=pl.CostEstimate(flops=10**6, bytes_accessed=7 * 10**6, transcendentals=0),
        name="prepare",
    )(parity, inner, hbm["source"], hbm["diagonal"], hbm["bottom"], hbm["u"], *consts)
    far = swap(far_inner, far_outer)[::-1]

    blocks = -(-lat // LANE)
    first, inner, outer = pl.pallas_call(
        first_solve,
        in_specs=[SM] + [VM] * 6,
        out_specs=[VM] * 3,
        out_shape=[pltpu.VMEM((span, lat), F32)] + [pltpu.VMEM(((2 * OV + 1) * blocks, LANE), F32)] * 2,
        scratch_shapes=solve_scratch(span, lat),
        compiler_params=PARAMS,
        name="first_solve",
    )(parity, *near, masked, *held)
    near = swap(inner, outer)

    c_rows, z_rows, d_rows, face_e, face_n, edge, u_v = pl.pallas_call(
        absorb,
        in_specs=[SM] + [VM] * 5 + [HB],
        out_specs=[VM] * 7,
        out_shape=[pltpu.VMEM((span + 2 * OV, lat), F32)] * 2
        + [pltpu.VMEM((span, lat), F32)]
        + [pltpu.VMEM((cells, lat), F32)] * 2
        + [pltpu.VMEM((OV, lat), F32), pltpu.VMEM((KL, cells, lat), F32)],
        scratch_shapes=[pltpu.SemaphoreType.DMA],
        compiler_params=PARAMS,
        cost_estimate=pl.CostEstimate(flops=10**6, bytes_accessed=7 * 10**6, transcendentals=0),
        name="absorb",
    )(parity, first, *far, coef, depth, hbm["u"])

    z, y, second, inner, outer = pl.pallas_call(
        second_solve,
        in_specs=[SM] + [VM] * 7,
        out_specs=[VM] * 5,
        out_shape=[pltpu.VMEM((span + 2 * OV, lat), F32)]
        + [pltpu.VMEM((span, lat), F32)] * 2
        + [pltpu.VMEM(((OV + 1) * blocks, LANE), F32)] * 2,
        scratch_shapes=solve_scratch(span, lat),
        compiler_params=PARAMS,
        name="second_solve",
    )(parity, *near, z_rows, c_rows, *held)
    near = swap(inner, outer)

    w_rows, masked, row, v_v = pl.pallas_call(
        early_sums,
        in_specs=[VM] * 5 + [HB],
        out_specs=[VM] * 4,
        out_shape=[pltpu.VMEM((span, lat), F32), pltpu.VMEM((cells, lat), F32), pltpu.VMEM((1, LANE), F32)]
        + [pltpu.VMEM((KL, cells, lat), F32)],
        scratch_shapes=[pltpu.SemaphoreType.DMA],
        compiler_params=PARAMS,
        cost_estimate=pl.CostEstimate(flops=10**6, bytes_accessed=7 * 10**6, transcendentals=0),
        name="early_sums",
    )(z, y, c_rows, second, source_v, hbm["v"])

    w, sent = pl.pallas_call(
        sums,
        in_specs=[SM] + [VM] * 8,
        out_specs=[VM] * 2,
        out_shape=[pltpu.VMEM((span, lat), F32), pltpu.VMEM((devices, 1, LANE), F32)],
        compiler_params=PARAMS,
        name="sums",
    )(parity, *near, w_rows, z, y, c_rows, masked, row)
    ring = [list(reversed(range(devices)))]
    came = lax.all_to_all(sent, "lon", 0, 0, axis_index_groups=ring)

    return pl.pallas_call(
        finish,
        in_specs=[VM] * 10,
        out_specs=[HB] * 4,
        out_shape=[shape(cells, lat)] + [shape(KL, cells, lat)] * 3,
        scratch_shapes=[pltpu.VMEM((span, lat), F32)]
        + [pltpu.VMEM((KL, OV + cells, lat), F32)]
        + [pltpu.VMEM((KL, cells, lat), F32)] * 2
        + [pltpu.VMEM((cells, lat), F32), pltpu.SemaphoreType.DMA((1 + 3 * (cells // OV),))],
        compiler_params=PARAMS,
        name="finish",
    )(came, z, w, d_rows, face_e, face_n, edge, source_v, u_v, v_v)


def solution(mesh):
    return jax.shard_map(
        body,
        mesh=mesh,
        in_specs=(
            P(("members", "lon"), None),
            P(("members", "lon"), None),
            P(None, ("members", "lon"), None),
            P(None, ("members", "lon"), None),
            P(("members", "lon"), None),
        ),
        out_specs=(
            P(("members", "lon"), None),
            P(None, ("members", "lon"), None),
            P(None, ("members", "lon"), None),
            P(None, ("members", "lon"), None),
        ),
        check_vma=False,
    )
```

```python
import math

import jax
import jax.numpy as jnp
import ml_dtypes
import numpy as np
from jax import lax
from jax.experimental import pallas as pl
from jax.experimental.pallas import tpu as pltpu
from jax.sharding import PartitionSpec as P

LT = 112
OV = 8
KL = 6
LANE = 128
FAR = 24

tile_shift = 0.1
gravity_step = 0.5

F32 = jnp.float32
BF16 = jnp.bfloat16
VM = pl.BlockSpec(memory_space=pltpu.VMEM)
SM = pl.BlockSpec(memory_space=pltpu.SMEM)
HB = pl.BlockSpec(memory_space=pl.ANY)
PARAMS = pltpu.CompilerParams(vmem_limit_bytes=32 * 1024 * 1024)


def sine_basis(length):
    ordinal = np.arange(length, dtype=np.float64) + 1.0
    angles = math.pi * ordinal[:, None] * ordinal[None, :] / (length + 1)
    basis_matrix = np.sqrt(2.0 / (length + 1)) * np.sin(angles)
    eigen_value = 2.0 - 2.0 * np.cos(math.pi * ordinal / (length + 1))
    return basis_matrix, eigen_value


def halves(matrix):
    high = matrix.astype(ml_dtypes.bfloat16)
    low = (matrix - high.astype(np.float64)).astype(ml_dtypes.bfloat16)
    return high, low


def tables(span):
    lon_basis, lon_value = sine_basis(span)
    lat_basis, lat_value = sine_basis(LT + 2 * OV)
    high, low = halves(lat_basis)
    lat = np.block([[high, low], [high, np.zeros_like(low)]])
    high, low = halves(lon_basis)
    lon = np.concatenate([high, low, high], axis=1)
    scale = 1.0 / (lon_value[:, None] + lat_value[None, :] + tile_shift)
    return lat, lon, scale.astype(np.float32)


def split(x):
    high = x.astype(BF16)
    return high, (x - high.astype(F32)).astype(BF16)


def tile_solve(x, lat_basis, lon, scale, rows, spectral, out):
    span, lat = out.shape
    tiles = lat // LT
    lane = lax.broadcasted_iota(jnp.int32, (span, LANE), 1)

    def block_of(b):
        if b < 0:
            return jnp.zeros((span, LANE), F32)
        return x[:, b * LANE : (b + 1) * LANE]

    chunk = 20
    groups = [range(first, min(first + chunk, tiles)) for first in range(0, tiles, chunk)]
    held = {}

    def lanes_of(group):
        return slice(group[0] * LANE, (group[-1] + 1) * LANE)

    def cut(group):
        for t in group:
            block, start = divmod(t * LT - OV, LANE)
            left, right = [pltpu.roll(block_of(b), LANE - start, 1) for b in (block, block + 1)]
            high, low = split(jnp.where(lane < LANE - start, left, right))
            rows[t * span : (t + 1) * span, :LANE] = high
            rows[t * span : (t + 1) * span, LANE:] = low

    def along_lat(group):
        product = jnp.dot(
            rows[group[0] * span : (group[-1] + 1) * span], lat_basis[...], preferred_element_type=F32
        )
        return product[:, :LANE] + product[:, LANE:]

    def lat_there(group):
        high, low = split(along_lat(group))
        for i, t in enumerate(group):
            at = slice(t * LANE, (t + 1) * LANE)
            spectral[:span, at] = high[i * span : (i + 1) * span]
            spectral[span : 2 * span, at] = high[i * span : (i + 1) * span]
            spectral[2 * span :, at] = low[i * span : (i + 1) * span]

    def lon_there(group):
        c = jnp.dot(lon[...], spectral[:, lanes_of(group)], preferred_element_type=F32)
        high, low = split(c * jnp.concatenate([scale[...]] * len(group), axis=1))
        spectral[:, lanes_of(group)] = jnp.concatenate([high, high, low], axis=0)

    def lon_back(group):
        c = jnp.dot(lon[...], spectral[:, lanes_of(group)], preferred_element_type=F32)
        high, low = split(c)
        for i, t in enumerate(group):
            at = slice(t * span, (t + 1) * span)
            rows[at, :LANE] = high[:, i * LANE : (i + 1) * LANE]
            rows[at, LANE:] = low[:, i * LANE : (i + 1) * LANE]

    def lat_back(group):
        product = along_lat(group)
        for i, t in enumerate(group):
            block, start = divmod(t * LT - OV, LANE)
            part = pltpu.roll(product[i * span : (i + 1) * span], start, 1)
            for b, inside in ((block, lane >= start), (block + 1, lane < start)):
                if 0 <= b * LANE < lat:
                    piece = jnp.where(inside, part, 0.0)
                    held[b] = held[b] + piece if b in held else piece
        done = (group[-1] + 1) * LT - OV if group[-1] + 1 < tiles else lat + LANE
        for b in [b for b in held if (b + 1) * LANE <= done]:
            width = min(LANE, lat - b * LANE)
            out[:, b * LANE : b * LANE + width] = held.pop(b)[:, :width]

    stages = [cut, lat_there, lon_there, lon_back, lat_back]
    for step in range(len(groups) + len(stages) - 1):
        for i in reversed(range(len(stages))):
            if 0 <= step - i < len(groups):
                stages[i](groups[step - i])


def wide_lanes(lat):
    return -(-(lat + OV) // LANE) * LANE


def solve_scratch(span, lat):
    tiles = lat // LT
    return [
        pltpu.VMEM((span, wide_lanes(lat)), F32),
        pltpu.VMEM((tiles * span, 2 * LANE), BF16),
        pltpu.VMEM((3 * span, tiles * LANE), BF16),
    ]


def pick(parity, inner, outer):
    even = jnp.full(inner.shape, parity[0], jnp.int32) == 0
    return jnp.where(even, outer, inner), jnp.where(even, inner, outer)


def lat_beside(m):
    zero = jnp.zeros((m.shape[0], 1), m.dtype)
    return jnp.concatenate([m[:, 1:], zero], axis=1) + jnp.concatenate([zero, m[:, :-1]], axis=1)


def pack(message, rows):
    n, lat = rows.shape
    for block, at in enumerate(range(0, lat, LANE)):
        width = min(LANE, lat - at)
        message[block * n : (block + 1) * n, :width] = rows[:, at : at + width]


def unpack(message, n, lat):
    blocks = [message[i * n : (i + 1) * n] for i in range(-(-lat // LANE))]
    return jnp.concatenate(blocks, axis=1)[:, :lat]


def first_edges(parity, source, bottom, outer, inner, rows, depth, sems):
    last = source.shape[0] - OV
    copies = []
    for i, start in enumerate((parity[0] * last, (1 - parity[0]) * last)):
        at = pl.ds(pl.multiple_of(start, OV), OV)
        copies.append(pltpu.make_async_copy(source.at[at], rows.at[i], sems.at[2 * i]))
        copies.append(pltpu.make_async_copy(bottom.at[at], depth.at[i], sems.at[2 * i + 1]))
    for copy in copies:
        copy.start()
    for copy in copies:
        copy.wait()
    outer[...] = jnp.where(depth[0] > 0, rows[0], 0.0)
    inner[...] = jnp.where(depth[1] > 0, rows[1], 0.0)


def prepare(parity, after, source_h, diagonal_h, bottom_h, u_h, *refs):
    tables_h, (far_inner, far_outer, masked, coef, depth, source), held = refs[:3], refs[3:9], refs[9:12]
    diagonal, bottom, u_strip, sems = refs[12:]
    cells, lat = source.shape
    pairs = [(source_h, source), (bottom_h, bottom), (diagonal_h, diagonal)]
    pairs += [(u_h.at[:, pl.ds(cells - OV, OV)], u_strip)]
    pairs += list(zip(tables_h, held))
    copies = [pltpu.make_async_copy(a, b, sems.at[i]) for i, (a, b) in enumerate(pairs)]
    for copy in copies:
        copy.start()
    for copy in copies[:4]:
        copy.wait()
    wet = bottom[...] > 0
    masked[...] = jnp.where(wet, source[...], 0.0)
    coef[...] = jnp.where(wet, 4.0 + diagonal[...], 0.0)
    depth[...] = bottom[...].astype(F32)
    edge = OV + 1
    blank = jnp.zeros((2 * OV - edge - 1, lat), F32)
    to_west = jnp.concatenate([coef[:edge], blank, depth[:1]], axis=0)
    u_rows = [u_strip[level, OV - 1 : OV] for level in range(KL)]
    to_east = jnp.concatenate(u_rows + [depth[cells - 1 :], coef[cells - edge :]], axis=0)
    far_outer[: 2 * OV], far_inner[: 2 * OV] = pick(parity, to_east, to_west)
    for message in (far_outer, far_inner):
        message[2 * OV :] = jnp.zeros((FAR - 2 * OV, lat), F32)
    for copy in copies[4:]:
        copy.wait()


def first_solve(parity, outer_in, inner_in, masked, lat_basis, lon, scale,
                first, inner, outer, wide, rows, spectral):
    cells, lat = masked.shape
    west, east = pick(parity, inner_in[...], outer_in[...])
    wide[:OV, :lat] = west
    wide[OV : OV + cells, :lat] = masked[...]
    wide[OV + cells :, :lat] = east
    wide[:, lat:] = jnp.zeros((cells + 2 * OV, wide.shape[1] - lat), F32)
    tile_solve(wide, lat_basis, lon, scale, rows, spectral, first)
    to_outer, to_inner = pick(parity, first[cells - 1 :], first[: 2 * OV + 1])
    pack(inner, to_inner)
    pack(outer, to_outer)


def absorb(parity, first, inner_in, outer_in, coef, depth, u_h, c_rows, z_rows, d_rows, face_e, face_n, edge, u, sem):
    cells, lat = coef.shape
    copy = pltpu.make_async_copy(u_h, u, sem)
    copy.start()
    west, east = pick(parity, inner_in[: 2 * OV], outer_in[: 2 * OV])
    edge[...] = west[:OV]
    d_rows[:OV] = jnp.broadcast_to(west[KL : KL + 1], (OV, lat))
    d_rows[OV : OV + cells] = depth[...]
    d_rows[OV + cells :] = jnp.broadcast_to(east[2 * OV - 1 :], (OV, lat))
    c_rows[: 2 * OV] = west
    c_rows[: OV - 1] = jnp.zeros((OV - 1, lat), F32)
    c_rows[2 * OV : 2 * OV + cells] = coef[...]
    c_rows[2 * OV + cells :] = east
    c_rows[3 * OV + cells + 1 :] = jnp.zeros((OV - 1, lat), F32)
    z_rows[:OV] = jnp.zeros((OV, lat), F32)
    z_rows[3 * OV + cells :] = jnp.zeros((OV, lat), F32)
    inside = slice(OV, 3 * OV + cells)
    z_rows[inside] = jnp.where(c_rows[inside] > 0, first[...], 0.0)
    own = slice(OV, OV + cells)
    face_e[...] = jnp.minimum(d_rows[own], d_rows[OV + 1 : OV + cells + 1])
    zero = jnp.zeros((cells, 1), F32)
    face_n[...] = jnp.minimum(d_rows[own], jnp.concatenate([d_rows[own][:, 1:], zero], axis=1))
    copy.wait()


def second_solve(parity, outer_in, inner_in, z_rows, c_rows, lat_basis, lon, scale,
                 z, y, second, inner, outer, wide, rows, spectral):
    span, lat = y.shape
    cells = span - 2 * OV
    reach = 2 * OV + 1
    west, east = pick(parity, unpack(inner_in, reach, lat), unpack(outer_in, reach, lat))
    z[...] = z_rows[...]
    for came, start in ((west, OV - 1), (east, OV + cells)):
        at = slice(start, start + reach)
        z[at] += jnp.where(c_rows[at] > 0, came, 0.0)
    inside = slice(OV, OV + span)
    c, m = c_rows[inside], z[inside]
    beside = z[OV - 1 : OV - 1 + span] + z[OV + 1 : OV + 1 + span]
    image = jnp.where(c > 0, c * m - (beside + lat_beside(m)), 0.0)
    y[...] = image
    wide[:, :lat] = image
    wide[:, lat:] = jnp.zeros((span, wide.shape[1] - lat), F32)
    tile_solve(wide, lat_basis, lon, scale, rows, spectral, second)
    to_outer, to_inner = pick(parity, second[span - OV - 1 :], second[: OV + 1])
    pack(inner, to_inner)
    pack(outer, to_outer)


def dot(a, b):
    cells, lat = a.shape
    product = a * b
    rows = product[:OV]
    for at in range(OV, cells, OV):
        rows = rows + product[at : at + OV]
    whole = lat // LANE * LANE
    total = rows[:, :LANE]
    for at in range(LANE, whole, LANE):
        total = total + rows[:, at : at + LANE]
    if whole < lat:
        blank = jnp.zeros((OV, LANE - lat + whole), F32)
        total = total + jnp.concatenate([rows[:, whole:], blank], axis=1)
    return jnp.sum(jnp.sum(total, axis=0, keepdims=True), axis=1, keepdims=True)


def in_lanes(row, sums):
    lane = lax.broadcasted_iota(jnp.int32, row.shape, 1)
    for i, value in sums.items():
        row = jnp.where(lane == i, value, row)
    return row


def early_sums(z, y, c_rows, second, source, v_h, w_rows, masked, row, v, sem):
    copy = pltpu.make_async_copy(v_h, v, sem)
    copy.start()
    cells, lat = source.shape
    inside = slice(OV, 3 * OV + cells)
    w_rows[...] = jnp.where(c_rows[inside] > 0, second[...], 0.0)
    own = slice(2 * OV, 2 * OV + cells)
    wet = c_rows[own] > 0
    masked[...] = jnp.where(wet, source[...], 0.0)
    land = jnp.where(wet, 0.0, source[...])
    z_own = z[own]
    sums_of = {0: dot(masked[...], z_own), 1: dot(z_own, y[OV : OV + cells]), 6: dot(land, land)}
    row[...] = in_lanes(jnp.zeros((1, LANE), F32), sums_of)
    copy.wait()


def sums(parity, outer_in, inner_in, w_rows, z, y, c_rows, masked, row, w, sent):
    cells, lat = masked.shape
    west, east = pick(parity, unpack(inner_in, OV + 1, lat), unpack(outer_in, OV + 1, lat))
    w[...] = w_rows[...]
    for came, start in ((west, OV - 1), (east, cells)):
        wet = c_rows[OV + start : 2 * OV + start + 1] > 0
        w[start : start + OV + 1] += jnp.where(wet, came, 0.0)
    own = slice(OV, OV + cells)
    c, m = c_rows[2 * OV : 2 * OV + cells], w[own]
    beside = w[OV - 1 : OV - 1 + cells] + w[OV + 1 : OV + 1 + cells]
    x = jnp.where(c > 0, c * m - (beside + lat_beside(m)), 0.0)
    sums_of = {2: dot(masked[...], m), 3: dot(y[own], m), 4: dot(z[2 * OV : 2 * OV + cells], x), 5: dot(m, x)}
    sent[...] = jnp.broadcast_to(in_lanes(row[...], sums_of)[None], sent.shape)


def finish(came, z, w, d_rows, face_e, face_n, edge, source, u_vel, v_vel, solution, u_new, v_new, w_vel,
           s_rows, u_rows, v_out, w_out, s_out, sems):
    cells, lat = source.shape
    total = jnp.broadcast_to(jnp.sum(came[...], axis=0), (8, LANE))
    place = [lax.broadcasted_iota(jnp.int32, (8, LANE), axis) for axis in range(2)]
    total = jnp.sum(jnp.where(place[0] == place[1], total, 0.0), axis=1, keepdims=True)
    rz, zy, rw, yw, zx, wx, ll = [total[i : i + 1] for i in range(7)]
    step0 = (rz + ll) / (zy + ll)
    rest = (zy - rz) / (zy + ll)
    new = rz - step0 * (zy + rw) + step0 * step0 * yw + rest * rest * ll
    beta = new / (rz + ll)
    grown = 1.0 + beta
    bent = grown * grown * zy - grown * step0 * (zx + yw) + step0 * step0 * wx
    step1 = new / (bent + (rest + beta) * (rest + beta) * ll)
    of_z = jnp.broadcast_to(step0 + step1 * grown, (OV, lat))
    of_w = jnp.broadcast_to(-step1 * step0, (OV, lat))
    of_land = jnp.broadcast_to(step0 + step1 * (rest + beta), (OV, lat))

    copies = []

    def send(held, result):
        copies.append(pltpu.make_async_copy(held, result, sems.at[len(copies)]))
        copies[-1].start()

    def surface_rows(at):
        s = of_z * z[at + OV : at + 2 * OV] + of_w * w[at : at + OV]
        if OV <= at < OV + cells:
            s = jnp.where(d_rows[at : at + OV] > 0, s, of_land * source[at - OV : at])
            s_out[at - OV : at] = s
        s_rows[at : at + OV] = s

    surface_rows(0)
    surface_rows(OV)
    slope = jnp.broadcast_to(gravity_step * (s_rows[OV : OV + 1] - s_rows[OV - 1 : OV]), (OV, lat))
    d_west = jnp.broadcast_to(jnp.minimum(d_rows[OV - 1 : OV], d_rows[OV : OV + 1]), (OV, lat))
    levels = lax.broadcasted_iota(jnp.int32, (OV, lat), 0).astype(F32)
    left = jnp.where(d_west > levels, edge[...] - slope, 0.0)
    for level in range(KL):
        u_rows[level, OV - 1 : OV] = left[level : level + 1]
    zero = jnp.zeros((OV, 1), F32)
    for at in range(OV, OV + cells, OV):
        own = slice(at - OV, at)
        surface_rows(at + OV)
        s = s_rows[at : at + OV]
        d = d_rows[at : at + OV]
        slope = gravity_step * (s_rows[at + 1 : at + OV + 1] - s)
        face = face_e[own]
        for level in range(KL):
            u_rows[level, at : at + OV] = jnp.where(face > level, u_vel[level, own] - slope, 0.0)
        send(u_rows.at[:, at : at + OV], u_new.at[:, own])
        slope = gravity_step * (jnp.concatenate([s[:, 1:], zero], axis=1) - s)
        face = face_n[own]
        for level in range(KL):
            v_out[level, own] = jnp.where(face > level, v_vel[level, own] - slope, 0.0)
        send(v_out.at[:, own], v_new.at[:, own])
        w_sum = jnp.zeros((OV, lat), F32)
        for level in range(KL - 1, -1, -1):
            v = v_out[level, own]
            flow = u_rows[level, at : at + OV] - u_rows[level, at - 1 : at + OV - 1]
            flow = flow + (v - jnp.concatenate([zero, v[:, :-1]], axis=1))
            w_sum = w_sum + jnp.where(d > level, flow, 0.0)
            w_out[level, own] = w_sum
        send(w_out.at[:, own], w_vel.at[:, own])
        if at == cells:
            send(s_out, solution)
    for copy in copies:
        copy.wait()


def swap_pairs(block, outward):
    devices = lax.axis_size("lon")
    if outward:
        route = [(i, (i - 1 if i % 2 == 0 else i + 1) % devices) for i in range(devices)]
    else:
        route = [(i, i ^ 1) for i in range(devices)]
    return lax.ppermute(block, "lon", route)


def swap(inner, outer):
    outer = swap_pairs(outer, True)
    return outer, swap_pairs(inner, False)


def shape(*dims):
    return jax.ShapeDtypeStruct(dims, F32)


def body(source, diagonal, u_vel, v_vel, bottom):
    cells, lat = source.shape
    span = cells + 2 * OV
    devices = lax.axis_size("lon")
    parity = (lax.axis_index("lon") % 2).astype(jnp.int32).reshape(1)
    consts = [jnp.asarray(table) for table in tables(span)]
    hbm = {name: pltpu.with_memory_space_constraint(x, pltpu.HBM) for name, x in (
        ("source", source), ("diagonal", diagonal), ("u", u_vel), ("v", v_vel), ("bottom", bottom))}
    consts = [pltpu.with_memory_space_constraint(x, pltpu.HBM) for x in consts]

    outer, inner = pl.pallas_call(
        first_edges,
        in_specs=[SM, HB, HB],
        out_specs=[VM] * 2,
        out_shape=[pltpu.VMEM((OV, lat), F32)] * 2,
        scratch_shapes=[pltpu.VMEM((2, OV, lat), F32), pltpu.VMEM((2, OV, lat), jnp.int32),
                        pltpu.SemaphoreType.DMA((4,))],
        compiler_params=PARAMS,
        name="first_edges",
    )(parity, hbm["source"], hbm["bottom"])
    near = swap(inner, outer)

    far_inner, far_outer, masked, coef, depth, source_v, *held = pl.pallas_call(
        prepare,
        in_specs=[SM] + [HB] * 8,
        out_specs=[VM] * 9,
        out_shape=[pltpu.VMEM((FAR, lat), F32)] * 2
        + [pltpu.VMEM((cells, lat), F32)] * 4
        + [pltpu.VMEM(table.shape, table.dtype) for table in consts],
        scratch_shapes=[
            pltpu.VMEM((cells, lat), F32),
            pltpu.VMEM((cells, lat), jnp.int32),
            pltpu.VMEM((KL, OV, lat), F32),
            pltpu.SemaphoreType.DMA((7,)),
        ],
        compiler_params=PARAMS,
        cost_estimate=pl.CostEstimate(flops=10**6, bytes_accessed=7 * 10**6, transcendentals=0),
        name="prepare",
    )(parity, inner, hbm["source"], hbm["diagonal"], hbm["bottom"], hbm["u"], *consts)
    far = swap(far_inner, far_outer)[::-1]

    blocks = -(-lat // LANE)
    first, inner, outer = pl.pallas_call(
        first_solve,
        in_specs=[SM] + [VM] * 6,
        out_specs=[VM] * 3,
        out_shape=[pltpu.VMEM((span, lat), F32)] + [pltpu.VMEM(((2 * OV + 1) * blocks, LANE), F32)] * 2,
        scratch_shapes=solve_scratch(span, lat),
        compiler_params=PARAMS,
        name="first_solve",
    )(parity, *near, masked, *held)
    near = swap(inner, outer)

    c_rows, z_rows, d_rows, face_e, face_n, edge, u_v = pl.pallas_call(
        absorb,
        in_specs=[SM] + [VM] * 5 + [HB],
        out_specs=[VM] * 7,
        out_shape=[pltpu.VMEM((span + 2 * OV, lat), F32)] * 2
        + [pltpu.VMEM((span, lat), F32)]
        + [pltpu.VMEM((cells, lat), F32)] * 2
        + [pltpu.VMEM((OV, lat), F32), pltpu.VMEM((KL, cells, lat), F32)],
        scratch_shapes=[pltpu.SemaphoreType.DMA],
        compiler_params=PARAMS,
        cost_estimate=pl.CostEstimate(flops=10**6, bytes_accessed=7 * 10**6, transcendentals=0),
        name="absorb",
    )(parity, first, *far, coef, depth, hbm["u"])

    z, y, second, inner, outer = pl.pallas_call(
        second_solve,
        in_specs=[SM] + [VM] * 7,
        out_specs=[VM] * 5,
        out_shape=[pltpu.VMEM((span + 2 * OV, lat), F32)]
        + [pltpu.VMEM((span, lat), F32)] * 2
        + [pltpu.VMEM(((OV + 1) * blocks, LANE), F32)] * 2,
        scratch_shapes=solve_scratch(span, lat),
        compiler_params=PARAMS,
        name="second_solve",
    )(parity, *near, z_rows, c_rows, *held)
    near = swap(inner, outer)

    w_rows, masked, row, v_v = pl.pallas_call(
        early_sums,
        in_specs=[VM] * 5 + [HB],
        out_specs=[VM] * 4,
        out_shape=[pltpu.VMEM((span, lat), F32), pltpu.VMEM((cells, lat), F32), pltpu.VMEM((1, LANE), F32)]
        + [pltpu.VMEM((KL, cells, lat), F32)],
        scratch_shapes=[pltpu.SemaphoreType.DMA],
        compiler_params=PARAMS,
        cost_estimate=pl.CostEstimate(flops=10**6, bytes_accessed=7 * 10**6, transcendentals=0),
        name="early_sums",
    )(z, y, c_rows, second, source_v, hbm["v"])

    w, sent = pl.pallas_call(
        sums,
        in_specs=[SM] + [VM] * 8,
        out_specs=[VM] * 2,
        out_shape=[pltpu.VMEM((span, lat), F32), pltpu.VMEM((devices, 1, LANE), F32)],
        compiler_params=PARAMS,
        name="sums",
    )(parity, *near, w_rows, z, y, c_rows, masked, row)
    ring = [list(reversed(range(devices)))]
    came = lax.all_to_all(sent, "lon", 0, 0, axis_index_groups=ring)

    return pl.pallas_call(
        finish,
        in_specs=[VM] * 10,
        out_specs=[HB] * 4,
        out_shape=[shape(cells, lat)] + [shape(KL, cells, lat)] * 3,
        scratch_shapes=[pltpu.VMEM((span, lat), F32)]
        + [pltpu.VMEM((KL, OV + cells, lat), F32)]
        + [pltpu.VMEM((KL, cells, lat), F32)] * 2
        + [pltpu.VMEM((cells, lat), F32), pltpu.SemaphoreType.DMA((1 + 3 * (cells // OV),))],
        compiler_params=PARAMS,
        name="finish",
    )(came, z, w, d_rows, face_e, face_n, edge, source_v, u_v, v_v)


def solution(mesh):
    return jax.shard_map(
        body,
        mesh=mesh,
        in_specs=(
            P(("members", "lon"), None),
            P(("members", "lon"), None),
            P(None, ("members", "lon"), None),
            P(None, ("members", "lon"), None),
            P(("members", "lon"), None),
        ),
        out_specs=(
            P(("members", "lon"), None),
            P(None, ("members", "lon"), None),
            P(None, ("members", "lon"), None),
            P(None, ("members", "lon"), None),
        ),
        check_vma=False,
    )
```

```python
import math

import jax
import jax.numpy as jnp
import ml_dtypes
import numpy as np
from jax import lax
from jax.experimental import pallas as pl
from jax.experimental.pallas import tpu as pltpu
from jax.sharding import PartitionSpec as P

LT = 112
OV = 8
KL = 6
LANE = 128
FAR = 24

tile_shift = 0.1
gravity_step = 0.5

F32 = jnp.float32
BF16 = jnp.bfloat16
VM = pl.BlockSpec(memory_space=pltpu.VMEM)
SM = pl.BlockSpec(memory_space=pltpu.SMEM)
HB = pl.BlockSpec(memory_space=pl.ANY)
PARAMS = pltpu.CompilerParams(vmem_limit_bytes=32 * 1024 * 1024)


def sine_basis(length):
    ordinal = np.arange(length, dtype=np.float64) + 1.0
    angles = math.pi * ordinal[:, None] * ordinal[None, :] / (length + 1)
    basis_matrix = np.sqrt(2.0 / (length + 1)) * np.sin(angles)
    eigen_value = 2.0 - 2.0 * np.cos(math.pi * ordinal / (length + 1))
    return basis_matrix, eigen_value


def halves(matrix):
    high = matrix.astype(ml_dtypes.bfloat16)
    low = (matrix - high.astype(np.float64)).astype(ml_dtypes.bfloat16)
    return high, low


def tables(span):
    lon_basis, lon_value = sine_basis(span)
    lat_basis, lat_value = sine_basis(LT + 2 * OV)
    high, low = halves(lat_basis)
    lat = np.block([[high, low], [high, np.zeros_like(low)]])
    high, low = halves(lon_basis)
    lon = np.block([[high, high], [low, np.zeros_like(low)]])
    scale = 1.0 / (lon_value[:, None] + lat_value[None, :] + tile_shift)
    return lat, lon, scale.astype(np.float32)


def split(x):
    high = x.astype(BF16)
    return high, (x - high.astype(F32)).astype(BF16)


def tile_solve(x, lat_basis, lon, scale, rows, spectral, out):
    span, lat = out.shape
    tiles = lat // LT
    lane = lax.broadcasted_iota(jnp.int32, (span, LANE), 1)

    def block_of(b):
        if b < 0:
            return jnp.zeros((span, LANE), F32)
        return x[:, b * LANE : (b + 1) * LANE]

    chunk = 20
    groups = [range(first, min(first + chunk, tiles)) for first in range(0, tiles, chunk)]
    held = {}

    def lanes_of(group):
        return slice(group[0] * LANE, (group[-1] + 1) * LANE)

    def cut(group):
        for t in group:
            block, start = divmod(t * LT - OV, LANE)
            left, right = [pltpu.roll(block_of(b), LANE - start, 1) for b in (block, block + 1)]
            high, low = split(jnp.where(lane < LANE - start, left, right))
            rows[t * span : (t + 1) * span, :LANE] = high
            rows[t * span : (t + 1) * span, LANE:] = low

    def along_lat(group):
        product = jnp.dot(
            rows[group[0] * span : (group[-1] + 1) * span], lat_basis[...], preferred_element_type=F32
        )
        return product[:, :LANE] + product[:, LANE:]

    def along_lon(group):
        product = jnp.dot(lon[...], spectral[:, lanes_of(group)], preferred_element_type=F32)
        return product[:span] + product[span:]

    def lat_there(group):
        high, low = split(along_lat(group))
        for i, t in enumerate(group):
            at = slice(t * LANE, (t + 1) * LANE)
            spectral[:span, at] = high[i * span : (i + 1) * span]
            spectral[span:, at] = low[i * span : (i + 1) * span]

    def lon_there(group):
        c = along_lon(group)
        high, low = split(c * jnp.concatenate([scale[...]] * len(group), axis=1))
        spectral[:, lanes_of(group)] = jnp.concatenate([high, low], axis=0)

    def lon_back(group):
        high, low = split(along_lon(group))
        for i, t in enumerate(group):
            at = slice(t * span, (t + 1) * span)
            rows[at, :LANE] = high[:, i * LANE : (i + 1) * LANE]
            rows[at, LANE:] = low[:, i * LANE : (i + 1) * LANE]

    def lat_back(group):
        product = along_lat(group)
        for i, t in enumerate(group):
            block, start = divmod(t * LT - OV, LANE)
            part = pltpu.roll(product[i * span : (i + 1) * span], start, 1)
            for b, inside in ((block, lane >= start), (block + 1, lane < start)):
                if 0 <= b * LANE < lat:
                    piece = jnp.where(inside, part, 0.0)
                    held[b] = held[b] + piece if b in held else piece
        done = (group[-1] + 1) * LT - OV if group[-1] + 1 < tiles else lat + LANE
        for b in [b for b in held if (b + 1) * LANE <= done]:
            width = min(LANE, lat - b * LANE)
            out[:, b * LANE : b * LANE + width] = held.pop(b)[:, :width]

    stages = [cut, lat_there, lon_there, lon_back, lat_back]
    for step in range(len(groups) + len(stages) - 1):
        for i in reversed(range(len(stages))):
            if 0 <= step - i < len(groups):
                stages[i](groups[step - i])


def wide_lanes(lat):
    return -(-(lat + OV) // LANE) * LANE


def solve_scratch(span, lat):
    tiles = lat // LT
    return [
        pltpu.VMEM((span, wide_lanes(lat)), F32),
        pltpu.VMEM((tiles * span, 2 * LANE), BF16),
        pltpu.VMEM((2 * span, tiles * LANE), BF16),
    ]


def pick(parity, inner, outer):
    even = jnp.full(inner.shape, parity[0], jnp.int32) == 0
    return jnp.where(even, outer, inner), jnp.where(even, inner, outer)


def lat_beside(m):
    zero = jnp.zeros((m.shape[0], 1), m.dtype)
    return jnp.concatenate([m[:, 1:], zero], axis=1) + jnp.concatenate([zero, m[:, :-1]], axis=1)


def pack(message, rows):
    n, lat = rows.shape
    for block, at in enumerate(range(0, lat, LANE)):
        width = min(LANE, lat - at)
        message[block * n : (block + 1) * n, :width] = rows[:, at : at + width]


def unpack(message, n, lat):
    blocks = [message[i * n : (i + 1) * n] for i in range(-(-lat // LANE))]
    return jnp.concatenate(blocks, axis=1)[:, :lat]


def first_edges(parity, source, bottom, outer, inner, rows, depth, sems):
    last = source.shape[0] - OV
    copies = []
    for i, start in enumerate((parity[0] * last, (1 - parity[0]) * last)):
        at = pl.ds(pl.multiple_of(start, OV), OV)
        copies.append(pltpu.make_async_copy(source.at[at], rows.at[i], sems.at[2 * i]))
        copies.append(pltpu.make_async_copy(bottom.at[at], depth.at[i], sems.at[2 * i + 1]))
    for copy in copies:
        copy.start()
    for copy in copies:
        copy.wait()
    outer[...] = jnp.where(depth[0] > 0, rows[0], 0.0)
    inner[...] = jnp.where(depth[1] > 0, rows[1], 0.0)


def prepare(parity, after, source_h, diagonal_h, bottom_h, u_h, *refs):
    tables_h, (far_inner, far_outer, masked, coef, depth, source), held = refs[:3], refs[3:9], refs[9:12]
    diagonal, bottom, u_strip, sems = refs[12:]
    cells, lat = source.shape
    pairs = [(source_h, source), (bottom_h, bottom), (diagonal_h, diagonal)]
    pairs += [(u_h.at[:, pl.ds(cells - OV, OV)], u_strip)]
    pairs += list(zip(tables_h, held))
    copies = [pltpu.make_async_copy(a, b, sems.at[i]) for i, (a, b) in enumerate(pairs)]
    for copy in copies:
        copy.start()
    for copy in copies[:4]:
        copy.wait()
    wet = bottom[...] > 0
    masked[...] = jnp.where(wet, source[...], 0.0)
    coef[...] = jnp.where(wet, 4.0 + diagonal[...], 0.0)
    depth[...] = bottom[...].astype(F32)
    edge = OV + 1
    blank = jnp.zeros((2 * OV - edge - 1, lat), F32)
    to_west = jnp.concatenate([coef[:edge], blank, depth[:1]], axis=0)
    u_rows = [u_strip[level, OV - 1 : OV] for level in range(KL)]
    to_east = jnp.concatenate(u_rows + [depth[cells - 1 :], coef[cells - edge :]], axis=0)
    far_outer[: 2 * OV], far_inner[: 2 * OV] = pick(parity, to_east, to_west)
    for message in (far_outer, far_inner):
        message[2 * OV :] = jnp.zeros((FAR - 2 * OV, lat), F32)
    for copy in copies[4:]:
        copy.wait()


def first_solve(parity, outer_in, inner_in, masked, lat_basis, lon, scale,
                first, inner, outer, wide, rows, spectral):
    cells, lat = masked.shape
    west, east = pick(parity, inner_in[...], outer_in[...])
    wide[:OV, :lat] = west
    wide[OV : OV + cells, :lat] = masked[...]
    wide[OV + cells :, :lat] = east
    wide[:, lat:] = jnp.zeros((cells + 2 * OV, wide.shape[1] - lat), F32)
    tile_solve(wide, lat_basis, lon, scale, rows, spectral, first)
    to_outer, to_inner = pick(parity, first[cells - 1 :], first[: 2 * OV + 1])
    pack(inner, to_inner)
    pack(outer, to_outer)


def absorb(parity, first, inner_in, outer_in, coef, depth, u_h, c_rows, z_rows, d_rows, face_e, face_n, edge, u, sem):
    cells, lat = coef.shape
    copy = pltpu.make_async_copy(u_h, u, sem)
    copy.start()
    west, east = pick(parity, inner_in[: 2 * OV], outer_in[: 2 * OV])
    edge[...] = west[:OV]
    d_rows[:OV] = jnp.broadcast_to(west[KL : KL + 1], (OV, lat))
    d_rows[OV : OV + cells] = depth[...]
    d_rows[OV + cells :] = jnp.broadcast_to(east[2 * OV - 1 :], (OV, lat))
    c_rows[: 2 * OV] = west
    c_rows[: OV - 1] = jnp.zeros((OV - 1, lat), F32)
    c_rows[2 * OV : 2 * OV + cells] = coef[...]
    c_rows[2 * OV + cells :] = east
    c_rows[3 * OV + cells + 1 :] = jnp.zeros((OV - 1, lat), F32)
    z_rows[:OV] = jnp.zeros((OV, lat), F32)
    z_rows[3 * OV + cells :] = jnp.zeros((OV, lat), F32)
    inside = slice(OV, 3 * OV + cells)
    z_rows[inside] = jnp.where(c_rows[inside] > 0, first[...], 0.0)
    own = slice(OV, OV + cells)
    face_e[...] = jnp.minimum(d_rows[own], d_rows[OV + 1 : OV + cells + 1])
    zero = jnp.zeros((cells, 1), F32)
    face_n[...] = jnp.minimum(d_rows[own], jnp.concatenate([d_rows[own][:, 1:], zero], axis=1))
    copy.wait()


def second_solve(parity, outer_in, inner_in, z_rows, c_rows, lat_basis, lon, scale,
                 z, y, second, inner, outer, wide, rows, spectral):
    span, lat = y.shape
    cells = span - 2 * OV
    reach = 2 * OV + 1
    west, east = pick(parity, unpack(inner_in, reach, lat), unpack(outer_in, reach, lat))
    z[...] = z_rows[...]
    for came, start in ((west, OV - 1), (east, OV + cells)):
        at = slice(start, start + reach)
        z[at] += jnp.where(c_rows[at] > 0, came, 0.0)
    inside = slice(OV, OV + span)
    c, m = c_rows[inside], z[inside]
    beside = z[OV - 1 : OV - 1 + span] + z[OV + 1 : OV + 1 + span]
    image = jnp.where(c > 0, c * m - (beside + lat_beside(m)), 0.0)
    y[...] = image
    wide[:, :lat] = image
    wide[:, lat:] = jnp.zeros((span, wide.shape[1] - lat), F32)
    tile_solve(wide, lat_basis, lon, scale, rows, spectral, second)
    to_outer, to_inner = pick(parity, second[span - OV - 1 :], second[: OV + 1])
    pack(inner, to_inner)
    pack(outer, to_outer)


def dot(a, b):
    cells, lat = a.shape
    product = a * b
    rows = product[:OV]
    for at in range(OV, cells, OV):
        rows = rows + product[at : at + OV]
    whole = lat // LANE * LANE
    total = rows[:, :LANE]
    for at in range(LANE, whole, LANE):
        total = total + rows[:, at : at + LANE]
    if whole < lat:
        blank = jnp.zeros((OV, LANE - lat + whole), F32)
        total = total + jnp.concatenate([rows[:, whole:], blank], axis=1)
    return jnp.sum(jnp.sum(total, axis=0, keepdims=True), axis=1, keepdims=True)


def in_lanes(row, sums):
    lane = lax.broadcasted_iota(jnp.int32, row.shape, 1)
    for i, value in sums.items():
        row = jnp.where(lane == i, value, row)
    return row


def early_sums(z, y, c_rows, second, source, v_h, w_rows, masked, row, v, sem):
    copy = pltpu.make_async_copy(v_h, v, sem)
    copy.start()
    cells, lat = source.shape
    inside = slice(OV, 3 * OV + cells)
    w_rows[...] = jnp.where(c_rows[inside] > 0, second[...], 0.0)
    own = slice(2 * OV, 2 * OV + cells)
    wet = c_rows[own] > 0
    masked[...] = jnp.where(wet, source[...], 0.0)
    land = jnp.where(wet, 0.0, source[...])
    z_own = z[own]
    sums_of = {0: dot(masked[...], z_own), 1: dot(z_own, y[OV : OV + cells]), 6: dot(land, land)}
    row[...] = in_lanes(jnp.zeros((1, LANE), F32), sums_of)
    copy.wait()


def sums(parity, outer_in, inner_in, w_rows, z, y, c_rows, masked, row, w, sent):
    cells, lat = masked.shape
    west, east = pick(parity, unpack(inner_in, OV + 1, lat), unpack(outer_in, OV + 1, lat))
    w[...] = w_rows[...]
    for came, start in ((west, OV - 1), (east, cells)):
        wet = c_rows[OV + start : 2 * OV + start + 1] > 0
        w[start : start + OV + 1] += jnp.where(wet, came, 0.0)
    own = slice(OV, OV + cells)
    c, m = c_rows[2 * OV : 2 * OV + cells], w[own]
    beside = w[OV - 1 : OV - 1 + cells] + w[OV + 1 : OV + 1 + cells]
    x = jnp.where(c > 0, c * m - (beside + lat_beside(m)), 0.0)
    sums_of = {2: dot(masked[...], m), 3: dot(y[own], m), 4: dot(z[2 * OV : 2 * OV + cells], x), 5: dot(m, x)}
    sent[...] = jnp.broadcast_to(in_lanes(row[...], sums_of)[None], sent.shape)


def finish(came, z, w, d_rows, face_e, face_n, edge, source, u_vel, v_vel, solution, u_new, v_new, w_vel,
           s_rows, u_rows, v_out, w_out, s_out, sems):
    cells, lat = source.shape
    total = jnp.broadcast_to(jnp.sum(came[...], axis=0), (8, LANE))
    place = [lax.broadcasted_iota(jnp.int32, (8, LANE), axis) for axis in range(2)]
    total = jnp.sum(jnp.where(place[0] == place[1], total, 0.0), axis=1, keepdims=True)
    rz, zy, rw, yw, zx, wx, ll = [total[i : i + 1] for i in range(7)]
    step0 = (rz + ll) / (zy + ll)
    rest = (zy - rz) / (zy + ll)
    new = rz - step0 * (zy + rw) + step0 * step0 * yw + rest * rest * ll
    beta = new / (rz + ll)
    grown = 1.0 + beta
    bent = grown * grown * zy - grown * step0 * (zx + yw) + step0 * step0 * wx
    step1 = new / (bent + (rest + beta) * (rest + beta) * ll)
    of_z = jnp.broadcast_to(step0 + step1 * grown, (OV, lat))
    of_w = jnp.broadcast_to(-step1 * step0, (OV, lat))
    of_land = jnp.broadcast_to(step0 + step1 * (rest + beta), (OV, lat))

    copies = []

    def send(held, result):
        copies.append(pltpu.make_async_copy(held, result, sems.at[len(copies)]))
        copies[-1].start()

    def surface_rows(at):
        s = of_z * z[at + OV : at + 2 * OV] + of_w * w[at : at + OV]
        if OV <= at < OV + cells:
            s = jnp.where(d_rows[at : at + OV] > 0, s, of_land * source[at - OV : at])
            s_out[at - OV : at] = s
        s_rows[at : at + OV] = s

    surface_rows(0)
    surface_rows(OV)
    slope = jnp.broadcast_to(gravity_step * (s_rows[OV : OV + 1] - s_rows[OV - 1 : OV]), (OV, lat))
    d_west = jnp.broadcast_to(jnp.minimum(d_rows[OV - 1 : OV], d_rows[OV : OV + 1]), (OV, lat))
    levels = lax.broadcasted_iota(jnp.int32, (OV, lat), 0).astype(F32)
    left = jnp.where(d_west > levels, edge[...] - slope, 0.0)
    for level in range(KL):
        u_rows[level, OV - 1 : OV] = left[level : level + 1]
    zero = jnp.zeros((OV, 1), F32)
    for at in range(OV, OV + cells, OV):
        own = slice(at - OV, at)
        surface_rows(at + OV)
        s = s_rows[at : at + OV]
        d = d_rows[at : at + OV]
        slope = gravity_step * (s_rows[at + 1 : at + OV + 1] - s)
        face = face_e[own]
        for level in range(KL):
            u_rows[level, at : at + OV] = jnp.where(face > level, u_vel[level, own] - slope, 0.0)
        send(u_rows.at[:, at : at + OV], u_new.at[:, own])
        slope = gravity_step * (jnp.concatenate([s[:, 1:], zero], axis=1) - s)
        face = face_n[own]
        for level in range(KL):
            v_out[level, own] = jnp.where(face > level, v_vel[level, own] - slope, 0.0)
        send(v_out.at[:, own], v_new.at[:, own])
        w_sum = jnp.zeros((OV, lat), F32)
        for level in range(KL - 1, -1, -1):
            v = v_out[level, own]
            flow = u_rows[level, at : at + OV] - u_rows[level, at - 1 : at + OV - 1]
            flow = flow + (v - jnp.concatenate([zero, v[:, :-1]], axis=1))
            w_sum = w_sum + jnp.where(d > level, flow, 0.0)
            w_out[level, own] = w_sum
        send(w_out.at[:, own], w_vel.at[:, own])
        if at == cells:
            send(s_out, solution)
    for copy in copies:
        copy.wait()


def swap_pairs(block, outward):
    devices = lax.axis_size("lon")
    if outward:
        route = [(i, (i - 1 if i % 2 == 0 else i + 1) % devices) for i in range(devices)]
    else:
        route = [(i, i ^ 1) for i in range(devices)]
    return lax.ppermute(block, "lon", route)


def swap(inner, outer):
    outer = swap_pairs(outer, True)
    return outer, swap_pairs(inner, False)


def shape(*dims):
    return jax.ShapeDtypeStruct(dims, F32)


def body(source, diagonal, u_vel, v_vel, bottom):
    cells, lat = source.shape
    span = cells + 2 * OV
    devices = lax.axis_size("lon")
    parity = (lax.axis_index("lon") % 2).astype(jnp.int32).reshape(1)
    consts = [jnp.asarray(table) for table in tables(span)]
    hbm = {name: pltpu.with_memory_space_constraint(x, pltpu.HBM) for name, x in (
        ("source", source), ("diagonal", diagonal), ("u", u_vel), ("v", v_vel), ("bottom", bottom))}
    consts = [pltpu.with_memory_space_constraint(x, pltpu.HBM) for x in consts]

    outer, inner = pl.pallas_call(
        first_edges,
        in_specs=[SM, HB, HB],
        out_specs=[VM] * 2,
        out_shape=[pltpu.VMEM((OV, lat), F32)] * 2,
        scratch_shapes=[pltpu.VMEM((2, OV, lat), F32), pltpu.VMEM((2, OV, lat), jnp.int32),
                        pltpu.SemaphoreType.DMA((4,))],
        compiler_params=PARAMS,
        name="first_edges",
    )(parity, hbm["source"], hbm["bottom"])
    near = swap(inner, outer)

    far_inner, far_outer, masked, coef, depth, source_v, *held = pl.pallas_call(
        prepare,
        in_specs=[SM] + [HB] * 8,
        out_specs=[VM] * 9,
        out_shape=[pltpu.VMEM((FAR, lat), F32)] * 2
        + [pltpu.VMEM((cells, lat), F32)] * 4
        + [pltpu.VMEM(table.shape, table.dtype) for table in consts],
        scratch_shapes=[
            pltpu.VMEM((cells, lat), F32),
            pltpu.VMEM((cells, lat), jnp.int32),
            pltpu.VMEM((KL, OV, lat), F32),
            pltpu.SemaphoreType.DMA((7,)),
        ],
        compiler_params=PARAMS,
        cost_estimate=pl.CostEstimate(flops=10**6, bytes_accessed=7 * 10**6, transcendentals=0),
        name="prepare",
    )(parity, inner, hbm["source"], hbm["diagonal"], hbm["bottom"], hbm["u"], *consts)
    far = swap(far_inner, far_outer)[::-1]

    blocks = -(-lat // LANE)
    first, inner, outer = pl.pallas_call(
        first_solve,
        in_specs=[SM] + [VM] * 6,
        out_specs=[VM] * 3,
        out_shape=[pltpu.VMEM((span, lat), F32)] + [pltpu.VMEM(((2 * OV + 1) * blocks, LANE), F32)] * 2,
        scratch_shapes=solve_scratch(span, lat),
        compiler_params=PARAMS,
        name="first_solve",
    )(parity, *near, masked, *held)
    near = swap(inner, outer)

    c_rows, z_rows, d_rows, face_e, face_n, edge, u_v = pl.pallas_call(
        absorb,
        in_specs=[SM] + [VM] * 5 + [HB],
        out_specs=[VM] * 7,
        out_shape=[pltpu.VMEM((span + 2 * OV, lat), F32)] * 2
        + [pltpu.VMEM((span, lat), F32)]
        + [pltpu.VMEM((cells, lat), F32)] * 2
        + [pltpu.VMEM((OV, lat), F32), pltpu.VMEM((KL, cells, lat), F32)],
        scratch_shapes=[pltpu.SemaphoreType.DMA],
        compiler_params=PARAMS,
        cost_estimate=pl.CostEstimate(flops=10**6, bytes_accessed=7 * 10**6, transcendentals=0),
        name="absorb",
    )(parity, first, *far, coef, depth, hbm["u"])

    z, y, second, inner, outer = pl.pallas_call(
        second_solve,
        in_specs=[SM] + [VM] * 7,
        out_specs=[VM] * 5,
        out_shape=[pltpu.VMEM((span + 2 * OV, lat), F32)]
        + [pltpu.VMEM((span, lat), F32)] * 2
        + [pltpu.VMEM(((OV + 1) * blocks, LANE), F32)] * 2,
        scratch_shapes=solve_scratch(span, lat),
        compiler_params=PARAMS,
        name="second_solve",
    )(parity, *near, z_rows, c_rows, *held)
    near = swap(inner, outer)

    w_rows, masked, row, v_v = pl.pallas_call(
        early_sums,
        in_specs=[VM] * 5 + [HB],
        out_specs=[VM] * 4,
        out_shape=[pltpu.VMEM((span, lat), F32), pltpu.VMEM((cells, lat), F32), pltpu.VMEM((1, LANE), F32)]
        + [pltpu.VMEM((KL, cells, lat), F32)],
        scratch_shapes=[pltpu.SemaphoreType.DMA],
        compiler_params=PARAMS,
        cost_estimate=pl.CostEstimate(flops=10**6, bytes_accessed=7 * 10**6, transcendentals=0),
        name="early_sums",
    )(z, y, c_rows, second, source_v, hbm["v"])

    w, sent = pl.pallas_call(
        sums,
        in_specs=[SM] + [VM] * 8,
        out_specs=[VM] * 2,
        out_shape=[pltpu.VMEM((span, lat), F32), pltpu.VMEM((devices, 1, LANE), F32)],
        compiler_params=PARAMS,
        name="sums",
    )(parity, *near, w_rows, z, y, c_rows, masked, row)
    ring = [list(reversed(range(devices)))]
    came = lax.all_to_all(sent, "lon", 0, 0, axis_index_groups=ring)

    return pl.pallas_call(
        finish,
        in_specs=[VM] * 10,
        out_specs=[HB] * 4,
        out_shape=[shape(cells, lat)] + [shape(KL, cells, lat)] * 3,
        scratch_shapes=[pltpu.VMEM((span, lat), F32)]
        + [pltpu.VMEM((KL, OV + cells, lat), F32)]
        + [pltpu.VMEM((KL, cells, lat), F32)] * 2
        + [pltpu.VMEM((cells, lat), F32), pltpu.SemaphoreType.DMA((1 + 3 * (cells // OV),))],
        compiler_params=PARAMS,
        name="finish",
    )(came, z, w, d_rows, face_e, face_n, edge, source_v, u_v, v_v)


def solution(mesh):
    return jax.shard_map(
        body,
        mesh=mesh,
        in_specs=(
            P(("members", "lon"), None),
            P(("members", "lon"), None),
            P(None, ("members", "lon"), None),
            P(None, ("members", "lon"), None),
            P(("members", "lon"), None),
        ),
        out_specs=(
            P(("members", "lon"), None),
            P(None, ("members", "lon"), None),
            P(None, ("members", "lon"), None),
            P(None, ("members", "lon"), None),
        ),
        check_vma=False,
    )
```
